32 devices in a mesh: leaf: 8 (over z, y), rhs: 4 (over x, core).
Axes of the slice: x: 2, y: 2, z: 4, core: 2. Of those that a mesh axis runs over, the one named last changes fastest.
Arguments:
- densities: bfloat16 [64, 32768], P('rhs', 'leaf'), may hold values from -6 to 6
- bases: float32 [32, 32768], P(None, 'leaf'), may hold values from -0.5 to 0.5
- near_blocks: bfloat16 [256, 8, 128, 128], P('leaf', 'rhs'), may hold values from -0.1875 to 0.1875
- near_src: int32 [256, 8], P('leaf', 'rhs'), may hold values from 0 to 55, as said below
- send_leaf: int32 [8, 6, 4], replicated, may hold values from -1 to 31, as said below
- far_src: int32 [256, 8], P('leaf'), may hold values from 0 to 31
- leaf_coupling: float32 [256, 8, 32, 32], P('leaf'), may hold values from -0.375 to 0.375
- local_transfer: float32 [8, 64, 32, 32], P('leaf'), may hold values from -0.75 to 0.75
- upper_transfer: float32 [16, 32, 32], replicated, may hold values from -0.75 to 0.75
- up_coupling: float32 [16, 3, 32, 32], replicated, may hold values from -8 to 8
Outputs:
- product: float32 [64, 32768], P('rhs', 'leaf')
The draws below stay inside these ranges and needn't reach their ends.
Inputs may be any that keep to these rules, and one draw needn't show every extreme that they name: `send_leaf`: entry [e, j, c] is a leaf of device e (local index) whose panel e sends to its face neighbour e + o_j, or -1. Only existing face neighbours receive; the leaves of [e, j] are distinct and come before the -1 entries; every device sends exactly 4 leaves to at least one neighbour, among them its leaf 32 - 1, and exactly 4 to its neighbour at offset -s*s where that exists. `near_src`: A slot of the owner's panel buffer: below 32 a leaf of the same device, else slot 32 + j * 4 + c. It never names an empty slot, and every filled slot is named by some block of the device.
All inputs are finite; a program needn't handle non-finite values.
Results may differ from the reference program's by a relative error of at most 0.0003.
Values may be sent and summed in bfloat16 or wider, within the bound.
No kernel may reach another device: no remote copies, remote signals or barrier semaphores. Data moves between devices by JAX's collectives and lax.ppermute only.
A program may use at most 128 MiB of HBM per device.

```python
import jax
import jax.numpy as jnp
from jax import lax

LEAF_SIZE = 128
RANK = 32
RHS = 64
NEAR = 8
FAR = 8
CAP = 4
LEAVES_DEV = 32
LEAVES = 256
POINTS = 32768
N_LEAF = 8


def cube_side_drawn(device_count):
    return max((edge_len for edge_len in range(1, 65) if edge_len ** 3 <= device_count))


def routing_tables(key):
    side_len = cube_side_drawn(N_LEAF)
    device_ids = jnp.arange(N_LEAF, dtype=jnp.int32)
    coord_x = device_ids % side_len
    coord_y = device_ids // side_len % side_len
    coord_z = device_ids // (side_len * side_len)
    exists = jnp.stack([coord_x < side_len - 1, coord_x > 0, coord_y < side_len - 1, coord_y > 0, coord_z < side_len - 1, coord_z > 0], axis=1)
    base_key = jax.random.fold_in(key, 4242)
    key_count, key_force, key_order, key_pick = jax.random.split(base_key, 4)
    counts = jax.random.randint(key_count, (N_LEAF, 6), 1, CAP + 1)
    forced = jax.random.randint(key_force, (N_LEAF,), 0, 6)
    forced_ok = jnp.take_along_axis(exists, forced[:, None], axis=1)[:, 0]
    chosen_dir = jnp.where(forced_ok, forced, forced ^ 1)
    counts = jnp.where(jnp.arange(6)[None, :] == chosen_dir[:, None], CAP, counts)
    counts = jnp.where(jnp.arange(6)[None, :] == 5, CAP, counts)
    counts = jnp.where(exists, counts, 0)
    scores = jax.random.randint(key_order, (N_LEAF, 6, LEAVES_DEV), 0, 1 << 20) * LEAVES_DEV + jnp.arange(LEAVES_DEV)
    top_leaf = (jnp.arange(6)[None, :, None] == chosen_dir[:, None, None]) & (jnp.arange(LEAVES_DEV)[None, None, :] == LEAVES_DEV - 1)
    scores = jnp.where(top_leaf, -1, scores)
    order = jnp.argsort(scores, axis=-1)[..., :CAP].astype(jnp.int32)
    send_leaf = jnp.where(jnp.arange(CAP)[None, None, :] < counts[..., None], order, -1).astype(jnp.int32)
    offsets = jnp.array([1, -1, side_len, -side_len, side_len * side_len, -side_len * side_len], dtype=jnp.int32)
    senders = jnp.clip(device_ids[:, None] - offsets[None, :], 0, N_LEAF - 1)
    sender_counts = counts[senders, jnp.arange(6)[None, :]]
    incoming_ok = exists[:, jnp.array([1, 0, 3, 2, 5, 4])]
    live = incoming_ok[..., None] & (jnp.arange(CAP)[None, None, :] < sender_counts[..., None])
    live_flat = live.reshape(N_LEAF, 6 * CAP)
    rank_keys = jnp.where(live_flat, 0, 1) * (6 * CAP) + jnp.arange(6 * CAP)[None, :]
    remote_sorted = (jnp.argsort(rank_keys, axis=1) + LEAVES_DEV).astype(jnp.int32)
    live_total = jnp.sum(live_flat.astype(jnp.int32), axis=1)
    pool_size = live_total + LEAVES_DEV
    pick_total = LEAVES_DEV * (NEAR - 1)
    pick_scores = jax.random.randint(key_pick, (N_LEAF, pick_total), 0, 1 << 20) * pick_total + jnp.arange(pick_total)[None, :]
    pick_perm = jnp.argsort(pick_scores, axis=1).astype(jnp.int32)
    position = pick_perm % pool_size[:, None]
    remote_value = jnp.take_along_axis(remote_sorted, jnp.clip(position, 0, 6 * CAP - 1), axis=1)
    local_value = position - live_total[:, None]
    chosen_value = jnp.where(position < live_total[:, None], remote_value, local_value)
    chosen_value = chosen_value.reshape(N_LEAF, LEAVES_DEV, NEAR - 1)
    self_slot = jnp.broadcast_to(jnp.arange(LEAVES_DEV, dtype=jnp.int32)[None, :, None], (N_LEAF, LEAVES_DEV, 1))
    near_src = jnp.concatenate([self_slot, chosen_value], axis=2).reshape(LEAVES, NEAR).astype(jnp.int32)
    return (send_leaf, near_src)


def draw_send_leaf(key, part):
    return routing_tables(key)[0]


def draw_near_src(key, part):
    return routing_tables(key)[1]


def draw_up_coupling(key, part):
    leaf_bits = int(N_LEAF).bit_length() - 1
    subtree_bits = int(LEAVES_DEV).bit_length() - 1
    node_ids = jnp.arange(2 * N_LEAF, dtype=jnp.int32)
    level_of = jnp.zeros((2 * N_LEAF,), jnp.int32)
    for level_bit in range(1, leaf_bits + 1):
        level_of = level_of + (node_ids >= 1 << level_bit).astype(jnp.int32)
    halvings = (leaf_bits - level_of + subtree_bits).astype(jnp.float32)
    spread = jnp.exp2(0.5 * halvings) / jnp.sqrt(jnp.float32(3 * RANK))
    draw_key = jax.random.fold_in(key, 5151)
    raw_values = jax.random.normal(draw_key, (2 * N_LEAF, 3, RANK, RANK), jnp.float32)
    return jnp.clip(raw_values * spread[:, None, None, None], -8.0, 8.0)


def with_ends(entries, own_key, smallest, high):
    place = [jax.random.randint(jax.random.fold_in(own_key, axis), (), 0, length) for axis, length in enumerate(entries.shape)]
    main_axis = entries.shape.index(max(entries.shape))
    beside = place[:main_axis] + [(place[main_axis] + 1) % entries.shape[main_axis]] + place[main_axis + 1:]
    return entries.at[tuple(place)].set(smallest).at[tuple(beside)].set(high)


def block_scale(own_key, extent, cuts, low, largest):
    factor_of, own = 1.0, jax.random.fold_in(own_key, 6)
    for dim, parts in cuts:
        draws = jnp.exp(jax.random.uniform(jax.random.fold_in(own, dim), (parts,), jnp.float32, low / len(cuts), largest / len(cuts)))
        factor_of = factor_of * jnp.repeat(draws, extent[dim] // parts).reshape([-1 if axis == dim else 1 for axis in range(len(extent))])
    return factor_of


def noise(stream_key, extent, deviation, limit, cuts=(), kind=jnp.bfloat16):
    factor_of = block_scale(stream_key, extent, cuts, -0.22, 0.18) if cuts else 1.0
    values = jax.random.normal(stream_key, extent, jnp.float32) * deviation * factor_of
    return jnp.minimum(jnp.maximum(values, -limit), limit).astype(kind)


def setup_inputs(seed: int = 0) -> dict:
    splits = jax.random.split(jax.random.key(seed), 11)
    densities = noise(splits[0], (RHS, POINTS), 1.0, 6.0, ((0, 4), (1, 8)))
    bases = noise(splits[1], (RANK, POINTS), LEAF_SIZE ** -0.5, 0.5, ((1, 8),), jnp.float32)
    near_blocks = noise(splits[2], (LEAVES, NEAR, LEAF_SIZE, LEAF_SIZE), (LEAF_SIZE * NEAR) ** -0.5, 0.1875, ((0, 8), (1, 4)))
    near_src = draw_near_src(jax.random.fold_in(splits[10], 71), 0)
    send_leaf = draw_send_leaf(jax.random.fold_in(splits[10], 71), 0)
    far_src = with_ends(jax.random.randint(splits[5], (LEAVES, FAR), 0, LEAVES_DEV), jax.random.fold_in(splits[5], 1), 0, LEAVES_DEV - 1).astype(jnp.int32)
    leaf_coupling = noise(splits[6], (LEAVES, FAR, RANK, RANK), (RANK * FAR) ** -0.5, 0.375, ((0, 8),), jnp.float32)
    local_transfer = noise(splits[7], (N_LEAF, 2 * LEAVES_DEV, RANK, RANK), (2 * RANK) ** -0.5, 0.75, ((0, 8),), jnp.float32)
    upper_transfer = noise(splits[8], (2 * N_LEAF, RANK, RANK), (2 * RANK) ** -0.5, 0.75, (), jnp.float32)
    up_coupling = draw_up_coupling(jax.random.fold_in(splits[10], 71), 0)
    return {"densities": densities, "bases": bases, "near_blocks": near_blocks, "near_src": near_src, "send_leaf": send_leaf, "far_src": far_src, "leaf_coupling": leaf_coupling, "local_transfer": local_transfer, "upper_transfer": upper_transfer, "up_coupling": up_coupling}


TOP_PREC = lax.Precision.HIGHEST
FACE_SIGNS = ((1, 0), (-1, 0), (1, 1), (-1, 1), (1, 2), (-1, 2))


def cube_side(device_count):
    return max(edge_len for edge_len in range(1, 65) if edge_len ** 3 <= device_count)


def face_offsets(device_count):
    side_len = cube_side(device_count)
    return [face_sign * side_len ** axis_pos for face_sign, axis_pos in FACE_SIGNS]


def lift_pairs(child_coef, child_maps):
    lifted = jnp.einsum('...nrs,...nqr->...nqs', child_maps, child_coef, precision=TOP_PREC)
    return lifted[..., 0::2, :, :] + lifted[..., 1::2, :, :]


def apply_maps(node_maps, coef_rows):
    return jnp.einsum('...nrs,...nqs->...nqr', node_maps, coef_rows, precision=TOP_PREC)


def couple_level(coef_level, maps_level):
    level_width = coef_level.shape[0]
    even_node = (jnp.arange(level_width) % 2) == 0
    padded = jnp.pad(coef_level, ((3, 3), (0, 0), (0, 0)))
    minus_two = padded[1:level_width + 1]
    plus_two = padded[5:level_width + 5]
    third_node = jnp.where(even_node[:, None, None], padded[6:level_width + 6], padded[0:level_width])
    first_terms = apply_maps(maps_level[:, 0], minus_two) + apply_maps(maps_level[:, 1], plus_two)
    return first_terms + apply_maps(maps_level[:, 2], third_node)


def upper_tree(roots, upper_transfer, up_coupling):
    node_total = roots.shape[0]
    coef_levels = {node_total: roots}
    level_width = node_total
    while level_width > 4:
        coef_levels[level_width // 2] = lift_pairs(coef_levels[level_width], upper_transfer[level_width:2 * level_width])
        level_width = level_width // 2
    level_field = couple_level(coef_levels[4], up_coupling[4:8])
    level_width = 4
    while level_width < node_total:
        level_width = level_width * 2
        coupled = couple_level(coef_levels[level_width], up_coupling[level_width:2 * level_width])
        level_field = coupled + apply_maps(upper_transfer[level_width:2 * level_width], jnp.repeat(level_field, 2, axis=0))
    return level_field


def slot_table(send_leaf):
    offsets = face_offsets(N_LEAF)
    device_ids = jnp.arange(N_LEAF, dtype=jnp.int32)
    leaf_ids = []
    live_parts = []
    for direction in range(6):
        sender = device_ids - offsets[direction]
        inside = (sender >= 0) & (sender < N_LEAF)
        clipped = jnp.clip(sender, 0, N_LEAF - 1).astype(jnp.int32)
        sent_leaf = send_leaf[clipped, direction, :]
        live_parts.append(inside[:, None] & (sent_leaf >= 0))
        leaf_ids.append(clipped[:, None] * LEAVES_DEV + jnp.maximum(sent_leaf, 0))
    local_ids = device_ids[:, None] * LEAVES_DEV + jnp.arange(LEAVES_DEV, dtype=jnp.int32)[None, :]
    local_live = jnp.ones(local_ids.shape, dtype=jnp.bool_)
    all_ids = jnp.concatenate([local_ids] + leaf_ids, axis=1).astype(jnp.int32)
    all_live = jnp.concatenate([local_live] + live_parts, axis=1)
    return all_ids, all_live


def reference(densities, bases, near_blocks, near_src, send_leaf, far_src, leaf_coupling, local_transfer, upper_transfer, up_coupling):
    all_ids, all_live = slot_table(send_leaf)
    panels_all = densities.reshape(RHS, LEAVES, LEAF_SIZE)
    blocks_dev = near_blocks.reshape(N_LEAF, LEAVES_DEV, NEAR, LEAF_SIZE, LEAF_SIZE)
    sources_dev = near_src.reshape(N_LEAF, LEAVES_DEV, NEAR)

    def near_device(packed):
        blocks, sources, id_row, live_row = packed
        chosen = jnp.take(id_row, sources, axis=0)
        alive = jnp.take(live_row, sources, axis=0)
        picked = jnp.take(panels_all, chosen, axis=1)
        picked = jnp.where(alive[None, :, :, None], picked, jnp.zeros_like(picked))
        return jnp.einsum('tkij,qtkj->qti', blocks.astype(jnp.float32), picked.astype(jnp.float32), precision=TOP_PREC)

    near_parts = lax.map(near_device, (blocks_dev, sources_dev, all_ids, all_live))
    near_field = jnp.transpose(near_parts, (1, 0, 2, 3)).reshape(RHS, POINTS)

    basis_view = bases.reshape(RANK, LEAVES, LEAF_SIZE)
    leaf_coef = jnp.einsum('rti,qti->tqr', basis_view, panels_all.astype(jnp.float32), precision=TOP_PREC)
    leaf_coef = leaf_coef.reshape(N_LEAF, LEAVES_DEV, RHS, RANK)
    coef_levels = {LEAVES_DEV: leaf_coef}
    level_width = LEAVES_DEV
    while level_width > 1:
        coef_levels[level_width // 2] = lift_pairs(coef_levels[level_width], local_transfer[:, level_width:2 * level_width])
        level_width = level_width // 2
    root_field = upper_tree(coef_levels[1][:, 0], upper_transfer, up_coupling)

    far_dev = far_src.reshape(N_LEAF, LEAVES_DEV, FAR)
    picked_coef = jax.vmap(lambda coef_rows, far_index: jnp.take(coef_rows, far_index, axis=0))(leaf_coef, far_dev)
    coupling_view = leaf_coupling.reshape(N_LEAF, LEAVES_DEV, FAR, RANK, RANK)
    leaf_local = jnp.einsum('...tjrs,...tjqs->...tqr', coupling_view, picked_coef, precision=TOP_PREC)

    level_field = root_field[:, None]
    level_width = 1
    while level_width < LEAVES_DEV:
        level_width = level_width * 2
        level_field = apply_maps(local_transfer[:, level_width:2 * level_width], jnp.repeat(level_field, 2, axis=1))
    leaf_field = level_field + leaf_local
    far_part = jnp.einsum('rti,tqr->qti', basis_view, leaf_field.reshape(LEAVES, RHS, RANK), precision=TOP_PREC)
    return near_field + far_part.reshape(RHS, POINTS)
```

```python
import functools

import jax
import jax.numpy as jnp
from jax import lax
from jax.experimental import pallas as pl
from jax.experimental.pallas import tpu as pltpu
from jax.sharding import Mesh
from jax.sharding import PartitionSpec as P

FACE_SIGNS = ((1, 0), (-1, 0), (1, 1), (-1, 1), (1, 2), (-1, 2))
F32 = jnp.float32
BF16 = jnp.bfloat16
LANES = 128
VMEM = pl.BlockSpec(memory_space=pltpu.VMEM)
SMEM = pl.BlockSpec(memory_space=pltpu.SMEM)


def cube_side(device_count):
    return max((edge_len for edge_len in range(1, 65) if edge_len**3 <= device_count))


def face_offsets(device_count):
    side_len = cube_side(device_count)
    return [face_sign * side_len**axis_pos for face_sign, axis_pos in FACE_SIGNS]


def halves(value):
    high = value.astype(BF16)
    return high, (value - high.astype(F32)).astype(BF16)


def dot_nn(left, right):
    return lax.dot_general(left, right, (((1,), (0,)), ((), ())), preferred_element_type=F32)


def dot_nt(left, right):
    return lax.dot_general(left, right, (((1,), (1,)), ((), ())), preferred_element_type=F32)


def split_dot(dot, rows, right_high, right_low):
    count = rows.shape[0]
    high, low = halves(rows)
    both = jnp.concatenate([high, low], axis=0)
    out = dot(both, right_high) + dot(both, right_low)
    return out[:count] + out[count:]


def spread_bases(block, group):
    rank, lanes = block.shape
    width = lanes // group
    zero = jnp.zeros((rank, width), block.dtype)
    rows = []
    for slot in range(group):
        pieces = [zero] * group
        pieces[slot] = block[:, slot * width : (slot + 1) * width]
        rows.append(jnp.concatenate(pieces, axis=1))
    return jnp.concatenate(rows, axis=0)


def level_tiles(leaf_count, group):
    tiles = {}
    level = 1
    while level < leaf_count:
        children = 2 * level
        span = max(group, min(children, 2 * group))
        tiles[level] = [(children + first, span) for first in range(0, children, span)]
        level = children
    return tiles


def tile_mask(first, span, level, rank, group):
    row = lax.broadcasted_iota(jnp.int32, (span * rank, group * rank), 0)
    lane = lax.broadcasted_iota(jnp.int32, (span * rank, group * rank), 1)
    child = row // rank
    return (child // 2 == lane // rank) & (child + first < 4 * level)


def up_kernel(
    offsets, far_groups, where_ref, send_ref, dens_ref, bases_ref, maps_ref,
    coef_ref, high_ref, low_ref, out_ref, spread_ref,
):
    columns, points = dens_ref.shape
    rank = bases_ref.shape[0]
    group = LANES // rank
    node_count = maps_ref.shape[2]
    leaf_count = node_count // 2
    width = points // leaf_count
    device = where_ref[0]
    device_count = out_ref.shape[0] // far_groups
    cap = send_ref.shape[1]
    out_ref[...] = jnp.zeros_like(out_ref)
    for direction, offset in enumerate(offsets):
        target = device + offset

        @pl.when((target >= 0) & (target < device_count))
        def _():
            for place in range(cap):
                leaf = jnp.maximum(send_ref[direction, place, device], 0)
                panel = dens_ref[:, pl.ds(pl.multiple_of(leaf * width, LANES), width)]
                for copy in range(far_groups):
                    out_ref[target * far_groups + copy, place * columns : (place + 1) * columns, :] = panel
    step = group * width
    coefs = []
    for first in range(0, points, step):
        high, low = halves(bases_ref[:, first : first + step])
        dens = dens_ref[:, first : first + step]
        coefs.append(
            dot_nt(dens, spread_bases(high, group)) + dot_nt(dens, spread_bases(low, group))
        )
    coef = jnp.concatenate(coefs, axis=1)
    coef_ref[...] = coef
    for row in range(rank):
        slab = jnp.concatenate([maps_ref[row]] * group, axis=0)
        spread_ref[pl.ds(row, node_count, stride=rank), :] = slab.T
    level = leaf_count // 2
    tiles = level_tiles(leaf_count, group)
    while level >= 1:
        parents = []
        for index, (first, span) in enumerate(tiles[level]):
            rows = slice(first * rank, (first + span) * rank)
            masked = jnp.where(tile_mask(first, span, level, rank, group), spread_ref[rows, :], 0.0)
            high, low = halves(masked)
            place = first - 2 * level
            if level > 1:
                high_ref[rows, :] = high
                low_ref[rows, :] = low
            else:
                high_ref[0 : span * rank, :] = high
                low_ref[0 : span * rank, :] = low
            lanes = slice(place * rank, (place + span) * rank)
            parents.append(split_dot(dot_nn, coef[:, lanes], high, low))
        coef = jnp.concatenate(parents, axis=1) if len(parents) > 1 else parents[0]
        level //= 2
    high = coef.astype(BF16).astype(F32)
    rest = coef - high
    middle = rest.astype(BF16).astype(F32)
    last = (rest - middle).astype(BF16).astype(F32)
    packed = high + pltpu.roll(middle, rank, 1) + pltpu.roll(last, 2 * rank, 1)
    packed = packed.astype(BF16)
    for index in range(out_ref.shape[0]):
        out_ref[index, cap * columns : (cap + 1) * columns, :] = packed


def near_kernel(
    offsets, far_groups, share, where_ref, *refs,
):
    source_refs = refs[:share]
    dens_refs = refs[share : share + far_groups]
    got_ref = refs[share + far_groups]
    block_refs = refs[share + far_groups + 1 : 2 * share + far_groups + 1]
    out_refs = refs[2 * share + far_groups + 1 : -1]
    buffer_ref = refs[-1]
    device, own = where_ref[0], where_ref[1]
    columns, points = dens_refs[0].shape
    leaf_count, near_count, width, _ = block_refs[0].shape
    device_count = got_ref.shape[0] // far_groups
    cap = got_ref.shape[1] // columns - 1
    for part in range(far_groups):
        rows = slice(part * columns, (part + 1) * columns)
        for leaf in range(leaf_count):
            buffer_ref[leaf, rows, :] = dens_refs[part][:, leaf * width : (leaf + 1) * width]
        owner = lax.rem(own + part, far_groups)
        for direction, offset in enumerate(offsets):
            sender = jnp.clip(device - offset, 0, device_count - 1) * far_groups + owner
            for place in range(cap):
                buffer_ref[leaf_count + direction * cap + place, rows, :] = got_ref[
                    sender, place * columns : (place + 1) * columns, :
                ]
    for leaf in range(leaf_count):
        total = None
        for source_ref, block_ref in zip(source_refs, block_refs):
            for block in range(near_count):
                term = dot_nt(buffer_ref[source_ref[block, leaf]], block_ref[leaf, block])
                total = term if total is None else total + term
        for part, out_ref in enumerate(out_refs):
            out_ref[:, leaf * width : (leaf + 1) * width] = total[
                part * columns : (part + 1) * columns
            ]


def far_kernel(
    far_groups, where_ref, far_ref, near_ref, coef_ref, bases_ref, coupling_ref, high_ref, low_ref,
    upper_ref, cross_ref, got_ref, out_ref, turned_ref, local_ref, tree_ref,
):
    device, own = where_ref[0], where_ref[1]
    columns, points = near_ref.shape
    rank = bases_ref.shape[0]
    group = LANES // rank
    leaf_count, far_count = coupling_ref.shape[:2]
    device_count = got_ref.shape[0] // far_groups
    cap = got_ref.shape[1] // columns - 1
    high, low = halves(coef_ref[...])
    both = jnp.concatenate([high.astype(F32), low.astype(F32)], axis=0)
    for first in range(0, leaf_count * rank, LANES):
        turned_ref[first : first + LANES, :] = both[:, first : first + LANES].T.astype(BF16)
    for leaf in range(leaf_count):
        maps = jnp.concatenate([coupling_ref[leaf, j] for j in range(far_count)], axis=1)
        maps = jnp.concatenate(halves(maps), axis=0)
        picked = jnp.concatenate(
            [
                turned_ref[pl.ds(pl.multiple_of(far_ref[j, leaf] * rank, rank), rank), :]
                for j in range(far_count)
            ],
            axis=0,
        )
        out = dot_nn(maps, picked)
        local_ref[leaf * rank : (leaf + 1) * rank, :] = out[:rank] + out[rank:]
    lane = lax.broadcasted_iota(jnp.int32, (LANES, rank), 0)
    column = lax.broadcasted_iota(jnp.int32, (LANES, rank), 1)
    gather = jnp.where((lane % rank == column) & (lane < 3 * rank), 1.0, 0.0).astype(BF16)
    for index in range(device_count):
        piece = got_ref[index * far_groups + own, cap * columns : (cap + 1) * columns, :]
        tree_ref[device_count + index] = dot_nn(piece, gather)
    level = device_count // 2
    while level >= 4:
        for node in range(level, 2 * level):
            total = None
            for child in (2 * node, 2 * node + 1):
                term = split_dot(dot_nn, tree_ref[child], *halves(upper_ref[child]))
                total = term if total is None else total + term
            tree_ref[node] = total
        level //= 2
    field = None
    level = 4
    while level <= device_count:
        place = device // (device_count // level)
        node = level + place
        third = jnp.where(place % 2 == 0, place + 3, place - 3)
        total = None
        for slot, other in enumerate((place - 2, place + 2, third)):
            inside = (other >= 0) & (other < level)
            value = tree_ref[level + jnp.clip(other, 0, level - 1)]
            value = jnp.where(inside, value, 0.0)
            term = split_dot(dot_nt, value, *halves(cross_ref[node, slot]))
            total = term if total is None else total + term
        if field is not None:
            total = total + split_dot(dot_nt, field, *halves(upper_ref[node]))
        field = total
        level *= 2
    field = jnp.concatenate([field, jnp.zeros((columns, LANES - rank), F32)], axis=1)
    tiles = level_tiles(leaf_count, group)
    level = 1
    while level < leaf_count:
        children = []
        for index, (first, span) in enumerate(tiles[level]):
            start = first * rank if level > 1 else 0
            rows = slice(start, start + span * rank)
            lanes = slice(index * LANES, (index + 1) * LANES)
            children.append(split_dot(dot_nt, field[:, lanes], high_ref[rows, :], low_ref[rows, :]))
        field = jnp.concatenate(children, axis=1) if len(children) > 1 else children[0]
        level *= 2
    width = points // leaf_count
    step = group * width
    for index in range(leaf_count // group):
        lanes = slice(index * LANES, (index + 1) * LANES)
        turned = local_ref[lanes, :].T
        rows = field[:, lanes] + turned[:columns] + turned[columns:]
        spots = slice(index * step, (index + 1) * step)
        high, low = halves(bases_ref[:, spots])
        out_ref[:, spots] = near_ref[:, spots] + split_dot(
            dot_nn, rows, spread_bases(high, group), spread_bases(low, group)
        )


def local(
    densities,
    bases,
    near_blocks,
    near_src,
    send_leaf,
    far_src,
    leaf_coupling,
    local_transfer,
    upper_transfer,
    up_coupling,
):
    leaf_devices = lax.axis_size("leaf")
    far_groups = lax.axis_size("far")
    share = lax.axis_size("mate")
    offsets = face_offsets(leaf_devices)
    columns, points = densities.shape
    leaf_count, _, width, _ = near_blocks.shape
    rank = bases.shape[0]
    cap = send_leaf.shape[2]
    node_count = local_transfer.shape[1]
    place = jnp.stack([lax.axis_index("leaf"), lax.axis_index("far")]).astype(jnp.int32)
    params = pltpu.CompilerParams(vmem_limit_bytes=40 * 2**20)

    def rotated(value, axis, shift):
        count = lax.axis_size(axis)
        return lax.ppermute(value, axis, [(i, (i - shift) % count) for i in range(count)])

    sources = near_src.T
    panels = [densities] + [rotated(densities, "far", part) for part in range(1, far_groups)]
    all_sources = [sources] + [rotated(sources, "mate", part) for part in range(1, share)]
    all_blocks = [near_blocks] + [rotated(near_blocks, "mate", part) for part in range(1, share)]

    chunk = (cap + 1) * columns
    coef, high, low, outgoing = pl.pallas_call(
        functools.partial(up_kernel, offsets, far_groups),
        out_shape=[
            jax.ShapeDtypeStruct((columns, leaf_count * rank), F32),
            jax.ShapeDtypeStruct((node_count * rank, LANES), BF16),
            jax.ShapeDtypeStruct((node_count * rank, LANES), BF16),
            jax.ShapeDtypeStruct((leaf_devices * far_groups, chunk, LANES), BF16),
        ],
        in_specs=[SMEM, SMEM, VMEM, VMEM, VMEM],
        out_specs=[VMEM] * 4,
        scratch_shapes=[pltpu.VMEM((node_count * rank, LANES), F32)],
        compiler_params=params,
        name="up",
    )(place, send_leaf.transpose(1, 2, 0), densities, bases, local_transfer[0].transpose(1, 2, 0))
    arrived = lax.all_to_all(outgoing, ("leaf", "far"), 0, 0, tiled=True)

    slots = leaf_count + len(offsets) * cap
    partials = pl.pallas_call(
        functools.partial(near_kernel, offsets, far_groups, share),
        out_shape=[jax.ShapeDtypeStruct((columns, points), F32)] * far_groups,
        in_specs=[SMEM] * (1 + share) + [VMEM] * (far_groups + 1 + share),
        out_specs=[VMEM] * far_groups,
        scratch_shapes=[pltpu.VMEM((slots, far_groups * columns, width), BF16)],
        compiler_params=params,
        name="near",
    )(place, *all_sources, *panels, arrived, *all_blocks)
    received = [rotated(partials[part], "far", -part) for part in range(1, far_groups)]
    total = pl.pallas_call(
        functools.partial(far_kernel, far_groups),
        out_shape=jax.ShapeDtypeStruct((columns, points), F32),
        in_specs=[SMEM] * 2 + [VMEM] * 9,
        out_specs=VMEM,
        scratch_shapes=[
            pltpu.VMEM((leaf_count * rank, 2 * columns), BF16),
            pltpu.VMEM((leaf_count * rank, 2 * columns), F32),
            pltpu.VMEM((2 * leaf_devices, columns, rank), F32),
        ],
        compiler_params=params,
        name="far",
    )(
        place, far_src.T, partials[0], coef, bases, leaf_coupling, high, low, upper_transfer,
        up_coupling, arrived,
    )
    for value in received:
        total = total + value
    return total


def solution(mesh):
    leaf_devices, rhs_devices = mesh.shape["leaf"], mesh.shape["rhs"]
    share = 2 if rhs_devices % 2 == 0 else 1
    split = Mesh(
        mesh.devices.reshape(leaf_devices, rhs_devices // share, share), ("leaf", "far", "mate")
    )
    rhs = ("far", "mate")
    in_specs = (
        P(rhs, "leaf"),
        P(None, "leaf"),
        P("leaf", rhs, None, None),
        P("leaf", rhs),
        P(),
        P("leaf", None),
        P("leaf", None, None, None),
        P("leaf", None, None, None),
        P(),
        P(),
    )
    return jax.shard_map(
        local, mesh=split, in_specs=in_specs, out_specs=P(rhs, "leaf"), check_vma=False
    )
```

```python
import functools

import jax
import jax.numpy as jnp
from jax import lax
from jax.experimental import pallas as pl
from jax.experimental.pallas import tpu as pltpu
from jax.sharding import Mesh
from jax.sharding import PartitionSpec as P

FACE_SIGNS = ((1, 0), (-1, 0), (1, 1), (-1, 1), (1, 2), (-1, 2))
F32 = jnp.float32
BF16 = jnp.bfloat16
LANES = 128
VMEM = pl.BlockSpec(memory_space=pltpu.VMEM)
HBM = pl.BlockSpec(memory_space=pltpu.HBM)
SMEM = pl.BlockSpec(memory_space=pltpu.SMEM)


def cube_side(device_count):
    return max((edge_len for edge_len in range(1, 65) if edge_len**3 <= device_count))


def face_offsets(device_count):
    side_len = cube_side(device_count)
    return [face_sign * side_len**axis_pos for face_sign, axis_pos in FACE_SIGNS]


def shifted(value, axis, steps):
    count = lax.axis_size(axis)
    first, last = (max(0, -steps), min(count, count - steps))
    return lax.ppermute(value, axis, [(source, source + steps) for source in range(first, last)])


def halves(value):
    high = value.astype(BF16)
    return high, (value - high.astype(F32)).astype(BF16)


def dot_nn(left, right):
    return lax.dot_general(left, right, (((1,), (0,)), ((), ())), preferred_element_type=F32)


def dot_nt(left, right):
    return lax.dot_general(left, right, (((1,), (1,)), ((), ())), preferred_element_type=F32)


def split_dot(dot, rows, right_high, right_low):
    count = rows.shape[0]
    high, low = halves(rows)
    both = jnp.concatenate([high, low], axis=0)
    out = dot(both, right_high) + dot(both, right_low)
    return out[:count] + out[count:]


def spread_bases(block, group):
    rank, lanes = block.shape
    width = lanes // group
    zero = jnp.zeros((rank, width), block.dtype)
    rows = []
    for slot in range(group):
        pieces = [zero] * group
        pieces[slot] = block[:, slot * width : (slot + 1) * width]
        rows.append(jnp.concatenate(pieces, axis=1))
    return jnp.concatenate(rows, axis=0)


def level_tiles(leaf_count, group):
    tiles = {}
    level = 1
    while level < leaf_count:
        children = 2 * level
        span = max(group, min(children, 2 * group))
        tiles[level] = [(children + first, span) for first in range(0, children, span)]
        level = children
    return tiles


def tile_mask(first, span, level, rank, group):
    row = lax.broadcasted_iota(jnp.int32, (span * rank, group * rank), 0)
    lane = lax.broadcasted_iota(jnp.int32, (span * rank, group * rank), 1)
    child = row // rank
    return (child // 2 == lane // rank) & (child + first < 4 * level)


def fetch(pairs, sems):
    copies = []
    for index, (source, target) in enumerate(pairs):
        copy = pltpu.make_async_copy(source, target, sems.at[index])
        copy.start()
        copies.append(copy)
    return copies


def up_kernel(
    dens_hbm, bases_hbm, maps_hbm, coef_ref, high_ref, low_ref, root_ref,
    dens_ref, bases_ref, maps_ref, spread_ref, sems,
):
    copies = fetch([(dens_hbm, dens_ref), (bases_hbm, bases_ref), (maps_hbm, maps_ref)], sems)
    columns, points = dens_ref.shape
    rank = bases_ref.shape[0]
    group = LANES // rank
    node_count = maps_ref.shape[2]
    leaf_count = node_count // 2
    width = points // leaf_count
    copies[0].wait()
    copies[1].wait()
    step = group * width
    coefs = []
    for first in range(0, points, step):
        high, low = halves(bases_ref[:, first : first + step])
        dens = dens_ref[:, first : first + step]
        coefs.append(
            dot_nt(dens, spread_bases(high, group)) + dot_nt(dens, spread_bases(low, group))
        )
    coef = jnp.concatenate(coefs, axis=1)
    coef_ref[...] = coef
    copies[2].wait()
    for row in range(rank):
        slab = jnp.concatenate([maps_ref[row]] * group, axis=0)
        spread_ref[pl.ds(row, node_count, stride=rank), :] = slab.T
    level = leaf_count // 2
    tiles = level_tiles(leaf_count, group)
    while level >= 1:
        parents = []
        for index, (first, span) in enumerate(tiles[level]):
            rows = slice(first * rank, (first + span) * rank)
            masked = jnp.where(tile_mask(first, span, level, rank, group), spread_ref[rows, :], 0.0)
            high, low = halves(masked)
            place = first - 2 * level
            if level > 1:
                high_ref[rows, :] = high
                low_ref[rows, :] = low
            else:
                high_ref[0 : span * rank, :] = high
                low_ref[0 : span * rank, :] = low
            lanes = slice(place * rank, (place + span) * rank)
            parents.append(split_dot(dot_nn, coef[:, lanes], high, low))
        coef = jnp.concatenate(parents, axis=1) if len(parents) > 1 else parents[0]
        level //= 2
    high = coef.astype(BF16).astype(F32)
    rest = coef - high
    middle = rest.astype(BF16).astype(F32)
    last = (rest - middle).astype(BF16).astype(F32)
    packed = high + pltpu.roll(middle, rank, 1) + pltpu.roll(last, 2 * rank, 1)
    root_ref[...] = packed.astype(BF16)


def select_kernel(
    faces, far_groups, where_ref, send_hbm, dens_hbm, root_ref, *refs,
):
    other_refs = refs[: far_groups - 1]
    out_refs = refs[far_groups - 1 : -3]
    send_ref, dens_ref, sems = refs[-3:]
    copies = fetch([(send_hbm, send_ref), (dens_hbm, dens_ref)], sems)
    device = where_ref[0]
    columns = dens_ref.shape[0]
    cap = send_ref.shape[1]
    for copy in copies:
        copy.wait()
    for (directions, stride), out_ref in zip(faces, out_refs):
        direction = directions[0]
        if len(directions) > 1:
            direction = direction + device // stride % 2
        for place in range(cap):
            leaf = jnp.maximum(send_ref[direction, place, device], 0)
            for part, panel_ref in enumerate((dens_ref, *other_refs)):
                row = (place * far_groups + part) * columns
                out_ref[row : row + columns, :] = panel_ref[
                    :, pl.ds(pl.multiple_of(leaf * LANES, LANES), LANES)
                ]
        out_ref[cap * far_groups * columns :, :] = root_ref[...]


def near_kernel(
    faces, far_groups, share, *refs,
):
    source_hbms, refs = refs[:share], refs[share:]
    dens_hbm, refs = refs[0], refs[1:]
    other_refs, refs = refs[: far_groups - 1], refs[far_groups - 1 :]
    got_refs, refs = refs[: len(faces)], refs[len(faces) :]
    block_hbm, refs = refs[0], refs[1:]
    mate_refs, refs = refs[: share - 1], refs[share - 1 :]
    out_refs, refs = refs[:far_groups], refs[far_groups:]
    source_refs, refs = refs[:share], refs[share:]
    dens_ref, block_ref, buffer_ref, small_sems, sems = refs
    columns, points = dens_ref.shape
    leaf_count, near_count, width, _ = block_ref.shape
    chunk_count = sems.shape[0]
    chunk = leaf_count // chunk_count
    copies = fetch(
        [(dens_hbm, dens_ref)] + list(zip(source_hbms, source_refs)), small_sems
    )
    block_copies = fetch(
        [
            (block_hbm.at[pl.ds(index * chunk, chunk)], block_ref.at[pl.ds(index * chunk, chunk)])
            for index in range(chunk_count)
        ],
        sems,
    )
    cap = (got_refs[0].shape[0] // columns - 1) // far_groups
    for (directions, _), got_ref in zip(faces, got_refs):
        for direction in directions:
            for place in range(cap):
                row = place * far_groups * columns
                buffer_ref[leaf_count + direction * cap + place] = got_ref[
                    row : row + far_groups * columns, :
                ]
    copies[0].wait()
    for part, panel_ref in enumerate((dens_ref, *other_refs)):
        rows = slice(part * columns, (part + 1) * columns)
        for leaf in range(leaf_count):
            buffer_ref[leaf, rows, :] = panel_ref[:, leaf * width : (leaf + 1) * width]
    for copy in copies[1:]:
        copy.wait()
    for leaf in range(leaf_count):
        if leaf % chunk == 0:
            block_copies[leaf // chunk].wait()
        panels, blocks = [], []
        for source_ref, blocks_ref in zip(source_refs, (block_ref, *mate_refs)):
            for block in range(near_count):
                panels.append(buffer_ref[source_ref[block, leaf]])
                blocks.append(blocks_ref[leaf, block])
        total = dot_nt(jnp.concatenate(panels, axis=1), jnp.concatenate(blocks, axis=1))
        for part, out_ref in enumerate(out_refs):
            out_ref[:, leaf * width : (leaf + 1) * width] = total[
                part * columns : (part + 1) * columns
            ]


def far_kernel(
    roots, where_ref, far_hbm, near_ref, coef_ref, bases_ref, coupling_ref, high_ref, low_ref,
    upper_hbm, cross_hbm, *refs,
):
    root_refs = refs[: len(roots)]
    out_ref, far_ref, upper_ref, cross_ref, turned_ref, local_ref, tree_ref, sems = refs[len(roots) :]
    copies = fetch([(far_hbm, far_ref), (upper_hbm, upper_ref), (cross_hbm, cross_ref)], sems)
    device = where_ref[0]
    columns, points = near_ref.shape
    rank = bases_ref.shape[0]
    group = LANES // rank
    leaf_count, far_count = coupling_ref.shape[:2]
    device_count = upper_ref.shape[0] // 2
    high, low = halves(coef_ref[...])
    both = jnp.concatenate([high.astype(F32), low.astype(F32)], axis=0)
    for first in range(0, leaf_count * rank, LANES):
        turned_ref[first : first + LANES, :] = both[:, first : first + LANES].T.astype(BF16)
    for copy in copies:
        copy.wait()
    for leaf in range(leaf_count):
        maps = jnp.concatenate([coupling_ref[leaf, j] for j in range(far_count)], axis=1)
        maps = jnp.concatenate(halves(maps), axis=0)
        picked = jnp.concatenate(
            [
                turned_ref[pl.ds(pl.multiple_of(far_ref[j, leaf] * rank, rank), rank), :]
                for j in range(far_count)
            ],
            axis=0,
        )
        out = dot_nn(maps, picked)
        local_ref[leaf * rank : (leaf + 1) * rank, :] = out[:rank] + out[rank:]
    lane = lax.broadcasted_iota(jnp.int32, (LANES, rank), 0)
    column = lax.broadcasted_iota(jnp.int32, (LANES, rank), 1)
    gather = jnp.where((lane % rank == column) & (lane < 3 * rank), 1.0, 0.0).astype(BF16)
    for turn, root_ref in zip(roots, root_refs):
        if turn is None:
            for index in range(device_count):
                tree_ref[device_count + index] = dot_nn(root_ref[index], gather)
        else:
            piece = root_ref[root_ref.shape[0] - columns :, :]
            tree_ref[device_count + (device ^ turn)] = dot_nn(piece, gather)
    level = device_count // 2
    while level >= 4:
        for node in range(level, 2 * level):
            total = None
            for child in (2 * node, 2 * node + 1):
                term = split_dot(dot_nn, tree_ref[child], *halves(upper_ref[child]))
                total = term if total is None else total + term
            tree_ref[node] = total
        level //= 2
    field = None
    level = 4
    while level <= device_count:
        place = device // (device_count // level)
        node = level + place
        third = jnp.where(place % 2 == 0, place + 3, place - 3)
        total = None
        for slot, other in enumerate((place - 2, place + 2, third)):
            inside = (other >= 0) & (other < level)
            value = tree_ref[level + jnp.clip(other, 0, level - 1)]
            value = jnp.where(inside, value, 0.0)
            term = split_dot(dot_nt, value, *halves(cross_ref[node, slot]))
            total = term if total is None else total + term
        if field is not None:
            total = total + split_dot(dot_nt, field, *halves(upper_ref[node]))
        field = total
        level *= 2
    field = jnp.concatenate([field, jnp.zeros((columns, LANES - rank), F32)], axis=1)
    tiles = level_tiles(leaf_count, group)
    level = 1
    while level < leaf_count:
        children = []
        for index, (first, span) in enumerate(tiles[level]):
            start = first * rank if level > 1 else 0
            rows = slice(start, start + span * rank)
            lanes = slice(index * LANES, (index + 1) * LANES)
            children.append(split_dot(dot_nt, field[:, lanes], high_ref[rows, :], low_ref[rows, :]))
        field = jnp.concatenate(children, axis=1) if len(children) > 1 else children[0]
        level *= 2
    width = points // leaf_count
    step = group * width
    for index in range(leaf_count // group):
        lanes = slice(index * LANES, (index + 1) * LANES)
        turned = local_ref[lanes, :].T
        rows = field[:, lanes] + turned[:columns] + turned[columns:]
        spots = slice(index * step, (index + 1) * step)
        high, low = halves(bases_ref[:, spots])
        out_ref[:, spots] = near_ref[:, spots] + split_dot(
            dot_nn, rows, spread_bases(high, group), spread_bases(low, group)
        )


def hint(micros):
    return pl.CostEstimate(flops=0, bytes_accessed=int(micros * 3.69e6), transcendentals=0)


def local(
    densities,
    bases,
    near_blocks,
    near_src,
    send_leaf,
    far_src,
    leaf_coupling,
    local_transfer,
    upper_transfer,
    up_coupling,
):
    leaf_devices = lax.axis_size("leaf")
    far_groups = lax.axis_size("far")
    share = lax.axis_size("mate")
    side = cube_side(leaf_devices)
    offsets = face_offsets(leaf_devices)
    columns, points = densities.shape
    leaf_count, near_count, width, _ = near_blocks.shape
    rank = bases.shape[0]
    cap = send_leaf.shape[2]
    node_count = local_transfer.shape[1]
    where = lax.axis_index("leaf").astype(jnp.int32).reshape(1)
    params = pltpu.CompilerParams(vmem_limit_bytes=16 * 2**20)
    dma = pltpu.SemaphoreType.DMA

    def rotated(value, axis, shift):
        count = lax.axis_size(axis)
        return lax.ppermute(value, axis, [(i, (i - shift) % count) for i in range(count)])

    def crossed(value, turn):
        return lax.ppermute(value, "leaf", [(i, i ^ turn) for i in range(leaf_devices)])

    sources = near_src.T
    others = [rotated(densities, "far", part) for part in range(1, far_groups)]
    all_sources = [sources] + [rotated(sources, "mate", part) for part in range(1, share)]
    mate_blocks = [rotated(near_blocks, "mate", part) for part in range(1, share)]

    coef, high, low, root = pl.pallas_call(
        up_kernel,
        out_shape=[
            jax.ShapeDtypeStruct((columns, leaf_count * rank), F32),
            jax.ShapeDtypeStruct((node_count * rank, LANES), BF16),
            jax.ShapeDtypeStruct((node_count * rank, LANES), BF16),
            jax.ShapeDtypeStruct((columns, LANES), BF16),
        ],
        in_specs=[HBM] * 3,
        out_specs=[VMEM] * 4,
        scratch_shapes=[
            pltpu.VMEM(densities.shape, BF16),
            pltpu.VMEM(bases.shape, F32),
            pltpu.VMEM((rank, rank, node_count), F32),
            pltpu.VMEM((node_count * rank, LANES), F32),
            dma((3,)),
        ],
        compiler_params=params,
        cost_estimate=hint(4),
        name="up",
    )(densities, bases, local_transfer[0].transpose(1, 2, 0))

    if side == 2:
        faces = [((2 * axis, 2 * axis + 1), 2**axis) for axis in range(3)]
    else:
        faces = [((direction,), offset) for direction, offset in enumerate(offsets)]
    send = send_leaf.transpose(1, 2, 0)
    chunk = (cap * far_groups + 1) * columns
    outgoing = pl.pallas_call(
        functools.partial(select_kernel, faces, far_groups),
        out_shape=[jax.ShapeDtypeStruct((chunk, LANES), BF16)] * len(faces),
        in_specs=[SMEM, HBM, HBM] + [VMEM] * far_groups,
        out_specs=[VMEM] * len(faces),
        scratch_shapes=[
            pltpu.SMEM(send.shape, jnp.int32),
            pltpu.VMEM(densities.shape, BF16),
            dma((2,)),
        ],
        compiler_params=params,
        cost_estimate=hint(1),
        name="select",
    )(where, send, densities, root, *others)
    if side == 2:
        arrived = [crossed(value, stride) for (_, stride), value in zip(faces, outgoing)]
        roots = {0: root}
        for (_, stride), value in zip(faces, arrived):
            roots[stride] = value
        for turn in range(leaf_devices):
            if turn not in roots:
                roots[turn] = crossed(root, turn)
    else:
        arrived = [shifted(value, "leaf", stride) for (_, stride), value in zip(faces, outgoing)]
        roots = {None: lax.all_gather(root, "leaf", axis=0)}

    slots = leaf_count + len(offsets) * cap
    partials = pl.pallas_call(
        functools.partial(near_kernel, faces, far_groups, share),
        out_shape=[jax.ShapeDtypeStruct((columns, points), F32)] * far_groups,
        in_specs=[HBM] * (share + 1)
        + [VMEM] * (far_groups - 1 + len(faces))
        + [HBM]
        + [VMEM] * (share - 1),
        out_specs=[VMEM] * far_groups,
        scratch_shapes=[pltpu.SMEM(sources.shape, jnp.int32)] * share
        + [
            pltpu.VMEM(densities.shape, BF16),
            pltpu.VMEM(near_blocks.shape, BF16),
            pltpu.VMEM((slots, far_groups * columns, width), BF16),
            dma((1 + share,)),
            dma((4,)),
        ],
        compiler_params=params,
        cost_estimate=hint(3),
        name="near",
    )(*all_sources, densities, *others, *arrived, near_blocks, *mate_blocks)
    received = [rotated(partials[part], "far", -part) for part in range(1, far_groups)]
    far_table = far_src.T
    total = pl.pallas_call(
        functools.partial(far_kernel, list(roots)),
        out_shape=jax.ShapeDtypeStruct((columns, points), F32),
        in_specs=[SMEM, HBM] + [VMEM] * 6 + [HBM] * 2 + [VMEM] * len(roots),
        out_specs=VMEM,
        scratch_shapes=[
            pltpu.SMEM(far_table.shape, jnp.int32),
            pltpu.VMEM(upper_transfer.shape, F32),
            pltpu.VMEM(up_coupling.shape, F32),
            pltpu.VMEM((leaf_count * rank, 2 * columns), BF16),
            pltpu.VMEM((leaf_count * rank, 2 * columns), F32),
            pltpu.VMEM((2 * leaf_devices, columns, rank), F32),
            dma((3,)),
        ],
        compiler_params=params,
        cost_estimate=hint(3.5),
        name="far",
    )(
        where, far_table, partials[0], coef, bases, leaf_coupling, high, low, upper_transfer,
        up_coupling, *roots.values(),
    )
    for value in received:
        total = total + value
    return total


def solution(mesh):
    leaf_devices, rhs_devices = mesh.shape["leaf"], mesh.shape["rhs"]
    share = 2 if rhs_devices % 2 == 0 else 1
    split = Mesh(
        mesh.devices.reshape(leaf_devices, rhs_devices // share, share), ("leaf", "far", "mate")
    )
    rhs = ("far", "mate")
    in_specs = (
        P(rhs, "leaf"),
        P(None, "leaf"),
        P("leaf", rhs, None, None),
        P("leaf", rhs),
        P(),
        P("leaf", None),
        P("leaf", None, None, None),
        P("leaf", None, None, None),
        P(),
        P(),
    )
    return jax.shard_map(
        local, mesh=split, in_specs=in_specs, out_specs=P(rhs, "leaf"), check_vma=False
    )
```

```python
import functools

import jax
import jax.numpy as jnp
from jax import lax
from jax.experimental import pallas as pl
from jax.experimental.pallas import tpu as pltpu
from jax.sharding import Mesh
from jax.sharding import PartitionSpec as P

FACE_SIGNS = ((1, 0), (-1, 0), (1, 1), (-1, 1), (1, 2), (-1, 2))
F32 = jnp.float32
BF16 = jnp.bfloat16
LANES = 128
VMEM = pl.BlockSpec(memory_space=pltpu.VMEM)
HBM = pl.BlockSpec(memory_space=pltpu.HBM)
SMEM = pl.BlockSpec(memory_space=pltpu.SMEM)


def cube_side(device_count):
    return max((edge_len for edge_len in range(1, 65) if edge_len**3 <= device_count))


def face_offsets(device_count):
    side_len = cube_side(device_count)
    return [face_sign * side_len**axis_pos for face_sign, axis_pos in FACE_SIGNS]


def shifted(value, axis, steps):
    count = lax.axis_size(axis)
    first, last = (max(0, -steps), min(count, count - steps))
    return lax.ppermute(value, axis, [(source, source + steps) for source in range(first, last)])


def halves(value):
    high = value.astype(BF16)
    return high, (value - high.astype(F32)).astype(BF16)


def dot_nn(left, right):
    return lax.dot_general(left, right, (((1,), (0,)), ((), ())), preferred_element_type=F32)


def dot_nt(left, right):
    return lax.dot_general(left, right, (((1,), (1,)), ((), ())), preferred_element_type=F32)


def split_dot(dot, rows, right_high, right_low):
    count = rows.shape[0]
    high, low = halves(rows)
    both = jnp.concatenate([high, low], axis=0)
    out = dot(both, right_high) + dot(both, right_low)
    return out[:count] + out[count:]


def spread_bases(block, group):
    rank, lanes = block.shape
    width = lanes // group
    zero = jnp.zeros((rank, width), block.dtype)
    rows = []
    for slot in range(group):
        pieces = [zero] * group
        pieces[slot] = block[:, slot * width : (slot + 1) * width]
        rows.append(jnp.concatenate(pieces, axis=1))
    return jnp.concatenate(rows, axis=0)


def level_tiles(leaf_count, group):
    tiles = {}
    level = 1
    while level < leaf_count:
        children = 2 * level
        span = max(group, min(children, 2 * group))
        tiles[level] = [(children + first, span) for first in range(0, children, span)]
        level = children
    return tiles


def tile_mask(first, span, level, rank, group):
    row = lax.broadcasted_iota(jnp.int32, (span * rank, group * rank), 0)
    lane = lax.broadcasted_iota(jnp.int32, (span * rank, group * rank), 1)
    child = row // rank
    return (child // 2 == lane // rank) & (child + first < 4 * level)


def fetch(pairs, sems):
    copies = []
    for index, (source, target) in enumerate(pairs):
        copy = pltpu.make_async_copy(source, target, sems.at[index])
        copy.start()
        copies.append(copy)
    return copies


def up_kernel(
    dens_hbm, bases_hbm, maps_hbm, coef_ref, high_ref, low_ref, root_ref,
    dens_ref, bases_ref, maps_ref, spread_ref, sems,
):
    copies = fetch([(dens_hbm, dens_ref), (bases_hbm, bases_ref), (maps_hbm, maps_ref)], sems)
    columns, points = dens_ref.shape
    rank = bases_ref.shape[0]
    group = LANES // rank
    node_count = maps_ref.shape[2]
    leaf_count = node_count // 2
    width = points // leaf_count
    copies[0].wait()
    copies[1].wait()
    step = group * width
    coefs = []
    for first in range(0, points, step):
        high, low = halves(bases_ref[:, first : first + step])
        dens = dens_ref[:, first : first + step]
        coefs.append(
            dot_nt(dens, spread_bases(high, group)) + dot_nt(dens, spread_bases(low, group))
        )
    coef = jnp.concatenate(coefs, axis=1)
    coef_ref[...] = coef
    copies[2].wait()
    for row in range(rank):
        slab = jnp.concatenate([maps_ref[row]] * group, axis=0)
        spread_ref[pl.ds(row, node_count, stride=rank), :] = slab.T
    level = leaf_count // 2
    tiles = level_tiles(leaf_count, group)
    while level >= 1:
        parents = []
        for index, (first, span) in enumerate(tiles[level]):
            rows = slice(first * rank, (first + span) * rank)
            masked = jnp.where(tile_mask(first, span, level, rank, group), spread_ref[rows, :], 0.0)
            high, low = halves(masked)
            place = first - 2 * level
            if level > 1:
                high_ref[rows, :] = high
                low_ref[rows, :] = low
            else:
                high_ref[0 : span * rank, :] = high
                low_ref[0 : span * rank, :] = low
            lanes = slice(place * rank, (place + span) * rank)
            parents.append(split_dot(dot_nn, coef[:, lanes], high, low))
        coef = jnp.concatenate(parents, axis=1) if len(parents) > 1 else parents[0]
        level //= 2
    high = coef.astype(BF16).astype(F32)
    rest = coef - high
    middle = rest.astype(BF16).astype(F32)
    last = (rest - middle).astype(BF16).astype(F32)
    packed = high + pltpu.roll(middle, rank, 1) + pltpu.roll(last, 2 * rank, 1)
    root_ref[...] = packed.astype(BF16)


def select_kernel(
    faces, far_groups, extra, where_ref, send_hbm, dens_hbm, root_ref, *refs,
):
    other_refs = refs[: far_groups - 1]
    out_refs = refs[far_groups - 1 + extra : -3]
    send_ref, dens_ref, sems = refs[-3:]
    copies = fetch([(send_hbm, send_ref), (dens_hbm, dens_ref)], sems)
    device = where_ref[0]
    columns = dens_ref.shape[0]
    cap = send_ref.shape[1]
    for copy in copies:
        copy.wait()
    for (directions, stride), out_ref in zip(faces, out_refs):
        direction = directions[0]
        if len(directions) > 1:
            direction = direction + device // stride % 2
        for place in range(cap):
            leaf = jnp.maximum(send_ref[direction, place, device], 0)
            for part, panel_ref in enumerate((dens_ref, *other_refs)):
                row = (place * far_groups + part) * columns
                out_ref[row : row + columns, :] = panel_ref[
                    :, pl.ds(pl.multiple_of(leaf * LANES, LANES), LANES)
                ]
        out_ref[cap * far_groups * columns :, :] = root_ref[...]


def near_kernel(
    faces, far_groups, share, *refs,
):
    source_hbms, refs = refs[:share], refs[share:]
    dens_hbm, refs = refs[0], refs[1:]
    other_refs, refs = refs[: far_groups - 1], refs[far_groups - 1 :]
    got_refs, refs = refs[: len(faces)], refs[len(faces) :]
    block_hbm, refs = refs[0], refs[1:]
    mate_refs, refs = refs[: share - 1], refs[share - 1 :]
    out_refs, refs = refs[:far_groups], refs[far_groups:]
    source_refs, refs = refs[:share], refs[share:]
    dens_ref, block_ref, buffer_ref, small_sems, sems = refs
    columns, points = dens_ref.shape
    leaf_count, near_count, width, _ = block_ref.shape
    chunk_count = sems.shape[0]
    chunk = leaf_count // chunk_count
    copies = fetch(
        [(dens_hbm, dens_ref)] + list(zip(source_hbms, source_refs)), small_sems
    )
    block_copies = fetch(
        [
            (block_hbm.at[pl.ds(index * chunk, chunk)], block_ref.at[pl.ds(index * chunk, chunk)])
            for index in range(chunk_count)
        ],
        sems,
    )
    cap = (got_refs[0].shape[0] // columns - 1) // far_groups
    for (directions, _), got_ref in zip(faces, got_refs):
        for direction in directions:
            for place in range(cap):
                row = place * far_groups * columns
                buffer_ref[leaf_count + direction * cap + place] = got_ref[
                    row : row + far_groups * columns, :
                ]
    copies[0].wait()
    for part, panel_ref in enumerate((dens_ref, *other_refs)):
        rows = slice(part * columns, (part + 1) * columns)
        for leaf in range(leaf_count):
            buffer_ref[leaf, rows, :] = panel_ref[:, leaf * width : (leaf + 1) * width]
    for copy in copies[1:]:
        copy.wait()
    tables = list(zip(source_refs[1:], mate_refs)) + [(source_refs[0], block_ref)]
    for turn, (source_ref, blocks_ref) in enumerate(tables):
        for leaf in range(leaf_count):
            if blocks_ref is block_ref and leaf % chunk == 0:
                block_copies[leaf // chunk].wait()
            panels = [buffer_ref[source_ref[block, leaf]] for block in range(near_count)]
            blocks = [blocks_ref[leaf, block] for block in range(near_count)]
            total = dot_nt(jnp.concatenate(panels, axis=1), jnp.concatenate(blocks, axis=1))
            lanes = slice(leaf * width, (leaf + 1) * width)
            for part, out_ref in enumerate(out_refs):
                term = total[part * columns : (part + 1) * columns]
                out_ref[:, lanes] = term if turn == 0 else out_ref[:, lanes] + term


def couple_kernel(
    far_hbm, coef_ref, coupling_ref, out_ref, far_ref, turned_ref, sems,
):
    copies = fetch([(far_hbm, far_ref)], sems)
    columns, lanes = coef_ref.shape
    leaf_count, far_count, rank = coupling_ref.shape[:3]
    high, low = halves(coef_ref[...])
    both = jnp.concatenate([high.astype(F32), low.astype(F32)], axis=0)
    for first in range(0, lanes, LANES):
        turned_ref[first : first + LANES, :] = both[:, first : first + LANES].T.astype(BF16)
    copies[0].wait()
    group = LANES // rank
    parts = []
    for leaf in range(leaf_count):
        maps = jnp.concatenate([coupling_ref[leaf, j] for j in range(far_count)], axis=1)
        maps = jnp.concatenate(halves(maps), axis=0)
        picked = jnp.concatenate(
            [
                turned_ref[pl.ds(pl.multiple_of(far_ref[j, leaf] * rank, rank), rank), :]
                for j in range(far_count)
            ],
            axis=0,
        )
        out = dot_nn(maps, picked)
        parts.append(out[:rank] + out[rank:])
        if len(parts) == group:
            turned = jnp.concatenate(parts, axis=0).T
            spot = (leaf + 1 - group) * rank
            out_ref[:, spot : spot + LANES] = turned[:columns] + turned[columns:]
            parts = []


def far_kernel(
    roots, where_ref, near_ref, local_ref, bases_ref, high_ref, low_ref, upper_hbm, cross_hbm,
    *refs,
):
    root_refs = refs[: len(roots)]
    out_ref, upper_ref, cross_ref, tree_ref, sems = refs[len(roots) :]
    copies = fetch([(upper_hbm, upper_ref), (cross_hbm, cross_ref)], sems)
    device = where_ref[0]
    columns, points = near_ref.shape
    rank = bases_ref.shape[0]
    group = LANES // rank
    leaf_count = high_ref.shape[0] // (2 * rank)
    device_count = upper_ref.shape[0] // 2
    lane = lax.broadcasted_iota(jnp.int32, (LANES, rank), 0)
    column = lax.broadcasted_iota(jnp.int32, (LANES, rank), 1)
    gather = jnp.where((lane % rank == column) & (lane < 3 * rank), 1.0, 0.0).astype(BF16)
    for tiles, root_ref in zip(roots, root_refs):
        if tiles is None:
            for index in range(device_count):
                tree_ref[device_count + index] = dot_nn(root_ref[index], gather)
        else:
            for turn, row in tiles:
                piece = root_ref[row : row + columns, :]
                tree_ref[device_count + (device ^ turn)] = dot_nn(piece, gather)
    for copy in copies:
        copy.wait()
    level = device_count // 2
    while level >= 4:
        for node in range(level, 2 * level):
            total = None
            for child in (2 * node, 2 * node + 1):
                term = split_dot(dot_nn, tree_ref[child], *halves(upper_ref[child]))
                total = term if total is None else total + term
            tree_ref[node] = total
        level //= 2
    field = None
    level = 4
    while level <= device_count:
        place = device // (device_count // level)
        node = level + place
        third = jnp.where(place % 2 == 0, place + 3, place - 3)
        total = None
        for slot, other in enumerate((place - 2, place + 2, third)):
            inside = (other >= 0) & (other < level)
            value = tree_ref[level + jnp.clip(other, 0, level - 1)]
            value = jnp.where(inside, value, 0.0)
            term = split_dot(dot_nt, value, *halves(cross_ref[node, slot]))
            total = term if total is None else total + term
        if field is not None:
            total = total + split_dot(dot_nt, field, *halves(upper_ref[node]))
        field = total
        level *= 2
    field = jnp.concatenate([field, jnp.zeros((columns, LANES - rank), F32)], axis=1)
    tiles = level_tiles(leaf_count, group)
    level = 1
    while level < leaf_count:
        children = []
        for index, (first, span) in enumerate(tiles[level]):
            start = first * rank if level > 1 else 0
            rows = slice(start, start + span * rank)
            lanes = slice(index * LANES, (index + 1) * LANES)
            children.append(split_dot(dot_nt, field[:, lanes], high_ref[rows, :], low_ref[rows, :]))
        field = jnp.concatenate(children, axis=1) if len(children) > 1 else children[0]
        level *= 2
    width = points // leaf_count
    step = group * width
    for index in range(leaf_count // group):
        lanes = slice(index * LANES, (index + 1) * LANES)
        rows = field[:, lanes] + local_ref[:, lanes]
        spots = slice(index * step, (index + 1) * step)
        high, low = halves(bases_ref[:, spots])
        out_ref[:, spots] = near_ref[:, spots] + split_dot(
            dot_nn, rows, spread_bases(high, group), spread_bases(low, group)
        )


def hbm(value):
    return pltpu.with_memory_space_constraint(value, pltpu.HBM)


def hint(micros):
    return pl.CostEstimate(flops=0, bytes_accessed=int(micros * 3.69e6), transcendentals=0)


def local(
    densities,
    bases,
    near_blocks,
    near_src,
    send_leaf,
    far_src,
    leaf_coupling,
    local_transfer,
    upper_transfer,
    up_coupling,
):
    leaf_devices = lax.axis_size("leaf")
    far_groups = lax.axis_size("far")
    share = lax.axis_size("mate")
    side = cube_side(leaf_devices)
    offsets = face_offsets(leaf_devices)
    columns, points = densities.shape
    leaf_count, near_count, width, _ = near_blocks.shape
    rank = bases.shape[0]
    cap = send_leaf.shape[2]
    node_count = local_transfer.shape[1]
    where = lax.axis_index("leaf").astype(jnp.int32).reshape(1)
    params = pltpu.CompilerParams(vmem_limit_bytes=16 * 2**20)
    dma = pltpu.SemaphoreType.DMA

    def rotated(value, axis, shift):
        count = lax.axis_size(axis)
        return lax.ppermute(value, axis, [(i, (i - shift) % count) for i in range(count)])

    def crossed(value, turn):
        return lax.ppermute(value, "leaf", [(i, i ^ turn) for i in range(leaf_devices)])

    sources = near_src.T
    others = [rotated(densities, "far", part) for part in range(1, far_groups)]
    all_sources = [sources] + [rotated(sources, "mate", part) for part in range(1, share)]
    mate_blocks = [rotated(near_blocks, "mate", part) for part in range(1, share)]

    coef, high, low, root = pl.pallas_call(
        up_kernel,
        out_shape=[
            jax.ShapeDtypeStruct((columns, leaf_count * rank), F32),
            jax.ShapeDtypeStruct((node_count * rank, LANES), BF16),
            jax.ShapeDtypeStruct((node_count * rank, LANES), BF16),
            jax.ShapeDtypeStruct((columns, LANES), BF16),
        ],
        in_specs=[HBM] * 3,
        out_specs=[VMEM] * 4,
        scratch_shapes=[
            pltpu.VMEM(densities.shape, BF16),
            pltpu.VMEM(bases.shape, F32),
            pltpu.VMEM((rank, rank, node_count), F32),
            pltpu.VMEM((node_count * rank, LANES), F32),
            dma((3,)),
        ],
        compiler_params=params,
        cost_estimate=hint(4),
        name="up",
    )(hbm(densities), hbm(bases), hbm(local_transfer[0].transpose(1, 2, 0)))

    if side == 2:
        faces = [((2 * axis, 2 * axis + 1), 2**axis) for axis in range(3)]
    else:
        faces = [((direction,), offset) for direction, offset in enumerate(offsets)]
    send = send_leaf.transpose(1, 2, 0)
    chunk = (cap * far_groups + 1) * columns
    outgoing = pl.pallas_call(
        functools.partial(select_kernel, faces, far_groups, share - 1),
        out_shape=[jax.ShapeDtypeStruct((chunk, LANES), BF16)] * len(faces),
        in_specs=[SMEM, HBM, HBM] + [VMEM] * far_groups + [HBM] * (share - 1),
        out_specs=[VMEM] * len(faces),
        scratch_shapes=[
            pltpu.SMEM(send.shape, jnp.int32),
            pltpu.VMEM(densities.shape, BF16),
            dma((2,)),
        ],
        compiler_params=params,
        cost_estimate=hint(1),
        name="select",
    )(where, hbm(send), hbm(densities), root, *others, *all_sources[1:])
    tail = cap * far_groups * columns
    if side == 2:
        arrived = [crossed(value, stride) for (_, stride), value in zip(faces, outgoing)]
        near_roots = [value[tail:] for value in arrived[:2]]
        third = crossed(near_roots[0], 2)
        rest = crossed(jnp.concatenate(near_roots + [third], axis=0), 4)
        roots = [
            ([(0, 0)], root),
            ([(3, 0)], third),
            ([(5, 0), (6, columns), (7, 2 * columns)], rest),
        ]
        roots += [([(stride, tail)], value) for (_, stride), value in zip(faces, arrived)]
    else:
        arrived = [shifted(value, "leaf", stride) for (_, stride), value in zip(faces, outgoing)]
        roots = [(None, lax.all_gather(root, "leaf", axis=0))]

    slots = leaf_count + len(offsets) * cap
    partials = pl.pallas_call(
        functools.partial(near_kernel, faces, far_groups, share),
        out_shape=[jax.ShapeDtypeStruct((columns, points), F32)] * far_groups,
        in_specs=[HBM] * (share + 1)
        + [VMEM] * (far_groups - 1 + len(faces))
        + [HBM]
        + [VMEM] * (share - 1),
        out_specs=[VMEM] * far_groups,
        scratch_shapes=[pltpu.SMEM(sources.shape, jnp.int32)] * share
        + [
            pltpu.VMEM(densities.shape, BF16),
            pltpu.VMEM(near_blocks.shape, BF16),
            pltpu.VMEM((slots, far_groups * columns, width), BF16),
            dma((1 + share,)),
            dma((4,)),
        ],
        compiler_params=params,
        cost_estimate=hint(3),
        name="near",
    )(
        *map(hbm, all_sources), hbm(densities), *others, *arrived, hbm(near_blocks), *mate_blocks,
    )
    received = [rotated(partials[part], "far", -part) for part in range(1, far_groups)]
    far_table = far_src.T
    leaf_local = pl.pallas_call(
        couple_kernel,
        out_shape=jax.ShapeDtypeStruct(coef.shape, F32),
        in_specs=[HBM, VMEM, VMEM],
        out_specs=VMEM,
        scratch_shapes=[
            pltpu.SMEM(far_table.shape, jnp.int32),
            pltpu.VMEM((leaf_count * rank, 2 * columns), BF16),
            dma((1,)),
        ],
        compiler_params=params,
        cost_estimate=hint(2),
        name="couple",
    )(hbm(far_table), coef, leaf_coupling)
    total = pl.pallas_call(
        functools.partial(far_kernel, [tiles for tiles, _ in roots]),
        out_shape=jax.ShapeDtypeStruct((columns, points), F32),
        in_specs=[SMEM] + [VMEM] * 5 + [HBM] * 2 + [VMEM] * len(roots),
        out_specs=VMEM,
        scratch_shapes=[
            pltpu.VMEM(upper_transfer.shape, F32),
            pltpu.VMEM(up_coupling.shape, F32),
            pltpu.VMEM((2 * leaf_devices, columns, rank), F32),
            dma((2,)),
        ],
        compiler_params=params,
        cost_estimate=hint(2),
        name="far",
    )(
        where, partials[0], leaf_local, bases, high, low, hbm(upper_transfer), hbm(up_coupling),
        *[value for _, value in roots],
    )
    for value in received:
        total = total + value
    return total


def solution(mesh):
    leaf_devices, rhs_devices = mesh.shape["leaf"], mesh.shape["rhs"]
    share = 2 if rhs_devices % 2 == 0 else 1
    split = Mesh(
        mesh.devices.reshape(leaf_devices, rhs_devices // share, share), ("leaf", "far", "mate")
    )
    rhs = ("far", "mate")
    in_specs = (
        P(rhs, "leaf"),
        P(None, "leaf"),
        P("leaf", rhs, None, None),
        P("leaf", rhs),
        P(),
        P("leaf", None),
        P("leaf", None, None, None),
        P("leaf", None, None, None),
        P(),
        P(),
    )
    return jax.shard_map(
        local, mesh=split, in_specs=in_specs, out_specs=P(rhs, "leaf"), check_vma=False
    )
```

```python
import functools

import jax
import jax.numpy as jnp
from jax import lax
from jax.experimental import pallas as pl
from jax.experimental.pallas import tpu as pltpu
from jax.sharding import Mesh
from jax.sharding import PartitionSpec as P

FACE_SIGNS = ((1, 0), (-1, 0), (1, 1), (-1, 1), (1, 2), (-1, 2))
F32 = jnp.float32
BF16 = jnp.bfloat16
LANES = 128
VMEM = pl.BlockSpec(memory_space=pltpu.VMEM)
HBM = pl.BlockSpec(memory_space=pltpu.HBM)
SMEM = pl.BlockSpec(memory_space=pltpu.SMEM)


def cube_side(device_count):
    return max((edge_len for edge_len in range(1, 65) if edge_len**3 <= device_count))


def face_offsets(device_count):
    side_len = cube_side(device_count)
    return [face_sign * side_len**axis_pos for face_sign, axis_pos in FACE_SIGNS]


def shifted(value, axis, steps):
    count = lax.axis_size(axis)
    first, last = (max(0, -steps), min(count, count - steps))
    return lax.ppermute(value, axis, [(source, source + steps) for source in range(first, last)])


def halves(value):
    high = value.astype(BF16)
    return high, (value - high.astype(F32)).astype(BF16)


def dot_nn(left, right):
    return lax.dot_general(left, right, (((1,), (0,)), ((), ())), preferred_element_type=F32)


def dot_nt(left, right):
    return lax.dot_general(left, right, (((1,), (1,)), ((), ())), preferred_element_type=F32)


def split_dot(dot, rows, right_high, right_low):
    count = rows.shape[0]
    high, low = halves(rows)
    both = jnp.concatenate([high, low], axis=0)
    out = dot(both, right_high) + dot(both, right_low)
    return out[:count] + out[count:]


def spread_bases(block, group):
    rank, lanes = block.shape
    width = lanes // group
    zero = jnp.zeros((rank, width), block.dtype)
    rows = []
    for slot in range(group):
        pieces = [zero] * group
        pieces[slot] = block[:, slot * width : (slot + 1) * width]
        rows.append(jnp.concatenate(pieces, axis=1))
    return jnp.concatenate(rows, axis=0)


def level_tiles(leaf_count, group):
    tiles = {}
    level = 1
    while level < leaf_count:
        children = 2 * level
        span = max(group, min(children, 2 * group))
        tiles[level] = [(children + first, span) for first in range(0, children, span)]
        level = children
    return tiles


def tile_mask(first, span, level, rank, group):
    row = lax.broadcasted_iota(jnp.int32, (span * rank, group * rank), 0)
    lane = lax.broadcasted_iota(jnp.int32, (span * rank, group * rank), 1)
    child = row // rank
    return (child // 2 == lane // rank) & (child + first < 4 * level)


def fetch(pairs, sems):
    copies = []
    for index, (source, target) in enumerate(pairs):
        copy = pltpu.make_async_copy(source, target, sems.at[index])
        copy.start()
        copies.append(copy)
    return copies


def up_kernel(
    dens_hbm, bases_hbm, maps_hbm, coef_ref, high_ref, low_ref, root_ref,
    dens_ref, bases_ref, maps_ref, spread_ref, sems,
):
    copies = fetch([(dens_hbm, dens_ref), (bases_hbm, bases_ref), (maps_hbm, maps_ref)], sems)
    columns, points = dens_ref.shape
    rank = bases_ref.shape[0]
    group = LANES // rank
    node_count = maps_ref.shape[2]
    leaf_count = node_count // 2
    width = points // leaf_count
    copies[0].wait()
    copies[1].wait()
    step = group * width
    coefs = []
    for first in range(0, points, step):
        high, low = halves(bases_ref[:, first : first + step])
        dens = dens_ref[:, first : first + step]
        coefs.append(
            dot_nt(dens, spread_bases(high, group)) + dot_nt(dens, spread_bases(low, group))
        )
    coef = jnp.concatenate(coefs, axis=1)
    coef_ref[...] = coef
    copies[2].wait()
    for row in range(rank):
        slab = jnp.concatenate([maps_ref[row]] * group, axis=0)
        spread_ref[pl.ds(row, node_count, stride=rank), :] = slab.T
    level = leaf_count // 2
    tiles = level_tiles(leaf_count, group)
    while level >= 1:
        parents = []
        for index, (first, span) in enumerate(tiles[level]):
            rows = slice(first * rank, (first + span) * rank)
            masked = jnp.where(tile_mask(first, span, level, rank, group), spread_ref[rows, :], 0.0)
            high, low = halves(masked)
            place = first - 2 * level
            if level > 1:
                high_ref[rows, :] = high
                low_ref[rows, :] = low
            else:
                high_ref[0 : span * rank, :] = high
                low_ref[0 : span * rank, :] = low
            lanes = slice(place * rank, (place + span) * rank)
            parents.append(split_dot(dot_nn, coef[:, lanes], high, low))
        coef = jnp.concatenate(parents, axis=1) if len(parents) > 1 else parents[0]
        level //= 2
    high = coef.astype(BF16).astype(F32)
    rest = coef - high
    middle = rest.astype(BF16).astype(F32)
    last = (rest - middle).astype(BF16).astype(F32)
    packed = high + pltpu.roll(middle, rank, 1) + pltpu.roll(last, 2 * rank, 1)
    root_ref[...] = packed.astype(BF16)


def select_kernel(
    faces, far_groups, extra, where_ref, send_hbm, dens_hbm, root_ref, *refs,
):
    other_refs = refs[: far_groups - 1]
    out_refs = refs[far_groups - 1 + extra : -3]
    send_ref, dens_ref, sems = refs[-3:]
    copies = fetch([(send_hbm, send_ref), (dens_hbm, dens_ref)], sems)
    device = where_ref[0]
    columns = dens_ref.shape[0]
    cap = send_ref.shape[1]
    for copy in copies:
        copy.wait()
    for (directions, stride), out_ref in zip(faces, out_refs):
        direction = directions[0]
        if len(directions) > 1:
            direction = direction + device // stride % 2
        for place in range(cap):
            leaf = jnp.maximum(send_ref[direction, place, device], 0)
            for part, panel_ref in enumerate((dens_ref, *other_refs)):
                row = (place * far_groups + part) * columns
                out_ref[row : row + columns, :] = panel_ref[
                    :, pl.ds(pl.multiple_of(leaf * LANES, LANES), LANES)
                ]
        out_ref[cap * far_groups * columns :, :] = root_ref[...]


def near_kernel(
    faces, far_groups, share, *refs,
):
    source_hbms, refs = refs[:share], refs[share:]
    dens_hbm, refs = refs[0], refs[1:]
    other_refs, refs = refs[: far_groups - 1], refs[far_groups - 1 :]
    got_refs, refs = refs[: len(faces)], refs[len(faces) :]
    block_hbm, refs = refs[0], refs[1:]
    mate_refs, refs = refs[: share - 1], refs[share - 1 :]
    out_refs, refs = refs[:far_groups], refs[far_groups:]
    source_refs, refs = refs[:share], refs[share:]
    dens_ref, block_ref, buffer_ref, small_sems, sems = refs
    columns, points = dens_ref.shape
    leaf_count, near_count, width, _ = block_ref.shape
    chunk_count = sems.shape[0]
    chunk = leaf_count // chunk_count
    copies = fetch(
        [(dens_hbm, dens_ref)] + list(zip(source_hbms, source_refs)), small_sems
    )
    block_copies = fetch(
        [
            (block_hbm.at[pl.ds(index * chunk, chunk)], block_ref.at[pl.ds(index * chunk, chunk)])
            for index in range(chunk_count)
        ],
        sems,
    )
    cap = (got_refs[0].shape[0] // columns - 1) // far_groups
    for (directions, _), got_ref in zip(faces, got_refs):
        for direction in directions:
            for place in range(cap):
                row = place * far_groups * columns
                buffer_ref[leaf_count + direction * cap + place] = got_ref[
                    row : row + far_groups * columns, :
                ]
    copies[0].wait()
    for part, panel_ref in enumerate((dens_ref, *other_refs)):
        rows = slice(part * columns, (part + 1) * columns)
        for leaf in range(leaf_count):
            buffer_ref[leaf, rows, :] = panel_ref[:, leaf * width : (leaf + 1) * width]
    for copy in copies[1:]:
        copy.wait()
    tables = list(zip(source_refs[1:], mate_refs)) + [(source_refs[0], block_ref)]
    for turn, (source_ref, blocks_ref) in enumerate(tables):
        for leaf in range(leaf_count):
            if blocks_ref is block_ref and leaf % chunk == 0:
                block_copies[leaf // chunk].wait()
            panels = [buffer_ref[source_ref[block, leaf]] for block in range(near_count)]
            blocks = [blocks_ref[leaf, block] for block in range(near_count)]
            total = dot_nt(jnp.concatenate(panels, axis=1), jnp.concatenate(blocks, axis=1))
            lanes = slice(leaf * width, (leaf + 1) * width)
            for part, out_ref in enumerate(out_refs):
                term = total[part * columns : (part + 1) * columns]
                out_ref[:, lanes] = term if turn == 0 else out_ref[:, lanes] + term


def couple_kernel(
    far_hbm, coef_ref, coupling_ref, out_ref, far_ref, turned_ref, sems,
):
    copies = fetch([(far_hbm, far_ref)], sems)
    columns, lanes = coef_ref.shape
    leaf_count, far_count, rank = coupling_ref.shape[:3]
    high, low = halves(coef_ref[...])
    both = jnp.concatenate([high.astype(F32), low.astype(F32)], axis=0)
    for first in range(0, lanes, LANES):
        turned_ref[first : first + LANES, :] = both[:, first : first + LANES].T.astype(BF16)
    copies[0].wait()
    group = LANES // rank
    parts = []
    for leaf in range(leaf_count):
        maps = jnp.concatenate([coupling_ref[leaf, j] for j in range(far_count)], axis=1)
        maps = jnp.concatenate(halves(maps), axis=0)
        picked = jnp.concatenate(
            [
                turned_ref[pl.ds(pl.multiple_of(far_ref[j, leaf] * rank, rank), rank), :]
                for j in range(far_count)
            ],
            axis=0,
        )
        out = dot_nn(maps, picked)
        parts.append(out[:rank] + out[rank:])
        if len(parts) == group:
            turned = jnp.concatenate(parts, axis=0).T
            spot = (leaf + 1 - group) * rank
            out_ref[:, spot : spot + LANES] = turned[:columns] + turned[columns:]
            parts = []


def far_kernel(
    roots, where_ref, near_ref, local_ref, bases_ref, high_ref, low_ref, upper_hbm, cross_hbm,
    *refs,
):
    root_refs = refs[: len(roots)]
    out_ref, upper_ref, cross_ref, tree_ref, sems = refs[len(roots) :]
    copies = fetch([(upper_hbm, upper_ref), (cross_hbm, cross_ref)], sems)
    device = where_ref[0]
    columns, points = near_ref.shape
    rank = bases_ref.shape[0]
    group = LANES // rank
    leaf_count = high_ref.shape[0] // (2 * rank)
    device_count = upper_ref.shape[0] // 2
    lane = lax.broadcasted_iota(jnp.int32, (LANES, rank), 0)
    column = lax.broadcasted_iota(jnp.int32, (LANES, rank), 1)
    gather = jnp.where((lane % rank == column) & (lane < 3 * rank), 1.0, 0.0).astype(BF16)
    for tiles, root_ref in zip(roots, root_refs):
        if tiles is None:
            for index in range(device_count):
                tree_ref[device_count + index] = dot_nn(root_ref[index], gather)
        else:
            for turn, row in tiles:
                piece = root_ref[row : row + columns, :]
                tree_ref[device_count + (device ^ turn)] = dot_nn(piece, gather)
    for copy in copies:
        copy.wait()
    level = device_count // 2
    while level >= 4:
        for node in range(level, 2 * level):
            total = None
            for child in (2 * node, 2 * node + 1):
                term = split_dot(dot_nn, tree_ref[child], *halves(upper_ref[child]))
                total = term if total is None else total + term
            tree_ref[node] = total
        level //= 2
    field = None
    level = 4
    while level <= device_count:
        place = device // (device_count // level)
        node = level + place
        third = jnp.where(place % 2 == 0, place + 3, place - 3)
        total = None
        for slot, other in enumerate((place - 2, place + 2, third)):
            inside = (other >= 0) & (other < level)
            value = tree_ref[level + jnp.clip(other, 0, level - 1)]
            value = jnp.where(inside, value, 0.0)
            term = split_dot(dot_nt, value, *halves(cross_ref[node, slot]))
            total = term if total is None else total + term
        if field is not None:
            total = total + split_dot(dot_nt, field, *halves(upper_ref[node]))
        field = total
        level *= 2
    field = jnp.concatenate([field, jnp.zeros((columns, LANES - rank), F32)], axis=1)
    tiles = level_tiles(leaf_count, group)
    level = 1
    while level < leaf_count:
        children = []
        for index, (first, span) in enumerate(tiles[level]):
            start = first * rank if level > 1 else 0
            rows = slice(start, start + span * rank)
            lanes = slice(index * LANES, (index + 1) * LANES)
            children.append(split_dot(dot_nt, field[:, lanes], high_ref[rows, :], low_ref[rows, :]))
        field = jnp.concatenate(children, axis=1) if len(children) > 1 else children[0]
        level *= 2
    width = points // leaf_count
    step = group * width
    for index in range(leaf_count // group):
        lanes = slice(index * LANES, (index + 1) * LANES)
        rows = field[:, lanes] + local_ref[:, lanes]
        spots = slice(index * step, (index + 1) * step)
        high, low = halves(bases_ref[:, spots])
        out_ref[:, spots] = near_ref[:, spots] + split_dot(
            dot_nn, rows, spread_bases(high, group), spread_bases(low, group)
        )


def hbm(value):
    return pltpu.with_memory_space_constraint(value, pltpu.HBM)


def hint(micros):
    return pl.CostEstimate(flops=0, bytes_accessed=int(micros * 3.69e6), transcendentals=0)


def local(
    densities,
    bases,
    near_blocks,
    near_src,
    send_leaf,
    far_src,
    leaf_coupling,
    local_transfer,
    upper_transfer,
    up_coupling,
):
    leaf_devices = lax.axis_size("leaf")
    far_groups = lax.axis_size("far")
    share = lax.axis_size("mate")
    side = cube_side(leaf_devices)
    offsets = face_offsets(leaf_devices)
    columns, points = densities.shape
    leaf_count, near_count, width, _ = near_blocks.shape
    rank = bases.shape[0]
    cap = send_leaf.shape[2]
    node_count = local_transfer.shape[1]
    where = lax.axis_index("leaf").astype(jnp.int32).reshape(1)
    params = pltpu.CompilerParams(vmem_limit_bytes=16 * 2**20)
    dma = pltpu.SemaphoreType.DMA

    def rotated(value, axis, shift):
        count = lax.axis_size(axis)
        return lax.ppermute(value, axis, [(i, (i - shift) % count) for i in range(count)])

    def crossed(value, turn):
        return lax.ppermute(value, "leaf", [(i, i ^ turn) for i in range(leaf_devices)])

    sources = near_src.T
    others = [rotated(densities, "far", part) for part in range(1, far_groups)]
    all_sources = [sources] + [rotated(sources, "mate", part) for part in range(1, share)]
    coef, high, low, root = pl.pallas_call(
        up_kernel,
        out_shape=[
            jax.ShapeDtypeStruct((columns, leaf_count * rank), F32),
            jax.ShapeDtypeStruct((node_count * rank, LANES), BF16),
            jax.ShapeDtypeStruct((node_count * rank, LANES), BF16),
            jax.ShapeDtypeStruct((columns, LANES), BF16),
        ],
        in_specs=[HBM] * 3,
        out_specs=[VMEM] * 4,
        scratch_shapes=[
            pltpu.VMEM(densities.shape, BF16),
            pltpu.VMEM(bases.shape, F32),
            pltpu.VMEM((rank, rank, node_count), F32),
            pltpu.VMEM((node_count * rank, LANES), F32),
            dma((3,)),
        ],
        compiler_params=params,
        cost_estimate=hint(4),
        name="up",
    )(hbm(densities), hbm(bases), hbm(local_transfer[0].transpose(1, 2, 0)))

    later_blocks, others, all_sources, root = lax.optimization_barrier(
        (near_blocks, others, all_sources, root)
    )
    mate_blocks = [rotated(later_blocks, "mate", part) for part in range(1, share)]

    if side == 2:
        faces = [((2 * axis, 2 * axis + 1), 2**axis) for axis in range(3)]
    else:
        faces = [((direction,), offset) for direction, offset in enumerate(offsets)]
    send = send_leaf.transpose(1, 2, 0)
    chunk = (cap * far_groups + 1) * columns
    outgoing = pl.pallas_call(
        functools.partial(select_kernel, faces, far_groups, share - 1),
        out_shape=[jax.ShapeDtypeStruct((chunk, LANES), BF16)] * len(faces),
        in_specs=[SMEM, HBM, HBM] + [VMEM] * far_groups + [HBM] * (share - 1),
        out_specs=[VMEM] * len(faces),
        scratch_shapes=[
            pltpu.SMEM(send.shape, jnp.int32),
            pltpu.VMEM(densities.shape, BF16),
            dma((2,)),
        ],
        compiler_params=params,
        cost_estimate=hint(1),
        name="select",
    )(where, hbm(send), hbm(densities), root, *others, *all_sources[1:])
    tail = cap * far_groups * columns
    if side == 2:
        arrived = [crossed(value, stride) for (_, stride), value in zip(faces, outgoing)]
        held = jnp.concatenate([root] + [value[tail:] for value in arrived], axis=0)
        whole = leaf_devices - 1
        opposite = crossed(held, whole)
        turns = [0] + [stride for _, stride in faces]
        roots = [
            ([(0, 0)], root),
            ([(turn ^ whole, row * columns) for row, turn in enumerate(turns)], opposite),
        ]
        roots += [([(stride, tail)], value) for (_, stride), value in zip(faces, arrived)]
    else:
        arrived = [shifted(value, "leaf", stride) for (_, stride), value in zip(faces, outgoing)]
        roots = [(None, lax.all_gather(root, "leaf", axis=0))]

    slots = leaf_count + len(offsets) * cap
    partials = pl.pallas_call(
        functools.partial(near_kernel, faces, far_groups, share),
        out_shape=[jax.ShapeDtypeStruct((columns, points), F32)] * far_groups,
        in_specs=[HBM] * (share + 1)
        + [VMEM] * (far_groups - 1 + len(faces))
        + [HBM]
        + [VMEM] * (share - 1),
        out_specs=[VMEM] * far_groups,
        scratch_shapes=[pltpu.SMEM(sources.shape, jnp.int32)] * share
        + [
            pltpu.VMEM(densities.shape, BF16),
            pltpu.VMEM(near_blocks.shape, BF16),
            pltpu.VMEM((slots, far_groups * columns, width), BF16),
            dma((1 + share,)),
            dma((4,)),
        ],
        compiler_params=params,
        cost_estimate=hint(3),
        name="near",
    )(
        *map(hbm, all_sources), hbm(densities), *others, *arrived, hbm(near_blocks), *mate_blocks,
    )
    received = [rotated(partials[part], "far", -part) for part in range(1, far_groups)]
    far_table = far_src.T
    leaf_local = pl.pallas_call(
        couple_kernel,
        out_shape=jax.ShapeDtypeStruct(coef.shape, F32),
        in_specs=[HBM, VMEM, VMEM],
        out_specs=VMEM,
        scratch_shapes=[
            pltpu.SMEM(far_table.shape, jnp.int32),
            pltpu.VMEM((leaf_count * rank, 2 * columns), BF16),
            dma((1,)),
        ],
        compiler_params=params,
        cost_estimate=hint(2),
        name="couple",
    )(hbm(far_table), coef, leaf_coupling)
    total = pl.pallas_call(
        functools.partial(far_kernel, [tiles for tiles, _ in roots]),
        out_shape=jax.ShapeDtypeStruct((columns, points), F32),
        in_specs=[SMEM] + [VMEM] * 5 + [HBM] * 2 + [VMEM] * len(roots),
        out_specs=VMEM,
        scratch_shapes=[
            pltpu.VMEM(upper_transfer.shape, F32),
            pltpu.VMEM(up_coupling.shape, F32),
            pltpu.VMEM((2 * leaf_devices, columns, rank), F32),
            dma((2,)),
        ],
        compiler_params=params,
        cost_estimate=hint(2),
        name="far",
    )(
        where, partials[0], leaf_local, bases, high, low, hbm(upper_transfer), hbm(up_coupling),
        *[value for _, value in roots],
    )
    for value in received:
        total = total + value
    return total


def solution(mesh):
    leaf_devices, rhs_devices = mesh.shape["leaf"], mesh.shape["rhs"]
    share = 2 if rhs_devices % 2 == 0 else 1
    split = Mesh(
        mesh.devices.reshape(leaf_devices, rhs_devices // share, share), ("leaf", "far", "mate")
    )
    rhs = ("far", "mate")
    in_specs = (
        P(rhs, "leaf"),
        P(None, "leaf"),
        P("leaf", rhs, None, None),
        P("leaf", rhs),
        P(),
        P("leaf", None),
        P("leaf", None, None, None),
        P("leaf", None, None, None),
        P(),
        P(),
    )
    return jax.shard_map(
        local, mesh=split, in_specs=in_specs, out_specs=P(rhs, "leaf"), check_vma=False
    )
```

```python
import functools

import jax
import jax.numpy as jnp
from jax import lax
from jax.experimental import pallas as pl
from jax.experimental.pallas import tpu as pltpu
from jax.sharding import Mesh
from jax.sharding import PartitionSpec as P

FACE_SIGNS = ((1, 0), (-1, 0), (1, 1), (-1, 1), (1, 2), (-1, 2))
F32 = jnp.float32
BF16 = jnp.bfloat16
LANES = 128
VMEM = pl.BlockSpec(memory_space=pltpu.VMEM)
HBM = pl.BlockSpec(memory_space=pltpu.HBM)
SMEM = pl.BlockSpec(memory_space=pltpu.SMEM)


def cube_side(device_count):
    return max((edge_len for edge_len in range(1, 65) if edge_len**3 <= device_count))


def face_offsets(device_count):
    side_len = cube_side(device_count)
    return [face_sign * side_len**axis_pos for face_sign, axis_pos in FACE_SIGNS]


def shifted(value, axis, steps):
    count = lax.axis_size(axis)
    first, last = (max(0, -steps), min(count, count - steps))
    return lax.ppermute(value, axis, [(source, source + steps) for source in range(first, last)])


def halves(value):
    high = value.astype(BF16)
    return high, (value - high.astype(F32)).astype(BF16)


def dot_nn(left, right):
    return lax.dot_general(left, right, (((1,), (0,)), ((), ())), preferred_element_type=F32)


def dot_nt(left, right):
    return lax.dot_general(left, right, (((1,), (1,)), ((), ())), preferred_element_type=F32)


def split_dot(dot, rows, right_high, right_low):
    count = rows.shape[0]
    high, low = halves(rows)
    both = jnp.concatenate([high, low], axis=0)
    out = dot(both, right_high) + dot(both, right_low)
    return out[:count] + out[count:]


def spread_bases(block, group):
    rank, lanes = block.shape
    width = lanes // group
    zero = jnp.zeros((rank, width), block.dtype)
    rows = []
    for slot in range(group):
        pieces = [zero] * group
        pieces[slot] = block[:, slot * width : (slot + 1) * width]
        rows.append(jnp.concatenate(pieces, axis=1))
    return jnp.concatenate(rows, axis=0)


def fetch(pairs, sems):
    copies = []
    for index, (source, target) in enumerate(pairs):
        copy = pltpu.make_async_copy(source, target, sems.at[index])
        copy.start()
        copies.append(copy)
    return copies


def up_kernel(
    dens_hbm, bases_hbm, maps_hbm, send_hbm, source_hbm,
    dens_ref, send_ref, source_ref, high_ref, low_ref, root_ref,
    bases_ref, maps_ref, spread_ref, chain_ref, sems,
):
    copies = fetch(
        [
            (maps_hbm, maps_ref),
            (bases_hbm, bases_ref),
            (dens_hbm, dens_ref),
            (send_hbm, send_ref),
            (source_hbm, source_ref),
        ],
        sems,
    )
    columns, points = dens_ref.shape
    rank, _, node_count = maps_ref.shape
    group = LANES // rank
    leaf_count = node_count // 2
    width = points // leaf_count
    copies[0].wait()
    node = lax.broadcasted_iota(jnp.int32, (node_count, LANES), 0)
    block = lax.broadcasted_iota(jnp.int32, (node_count, LANES), 1) // rank
    parent = node // 2 % group
    for first in range(0, rank, group):
        slab = maps_ref[first : first + group].reshape(group * rank, node_count).T
        turned = [slab] + [pltpu.roll(slab, turn * rank, 1) for turn in range(1, group)]
        for row in range(group):
            placed = jnp.zeros_like(slab)
            for place in range(group):
                here = (parent == place) & (block == place)
                placed = jnp.where(here, turned[(place - row) % group], placed)
            spread_ref[pl.ds(first + row, node_count, stride=rank), :] = placed
    tile = 2 * group * rank

    def children(parents, index):
        high, low = halves(spread_ref[index * tile : (index + 1) * tile, :])
        return split_dot(dot_nt, parents, high, low)

    row = lax.broadcasted_iota(jnp.int32, (rank, LANES), 0)
    lane = lax.broadcasted_iota(jnp.int32, (rank, LANES), 1)
    level = 1
    parents = jnp.where(lane == row + rank, 1.0, 0.0)
    while level < group:
        below = children(parents, 0)
        level *= 2
        parents = below[:, (level // group) * LANES : (level // group + 1) * LANES]
    chain_ref[:, LANES : 2 * LANES] = parents
    while level < leaf_count:
        for index in range(level // group, 2 * level // group):
            lanes = slice(index * LANES, (index + 1) * LANES)
            chain_ref[:, index * tile : (index + 1) * tile] = children(chain_ref[:, lanes], index)
        level *= 2
    for copy in copies[1:]:
        copy.wait()
    step = group * width
    root = jnp.zeros((columns, rank), F32)
    for index in range(leaf_count // group):
        spots = slice(index * step, (index + 1) * step)
        start = (leaf_count // group + index) * LANES
        high, low = halves(bases_ref[:, spots])
        basis = split_dot(
            dot_nn, chain_ref[:, start : start + LANES],
            spread_bases(high, group), spread_bases(low, group),
        )
        high, low = halves(basis)
        high_ref[:, spots] = high
        low_ref[:, spots] = low
        dens = dens_ref[:, spots]
        root += dot_nt(dens, high) + dot_nt(dens, low)
    root = jnp.concatenate([root, jnp.zeros((columns, LANES - rank), F32)], axis=1)
    high = root.astype(BF16).astype(F32)
    rest = root - high
    middle = rest.astype(BF16).astype(F32)
    last = (rest - middle).astype(BF16).astype(F32)
    packed = high + pltpu.roll(middle, rank, 1) + pltpu.roll(last, 2 * rank, 1)
    root_ref[...] = packed.astype(BF16)


def select_kernel(
    faces, far_groups, where_ref, send_vmem, dens_ref, root_ref, *refs,
):
    other_refs = refs[: far_groups - 1]
    out_refs = refs[far_groups - 1 : -2]
    send_ref, sems = refs[-2:]
    copies = fetch([(send_vmem, send_ref)], sems)
    device = where_ref[0]
    columns = dens_ref.shape[0]
    cap = send_ref.shape[1]
    copies[0].wait()
    for (directions, stride), out_ref in zip(faces, out_refs):
        direction = directions[0]
        if len(directions) > 1:
            direction = direction + device // stride % 2
        for place in range(cap):
            leaf = jnp.maximum(send_ref[direction, place, device], 0)
            for part, panel_ref in enumerate((dens_ref, *other_refs)):
                row = (place * far_groups + part) * columns
                out_ref[row : row + columns, :] = panel_ref[
                    :, pl.ds(pl.multiple_of(leaf * LANES, LANES), LANES)
                ]
        out_ref[cap * far_groups * columns :, :] = root_ref[...]


def near_kernel(
    faces, far_groups, share, *refs,
):
    source_vmems, refs = refs[:share], refs[share:]
    dens_ref, refs = refs[0], refs[1:]
    other_refs, refs = refs[: far_groups - 1], refs[far_groups - 1 :]
    got_refs, refs = refs[: len(faces)], refs[len(faces) :]
    block_hbm, refs = refs[0], refs[1:]
    mate_refs, refs = refs[: share - 1], refs[share - 1 :]
    out_refs, refs = refs[:far_groups], refs[far_groups:]
    source_refs, refs = refs[:share], refs[share:]
    block_ref, buffer_ref, small_sems, sems = refs
    columns, points = dens_ref.shape
    leaf_count, near_count, width, _ = block_ref.shape
    chunk_count = sems.shape[0]
    chunk = leaf_count // chunk_count
    copies = fetch(list(zip(source_vmems, source_refs)), small_sems)
    block_copies = fetch(
        [
            (block_hbm.at[pl.ds(index * chunk, chunk)], block_ref.at[pl.ds(index * chunk, chunk)])
            for index in range(chunk_count)
        ],
        sems,
    )
    cap = (got_refs[0].shape[0] // columns - 1) // far_groups
    for (directions, _), got_ref in zip(faces, got_refs):
        for direction in directions:
            for place in range(cap):
                row = place * far_groups * columns
                buffer_ref[leaf_count + direction * cap + place] = got_ref[
                    row : row + far_groups * columns, :
                ]
    for part, panel_ref in enumerate((dens_ref, *other_refs)):
        rows = slice(part * columns, (part + 1) * columns)
        for leaf in range(leaf_count):
            buffer_ref[leaf, rows, :] = panel_ref[:, leaf * width : (leaf + 1) * width]
    for copy in copies:
        copy.wait()
    tables = list(zip(source_refs[1:], mate_refs)) + [(source_refs[0], block_ref)]
    for turn, (source_ref, blocks_ref) in enumerate(tables):
        for leaf in range(leaf_count):
            if blocks_ref is block_ref and leaf % chunk == 0:
                block_copies[leaf // chunk].wait()
            panels = [buffer_ref[source_ref[block, leaf]] for block in range(near_count)]
            blocks = [blocks_ref[leaf, block] for block in range(near_count)]
            total = dot_nt(jnp.concatenate(panels, axis=1), jnp.concatenate(blocks, axis=1))
            lanes = slice(leaf * width, (leaf + 1) * width)
            for part, out_ref in enumerate(out_refs):
                term = total[part * columns : (part + 1) * columns]
                out_ref[:, lanes] = term if turn == 0 else out_ref[:, lanes] + term


def couple_kernel(
    far_hbm, dens_ref, bases_ref, coupling_ref, near_ref, out_ref, far_ref, turned_ref, sems,
):
    copies = fetch([(far_hbm, far_ref)], sems)
    columns, points = dens_ref.shape
    leaf_count, far_count, rank = coupling_ref.shape[:3]
    width = points // leaf_count
    group = LANES // rank
    upper = lax.broadcasted_iota(jnp.int32, (rank, 2 * columns), 1) < columns
    for leaf in range(leaf_count):
        spots = slice(leaf * width, (leaf + 1) * width)
        rows = jnp.concatenate(halves(bases_ref[:, spots]), axis=0)
        dens = dens_ref[:, spots]
        twice = dot_nt(rows, jnp.concatenate([dens, dens], axis=0))
        high, low = halves(twice[:rank] + twice[rank:])
        turned_ref[leaf * rank : (leaf + 1) * rank, :] = jnp.where(
            upper, high.astype(F32), low.astype(F32)
        ).astype(BF16)
    copies[0].wait()
    parts = []
    for leaf in range(leaf_count):
        maps = jnp.concatenate([coupling_ref[leaf, j] for j in range(far_count)], axis=1)
        maps = jnp.concatenate(halves(maps), axis=0)
        picked = jnp.concatenate(
            [
                turned_ref[pl.ds(pl.multiple_of(far_ref[j, leaf] * rank, rank), rank), :]
                for j in range(far_count)
            ],
            axis=0,
        )
        out = dot_nn(maps, picked)
        parts.append(out[:rank] + out[rank:])
        if len(parts) == group:
            turned = jnp.concatenate(parts, axis=0).T
            field = turned[:columns] + turned[columns:]
            spots = slice((leaf + 1 - group) * width, (leaf + 1) * width)
            high, low = halves(bases_ref[:, spots])
            out_ref[:, spots] = near_ref[:, spots] + split_dot(
                dot_nn, field, spread_bases(high, group), spread_bases(low, group)
            )
            parts = []


def far_kernel(
    roots, added, where_ref, upper_ref, cross_ref, high_ref, low_ref, *refs,
):
    term_refs, refs = refs[:added], refs[added:]
    root_refs, refs = refs[: len(roots)], refs[len(roots) :]
    out_hbm, tile_ref, tree_ref, sum_ref, sems = refs
    device = where_ref[0]
    columns, points = sum_ref.shape
    rank = upper_ref.shape[1]
    device_count = upper_ref.shape[0] // 2
    for tiles, root_ref in zip(roots, root_refs):
        if tiles is None:
            for index in range(device_count):
                tile_ref[index] = root_ref[index]
        else:
            for turn, row in tiles:
                tile_ref[device ^ turn] = root_ref[row : row + columns, :]
    zero = jnp.zeros((LANES - 3 * rank, rank), BF16)

    def lifted(child):
        if child >= device_count:
            high, low = (
                jnp.concatenate([half] * 3 + [zero], axis=0) for half in halves(upper_ref[child])
            )
            tile = tile_ref[child - device_count]
            return dot_nn(tile, high) + dot_nn(tile, low)
        return split_dot(dot_nn, tree_ref[child], *halves(upper_ref[child]))

    level = device_count // 2
    while level >= 4:
        for node in range(level, 2 * level):
            tree_ref[node] = lifted(2 * node) + lifted(2 * node + 1)
        level //= 2
    lane = lax.broadcasted_iota(jnp.int32, (LANES, rank), 0)
    column = lax.broadcasted_iota(jnp.int32, (LANES, rank), 1)
    gather = jnp.where((lane % rank == column) & (lane < 3 * rank), 1.0, 0.0).astype(BF16)
    field = None
    level = 4
    while level <= device_count:
        place = device // (device_count // level)
        node = level + place
        third = jnp.where(place % 2 == 0, place + 3, place - 3)
        total = None
        for slot, other in enumerate((place - 2, place + 2, third)):
            inside = (other >= 0) & (other < level)
            other = jnp.clip(other, 0, level - 1)
            if level == device_count:
                value = dot_nn(tile_ref[other], gather)
            else:
                value = tree_ref[level + other]
            value = jnp.where(inside, value, 0.0)
            term = split_dot(dot_nt, value, *halves(cross_ref[node, slot]))
            total = term if total is None else total + term
        if field is not None:
            total = total + split_dot(dot_nt, field, *halves(upper_ref[node]))
        field = total
        level *= 2
    chunk_count = sems.shape[0]
    step = points // chunk_count
    copies = []
    for index in range(chunk_count):
        spots = slice(index * step, (index + 1) * step)
        total = split_dot(dot_nn, field, high_ref[:, spots], low_ref[:, spots])
        for term_ref in term_refs:
            total = total + term_ref[:, spots]
        sum_ref[:, spots] = total
        copy = pltpu.make_async_copy(
            sum_ref.at[:, pl.ds(index * step, step)],
            out_hbm.at[:, pl.ds(index * step, step)],
            sems.at[index],
        )
        copy.start()
        copies.append(copy)
    for copy in copies:
        copy.wait()


def hbm(value):
    return pltpu.with_memory_space_constraint(value, pltpu.HBM)


def hint(micros):
    return pl.CostEstimate(flops=0, bytes_accessed=int(micros * 3.69e6), transcendentals=0)


def local(
    densities,
    bases,
    near_blocks,
    near_src,
    send_leaf,
    far_src,
    leaf_coupling,
    local_transfer,
    upper_transfer,
    up_coupling,
):
    leaf_devices = lax.axis_size("leaf")
    far_groups = lax.axis_size("far")
    share = lax.axis_size("mate")
    side = cube_side(leaf_devices)
    offsets = face_offsets(leaf_devices)
    columns, points = densities.shape
    leaf_count, near_count, width, _ = near_blocks.shape
    rank = bases.shape[0]
    cap = send_leaf.shape[2]
    node_count = local_transfer.shape[1]
    where = lax.axis_index("leaf").astype(jnp.int32).reshape(1)
    params = pltpu.CompilerParams(vmem_limit_bytes=16 * 2**20)
    dma = pltpu.SemaphoreType.DMA

    def rotated(value, axis, shift):
        count = lax.axis_size(axis)
        return lax.ppermute(value, axis, [(i, (i - shift) % count) for i in range(count)])

    def crossed(value, turn):
        return lax.ppermute(value, "leaf", [(i, i ^ turn) for i in range(leaf_devices)])

    sources = near_src.T
    others = [rotated(densities, "far", part) for part in range(1, far_groups)]
    all_sources = [sources] + [rotated(sources, "mate", part) for part in range(1, share)]
    send = send_leaf.transpose(1, 2, 0)
    dens, send, sources, high, low, root = pl.pallas_call(
        up_kernel,
        out_shape=[
            jax.ShapeDtypeStruct(densities.shape, BF16),
            jax.ShapeDtypeStruct(send.shape, jnp.int32),
            jax.ShapeDtypeStruct(sources.shape, jnp.int32),
            jax.ShapeDtypeStruct((rank, points), BF16),
            jax.ShapeDtypeStruct((rank, points), BF16),
            jax.ShapeDtypeStruct((columns, LANES), BF16),
        ],
        in_specs=[HBM] * 5,
        out_specs=[VMEM] * 6,
        scratch_shapes=[
            pltpu.VMEM(bases.shape, F32),
            pltpu.VMEM((rank, rank, node_count), F32),
            pltpu.VMEM((node_count * rank, LANES), F32),
            pltpu.VMEM((rank, node_count * rank), F32),
            dma((5,)),
        ],
        compiler_params=params,
        cost_estimate=hint(3.5),
        name="up",
    )(
        hbm(densities), hbm(bases), hbm(local_transfer[0].transpose(1, 2, 0)), hbm(send),
        hbm(sources),
    )
    all_sources[0] = sources

    later_blocks, others, all_sources, root = lax.optimization_barrier(
        (near_blocks, others, all_sources, root)
    )
    mate_blocks = [rotated(later_blocks, "mate", part) for part in range(1, share)]

    if side == 2:
        faces = [((2 * axis, 2 * axis + 1), 2**axis) for axis in range(3)]
    else:
        faces = [((direction,), offset) for direction, offset in enumerate(offsets)]
    chunk = (cap * far_groups + 1) * columns
    outgoing = pl.pallas_call(
        functools.partial(select_kernel, faces, far_groups),
        out_shape=[jax.ShapeDtypeStruct((chunk, LANES), BF16)] * len(faces),
        in_specs=[SMEM] + [VMEM] * (2 + far_groups),
        out_specs=[VMEM] * len(faces),
        scratch_shapes=[
            pltpu.SMEM(send.shape, jnp.int32),
            dma((1,)),
        ],
        compiler_params=params,
        cost_estimate=hint(1),
        name="select",
    )(where, send, dens, root, *others)
    tail = cap * far_groups * columns
    if side == 2:
        arrived = [crossed(value, stride) for (_, stride), value in zip(faces, outgoing)]
        held = jnp.concatenate([root] + [value[tail:] for value in arrived], axis=0)
        whole = leaf_devices - 1
        opposite = crossed(held, whole)
        turns = [0] + [stride for _, stride in faces]
        roots = [
            ([(0, 0)], root),
            ([(turn ^ whole, row * columns) for row, turn in enumerate(turns)], opposite),
        ]
        roots += [([(stride, tail)], value) for (_, stride), value in zip(faces, arrived)]
    else:
        arrived = [shifted(value, "leaf", stride) for (_, stride), value in zip(faces, outgoing)]
        roots = [(None, lax.all_gather(root, "leaf", axis=0))]

    slots = leaf_count + len(offsets) * cap
    partials = pl.pallas_call(
        functools.partial(near_kernel, faces, far_groups, share),
        out_shape=[jax.ShapeDtypeStruct((columns, points), F32)] * far_groups,
        in_specs=[VMEM] * (share + far_groups + len(faces))
        + [HBM]
        + [VMEM] * (share - 1),
        out_specs=[VMEM] * far_groups,
        scratch_shapes=[pltpu.SMEM(sources.shape, jnp.int32)] * share
        + [
            pltpu.VMEM(near_blocks.shape, BF16),
            pltpu.VMEM((slots, far_groups * columns, width), BF16),
            dma((share,)),
            dma((4,)),
        ],
        compiler_params=params,
        cost_estimate=hint(3),
        name="near",
    )(
        *all_sources, dens, *others, *arrived, hbm(near_blocks), *mate_blocks,
    )
    received = [rotated(partials[part], "far", -part) for part in range(1, far_groups)]
    far_table = far_src.T
    partial = pl.pallas_call(
        couple_kernel,
        out_shape=jax.ShapeDtypeStruct((columns, points), F32),
        in_specs=[HBM] + [VMEM] * 4,
        out_specs=VMEM,
        scratch_shapes=[
            pltpu.SMEM(far_table.shape, jnp.int32),
            pltpu.VMEM((leaf_count * rank, 2 * columns), BF16),
            dma((1,)),
        ],
        compiler_params=params,
        cost_estimate=hint(3),
        name="couple",
    )(hbm(far_table), dens, bases, leaf_coupling, partials[0])
    terms = [partial] + received
    return pl.pallas_call(
        functools.partial(far_kernel, [tiles for tiles, _ in roots], len(terms)),
        out_shape=jax.ShapeDtypeStruct((columns, points), F32),
        in_specs=[SMEM] + [VMEM] * (4 + len(terms) + len(roots)),
        out_specs=HBM,
        scratch_shapes=[
            pltpu.VMEM((leaf_devices, columns, LANES), BF16),
            pltpu.VMEM((2 * leaf_devices, columns, rank), F32),
            pltpu.VMEM((columns, points), F32),
            dma((4,)),
        ],
        compiler_params=params,
        cost_estimate=hint(2),
        name="far",
    )(where, upper_transfer, up_coupling, high, low, *terms, *[value for _, value in roots])


def solution(mesh):
    leaf_devices, rhs_devices = mesh.shape["leaf"], mesh.shape["rhs"]
    share = 2 if rhs_devices % 2 == 0 else 1
    split = Mesh(
        mesh.devices.reshape(leaf_devices, rhs_devices // share, share), ("leaf", "far", "mate")
    )
    rhs = ("far", "mate")
    in_specs = (
        P(rhs, "leaf"),
        P(None, "leaf"),
        P("leaf", rhs, None, None),
        P("leaf", rhs),
        P(),
        P("leaf", None),
        P("leaf", None, None, None),
        P("leaf", None, None, None),
        P(),
        P(),
    )
    return jax.shard_map(
        local, mesh=split, in_specs=in_specs, out_specs=P(rhs, "leaf"), check_vma=False
    )
```

```python
import functools

import jax
import jax.numpy as jnp
from jax import lax
from jax.experimental import pallas as pl
from jax.experimental.pallas import tpu as pltpu
from jax.sharding import Mesh
from jax.sharding import PartitionSpec as P

FACE_SIGNS = ((1, 0), (-1, 0), (1, 1), (-1, 1), (1, 2), (-1, 2))
F32 = jnp.float32
BF16 = jnp.bfloat16
LANES = 128
VMEM = pl.BlockSpec(memory_space=pltpu.VMEM)
HBM = pl.BlockSpec(memory_space=pltpu.HBM)
SMEM = pl.BlockSpec(memory_space=pltpu.SMEM)


def cube_side(device_count):
    return max((edge_len for edge_len in range(1, 65) if edge_len**3 <= device_count))


def face_offsets(device_count):
    side_len = cube_side(device_count)
    return [face_sign * side_len**axis_pos for face_sign, axis_pos in FACE_SIGNS]


def shifted(value, axis, steps):
    count = lax.axis_size(axis)
    first, last = (max(0, -steps), min(count, count - steps))
    return lax.ppermute(value, axis, [(source, source + steps) for source in range(first, last)])


def halves(value):
    high = value.astype(BF16)
    return high, (value - high.astype(F32)).astype(BF16)


def dot_nn(left, right):
    return lax.dot_general(left, right, (((1,), (0,)), ((), ())), preferred_element_type=F32)


def dot_nt(left, right):
    return lax.dot_general(left, right, (((1,), (1,)), ((), ())), preferred_element_type=F32)


def split_dot(dot, rows, right_high, right_low):
    count = rows.shape[0]
    high, low = halves(rows)
    both = jnp.concatenate([high, low], axis=0)
    out = dot(both, right_high) + dot(both, right_low)
    return out[:count] + out[count:]


def spread_bases(block, group):
    rank, lanes = block.shape
    width = lanes // group
    zero = jnp.zeros((rank, width), block.dtype)
    rows = []
    for slot in range(group):
        pieces = [zero] * group
        pieces[slot] = block[:, slot * width : (slot + 1) * width]
        rows.append(jnp.concatenate(pieces, axis=1))
    return jnp.concatenate(rows, axis=0)


def fetch(pairs, sems):
    copies = []
    for index, (source, target) in enumerate(pairs):
        copy = pltpu.make_async_copy(source, target, sems.at[index])
        copy.start()
        copies.append(copy)
    return copies


def up_kernel(
    dens_hbm, bases_hbm, maps_hbm, send_hbm, source_hbm,
    dens_ref, bases_ref, send_ref, source_ref, high_ref, low_ref, root_ref,
    maps_ref, spread_ref, chain_ref, sems,
):
    copies = fetch(
        [
            (maps_hbm, maps_ref),
            (bases_hbm, bases_ref),
            (dens_hbm, dens_ref),
            (send_hbm, send_ref),
            (source_hbm, source_ref),
        ],
        sems,
    )
    columns, points = dens_ref.shape
    rank, _, node_count = maps_ref.shape
    group = LANES // rank
    leaf_count = node_count // 2
    width = points // leaf_count
    copies[0].wait()
    node = lax.broadcasted_iota(jnp.int32, (node_count, LANES), 0)
    block = lax.broadcasted_iota(jnp.int32, (node_count, LANES), 1) // rank
    parent = node // 2 % group
    for first in range(0, rank, group):
        slab = maps_ref[first : first + group].reshape(group * rank, node_count).T
        turned = [slab] + [pltpu.roll(slab, turn * rank, 1) for turn in range(1, group)]
        for row in range(group):
            placed = jnp.zeros_like(slab)
            for place in range(group):
                here = (parent == place) & (block == place)
                placed = jnp.where(here, turned[(place - row) % group], placed)
            spread_ref[pl.ds(first + row, node_count, stride=rank), :] = placed
    tile = 2 * group * rank

    def children(parents, index):
        high, low = halves(spread_ref[index * tile : (index + 1) * tile, :])
        return split_dot(dot_nt, parents, high, low)

    row = lax.broadcasted_iota(jnp.int32, (rank, LANES), 0)
    lane = lax.broadcasted_iota(jnp.int32, (rank, LANES), 1)
    level = 1
    parents = jnp.where(lane == row + rank, 1.0, 0.0)
    while level < group:
        below = children(parents, 0)
        level *= 2
        parents = below[:, (level // group) * LANES : (level // group + 1) * LANES]
    chain_ref[:, LANES : 2 * LANES] = parents
    while level < leaf_count:
        for index in range(level // group, 2 * level // group):
            lanes = slice(index * LANES, (index + 1) * LANES)
            chain_ref[:, index * tile : (index + 1) * tile] = children(chain_ref[:, lanes], index)
        level *= 2
    for copy in copies[1:]:
        copy.wait()
    step = group * width
    root = jnp.zeros((columns, rank), F32)
    for index in range(leaf_count // group):
        spots = slice(index * step, (index + 1) * step)
        start = (leaf_count // group + index) * LANES
        high, low = halves(bases_ref[:, spots])
        basis = split_dot(
            dot_nn, chain_ref[:, start : start + LANES],
            spread_bases(high, group), spread_bases(low, group),
        )
        high, low = halves(basis)
        high_ref[:, spots] = high
        low_ref[:, spots] = low
        dens = dens_ref[:, spots]
        root += dot_nt(dens, high) + dot_nt(dens, low)
    root = jnp.concatenate([root, jnp.zeros((columns, LANES - rank), F32)], axis=1)
    high = root.astype(BF16).astype(F32)
    rest = root - high
    middle = rest.astype(BF16).astype(F32)
    last = (rest - middle).astype(BF16).astype(F32)
    packed = high + pltpu.roll(middle, rank, 1) + pltpu.roll(last, 2 * rank, 1)
    root_ref[...] = packed.astype(BF16)


def select_kernel(
    faces, far_groups, send_vmem, dens_ref, root_ref, *refs,
):
    other_refs = refs[: far_groups - 1]
    out_refs = refs[far_groups - 1 : -2]
    send_ref, sems = refs[-2:]
    copies = fetch([(send_vmem, send_ref)], sems)
    device = lax.axis_index("leaf")
    columns = dens_ref.shape[0]
    cap = send_ref.shape[1]
    copies[0].wait()
    for (directions, stride), out_ref in zip(faces, out_refs):
        direction = directions[0]
        if len(directions) > 1:
            direction = direction + device // stride % 2
        for place in range(cap):
            leaf = jnp.maximum(send_ref[direction, place, device], 0)
            for part, panel_ref in enumerate((dens_ref, *other_refs)):
                row = (place * far_groups + part) * columns
                out_ref[row : row + columns, :] = panel_ref[
                    :, pl.ds(pl.multiple_of(leaf * LANES, LANES), LANES)
                ]
        out_ref[cap * far_groups * columns :, :] = root_ref[...]


def near_kernel(
    faces, far_groups, share, *refs,
):
    source_vmems, refs = refs[:share], refs[share:]
    dens_ref, refs = refs[0], refs[1:]
    other_refs, refs = refs[: far_groups - 1], refs[far_groups - 1 :]
    got_refs, refs = refs[: len(faces)], refs[len(faces) :]
    block_hbm, refs = refs[0], refs[1:]
    mate_refs, refs = refs[: share - 1], refs[share - 1 :]
    refs = refs[1:]
    out_refs, refs = refs[:far_groups], refs[far_groups:]
    source_refs, refs = refs[:share], refs[share:]
    block_ref, buffer_ref, small_sems, sems = refs
    columns, points = dens_ref.shape
    leaf_count, near_count, width, _ = block_ref.shape
    chunk_count = sems.shape[0]
    chunk = leaf_count // chunk_count
    copies = fetch(list(zip(source_vmems, source_refs)), small_sems)
    block_copies = fetch(
        [
            (block_hbm.at[pl.ds(index * chunk, chunk)], block_ref.at[pl.ds(index * chunk, chunk)])
            for index in range(chunk_count)
        ],
        sems,
    )
    cap = (buffer_ref.shape[0] - leaf_count) // len(FACE_SIGNS)
    for (directions, _), got_ref in zip(faces, got_refs):
        for direction in directions:
            for place in range(cap):
                row = place * far_groups * columns
                buffer_ref[leaf_count + direction * cap + place] = got_ref[
                    row : row + far_groups * columns, :
                ]
    for part, panel_ref in enumerate((dens_ref, *other_refs)):
        rows = slice(part * columns, (part + 1) * columns)
        for leaf in range(leaf_count):
            buffer_ref[leaf, rows, :] = panel_ref[:, leaf * width : (leaf + 1) * width]
    for copy in copies:
        copy.wait()
    tables = list(zip(source_refs[1:], mate_refs)) + [(source_refs[0], block_ref)]
    for turn, (source_ref, blocks_ref) in enumerate(tables):
        for leaf in range(leaf_count):
            if blocks_ref is block_ref and leaf % chunk == 0:
                block_copies[leaf // chunk].wait()
            panels = [buffer_ref[source_ref[block, leaf]] for block in range(near_count)]
            blocks = [blocks_ref[leaf, block] for block in range(near_count)]
            total = dot_nt(jnp.concatenate(panels, axis=1), jnp.concatenate(blocks, axis=1))
            lanes = slice(leaf * width, (leaf + 1) * width)
            for part, out_ref in enumerate(out_refs):
                term = total[part * columns : (part + 1) * columns]
                out_ref[:, lanes] = term if turn == 0 else out_ref[:, lanes] + term


def couple_kernel(
    far_hbm, coupling_hbm, dens_ref, bases_ref, out_ref, far_ref, coupling_ref, turned_ref, sems,
):
    chunk_count = sems.shape[0] - 1
    chunk = coupling_ref.shape[0] // chunk_count
    copies = fetch(
        [(far_hbm, far_ref)]
        + [
            (coupling_hbm.at[pl.ds(index * chunk, chunk)], coupling_ref.at[pl.ds(index * chunk, chunk)])
            for index in range(chunk_count)
        ],
        sems,
    )
    columns, points = dens_ref.shape
    leaf_count, far_count, rank = coupling_ref.shape[:3]
    width = points // leaf_count
    group = LANES // rank
    upper = lax.broadcasted_iota(jnp.int32, (rank, 2 * columns), 1) < columns
    for leaf in range(leaf_count):
        spots = slice(leaf * width, (leaf + 1) * width)
        rows = jnp.concatenate(halves(bases_ref[:, spots]), axis=0)
        dens = dens_ref[:, spots]
        twice = dot_nt(rows, jnp.concatenate([dens, dens], axis=0))
        high, low = halves(twice[:rank] + twice[rank:])
        turned_ref[leaf * rank : (leaf + 1) * rank, :] = jnp.where(
            upper, high.astype(F32), low.astype(F32)
        ).astype(BF16)
    copies[0].wait()
    parts = []
    for leaf in range(leaf_count):
        if leaf % chunk == 0:
            copies[1 + leaf // chunk].wait()
        maps = jnp.concatenate([coupling_ref[leaf, j] for j in range(far_count)], axis=1)
        maps = jnp.concatenate(halves(maps), axis=0)
        picked = jnp.concatenate(
            [
                turned_ref[pl.ds(pl.multiple_of(far_ref[j, leaf] * rank, rank), rank), :]
                for j in range(far_count)
            ],
            axis=0,
        )
        out = dot_nn(maps, picked)
        parts.append(out[:rank] + out[rank:])
        if len(parts) == group:
            turned = jnp.concatenate(parts, axis=0).T
            spot = (leaf + 1 - group) * rank
            out_ref[:, spot : spot + LANES] = turned[:columns] + turned[columns:]
            parts = []


def project_kernel(leaf_count, local_ref, bases_ref, near_ref, out_ref):
    rank, points = bases_ref.shape
    group = LANES // rank
    step = group * points // leaf_count
    for index in range(leaf_count // group):
        spots = slice(index * step, (index + 1) * step)
        high, low = halves(bases_ref[:, spots])
        out_ref[:, spots] = near_ref[:, spots] + split_dot(
            dot_nn, local_ref[:, index * LANES : (index + 1) * LANES],
            spread_bases(high, group), spread_bases(low, group),
        )


def far_kernel(
    roots, added, upper_ref, cross_ref, high_ref, low_ref, *refs,
):
    term_refs, refs = refs[:added], refs[added:]
    root_refs, refs = refs[: len(roots)], refs[len(roots) :]
    out_hbm, tile_ref, tree_ref, sum_ref, sems = refs
    device = lax.axis_index("leaf")
    columns, points = sum_ref.shape
    rank = upper_ref.shape[1]
    device_count = upper_ref.shape[0] // 2
    for tiles, root_ref in zip(roots, root_refs):
        if tiles is None:
            for index in range(device_count):
                tile_ref[index] = root_ref[index]
        else:
            for turn, row in tiles:
                tile_ref[device ^ turn] = root_ref[row : row + columns, :]
    zero = jnp.zeros((LANES - 3 * rank, rank), BF16)

    def lifted(child):
        if child >= device_count:
            high, low = (
                jnp.concatenate([half] * 3 + [zero], axis=0) for half in halves(upper_ref[child])
            )
            tile = tile_ref[child - device_count]
            return dot_nn(tile, high) + dot_nn(tile, low)
        return split_dot(dot_nn, tree_ref[child], *halves(upper_ref[child]))

    level = device_count // 2
    while level >= 4:
        for node in range(level, 2 * level):
            tree_ref[node] = lifted(2 * node) + lifted(2 * node + 1)
        level //= 2
    lane = lax.broadcasted_iota(jnp.int32, (LANES, rank), 0)
    column = lax.broadcasted_iota(jnp.int32, (LANES, rank), 1)
    gather = jnp.where((lane % rank == column) & (lane < 3 * rank), 1.0, 0.0).astype(BF16)
    field = None
    level = 4
    while level <= device_count:
        place = device // (device_count // level)
        node = level + place
        third = jnp.where(place % 2 == 0, place + 3, place - 3)
        total = None
        for slot, other in enumerate((place - 2, place + 2, third)):
            inside = (other >= 0) & (other < level)
            other = jnp.clip(other, 0, level - 1)
            if level == device_count:
                value = dot_nn(tile_ref[other], gather)
            else:
                value = tree_ref[level + other]
            value = jnp.where(inside, value, 0.0)
            term = split_dot(dot_nt, value, *halves(cross_ref[node, slot]))
            total = term if total is None else total + term
        if field is not None:
            total = total + split_dot(dot_nt, field, *halves(upper_ref[node]))
        field = total
        level *= 2
    chunk_count = sems.shape[0]
    step = points // chunk_count
    copies = []
    for index in range(chunk_count):
        spots = slice(index * step, (index + 1) * step)
        total = split_dot(dot_nn, field, high_ref[:, spots], low_ref[:, spots])
        for term_ref in term_refs:
            total = total + term_ref[:, spots]
        sum_ref[:, spots] = total
        copy = pltpu.make_async_copy(
            sum_ref.at[:, pl.ds(index * step, step)],
            out_hbm.at[:, pl.ds(index * step, step)],
            sems.at[index],
        )
        copy.start()
        copies.append(copy)
    for copy in copies:
        copy.wait()


def hbm(value):
    return pltpu.with_memory_space_constraint(value, pltpu.HBM)


def hint(micros):
    return pl.CostEstimate(flops=0, bytes_accessed=int(micros * 3.69e6), transcendentals=0)


def local(
    densities,
    bases,
    near_blocks,
    near_src,
    send_leaf,
    far_src,
    leaf_coupling,
    local_transfer,
    upper_transfer,
    up_coupling,
):
    leaf_devices = lax.axis_size("leaf")
    far_groups = lax.axis_size("far")
    share = lax.axis_size("mate")
    side = cube_side(leaf_devices)
    offsets = face_offsets(leaf_devices)
    columns, points = densities.shape
    leaf_count, near_count, width, _ = near_blocks.shape
    rank = bases.shape[0]
    cap = send_leaf.shape[2]
    node_count = local_transfer.shape[1]
    params = pltpu.CompilerParams(vmem_limit_bytes=16 * 2**20)
    dma = pltpu.SemaphoreType.DMA

    def rotated(value, axis, shift):
        count = lax.axis_size(axis)
        return lax.ppermute(value, axis, [(i, (i - shift) % count) for i in range(count)])

    def crossed(value, turn):
        return lax.ppermute(value, "leaf", [(i, i ^ turn) for i in range(leaf_devices)])

    sources = near_src.T
    others = [rotated(densities, "far", part) for part in range(1, far_groups)]
    all_sources = [sources] + [rotated(sources, "mate", part) for part in range(1, share)]
    send = send_leaf.transpose(1, 2, 0)
    dens, basis, send, sources, high, low, root = pl.pallas_call(
        up_kernel,
        out_shape=[
            jax.ShapeDtypeStruct(densities.shape, BF16),
            jax.ShapeDtypeStruct(bases.shape, F32),
            jax.ShapeDtypeStruct(send.shape, jnp.int32),
            jax.ShapeDtypeStruct(sources.shape, jnp.int32),
            jax.ShapeDtypeStruct((rank, points), BF16),
            jax.ShapeDtypeStruct((rank, points), BF16),
            jax.ShapeDtypeStruct((columns, LANES), BF16),
        ],
        in_specs=[HBM] * 5,
        out_specs=[VMEM] * 7,
        scratch_shapes=[
            pltpu.VMEM((rank, rank, node_count), F32),
            pltpu.VMEM((node_count * rank, LANES), F32),
            pltpu.VMEM((rank, node_count * rank), F32),
            dma((5,)),
        ],
        compiler_params=params,
        cost_estimate=hint(3.5),
        name="up",
    )(
        hbm(densities), hbm(bases), hbm(local_transfer[0].transpose(1, 2, 0)), hbm(send),
        hbm(sources),
    )
    all_sources[0] = sources

    later_blocks, others, all_sources, root = lax.optimization_barrier(
        (near_blocks, others, all_sources, root)
    )
    mate_blocks = [rotated(later_blocks, "mate", part) for part in range(1, share)]

    if side == 2:
        faces = [((2 * axis, 2 * axis + 1), 2**axis) for axis in range(3)]
    else:
        faces = [((direction,), offset) for direction, offset in enumerate(offsets)]
    chunk = (cap * far_groups + 1) * columns
    outgoing = pl.pallas_call(
        functools.partial(select_kernel, faces, far_groups),
        out_shape=[jax.ShapeDtypeStruct((chunk, LANES), BF16)] * len(faces),
        in_specs=[VMEM] * (2 + far_groups),
        out_specs=[VMEM] * len(faces),
        scratch_shapes=[
            pltpu.SMEM(send.shape, jnp.int32),
            dma((1,)),
        ],
        compiler_params=params,
        cost_estimate=hint(1),
        name="select",
    )(send, dens, root, *others)
    outgoing, dens = lax.optimization_barrier((outgoing, dens))
    far_table = far_src.T
    leaf_local = pl.pallas_call(
        couple_kernel,
        out_shape=jax.ShapeDtypeStruct((columns, leaf_count * rank), F32),
        in_specs=[HBM] * 2 + [VMEM] * 2,
        out_specs=VMEM,
        scratch_shapes=[
            pltpu.SMEM(far_table.shape, jnp.int32),
            pltpu.VMEM(leaf_coupling.shape, F32),
            pltpu.VMEM((leaf_count * rank, 2 * columns), BF16),
            dma((5,)),
        ],
        compiler_params=params,
        cost_estimate=hint(2.3),
        name="couple",
    )(hbm(far_table), hbm(leaf_coupling), dens, basis)
    tail = cap * far_groups * columns
    if side == 2:
        first, second, third = (stride for _, stride in faces)
        arrived = [crossed(outgoing[0], first), crossed(outgoing[1], second)]
        last = jnp.concatenate([outgoing[2], arrived[0][tail:]], axis=0)
        arrived.append(crossed(last, third))
        held = jnp.concatenate([root, arrived[0][tail:], arrived[2][tail:]], axis=0)
        beside = crossed(held, second)
        turns = [0, first, third, third ^ first]
        roots = [
            ([(0, 0)], root),
            ([(first, tail)], arrived[0]),
            ([(third, tail), (third ^ first, tail + columns)], arrived[2]),
            ([(turn ^ second, row * columns) for row, turn in enumerate(turns)], beside),
        ]
    else:
        arrived = [shifted(value, "leaf", stride) for (_, stride), value in zip(faces, outgoing)]
        roots = [(None, lax.all_gather(root, "leaf", axis=0))]

    slots = leaf_count + len(offsets) * cap
    partials = pl.pallas_call(
        functools.partial(near_kernel, faces, far_groups, share),
        out_shape=[jax.ShapeDtypeStruct((columns, points), F32)] * far_groups,
        in_specs=[VMEM] * (share + far_groups + len(faces))
        + [HBM]
        + [VMEM] * share,
        out_specs=[VMEM] * far_groups,
        scratch_shapes=[pltpu.SMEM(sources.shape, jnp.int32)] * share
        + [
            pltpu.VMEM(near_blocks.shape, BF16),
            pltpu.VMEM((slots, far_groups * columns, width), BF16),
            dma((share,)),
            dma((4,)),
        ],
        compiler_params=params,
        cost_estimate=hint(3),
        name="near",
    )(
        *all_sources, dens, *others, *arrived, hbm(near_blocks), *mate_blocks, leaf_local,
    )
    received = [rotated(partials[part], "far", -part) for part in range(1, far_groups)]
    partial = pl.pallas_call(
        functools.partial(project_kernel, leaf_count),
        out_shape=jax.ShapeDtypeStruct((columns, points), F32),
        in_specs=[VMEM] * 3,
        out_specs=VMEM,
        compiler_params=params,
        cost_estimate=hint(1),
        name="project",
    )(leaf_local, basis, partials[0])
    terms = [partial] + received
    return pl.pallas_call(
        functools.partial(far_kernel, [tiles for tiles, _ in roots], len(terms)),
        out_shape=jax.ShapeDtypeStruct((columns, points), F32),
        in_specs=[VMEM] * (4 + len(terms) + len(roots)),
        out_specs=HBM,
        scratch_shapes=[
            pltpu.VMEM((leaf_devices, columns, LANES), BF16),
            pltpu.VMEM((2 * leaf_devices, columns, rank), F32),
            pltpu.VMEM((columns, points), F32),
            dma((4,)),
        ],
        compiler_params=params,
        cost_estimate=hint(2),
        name="far",
    )(upper_transfer, up_coupling, high, low, *terms, *[value for _, value in roots])


def solution(mesh):
    leaf_devices, rhs_devices = mesh.shape["leaf"], mesh.shape["rhs"]
    share = 2 if rhs_devices % 2 == 0 else 1
    split = Mesh(
        mesh.devices.reshape(leaf_devices, rhs_devices // share, share), ("leaf", "far", "mate")
    )
    rhs = ("far", "mate")
    in_specs = (
        P(rhs, "leaf"),
        P(None, "leaf"),
        P("leaf", rhs, None, None),
        P("leaf", rhs),
        P(),
        P("leaf", None),
        P("leaf", None, None, None),
        P("leaf", None, None, None),
        P(),
        P(),
    )
    return jax.shard_map(
        local, mesh=split, in_specs=in_specs, out_specs=P(rhs, "leaf"), check_vma=False
    )
```

```python
import functools

import jax
import jax.numpy as jnp
from jax import lax
from jax.experimental import pallas as pl
from jax.experimental.pallas import tpu as pltpu
from jax.sharding import Mesh
from jax.sharding import PartitionSpec as P

FACE_SIGNS = ((1, 0), (-1, 0), (1, 1), (-1, 1), (1, 2), (-1, 2))
F32 = jnp.float32
BF16 = jnp.bfloat16
LANES = 128
VMEM = pl.BlockSpec(memory_space=pltpu.VMEM)
HBM = pl.BlockSpec(memory_space=pltpu.HBM)
SMEM = pl.BlockSpec(memory_space=pltpu.SMEM)


def cube_side(device_count):
    return max((edge_len for edge_len in range(1, 65) if edge_len**3 <= device_count))


def face_offsets(device_count):
    side_len = cube_side(device_count)
    return [face_sign * side_len**axis_pos for face_sign, axis_pos in FACE_SIGNS]


def shifted(value, axis, steps):
    count = lax.axis_size(axis)
    first, last = (max(0, -steps), min(count, count - steps))
    return lax.ppermute(value, axis, [(source, source + steps) for source in range(first, last)])


def halves(value):
    high = value.astype(BF16)
    return high, (value - high.astype(F32)).astype(BF16)


def dot_nn(left, right):
    return lax.dot_general(left, right, (((1,), (0,)), ((), ())), preferred_element_type=F32)


def dot_nt(left, right):
    return lax.dot_general(left, right, (((1,), (1,)), ((), ())), preferred_element_type=F32)


def split_dot(dot, rows, right_high, right_low):
    count = rows.shape[0]
    high, low = halves(rows)
    both = jnp.concatenate([high, low], axis=0)
    out = dot(both, right_high) + dot(both, right_low)
    return out[:count] + out[count:]


def spread_bases(block, group):
    rank, lanes = block.shape
    width = lanes // group
    zero = jnp.zeros((rank, width), block.dtype)
    rows = []
    for slot in range(group):
        pieces = [zero] * group
        pieces[slot] = block[:, slot * width : (slot + 1) * width]
        rows.append(jnp.concatenate(pieces, axis=1))
    return jnp.concatenate(rows, axis=0)


def fetch(pairs, sems):
    copies = []
    for index, (source, target) in enumerate(pairs):
        copy = pltpu.make_async_copy(source, target, sems.at[index])
        copy.start()
        copies.append(copy)
    return copies


def up_kernel(
    dens_hbm, bases_hbm, maps_hbm, send_hbm, source_hbm,
    dens_ref, bases_ref, send_ref, source_ref, high_ref, low_ref, root_ref,
    maps_ref, spread_ref, chain_ref, sems,
):
    copies = fetch(
        [
            (maps_hbm, maps_ref),
            (bases_hbm, bases_ref),
            (dens_hbm, dens_ref),
            (send_hbm, send_ref),
            (source_hbm, source_ref),
        ],
        sems,
    )
    columns, points = dens_ref.shape
    rank, _, node_count = maps_ref.shape
    group = LANES // rank
    leaf_count = node_count // 2
    width = points // leaf_count
    copies[0].wait()
    node = lax.broadcasted_iota(jnp.int32, (node_count, LANES), 0)
    block = lax.broadcasted_iota(jnp.int32, (node_count, LANES), 1) // rank
    parent = node // 2 % group
    for first in range(0, rank, group):
        slab = maps_ref[first : first + group].reshape(group * rank, node_count).T
        turned = [slab] + [pltpu.roll(slab, turn * rank, 1) for turn in range(1, group)]
        for row in range(group):
            placed = jnp.zeros_like(slab)
            for place in range(group):
                here = (parent == place) & (block == place)
                placed = jnp.where(here, turned[(place - row) % group], placed)
            spread_ref[pl.ds(first + row, node_count, stride=rank), :] = placed
    tile = 2 * group * rank

    def children(parents, index):
        high, low = halves(spread_ref[index * tile : (index + 1) * tile, :])
        return split_dot(dot_nt, parents, high, low)

    row = lax.broadcasted_iota(jnp.int32, (rank, LANES), 0)
    lane = lax.broadcasted_iota(jnp.int32, (rank, LANES), 1)
    level = 1
    parents = jnp.where(lane == row + rank, 1.0, 0.0)
    while level < group:
        below = children(parents, 0)
        level *= 2
        parents = below[:, (level // group) * LANES : (level // group + 1) * LANES]
    chain_ref[:, LANES : 2 * LANES] = parents
    while level < leaf_count:
        for index in range(level // group, 2 * level // group):
            lanes = slice(index * LANES, (index + 1) * LANES)
            chain_ref[:, index * tile : (index + 1) * tile] = children(chain_ref[:, lanes], index)
        level *= 2
    for copy in copies[1:]:
        copy.wait()
    step = group * width
    root = jnp.zeros((columns, rank), F32)
    for index in range(leaf_count // group):
        spots = slice(index * step, (index + 1) * step)
        start = (leaf_count // group + index) * LANES
        high, low = halves(bases_ref[:, spots])
        basis = split_dot(
            dot_nn, chain_ref[:, start : start + LANES],
            spread_bases(high, group), spread_bases(low, group),
        )
        high, low = halves(basis)
        high_ref[:, spots] = high
        low_ref[:, spots] = low
        dens = dens_ref[:, spots]
        root += dot_nt(dens, high) + dot_nt(dens, low)
    root = jnp.concatenate([root, jnp.zeros((columns, LANES - rank), F32)], axis=1)
    high = root.astype(BF16).astype(F32)
    rest = root - high
    middle = rest.astype(BF16).astype(F32)
    last = (rest - middle).astype(BF16).astype(F32)
    packed = high + pltpu.roll(middle, rank, 1) + pltpu.roll(last, 2 * rank, 1)
    root_ref[...] = packed.astype(BF16)


def select_kernel(
    faces, far_groups, send_vmem, dens_ref, root_ref, *refs,
):
    other_refs = refs[: far_groups - 1]
    out_refs = refs[far_groups - 1 : -2]
    send_ref, sems = refs[-2:]
    copies = fetch([(send_vmem, send_ref)], sems)
    device = lax.axis_index("leaf")
    columns = dens_ref.shape[0]
    cap = send_ref.shape[1]
    copies[0].wait()
    for (directions, stride), out_ref in zip(faces, out_refs):
        direction = directions[0]
        if len(directions) > 1:
            direction = direction + device // stride % 2
        for place in range(cap):
            leaf = jnp.maximum(send_ref[direction, place, device], 0)
            for part, panel_ref in enumerate((dens_ref, *other_refs)):
                row = (place * far_groups + part) * columns
                out_ref[row : row + columns, :] = panel_ref[
                    :, pl.ds(pl.multiple_of(leaf * LANES, LANES), LANES)
                ]
        out_ref[cap * far_groups * columns :, :] = root_ref[...]


def near_kernel(
    faces, far_groups, share, *refs,
):
    source_vmems, refs = refs[:share], refs[share:]
    dens_ref, refs = refs[0], refs[1:]
    other_refs, refs = refs[: far_groups - 1], refs[far_groups - 1 :]
    got_refs, refs = refs[: len(faces)], refs[len(faces) :]
    block_hbm, refs = refs[0], refs[1:]
    mate_refs, refs = refs[: share - 1], refs[share - 1 :]
    refs = refs[1:]
    out_refs, refs = refs[:far_groups], refs[far_groups:]
    source_refs, refs = refs[:share], refs[share:]
    block_ref, buffer_ref, small_sems, sems = refs
    columns, points = dens_ref.shape
    leaf_count, near_count, width, _ = block_ref.shape
    chunk_count = sems.shape[0]
    chunk = leaf_count // chunk_count
    copies = fetch(list(zip(source_vmems, source_refs)), small_sems)
    block_copies = fetch(
        [
            (block_hbm.at[pl.ds(index * chunk, chunk)], block_ref.at[pl.ds(index * chunk, chunk)])
            for index in range(chunk_count)
        ],
        sems,
    )
    cap = (buffer_ref.shape[0] - leaf_count) // len(FACE_SIGNS)
    for (directions, _), got_ref in zip(faces, got_refs):
        for direction in directions:
            for place in range(cap):
                row = place * far_groups * columns
                buffer_ref[leaf_count + direction * cap + place] = got_ref[
                    row : row + far_groups * columns, :
                ]
    for part, panel_ref in enumerate((dens_ref, *other_refs)):
        rows = slice(part * columns, (part + 1) * columns)
        for leaf in range(leaf_count):
            buffer_ref[leaf, rows, :] = panel_ref[:, leaf * width : (leaf + 1) * width]
    for copy in copies:
        copy.wait()
    tables = list(zip(source_refs[1:], mate_refs)) + [(source_refs[0], block_ref)]
    for turn, (source_ref, blocks_ref) in enumerate(tables):
        for leaf in range(leaf_count):
            if blocks_ref is block_ref and leaf % chunk == 0:
                block_copies[leaf // chunk].wait()
            panels = [buffer_ref[source_ref[block, leaf]] for block in range(near_count)]
            blocks = [blocks_ref[leaf, block] for block in range(near_count)]
            total = dot_nt(jnp.concatenate(panels, axis=1), jnp.concatenate(blocks, axis=1))
            lanes = slice(leaf * width, (leaf + 1) * width)
            for part, out_ref in enumerate(out_refs):
                term = total[part * columns : (part + 1) * columns]
                out_ref[:, lanes] = term if turn == 0 else out_ref[:, lanes] + term


def coupled(leaves, far_ref, coupling_ref, turned_ref):
    far_count, rank = coupling_ref.shape[1:3]
    columns = turned_ref.shape[1] // 2
    group = LANES // rank
    parts = []
    for leaf in leaves:
        maps = jnp.concatenate([coupling_ref[leaf, j] for j in range(far_count)], axis=1)
        maps = jnp.concatenate(halves(maps), axis=0)
        picked = jnp.concatenate(
            [
                turned_ref[pl.ds(pl.multiple_of(far_ref[j, leaf] * rank, rank), rank), :]
                for j in range(far_count)
            ],
            axis=0,
        )
        out = dot_nn(maps, picked)
        parts.append(out[:rank] + out[rank:])
        if len(parts) == group:
            turned = jnp.concatenate(parts, axis=0).T
            yield turned[:columns] + turned[columns:]
            parts = []


def couple_kernel(
    far_hbm, coupling_hbm, dens_ref, bases_ref,
    table_ref, coupling_ref, turned_ref, out_ref, far_ref, sems, chunk_sems,
):
    copies = fetch([(far_hbm, far_ref), (far_hbm, table_ref)], sems)
    chunk_count = chunk_sems.shape[0]
    chunk = coupling_ref.shape[0] // chunk_count
    chunks = [pl.ds(index * chunk, chunk) for index in range(chunk_count)]
    block_copies = fetch([(coupling_hbm.at[c], coupling_ref.at[c]) for c in chunks], chunk_sems)
    columns, points = dens_ref.shape
    leaf_count, _, rank = coupling_ref.shape[:3]
    width = points // leaf_count
    upper = lax.broadcasted_iota(jnp.int32, (rank, 2 * columns), 1) < columns
    for leaf in range(leaf_count):
        spots = slice(leaf * width, (leaf + 1) * width)
        rows = jnp.concatenate(halves(bases_ref[:, spots]), axis=0)
        dens = dens_ref[:, spots]
        twice = dot_nt(rows, jnp.concatenate([dens, dens], axis=0))
        high, low = halves(twice[:rank] + twice[rank:])
        turned_ref[leaf * rank : (leaf + 1) * rank, :] = jnp.where(
            upper, high.astype(F32), low.astype(F32)
        ).astype(BF16)
    for copy in copies:
        copy.wait()
    done = out_ref.shape[1] // rank
    for index in range(chunk_count):
        block_copies[index].wait()
        leaves = range(index * chunk, min((index + 1) * chunk, done))
        for turn, field in enumerate(coupled(leaves, far_ref, coupling_ref, turned_ref)):
            spot = index * chunk * rank + turn * LANES
            out_ref[:, spot : spot + LANES] = field


def project_kernel(
    table_ref, coupling_ref, turned_ref, first_ref, bases_ref, near_ref, out_ref, far_ref, sems,
):
    copies = fetch([(table_ref, far_ref)], sems)
    rank, points = bases_ref.shape
    leaf_count = coupling_ref.shape[0]
    group = LANES // rank
    step = group * points // leaf_count

    def project(index, field):
        spots = slice(index * step, (index + 1) * step)
        high, low = halves(bases_ref[:, spots])
        out_ref[:, spots] = near_ref[:, spots] + split_dot(
            dot_nn, field, spread_bases(high, group), spread_bases(low, group)
        )

    done = first_ref.shape[1] // LANES
    for index in range(done):
        project(index, first_ref[:, index * LANES : (index + 1) * LANES])
    copies[0].wait()
    leaves = range(done * group, leaf_count)
    for index, field in enumerate(coupled(leaves, far_ref, coupling_ref, turned_ref)):
        project(done + index, field)


def far_kernel(
    roots, upper_ref, cross_ref, high_ref, low_ref, term_ref, *refs,
):
    root_refs, refs = refs[: len(roots)], refs[len(roots) :]
    out_ref, tile_ref, tree_ref = refs
    device = lax.axis_index("leaf")
    columns, points = out_ref.shape
    rank = upper_ref.shape[1]
    device_count = upper_ref.shape[0] // 2
    for tiles, root_ref in zip(roots, root_refs):
        if tiles is None:
            for index in range(device_count):
                tile_ref[index] = root_ref[index]
        else:
            for turn, row in tiles:
                tile_ref[device ^ turn] = root_ref[row : row + columns, :]
    zero = jnp.zeros((LANES - 3 * rank, rank), BF16)

    def lifted(child):
        if child >= device_count:
            high, low = (
                jnp.concatenate([half] * 3 + [zero], axis=0) for half in halves(upper_ref[child])
            )
            tile = tile_ref[child - device_count]
            return dot_nn(tile, high) + dot_nn(tile, low)
        return split_dot(dot_nn, tree_ref[child], *halves(upper_ref[child]))

    level = device_count // 2
    while level >= 4:
        for node in range(level, 2 * level):
            tree_ref[node] = lifted(2 * node) + lifted(2 * node + 1)
        level //= 2
    lane = lax.broadcasted_iota(jnp.int32, (LANES, rank), 0)
    column = lax.broadcasted_iota(jnp.int32, (LANES, rank), 1)
    gather = jnp.where((lane % rank == column) & (lane < 3 * rank), 1.0, 0.0).astype(BF16)
    field = None
    level = 4
    while level <= device_count:
        place = device // (device_count // level)
        node = level + place
        third = jnp.where(place % 2 == 0, place + 3, place - 3)
        total = None
        for slot, other in enumerate((place - 2, place + 2, third)):
            inside = (other >= 0) & (other < level)
            other = jnp.clip(other, 0, level - 1)
            if level == device_count:
                value = dot_nn(tile_ref[other], gather)
            else:
                value = tree_ref[level + other]
            value = jnp.where(inside, value, 0.0)
            term = split_dot(dot_nt, value, *halves(cross_ref[node, slot]))
            total = term if total is None else total + term
        if field is not None:
            total = total + split_dot(dot_nt, field, *halves(upper_ref[node]))
        field = total
        level *= 2
    step = 4 * LANES
    for first in range(0, points, step):
        spots = slice(first, first + step)
        out_ref[:, spots] = term_ref[:, spots] + split_dot(
            dot_nn, field, high_ref[:, spots], low_ref[:, spots]
        )


def add_kernel(*refs):
    term_refs, (out_hbm, sum_ref, sems) = refs[:-3], refs[-3:]
    chunk_count = sems.shape[0]
    step = sum_ref.shape[1] // chunk_count
    copies = []
    for index in range(chunk_count):
        spots = slice(index * step, (index + 1) * step)
        total = term_refs[0][:, spots]
        for term_ref in term_refs[1:]:
            total = total + term_ref[:, spots]
        sum_ref[:, spots] = total
        copies += fetch(
            [(sum_ref.at[:, pl.ds(index * step, step)], out_hbm.at[:, pl.ds(index * step, step)])],
            sems.at[pl.ds(index, 1)],
        )
    for copy in copies:
        copy.wait()


def hbm(value):
    return pltpu.with_memory_space_constraint(value, pltpu.HBM)


def hint(micros):
    return pl.CostEstimate(flops=0, bytes_accessed=int(micros * 3.69e6), transcendentals=0)


def local(
    densities,
    bases,
    near_blocks,
    near_src,
    send_leaf,
    far_src,
    leaf_coupling,
    local_transfer,
    upper_transfer,
    up_coupling,
):
    leaf_devices = lax.axis_size("leaf")
    far_groups = lax.axis_size("far")
    share = lax.axis_size("mate")
    side = cube_side(leaf_devices)
    offsets = face_offsets(leaf_devices)
    columns, points = densities.shape
    leaf_count, near_count, width, _ = near_blocks.shape
    rank = bases.shape[0]
    cap = send_leaf.shape[2]
    node_count = local_transfer.shape[1]
    params = pltpu.CompilerParams(vmem_limit_bytes=16 * 2**20)
    dma = pltpu.SemaphoreType.DMA

    def rotated(value, axis, shift):
        count = lax.axis_size(axis)
        return lax.ppermute(value, axis, [(i, (i - shift) % count) for i in range(count)])

    def crossed(value, turn):
        return lax.ppermute(value, "leaf", [(i, i ^ turn) for i in range(leaf_devices)])

    sources = near_src.T
    others = [rotated(densities, "far", part) for part in range(1, far_groups)]
    all_sources = [sources] + [rotated(sources, "mate", part) for part in range(1, share)]
    send = send_leaf.transpose(1, 2, 0)
    dens, basis, send, sources, high, low, root = pl.pallas_call(
        up_kernel,
        out_shape=[
            jax.ShapeDtypeStruct(densities.shape, BF16),
            jax.ShapeDtypeStruct(bases.shape, F32),
            jax.ShapeDtypeStruct(send.shape, jnp.int32),
            jax.ShapeDtypeStruct(sources.shape, jnp.int32),
            jax.ShapeDtypeStruct((rank, points), BF16),
            jax.ShapeDtypeStruct((rank, points), BF16),
            jax.ShapeDtypeStruct((columns, LANES), BF16),
        ],
        in_specs=[HBM] * 5,
        out_specs=[VMEM] * 7,
        scratch_shapes=[
            pltpu.VMEM((rank, rank, node_count), F32),
            pltpu.VMEM((node_count * rank, LANES), F32),
            pltpu.VMEM((rank, node_count * rank), F32),
            dma((5,)),
        ],
        compiler_params=params,
        cost_estimate=hint(3.5),
        name="up",
    )(
        hbm(densities), hbm(bases), hbm(local_transfer[0].transpose(1, 2, 0)), hbm(send),
        hbm(sources),
    )
    all_sources[0] = sources

    later_blocks, others, all_sources, root = lax.optimization_barrier(
        (near_blocks, others, all_sources, root)
    )
    mate_blocks = [rotated(later_blocks, "mate", part) for part in range(1, share)]

    if side == 2:
        faces = [((2 * axis, 2 * axis + 1), 2**axis) for axis in range(3)]
    else:
        faces = [((direction,), offset) for direction, offset in enumerate(offsets)]
    chunk = (cap * far_groups + 1) * columns
    outgoing = pl.pallas_call(
        functools.partial(select_kernel, faces, far_groups),
        out_shape=[jax.ShapeDtypeStruct((chunk, LANES), BF16)] * len(faces),
        in_specs=[VMEM] * (2 + far_groups),
        out_specs=[VMEM] * len(faces),
        scratch_shapes=[
            pltpu.SMEM(send.shape, jnp.int32),
            dma((1,)),
        ],
        compiler_params=params,
        cost_estimate=hint(1),
        name="select",
    )(send, dens, root, *others)
    outgoing, dens = lax.optimization_barrier((outgoing, dens))
    far_table = far_src.T
    first_leaves = leaf_count // 2
    *coupling, leaf_local = pl.pallas_call(
        couple_kernel,
        out_shape=[
            jax.ShapeDtypeStruct(far_table.shape, jnp.int32),
            jax.ShapeDtypeStruct(leaf_coupling.shape, F32),
            jax.ShapeDtypeStruct((leaf_count * rank, 2 * columns), BF16),
            jax.ShapeDtypeStruct((columns, first_leaves * rank), F32),
        ],
        in_specs=[HBM] * 2 + [VMEM] * 2,
        out_specs=[VMEM] * 4,
        scratch_shapes=[pltpu.SMEM(far_table.shape, jnp.int32), dma((2,)), dma((4,))],
        compiler_params=params,
        cost_estimate=hint(2),
        name="couple",
    )(hbm(far_table), hbm(leaf_coupling), dens, basis)
    tail = cap * far_groups * columns
    if side == 2:
        arrived = [crossed(value, stride) for (_, stride), value in zip(faces, outgoing)]
        held = jnp.concatenate([root] + [value[tail:] for value in arrived], axis=0)
        whole = leaf_devices - 1
        opposite = crossed(held, whole)
        turns = [0] + [stride for _, stride in faces]
        roots = [
            ([(0, 0)], root),
            ([(turn ^ whole, row * columns) for row, turn in enumerate(turns)], opposite),
        ]
        roots += [([(stride, tail)], value) for (_, stride), value in zip(faces, arrived)]
    else:
        arrived = [shifted(value, "leaf", stride) for (_, stride), value in zip(faces, outgoing)]
        roots = [(None, lax.all_gather(root, "leaf", axis=0))]

    slots = leaf_count + len(offsets) * cap
    partials = pl.pallas_call(
        functools.partial(near_kernel, faces, far_groups, share),
        out_shape=[jax.ShapeDtypeStruct((columns, points), F32)] * far_groups,
        in_specs=[VMEM] * (share + far_groups + len(faces))
        + [HBM]
        + [VMEM] * share,
        out_specs=[VMEM] * far_groups,
        scratch_shapes=[pltpu.SMEM(sources.shape, jnp.int32)] * share
        + [
            pltpu.VMEM(near_blocks.shape, BF16),
            pltpu.VMEM((slots, far_groups * columns, width), BF16),
            dma((share,)),
            dma((4,)),
        ],
        compiler_params=params,
        cost_estimate=hint(3),
        name="near",
    )(
        *all_sources, dens, *others, *arrived, hbm(near_blocks), *mate_blocks, leaf_local,
    )
    received = [rotated(partials[part], "far", -part) for part in range(1, far_groups)]
    partial = pl.pallas_call(
        project_kernel,
        out_shape=jax.ShapeDtypeStruct((columns, points), F32),
        in_specs=[VMEM] * 6,
        out_specs=VMEM,
        scratch_shapes=[pltpu.SMEM(far_table.shape, jnp.int32), dma((1,))],
        compiler_params=params,
        cost_estimate=hint(1.5),
        name="project",
    )(*coupling, leaf_local, basis, partials[0])
    total = pl.pallas_call(
        functools.partial(far_kernel, [tiles for tiles, _ in roots]),
        out_shape=jax.ShapeDtypeStruct((columns, points), F32),
        in_specs=[VMEM] * (5 + len(roots)),
        out_specs=VMEM,
        scratch_shapes=[
            pltpu.VMEM((leaf_devices, columns, LANES), BF16),
            pltpu.VMEM((2 * leaf_devices, columns, rank), F32),
        ],
        compiler_params=params,
        cost_estimate=hint(1.5),
        name="far",
    )(upper_transfer, up_coupling, high, low, partial, *[value for _, value in roots])
    return pl.pallas_call(
        add_kernel,
        out_shape=jax.ShapeDtypeStruct((columns, points), F32),
        in_specs=[VMEM] * (1 + len(received)),
        out_specs=HBM,
        scratch_shapes=[pltpu.VMEM((columns, points), F32), dma((4,))],
        compiler_params=params,
        cost_estimate=hint(0.5),
        name="add",
    )(total, *received)


def solution(mesh):
    leaf_devices, rhs_devices = mesh.shape["leaf"], mesh.shape["rhs"]
    share = 2 if rhs_devices % 2 == 0 else 1
    split = Mesh(
        mesh.devices.reshape(leaf_devices, rhs_devices // share, share), ("leaf", "far", "mate")
    )
    rhs = ("far", "mate")
    in_specs = (
        P(rhs, "leaf"),
        P(None, "leaf"),
        P("leaf", rhs, None, None),
        P("leaf", rhs),
        P(),
        P("leaf", None),
        P("leaf", None, None, None),
        P("leaf", None, None, None),
        P(),
        P(),
    )
    return jax.shard_map(
        local, mesh=split, in_specs=in_specs, out_specs=P(rhs, "leaf"), check_vma=False
    )
```

```python
import functools

import jax
import jax.numpy as jnp
from jax import lax
from jax.experimental import pallas as pl
from jax.experimental.pallas import tpu as pltpu
from jax.sharding import Mesh
from jax.sharding import PartitionSpec as P

FACE_SIGNS = ((1, 0), (-1, 0), (1, 1), (-1, 1), (1, 2), (-1, 2))
F32 = jnp.float32
BF16 = jnp.bfloat16
LANES = 128
VMEM = pl.BlockSpec(memory_space=pltpu.VMEM)
HBM = pl.BlockSpec(memory_space=pltpu.HBM)
SMEM = pl.BlockSpec(memory_space=pltpu.SMEM)


def cube_side(device_count):
    return max((edge_len for edge_len in range(1, 65) if edge_len**3 <= device_count))


def face_offsets(device_count):
    side_len = cube_side(device_count)
    return [face_sign * side_len**axis_pos for face_sign, axis_pos in FACE_SIGNS]


def shifted(value, axis, steps):
    count = lax.axis_size(axis)
    first, last = (max(0, -steps), min(count, count - steps))
    return lax.ppermute(value, axis, [(source, source + steps) for source in range(first, last)])


def halves(value):
    high = value.astype(BF16)
    return high, (value - high.astype(F32)).astype(BF16)


def dot_nn(left, right):
    return lax.dot_general(left, right, (((1,), (0,)), ((), ())), preferred_element_type=F32)


def dot_nt(left, right):
    return lax.dot_general(left, right, (((1,), (1,)), ((), ())), preferred_element_type=F32)


def split_dot(dot, rows, right_high, right_low):
    count = rows.shape[0]
    high, low = halves(rows)
    both = jnp.concatenate([high, low], axis=0)
    out = dot(both, right_high) + dot(both, right_low)
    return out[:count] + out[count:]


def spread_bases(block, group):
    rank, lanes = block.shape
    width = lanes // group
    zero = jnp.zeros((rank, width), block.dtype)
    rows = []
    for slot in range(group):
        pieces = [zero] * group
        pieces[slot] = block[:, slot * width : (slot + 1) * width]
        rows.append(jnp.concatenate(pieces, axis=1))
    return jnp.concatenate(rows, axis=0)


def fetch(pairs, sems):
    copies = []
    for index, (source, target) in enumerate(pairs):
        copy = pltpu.make_async_copy(source, target, sems.at[index])
        copy.start()
        copies.append(copy)
    return copies


def up_kernel(
    dens_hbm, bases_hbm, maps_hbm, send_hbm, source_hbm,
    dens_ref, bases_ref, send_ref, source_ref, high_ref, low_ref, root_ref,
    maps_ref, spread_ref, chain_ref, sems,
):
    copies = fetch(
        [
            (maps_hbm, maps_ref),
            (bases_hbm, bases_ref),
            (dens_hbm, dens_ref),
            (send_hbm, send_ref),
            (source_hbm, source_ref),
        ],
        sems,
    )
    columns, points = dens_ref.shape
    rank, _, node_count = maps_ref.shape
    group = LANES // rank
    leaf_count = node_count // 2
    width = points // leaf_count
    copies[0].wait()
    node = lax.broadcasted_iota(jnp.int32, (node_count, LANES), 0)
    block = lax.broadcasted_iota(jnp.int32, (node_count, LANES), 1) // rank
    parent = node // 2 % group
    for first in range(0, rank, group):
        slab = maps_ref[first : first + group].reshape(group * rank, node_count).T
        turned = [slab] + [pltpu.roll(slab, turn * rank, 1) for turn in range(1, group)]
        for row in range(group):
            placed = jnp.zeros_like(slab)
            for place in range(group):
                here = (parent == place) & (block == place)
                placed = jnp.where(here, turned[(place - row) % group], placed)
            spread_ref[pl.ds(first + row, node_count, stride=rank), :] = placed
    tile = 2 * group * rank

    def children(parents, index):
        high, low = halves(spread_ref[index * tile : (index + 1) * tile, :])
        return split_dot(dot_nt, parents, high, low)

    row = lax.broadcasted_iota(jnp.int32, (rank, LANES), 0)
    lane = lax.broadcasted_iota(jnp.int32, (rank, LANES), 1)
    level = 1
    parents = jnp.where(lane == row + rank, 1.0, 0.0)
    while level < group:
        below = children(parents, 0)
        level *= 2
        parents = below[:, (level // group) * LANES : (level // group + 1) * LANES]
    chain_ref[:, LANES : 2 * LANES] = parents
    while level < leaf_count:
        for index in range(level // group, 2 * level // group):
            lanes = slice(index * LANES, (index + 1) * LANES)
            chain_ref[:, index * tile : (index + 1) * tile] = children(chain_ref[:, lanes], index)
        level *= 2
    for copy in copies[1:]:
        copy.wait()
    step = group * width
    root = jnp.zeros((columns, rank), F32)
    for index in range(leaf_count // group):
        spots = slice(index * step, (index + 1) * step)
        start = (leaf_count // group + index) * LANES
        high, low = halves(bases_ref[:, spots])
        basis = split_dot(
            dot_nn, chain_ref[:, start : start + LANES],
            spread_bases(high, group), spread_bases(low, group),
        )
        high, low = halves(basis)
        high_ref[:, spots] = high
        low_ref[:, spots] = low
        dens = dens_ref[:, spots]
        root += dot_nt(dens, high) + dot_nt(dens, low)
    root = jnp.concatenate([root, jnp.zeros((columns, LANES - rank), F32)], axis=1)
    high = root.astype(BF16).astype(F32)
    rest = root - high
    middle = rest.astype(BF16).astype(F32)
    last = (rest - middle).astype(BF16).astype(F32)
    packed = high + pltpu.roll(middle, rank, 1) + pltpu.roll(last, 2 * rank, 1)
    root_ref[...] = packed.astype(BF16)


def select_kernel(
    faces, far_groups, send_vmem, dens_ref, root_ref, *refs,
):
    other_refs = refs[: far_groups - 1]
    out_refs = refs[far_groups - 1 : -2]
    send_ref, sems = refs[-2:]
    copies = fetch([(send_vmem, send_ref)], sems)
    device = lax.axis_index("leaf")
    columns = dens_ref.shape[0]
    cap = send_ref.shape[1]
    copies[0].wait()
    for (directions, stride), out_ref in zip(faces, out_refs):
        direction = directions[0]
        if len(directions) > 1:
            direction = direction + device // stride % 2
        for place in range(cap):
            leaf = jnp.maximum(send_ref[direction, place, device], 0)
            for part, panel_ref in enumerate((dens_ref, *other_refs)):
                row = (place * far_groups + part) * columns
                out_ref[row : row + columns, :] = panel_ref[
                    :, pl.ds(pl.multiple_of(leaf * LANES, LANES), LANES)
                ]
        for row in range(cap * far_groups * columns, out_ref.shape[0], columns):
            out_ref[row : row + columns, :] = root_ref[...]


def near_kernel(
    faces, far_groups, share, *refs,
):
    source_vmems, refs = refs[:share], refs[share:]
    dens_ref, refs = refs[0], refs[1:]
    other_refs, refs = refs[: far_groups - 1], refs[far_groups - 1 :]
    got_refs, refs = refs[: len(faces)], refs[len(faces) :]
    block_hbm, refs = refs[0], refs[1:]
    mate_refs, refs = refs[: share - 1], refs[share - 1 :]
    refs = refs[1:]
    out_refs, refs = refs[:far_groups], refs[far_groups:]
    source_refs, refs = refs[:share], refs[share:]
    block_ref, buffer_ref, small_sems, sems = refs
    columns, points = dens_ref.shape
    leaf_count, near_count, width, _ = block_ref.shape
    chunk_count = sems.shape[0]
    chunk = leaf_count // chunk_count
    copies = fetch(list(zip(source_vmems, source_refs)), small_sems)
    block_copies = fetch(
        [
            (block_hbm.at[pl.ds(index * chunk, chunk)], block_ref.at[pl.ds(index * chunk, chunk)])
            for index in range(chunk_count)
        ],
        sems,
    )
    cap = (buffer_ref.shape[0] - leaf_count) // len(FACE_SIGNS)
    for (directions, _), got_ref in zip(faces, got_refs):
        for direction in directions:
            for place in range(cap):
                row = place * far_groups * columns
                buffer_ref[leaf_count + direction * cap + place] = got_ref[
                    row : row + far_groups * columns, :
                ]
    for part, panel_ref in enumerate((dens_ref, *other_refs)):
        rows = slice(part * columns, (part + 1) * columns)
        for leaf in range(leaf_count):
            buffer_ref[leaf, rows, :] = panel_ref[:, leaf * width : (leaf + 1) * width]
    for copy in copies:
        copy.wait()
    tables = list(zip(source_refs[1:], mate_refs)) + [(source_refs[0], block_ref)]
    for turn, (source_ref, blocks_ref) in enumerate(tables):
        for leaf in range(leaf_count):
            if blocks_ref is block_ref and leaf % chunk == 0:
                block_copies[leaf // chunk].wait()
            panels = [buffer_ref[source_ref[block, leaf]] for block in range(near_count)]
            blocks = [blocks_ref[leaf, block] for block in range(near_count)]
            total = dot_nt(jnp.concatenate(panels, axis=1), jnp.concatenate(blocks, axis=1))
            lanes = slice(leaf * width, (leaf + 1) * width)
            for part, out_ref in enumerate(out_refs):
                term = total[part * columns : (part + 1) * columns]
                out_ref[:, lanes] = term if turn == 0 else out_ref[:, lanes] + term


def coupled(leaves, far_ref, coupling_ref, turned_ref):
    far_count, rank = coupling_ref.shape[1:3]
    columns = turned_ref.shape[1] // 2
    group = LANES // rank
    parts = []
    for leaf in leaves:
        maps = jnp.concatenate([coupling_ref[leaf, j] for j in range(far_count)], axis=1)
        maps = jnp.concatenate(halves(maps), axis=0)
        picked = jnp.concatenate(
            [
                turned_ref[pl.ds(pl.multiple_of(far_ref[j, leaf] * rank, rank), rank), :]
                for j in range(far_count)
            ],
            axis=0,
        )
        out = dot_nn(maps, picked)
        parts.append(out[:rank] + out[rank:])
        if len(parts) == group:
            turned = jnp.concatenate(parts, axis=0).T
            yield turned[:columns] + turned[columns:]
            parts = []


def couple_kernel(
    far_hbm, coupling_hbm, dens_ref, bases_ref,
    table_ref, coupling_ref, turned_ref, out_ref, far_ref, sems, chunk_sems,
):
    copies = fetch([(far_hbm, far_ref), (far_hbm, table_ref)], sems)
    chunk_count = chunk_sems.shape[0]
    chunk = coupling_ref.shape[0] // chunk_count
    chunks = [pl.ds(index * chunk, chunk) for index in range(chunk_count)]
    block_copies = fetch([(coupling_hbm.at[c], coupling_ref.at[c]) for c in chunks], chunk_sems)
    columns, points = dens_ref.shape
    leaf_count, _, rank = coupling_ref.shape[:3]
    width = points // leaf_count
    upper = lax.broadcasted_iota(jnp.int32, (rank, 2 * columns), 1) < columns
    for leaf in range(leaf_count):
        spots = slice(leaf * width, (leaf + 1) * width)
        rows = jnp.concatenate(halves(bases_ref[:, spots]), axis=0)
        dens = dens_ref[:, spots]
        twice = dot_nt(rows, jnp.concatenate([dens, dens], axis=0))
        high, low = halves(twice[:rank] + twice[rank:])
        turned_ref[leaf * rank : (leaf + 1) * rank, :] = jnp.where(
            upper, high.astype(F32), low.astype(F32)
        ).astype(BF16)
    for copy in copies:
        copy.wait()
    done = out_ref.shape[1] // rank
    for index in range(chunk_count):
        block_copies[index].wait()
        leaves = range(index * chunk, min((index + 1) * chunk, done))
        for turn, field in enumerate(coupled(leaves, far_ref, coupling_ref, turned_ref)):
            spot = index * chunk * rank + turn * LANES
            out_ref[:, spot : spot + LANES] = field


def project_kernel(
    table_ref, coupling_ref, turned_ref, first_ref, bases_ref, near_ref, out_ref, far_ref, sems,
):
    copies = fetch([(table_ref, far_ref)], sems)
    rank, points = bases_ref.shape
    leaf_count = coupling_ref.shape[0]
    group = LANES // rank
    step = group * points // leaf_count

    def project(index, field):
        spots = slice(index * step, (index + 1) * step)
        high, low = halves(bases_ref[:, spots])
        out_ref[:, spots] = near_ref[:, spots] + split_dot(
            dot_nn, field, spread_bases(high, group), spread_bases(low, group)
        )

    done = first_ref.shape[1] // LANES
    for index in range(done):
        project(index, first_ref[:, index * LANES : (index + 1) * LANES])
    copies[0].wait()
    leaves = range(done * group, leaf_count)
    for index, field in enumerate(coupled(leaves, far_ref, coupling_ref, turned_ref)):
        project(done + index, field)


def far_kernel(
    roots, upper_ref, cross_ref, high_ref, low_ref, term_ref, *refs,
):
    root_refs, refs = refs[: len(roots)], refs[len(roots) :]
    out_ref, tile_ref, tree_ref = refs
    device = lax.axis_index("leaf")
    columns, points = out_ref.shape
    rank = upper_ref.shape[1]
    device_count = upper_ref.shape[0] // 2
    for tiles, root_ref in zip(roots, root_refs):
        if tiles is None:
            for index in range(device_count):
                tile_ref[index] = root_ref[index]
        else:
            for turn, row in tiles:
                tile_ref[device ^ turn] = root_ref[row : row + columns, :]
    zero = jnp.zeros((LANES - 3 * rank, rank), BF16)

    def lifted(child):
        if child >= device_count:
            high, low = (
                jnp.concatenate([half] * 3 + [zero], axis=0) for half in halves(upper_ref[child])
            )
            tile = tile_ref[child - device_count]
            return dot_nn(tile, high) + dot_nn(tile, low)
        return split_dot(dot_nn, tree_ref[child], *halves(upper_ref[child]))

    level = device_count // 2
    while level >= 4:
        for node in range(level, 2 * level):
            tree_ref[node] = lifted(2 * node) + lifted(2 * node + 1)
        level //= 2
    lane = lax.broadcasted_iota(jnp.int32, (LANES, rank), 0)
    column = lax.broadcasted_iota(jnp.int32, (LANES, rank), 1)
    gather = jnp.where((lane % rank == column) & (lane < 3 * rank), 1.0, 0.0).astype(BF16)
    field = None
    level = 4
    while level <= device_count:
        place = device // (device_count // level)
        node = level + place
        third = jnp.where(place % 2 == 0, place + 3, place - 3)
        total = None
        for slot, other in enumerate((place - 2, place + 2, third)):
            inside = (other >= 0) & (other < level)
            other = jnp.clip(other, 0, level - 1)
            if level == device_count:
                value = dot_nn(tile_ref[other], gather)
            else:
                value = tree_ref[level + other]
            value = jnp.where(inside, value, 0.0)
            term = split_dot(dot_nt, value, *halves(cross_ref[node, slot]))
            total = term if total is None else total + term
        if field is not None:
            total = total + split_dot(dot_nt, field, *halves(upper_ref[node]))
        field = total
        level *= 2
    step = 4 * LANES
    for first in range(0, points, step):
        spots = slice(first, first + step)
        out_ref[:, spots] = term_ref[:, spots] + split_dot(
            dot_nn, field, high_ref[:, spots], low_ref[:, spots]
        )


def add_kernel(*refs):
    term_refs, (out_hbm, sum_ref, sems) = refs[:-3], refs[-3:]
    chunk_count = sems.shape[0]
    step = sum_ref.shape[1] // chunk_count
    copies = []
    for index in range(chunk_count):
        spots = slice(index * step, (index + 1) * step)
        total = term_refs[0][:, spots]
        for term_ref in term_refs[1:]:
            total = total + term_ref[:, spots]
        sum_ref[:, spots] = total
        copies += fetch(
            [(sum_ref.at[:, pl.ds(index * step, step)], out_hbm.at[:, pl.ds(index * step, step)])],
            sems.at[pl.ds(index, 1)],
        )
    for copy in copies:
        copy.wait()


def hbm(value):
    return pltpu.with_memory_space_constraint(value, pltpu.HBM)


def hint(micros):
    return pl.CostEstimate(flops=0, bytes_accessed=int(micros * 3.69e6), transcendentals=0)


def local(
    densities,
    bases,
    near_blocks,
    near_src,
    send_leaf,
    far_src,
    leaf_coupling,
    local_transfer,
    upper_transfer,
    up_coupling,
):
    leaf_devices = lax.axis_size("leaf")
    far_groups = lax.axis_size("far")
    share = lax.axis_size("mate")
    side = cube_side(leaf_devices)
    offsets = face_offsets(leaf_devices)
    columns, points = densities.shape
    leaf_count, near_count, width, _ = near_blocks.shape
    rank = bases.shape[0]
    cap = send_leaf.shape[2]
    node_count = local_transfer.shape[1]
    params = pltpu.CompilerParams(vmem_limit_bytes=16 * 2**20)
    dma = pltpu.SemaphoreType.DMA

    def rotated(value, axis, shift):
        count = lax.axis_size(axis)
        return lax.ppermute(value, axis, [(i, (i - shift) % count) for i in range(count)])

    def crossed(value, turn):
        return lax.ppermute(value, "leaf", [(i, i ^ turn) for i in range(leaf_devices)])

    sources = near_src.T
    others = [rotated(densities, "far", part) for part in range(1, far_groups)]
    all_sources = [sources] + [rotated(sources, "mate", part) for part in range(1, share)]
    send = send_leaf.transpose(1, 2, 0)
    dens, basis, send, sources, high, low, root = pl.pallas_call(
        up_kernel,
        out_shape=[
            jax.ShapeDtypeStruct(densities.shape, BF16),
            jax.ShapeDtypeStruct(bases.shape, F32),
            jax.ShapeDtypeStruct(send.shape, jnp.int32),
            jax.ShapeDtypeStruct(sources.shape, jnp.int32),
            jax.ShapeDtypeStruct((rank, points), BF16),
            jax.ShapeDtypeStruct((rank, points), BF16),
            jax.ShapeDtypeStruct((columns, LANES), BF16),
        ],
        in_specs=[HBM] * 5,
        out_specs=[VMEM] * 7,
        scratch_shapes=[
            pltpu.VMEM((rank, rank, node_count), F32),
            pltpu.VMEM((node_count * rank, LANES), F32),
            pltpu.VMEM((rank, node_count * rank), F32),
            dma((5,)),
        ],
        compiler_params=params,
        cost_estimate=hint(3.5),
        name="up",
    )(
        hbm(densities), hbm(bases), hbm(local_transfer[0].transpose(1, 2, 0)), hbm(send),
        hbm(sources),
    )
    all_sources[0] = sources

    beside = crossed(root, 1) if side == 2 else None
    later_blocks, others, all_sources, root = lax.optimization_barrier(
        (near_blocks, others, all_sources, root)
    )
    mate_blocks = [rotated(later_blocks, "mate", part) for part in range(1, share)]

    if side == 2:
        faces = [((2 * axis, 2 * axis + 1), 2**axis) for axis in range(3)]
    else:
        faces = [((direction,), offset) for direction, offset in enumerate(offsets)]
    chunks = [(cap * far_groups + (1 if stride > 1 else 4)) * columns for _, stride in faces]
    outgoing = pl.pallas_call(
        functools.partial(select_kernel, faces, far_groups),
        out_shape=[jax.ShapeDtypeStruct((chunk, LANES), BF16) for chunk in chunks],
        in_specs=[VMEM] * (2 + far_groups),
        out_specs=[VMEM] * len(faces),
        scratch_shapes=[
            pltpu.SMEM(send.shape, jnp.int32),
            dma((1,)),
        ],
        compiler_params=params,
        cost_estimate=hint(1),
        name="select",
    )(send, dens, root, *others)
    outgoing, dens = lax.optimization_barrier((outgoing, dens))
    far_table = far_src.T
    first_leaves = leaf_count // 2
    *coupling, leaf_local = pl.pallas_call(
        couple_kernel,
        out_shape=[
            jax.ShapeDtypeStruct(far_table.shape, jnp.int32),
            jax.ShapeDtypeStruct(leaf_coupling.shape, F32),
            jax.ShapeDtypeStruct((leaf_count * rank, 2 * columns), BF16),
            jax.ShapeDtypeStruct((columns, first_leaves * rank), F32),
        ],
        in_specs=[HBM] * 2 + [VMEM] * 2,
        out_specs=[VMEM] * 4,
        scratch_shapes=[pltpu.SMEM(far_table.shape, jnp.int32), dma((2,)), dma((4,))],
        compiler_params=params,
        cost_estimate=hint(2),
        name="couple",
    )(hbm(far_table), hbm(leaf_coupling), dens, basis)
    tail = cap * far_groups * columns
    if side == 2:
        payloads = [outgoing[0]] + [
            jnp.concatenate([value, beside], axis=0) for value in outgoing[1:]
        ]
        arrived = [crossed(value, stride) for (_, stride), value in zip(faces, payloads)]
        first, second, third = (stride for _, stride in faces)
        far_pair = crossed(arrived[2][tail:], second)
        roots = [([(0, 0)], root), ([(first, 0)], beside)]
        for stride, value, row in (
            (second, arrived[1], tail),
            (third, arrived[2], tail),
            (second ^ third, far_pair, 0),
        ):
            roots.append(([(stride, row), (stride ^ first, row + columns)], value))
    else:
        arrived = [shifted(value, "leaf", stride) for (_, stride), value in zip(faces, outgoing)]
        roots = [(None, lax.all_gather(root, "leaf", axis=0))]

    slots = leaf_count + len(offsets) * cap
    partials = pl.pallas_call(
        functools.partial(near_kernel, faces, far_groups, share),
        out_shape=[jax.ShapeDtypeStruct((columns, points), F32)] * far_groups,
        in_specs=[VMEM] * (share + far_groups + len(faces))
        + [HBM]
        + [VMEM] * share,
        out_specs=[VMEM] * far_groups,
        scratch_shapes=[pltpu.SMEM(sources.shape, jnp.int32)] * share
        + [
            pltpu.VMEM(near_blocks.shape, BF16),
            pltpu.VMEM((slots, far_groups * columns, width), BF16),
            dma((share,)),
            dma((4,)),
        ],
        compiler_params=params,
        cost_estimate=hint(3),
        name="near",
    )(
        *all_sources, dens, *others, *arrived, hbm(near_blocks), *mate_blocks, leaf_local,
    )
    received = [rotated(partials[part], "far", -part) for part in range(1, far_groups)]
    partial = pl.pallas_call(
        project_kernel,
        out_shape=jax.ShapeDtypeStruct((columns, points), F32),
        in_specs=[VMEM] * 6,
        out_specs=VMEM,
        scratch_shapes=[pltpu.SMEM(far_table.shape, jnp.int32), dma((1,))],
        compiler_params=params,
        cost_estimate=hint(1.5),
        name="project",
    )(*coupling, leaf_local, basis, partials[0])
    total = pl.pallas_call(
        functools.partial(far_kernel, [tiles for tiles, _ in roots]),
        out_shape=jax.ShapeDtypeStruct((columns, points), F32),
        in_specs=[VMEM] * (5 + len(roots)),
        out_specs=VMEM,
        scratch_shapes=[
            pltpu.VMEM((leaf_devices, columns, LANES), BF16),
            pltpu.VMEM((2 * leaf_devices, columns, rank), F32),
        ],
        compiler_params=params,
        cost_estimate=hint(1.5),
        name="far",
    )(upper_transfer, up_coupling, high, low, partial, *[value for _, value in roots])
    return pl.pallas_call(
        add_kernel,
        out_shape=jax.ShapeDtypeStruct((columns, points), F32),
        in_specs=[VMEM] * (1 + len(received)),
        out_specs=HBM,
        scratch_shapes=[pltpu.VMEM((columns, points), F32), dma((4,))],
        compiler_params=params,
        cost_estimate=hint(0.5),
        name="add",
    )(total, *received)


def solution(mesh):
    leaf_devices, rhs_devices = mesh.shape["leaf"], mesh.shape["rhs"]
    share = 2 if rhs_devices % 2 == 0 else 1
    split = Mesh(
        mesh.devices.reshape(leaf_devices, rhs_devices // share, share), ("leaf", "far", "mate")
    )
    rhs = ("far", "mate")
    in_specs = (
        P(rhs, "leaf"),
        P(None, "leaf"),
        P("leaf", rhs, None, None),
        P("leaf", rhs),
        P(),
        P("leaf", None),
        P("leaf", None, None, None),
        P("leaf", None, None, None),
        P(),
        P(),
    )
    return jax.shard_map(
        local, mesh=split, in_specs=in_specs, out_specs=P(rhs, "leaf"), check_vma=False
    )
```

```python
import functools

import jax
import jax.numpy as jnp
from jax import lax
from jax.experimental import pallas as pl
from jax.experimental.pallas import tpu as pltpu
from jax.sharding import Mesh
from jax.sharding import PartitionSpec as P

FACE_SIGNS = ((1, 0), (-1, 0), (1, 1), (-1, 1), (1, 2), (-1, 2))
F32 = jnp.float32
BF16 = jnp.bfloat16
LANES = 128
VMEM = pl.BlockSpec(memory_space=pltpu.VMEM)
HBM = pl.BlockSpec(memory_space=pltpu.HBM)
SMEM = pl.BlockSpec(memory_space=pltpu.SMEM)


def cube_side(device_count):
    return max((edge_len for edge_len in range(1, 65) if edge_len**3 <= device_count))


def face_offsets(device_count):
    side_len = cube_side(device_count)
    return [face_sign * side_len**axis_pos for face_sign, axis_pos in FACE_SIGNS]


def shifted(value, axis, steps):
    count = lax.axis_size(axis)
    first, last = (max(0, -steps), min(count, count - steps))
    return lax.ppermute(value, axis, [(source, source + steps) for source in range(first, last)])


def halves(value):
    high = value.astype(BF16)
    return high, (value - high.astype(F32)).astype(BF16)


def dot_nn(left, right):
    return lax.dot_general(left, right, (((1,), (0,)), ((), ())), preferred_element_type=F32)


def dot_nt(left, right):
    return lax.dot_general(left, right, (((1,), (1,)), ((), ())), preferred_element_type=F32)


def split_dot(dot, rows, right_high, right_low):
    count = rows.shape[0]
    high, low = halves(rows)
    both = jnp.concatenate([high, low], axis=0)
    out = dot(both, right_high) + dot(both, right_low)
    return out[:count] + out[count:]


def spread_bases(block, group):
    rank, lanes = block.shape
    width = lanes // group
    zero = jnp.zeros((rank, width), block.dtype)
    rows = []
    for slot in range(group):
        pieces = [zero] * group
        pieces[slot] = block[:, slot * width : (slot + 1) * width]
        rows.append(jnp.concatenate(pieces, axis=1))
    return jnp.concatenate(rows, axis=0)


def fetch(pairs, sems):
    copies = []
    for index, (source, target) in enumerate(pairs):
        copy = pltpu.make_async_copy(source, target, sems.at[index])
        copy.start()
        copies.append(copy)
    return copies


def up_kernel(
    dens_hbm, bases_hbm, maps_hbm, send_hbm, source_hbm,
    dens_ref, bases_ref, send_ref, source_ref, high_ref, low_ref, root_ref,
    maps_ref, spread_ref, chain_ref, sems,
):
    copies = fetch(
        [
            (maps_hbm, maps_ref),
            (bases_hbm, bases_ref),
            (dens_hbm, dens_ref),
            (send_hbm, send_ref),
            (source_hbm, source_ref),
        ],
        sems,
    )
    columns, points = dens_ref.shape
    rank, _, node_count = maps_ref.shape
    group = LANES // rank
    leaf_count = node_count // 2
    width = points // leaf_count
    copies[0].wait()
    node = lax.broadcasted_iota(jnp.int32, (node_count, LANES), 0)
    block = lax.broadcasted_iota(jnp.int32, (node_count, LANES), 1) // rank
    parent = node // 2 % group
    for first in range(0, rank, group):
        slab = maps_ref[first : first + group].reshape(group * rank, node_count).T
        turned = [slab] + [pltpu.roll(slab, turn * rank, 1) for turn in range(1, group)]
        for row in range(group):
            placed = jnp.zeros_like(slab)
            for place in range(group):
                here = (parent == place) & (block == place)
                placed = jnp.where(here, turned[(place - row) % group], placed)
            spread_ref[pl.ds(first + row, node_count, stride=rank), :] = placed
    tile = 2 * group * rank

    def children(parents, index):
        high, low = halves(spread_ref[index * tile : (index + 1) * tile, :])
        return split_dot(dot_nt, parents, high, low)

    row = lax.broadcasted_iota(jnp.int32, (rank, LANES), 0)
    lane = lax.broadcasted_iota(jnp.int32, (rank, LANES), 1)
    level = 1
    parents = jnp.where(lane == row + rank, 1.0, 0.0)
    while level < group:
        below = children(parents, 0)
        level *= 2
        parents = below[:, (level // group) * LANES : (level // group + 1) * LANES]
    chain_ref[:, LANES : 2 * LANES] = parents
    while level < leaf_count:
        for index in range(level // group, 2 * level // group):
            lanes = slice(index * LANES, (index + 1) * LANES)
            chain_ref[:, index * tile : (index + 1) * tile] = children(chain_ref[:, lanes], index)
        level *= 2
    for copy in copies[1:]:
        copy.wait()
    step = group * width
    root = jnp.zeros((columns, rank), F32)
    for index in range(leaf_count // group):
        spots = slice(index * step, (index + 1) * step)
        start = (leaf_count // group + index) * LANES
        high, low = halves(bases_ref[:, spots])
        basis = split_dot(
            dot_nn, chain_ref[:, start : start + LANES],
            spread_bases(high, group), spread_bases(low, group),
        )
        high, low = halves(basis)
        high_ref[:, spots] = high
        low_ref[:, spots] = low
        dens = dens_ref[:, spots]
        root += dot_nt(dens, high) + dot_nt(dens, low)
    root = jnp.concatenate([root, jnp.zeros((columns, LANES - rank), F32)], axis=1)
    high = root.astype(BF16).astype(F32)
    rest = root - high
    middle = rest.astype(BF16).astype(F32)
    last = (rest - middle).astype(BF16).astype(F32)
    packed = high + pltpu.roll(middle, rank, 1) + pltpu.roll(last, 2 * rank, 1)
    root_ref[...] = packed.astype(BF16)


def select_kernel(
    faces, far_groups, send_vmem, dens_ref, root_ref, *refs,
):
    other_refs = refs[: far_groups - 1]
    out_refs = refs[far_groups - 1 : -2]
    send_ref, sems = refs[-2:]
    copies = fetch([(send_vmem, send_ref)], sems)
    device = lax.axis_index("leaf")
    columns = dens_ref.shape[0]
    cap = send_ref.shape[1]
    copies[0].wait()
    for (directions, stride), out_ref in zip(faces, out_refs):
        direction = directions[0]
        if len(directions) > 1:
            direction = direction + device // stride % 2
        for place in range(cap):
            leaf = jnp.maximum(send_ref[direction, place, device], 0)
            for part, panel_ref in enumerate((dens_ref, *other_refs)):
                row = (place * far_groups + part) * columns
                out_ref[row : row + columns, :] = panel_ref[
                    :, pl.ds(pl.multiple_of(leaf * LANES, LANES), LANES)
                ]
        for row in range(cap * far_groups * columns, out_ref.shape[0], columns):
            out_ref[row : row + columns, :] = root_ref[...]


def near_kernel(
    faces, far_groups, share, *refs,
):
    source_vmems, refs = refs[:share], refs[share:]
    dens_ref, refs = refs[0], refs[1:]
    other_refs, refs = refs[: far_groups - 1], refs[far_groups - 1 :]
    got_refs, refs = refs[: len(faces)], refs[len(faces) :]
    block_hbm, refs = refs[0], refs[1:]
    mate_refs, refs = refs[: share - 1], refs[share - 1 :]
    refs = refs[1:]
    out_refs, refs = refs[:far_groups], refs[far_groups:]
    source_refs, refs = refs[:share], refs[share:]
    block_ref, buffer_ref, small_sems, sems = refs
    columns, points = dens_ref.shape
    leaf_count, near_count, width, _ = block_ref.shape
    chunk_count = sems.shape[0]
    chunk = leaf_count // chunk_count
    copies = fetch(list(zip(source_vmems, source_refs)), small_sems)
    block_copies = fetch(
        [
            (block_hbm.at[pl.ds(index * chunk, chunk)], block_ref.at[pl.ds(index * chunk, chunk)])
            for index in range(chunk_count)
        ],
        sems,
    )
    cap = (buffer_ref.shape[0] - leaf_count) // len(FACE_SIGNS)
    for (directions, _), got_ref in zip(faces, got_refs):
        for direction in directions:
            for place in range(cap):
                row = place * far_groups * columns
                buffer_ref[leaf_count + direction * cap + place] = got_ref[
                    row : row + far_groups * columns, :
                ]
    for part, panel_ref in enumerate((dens_ref, *other_refs)):
        rows = slice(part * columns, (part + 1) * columns)
        for leaf in range(leaf_count):
            buffer_ref[leaf, rows, :] = panel_ref[:, leaf * width : (leaf + 1) * width]
    for copy in copies:
        copy.wait()
    tables = list(zip(source_refs[1:], mate_refs)) + [(source_refs[0], block_ref)]
    for turn, (source_ref, blocks_ref) in enumerate(tables):
        for leaf in range(leaf_count):
            if blocks_ref is block_ref and leaf % chunk == 0:
                block_copies[leaf // chunk].wait()
            panels = [buffer_ref[source_ref[block, leaf]] for block in range(near_count)]
            blocks = [blocks_ref[leaf, block] for block in range(near_count)]
            total = dot_nt(jnp.concatenate(panels, axis=1), jnp.concatenate(blocks, axis=1))
            lanes = slice(leaf * width, (leaf + 1) * width)
            for part, out_ref in enumerate(out_refs):
                term = total[part * columns : (part + 1) * columns]
                out_ref[:, lanes] = term if turn == 0 else out_ref[:, lanes] + term


def coupled(leaves, far_ref, coupling_ref, turned_ref):
    far_count, rank = coupling_ref.shape[1:3]
    columns = turned_ref.shape[1] // 2
    group = LANES // rank
    parts = []
    for leaf in leaves:
        maps = jnp.concatenate([coupling_ref[leaf, j] for j in range(far_count)], axis=1)
        maps = jnp.concatenate(halves(maps), axis=0)
        picked = jnp.concatenate(
            [
                turned_ref[pl.ds(pl.multiple_of(far_ref[j, leaf] * rank, rank), rank), :]
                for j in range(far_count)
            ],
            axis=0,
        )
        out = dot_nn(maps, picked)
        parts.append(out[:rank] + out[rank:])
        if len(parts) == group:
            turned = jnp.concatenate(parts, axis=0).T
            yield turned[:columns] + turned[columns:]
            parts = []


def couple_kernel(
    far_hbm, coupling_hbm, dens_ref, bases_ref,
    table_ref, coupling_ref, turned_ref, out_ref, far_ref, sems, chunk_sems,
):
    copies = fetch([(far_hbm, far_ref), (far_hbm, table_ref)], sems)
    chunk_count = chunk_sems.shape[0]
    chunk = coupling_ref.shape[0] // chunk_count
    chunks = [pl.ds(index * chunk, chunk) for index in range(chunk_count)]
    block_copies = fetch([(coupling_hbm.at[c], coupling_ref.at[c]) for c in chunks], chunk_sems)
    columns, points = dens_ref.shape
    leaf_count, _, rank = coupling_ref.shape[:3]
    width = points // leaf_count
    upper = lax.broadcasted_iota(jnp.int32, (rank, 2 * columns), 1) < columns
    for leaf in range(leaf_count):
        spots = slice(leaf * width, (leaf + 1) * width)
        rows = jnp.concatenate(halves(bases_ref[:, spots]), axis=0)
        dens = dens_ref[:, spots]
        twice = dot_nt(rows, jnp.concatenate([dens, dens], axis=0))
        high, low = halves(twice[:rank] + twice[rank:])
        turned_ref[leaf * rank : (leaf + 1) * rank, :] = jnp.where(
            upper, high.astype(F32), low.astype(F32)
        ).astype(BF16)
    for copy in copies:
        copy.wait()
    done = out_ref.shape[1] // rank
    for index in range(chunk_count):
        block_copies[index].wait()
        leaves = range(index * chunk, min((index + 1) * chunk, done))
        for turn, field in enumerate(coupled(leaves, far_ref, coupling_ref, turned_ref)):
            spot = index * chunk * rank + turn * LANES
            out_ref[:, spot : spot + LANES] = field


def project_kernel(
    table_ref, coupling_ref, turned_ref, first_ref, bases_ref, near_ref, out_ref, far_ref, sems,
):
    copies = fetch([(table_ref, far_ref)], sems)
    rank, points = bases_ref.shape
    leaf_count = coupling_ref.shape[0]
    group = LANES // rank
    step = group * points // leaf_count

    def project(index, field):
        spots = slice(index * step, (index + 1) * step)
        high, low = halves(bases_ref[:, spots])
        out_ref[:, spots] = near_ref[:, spots] + split_dot(
            dot_nn, field, spread_bases(high, group), spread_bases(low, group)
        )

    done = first_ref.shape[1] // LANES
    for index in range(done):
        project(index, first_ref[:, index * LANES : (index + 1) * LANES])
    copies[0].wait()
    leaves = range(done * group, leaf_count)
    for index, field in enumerate(coupled(leaves, far_ref, coupling_ref, turned_ref)):
        project(done + index, field)


def far_kernel(
    roots, upper_ref, cross_ref, high_ref, low_ref, term_ref, *refs,
):
    root_refs, refs = refs[: len(roots)], refs[len(roots) :]
    out_ref, tile_ref, tree_ref = refs
    device = lax.axis_index("leaf")
    columns, points = out_ref.shape
    rank = upper_ref.shape[1]
    device_count = upper_ref.shape[0] // 2
    for tiles, root_ref in zip(roots, root_refs):
        if tiles is None:
            for index in range(device_count):
                tile_ref[index] = root_ref[index]
        else:
            for turn, row in tiles:
                tile_ref[device ^ turn] = root_ref[row : row + columns, :]
    zero = jnp.zeros((LANES - 3 * rank, rank), BF16)

    def lifted(child):
        if child >= device_count:
            high, low = (
                jnp.concatenate([half] * 3 + [zero], axis=0) for half in halves(upper_ref[child])
            )
            tile = tile_ref[child - device_count]
            return dot_nn(tile, high) + dot_nn(tile, low)
        return split_dot(dot_nn, tree_ref[child], *halves(upper_ref[child]))

    level = device_count // 2
    while level >= 4:
        for node in range(level, 2 * level):
            tree_ref[node] = lifted(2 * node) + lifted(2 * node + 1)
        level //= 2
    lane = lax.broadcasted_iota(jnp.int32, (LANES, rank), 0)
    column = lax.broadcasted_iota(jnp.int32, (LANES, rank), 1)
    gather = jnp.where((lane % rank == column) & (lane < 3 * rank), 1.0, 0.0).astype(BF16)
    field = None
    level = 4
    while level <= device_count:
        place = device // (device_count // level)
        node = level + place
        third = jnp.where(place % 2 == 0, place + 3, place - 3)
        total = None
        for slot, other in enumerate((place - 2, place + 2, third)):
            inside = (other >= 0) & (other < level)
            other = jnp.clip(other, 0, level - 1)
            if level == device_count:
                value = dot_nn(tile_ref[other], gather)
            else:
                value = tree_ref[level + other]
            value = jnp.where(inside, value, 0.0)
            term = split_dot(dot_nt, value, *halves(cross_ref[node, slot]))
            total = term if total is None else total + term
        if field is not None:
            total = total + split_dot(dot_nt, field, *halves(upper_ref[node]))
        field = total
        level *= 2
    step = 4 * LANES
    for first in range(0, points, step):
        spots = slice(first, first + step)
        out_ref[:, spots] = term_ref[:, spots] + split_dot(
            dot_nn, field, high_ref[:, spots], low_ref[:, spots]
        )


def add_kernel(*refs):
    term_refs, (out_hbm, sum_ref, sems) = refs[:-3], refs[-3:]
    chunk_count = sems.shape[0]
    step = sum_ref.shape[1] // chunk_count
    copies = []
    for index in range(chunk_count):
        spots = slice(index * step, (index + 1) * step)
        total = term_refs[0][:, spots]
        for term_ref in term_refs[1:]:
            total = total + term_ref[:, spots]
        sum_ref[:, spots] = total
        copies += fetch(
            [(sum_ref.at[:, pl.ds(index * step, step)], out_hbm.at[:, pl.ds(index * step, step)])],
            sems.at[pl.ds(index, 1)],
        )
    for copy in copies:
        copy.wait()


def hbm(value):
    return pltpu.with_memory_space_constraint(value, pltpu.HBM)


def hint(micros):
    return pl.CostEstimate(flops=0, bytes_accessed=int(micros * 3.69e6), transcendentals=0)


def local(
    densities,
    bases,
    near_blocks,
    near_src,
    send_leaf,
    far_src,
    leaf_coupling,
    local_transfer,
    upper_transfer,
    up_coupling,
):
    leaf_devices = lax.axis_size("leaf")
    far_groups = lax.axis_size("far")
    share = lax.axis_size("mate")
    side = cube_side(leaf_devices)
    offsets = face_offsets(leaf_devices)
    columns, points = densities.shape
    leaf_count, near_count, width, _ = near_blocks.shape
    rank = bases.shape[0]
    cap = send_leaf.shape[2]
    node_count = local_transfer.shape[1]
    params = pltpu.CompilerParams(vmem_limit_bytes=16 * 2**20)
    dma = pltpu.SemaphoreType.DMA

    def rotated(value, axis, shift):
        count = lax.axis_size(axis)
        return lax.ppermute(value, axis, [(i, (i - shift) % count) for i in range(count)])

    def crossed(value, turn):
        return lax.ppermute(value, "leaf", [(i, i ^ turn) for i in range(leaf_devices)])

    sources = near_src.T
    others = [rotated(densities, "far", part) for part in range(1, far_groups)]
    all_sources = [sources] + [rotated(sources, "mate", part) for part in range(1, share)]
    send = send_leaf.transpose(1, 2, 0)
    dens, basis, send, sources, high, low, root = pl.pallas_call(
        up_kernel,
        out_shape=[
            jax.ShapeDtypeStruct(densities.shape, BF16),
            jax.ShapeDtypeStruct(bases.shape, F32),
            jax.ShapeDtypeStruct(send.shape, jnp.int32),
            jax.ShapeDtypeStruct(sources.shape, jnp.int32),
            jax.ShapeDtypeStruct((rank, points), BF16),
            jax.ShapeDtypeStruct((rank, points), BF16),
            jax.ShapeDtypeStruct((columns, LANES), BF16),
        ],
        in_specs=[HBM] * 5,
        out_specs=[VMEM] * 7,
        scratch_shapes=[
            pltpu.VMEM((rank, rank, node_count), F32),
            pltpu.VMEM((node_count * rank, LANES), F32),
            pltpu.VMEM((rank, node_count * rank), F32),
            dma((5,)),
        ],
        compiler_params=params,
        cost_estimate=hint(3.5),
        name="up",
    )(
        hbm(densities), hbm(bases), hbm(local_transfer[0].transpose(1, 2, 0)), hbm(send),
        hbm(sources),
    )
    all_sources[0] = sources

    beside = crossed(root, 4) if side == 2 else None
    later_blocks, others, all_sources, root = lax.optimization_barrier(
        (near_blocks, others, all_sources, root)
    )
    mate_blocks = [rotated(later_blocks, "mate", part) for part in range(1, share)]

    if side == 2:
        faces = [((2 * axis, 2 * axis + 1), 2**axis) for axis in (2, 0, 1)]
    else:
        faces = [((direction,), offset) for direction, offset in enumerate(offsets)]
    chunks = [(cap * far_groups + (1 if place else 3)) * columns for place in range(len(faces))]
    outgoing = pl.pallas_call(
        functools.partial(select_kernel, faces, far_groups),
        out_shape=[jax.ShapeDtypeStruct((chunk, LANES), BF16) for chunk in chunks],
        in_specs=[VMEM] * (2 + far_groups),
        out_specs=[VMEM] * len(faces),
        scratch_shapes=[
            pltpu.SMEM(send.shape, jnp.int32),
            dma((1,)),
        ],
        compiler_params=params,
        cost_estimate=hint(1),
        name="select",
    )(send, dens, root, *others)
    outgoing, dens = lax.optimization_barrier((outgoing, dens))
    far_table = far_src.T
    first_leaves = leaf_count // 2
    *coupling, leaf_local = pl.pallas_call(
        couple_kernel,
        out_shape=[
            jax.ShapeDtypeStruct(far_table.shape, jnp.int32),
            jax.ShapeDtypeStruct(leaf_coupling.shape, F32),
            jax.ShapeDtypeStruct((leaf_count * rank, 2 * columns), BF16),
            jax.ShapeDtypeStruct((columns, first_leaves * rank), F32),
        ],
        in_specs=[HBM] * 2 + [VMEM] * 2,
        out_specs=[VMEM] * 4,
        scratch_shapes=[pltpu.SMEM(far_table.shape, jnp.int32), dma((2,)), dma((4,))],
        compiler_params=params,
        cost_estimate=hint(2),
        name="couple",
    )(hbm(far_table), hbm(leaf_coupling), dens, basis)
    tail = cap * far_groups * columns
    if side == 2:
        payloads = [outgoing[0]] + [
            jnp.concatenate([value, beside], axis=0) for value in outgoing[1:]
        ]
        arrived = [crossed(value, stride) for (_, stride), value in zip(faces, payloads)]
        first, second, third = (stride for _, stride in faces)
        far_pair = crossed(arrived[2][tail:], second)
        roots = [([(0, 0)], root), ([(first, 0)], beside)]
        for stride, value, row in (
            (second, arrived[1], tail),
            (third, arrived[2], tail),
            (second ^ third, far_pair, 0),
        ):
            roots.append(([(stride, row), (stride ^ first, row + columns)], value))
    else:
        arrived = [shifted(value, "leaf", stride) for (_, stride), value in zip(faces, outgoing)]
        roots = [(None, lax.all_gather(root, "leaf", axis=0))]

    slots = leaf_count + len(offsets) * cap
    partials = pl.pallas_call(
        functools.partial(near_kernel, faces, far_groups, share),
        out_shape=[jax.ShapeDtypeStruct((columns, points), F32)] * far_groups,
        in_specs=[VMEM] * (share + far_groups + len(faces))
        + [HBM]
        + [VMEM] * share,
        out_specs=[VMEM] * far_groups,
        scratch_shapes=[pltpu.SMEM(sources.shape, jnp.int32)] * share
        + [
            pltpu.VMEM(near_blocks.shape, BF16),
            pltpu.VMEM((slots, far_groups * columns, width), BF16),
            dma((share,)),
            dma((4,)),
        ],
        compiler_params=params,
        cost_estimate=hint(3),
        name="near",
    )(
        *all_sources, dens, *others, *arrived, hbm(near_blocks), *mate_blocks, leaf_local,
    )
    received = [rotated(partials[part], "far", -part) for part in range(1, far_groups)]
    partial = pl.pallas_call(
        project_kernel,
        out_shape=jax.ShapeDtypeStruct((columns, points), F32),
        in_specs=[VMEM] * 6,
        out_specs=VMEM,
        scratch_shapes=[pltpu.SMEM(far_table.shape, jnp.int32), dma((1,))],
        compiler_params=params,
        cost_estimate=hint(1.5),
        name="project",
    )(*coupling, leaf_local, basis, partials[0])
    total = pl.pallas_call(
        functools.partial(far_kernel, [tiles for tiles, _ in roots]),
        out_shape=jax.ShapeDtypeStruct((columns, points), F32),
        in_specs=[VMEM] * (5 + len(roots)),
        out_specs=VMEM,
        scratch_shapes=[
            pltpu.VMEM((leaf_devices, columns, LANES), BF16),
            pltpu.VMEM((2 * leaf_devices, columns, rank), F32),
        ],
        compiler_params=params,
        cost_estimate=hint(1.5),
        name="far",
    )(upper_transfer, up_coupling, high, low, partial, *[value for _, value in roots])
    return pl.pallas_call(
        add_kernel,
        out_shape=jax.ShapeDtypeStruct((columns, points), F32),
        in_specs=[VMEM] * (1 + len(received)),
        out_specs=HBM,
        scratch_shapes=[pltpu.VMEM((columns, points), F32), dma((4,))],
        compiler_params=params,
        cost_estimate=hint(0.5),
        name="add",
    )(total, *received)


def solution(mesh):
    leaf_devices, rhs_devices = mesh.shape["leaf"], mesh.shape["rhs"]
    share = 2 if rhs_devices % 2 == 0 else 1
    split = Mesh(
        mesh.devices.reshape(leaf_devices, rhs_devices // share, share), ("leaf", "far", "mate")
    )
    rhs = ("far", "mate")
    in_specs = (
        P(rhs, "leaf"),
        P(None, "leaf"),
        P("leaf", rhs, None, None),
        P("leaf", rhs),
        P(),
        P("leaf", None),
        P("leaf", None, None, None),
        P("leaf", None, None, None),
        P(),
        P(),
    )
    return jax.shard_map(
        local, mesh=split, in_specs=in_specs, out_specs=P(rhs, "leaf"), check_vma=False
    )
```

```python
import functools

import jax
import jax.numpy as jnp
from jax import lax
from jax.experimental import pallas as pl
from jax.experimental.pallas import tpu as pltpu
from jax.sharding import Mesh
from jax.sharding import PartitionSpec as P

FACE_SIGNS = ((1, 0), (-1, 0), (1, 1), (-1, 1), (1, 2), (-1, 2))
F32 = jnp.float32
BF16 = jnp.bfloat16
LANES = 128
STEPS = 32000.0
VMEM = pl.BlockSpec(memory_space=pltpu.VMEM)
HBM = pl.BlockSpec(memory_space=pltpu.HBM)
SMEM = pl.BlockSpec(memory_space=pltpu.SMEM)


def cube_side(device_count):
    return max((edge_len for edge_len in range(1, 65) if edge_len**3 <= device_count))


def face_offsets(device_count):
    side_len = cube_side(device_count)
    return [face_sign * side_len**axis_pos for face_sign, axis_pos in FACE_SIGNS]


def shifted(value, axis, steps):
    count = lax.axis_size(axis)
    first, last = (max(0, -steps), min(count, count - steps))
    return lax.ppermute(value, axis, [(source, source + steps) for source in range(first, last)])


def halves(value):
    high = value.astype(BF16)
    return high, (value - high.astype(F32)).astype(BF16)


def dot_nn(left, right):
    return lax.dot_general(left, right, (((1,), (0,)), ((), ())), preferred_element_type=F32)


def dot_nt(left, right):
    return lax.dot_general(left, right, (((1,), (1,)), ((), ())), preferred_element_type=F32)


def split_dot(dot, rows, right_high, right_low):
    count = rows.shape[0]
    high, low = halves(rows)
    both = jnp.concatenate([high, low], axis=0)
    out = dot(both, right_high) + dot(both, right_low)
    return out[:count] + out[count:]


def spread_bases(block, group):
    rank, lanes = block.shape
    width = lanes // group
    zero = jnp.zeros((rank, width), block.dtype)
    rows = []
    for slot in range(group):
        pieces = [zero] * group
        pieces[slot] = block[:, slot * width : (slot + 1) * width]
        rows.append(jnp.concatenate(pieces, axis=1))
    return jnp.concatenate(rows, axis=0)


def fetch(pairs, sems):
    copies = []
    for index, (source, target) in enumerate(pairs):
        copy = pltpu.make_async_copy(source, target, sems.at[index])
        copy.start()
        copies.append(copy)
    return copies


def up_kernel(
    dens_hbm, bases_hbm, maps_hbm, send_hbm, source_hbm,
    dens_ref, bases_ref, send_ref, source_ref, high_ref, low_ref, root_ref,
    maps_ref, spread_ref, chain_ref, sems,
):
    copies = fetch(
        [
            (maps_hbm, maps_ref),
            (bases_hbm, bases_ref),
            (dens_hbm, dens_ref),
            (send_hbm, send_ref),
            (source_hbm, source_ref),
        ],
        sems,
    )
    columns, points = dens_ref.shape
    rank, _, node_count = maps_ref.shape
    group = LANES // rank
    leaf_count = node_count // 2
    width = points // leaf_count
    copies[0].wait()
    node = lax.broadcasted_iota(jnp.int32, (node_count, LANES), 0)
    block = lax.broadcasted_iota(jnp.int32, (node_count, LANES), 1) // rank
    parent = node // 2 % group
    for first in range(0, rank, group):
        slab = maps_ref[first : first + group].reshape(group * rank, node_count).T
        turned = [slab] + [pltpu.roll(slab, turn * rank, 1) for turn in range(1, group)]
        for row in range(group):
            placed = jnp.zeros_like(slab)
            for place in range(group):
                here = (parent == place) & (block == place)
                placed = jnp.where(here, turned[(place - row) % group], placed)
            spread_ref[pl.ds(first + row, node_count, stride=rank), :] = placed
    tile = 2 * group * rank

    def children(parents, index):
        high, low = halves(spread_ref[index * tile : (index + 1) * tile, :])
        return split_dot(dot_nt, parents, high, low)

    row = lax.broadcasted_iota(jnp.int32, (rank, LANES), 0)
    lane = lax.broadcasted_iota(jnp.int32, (rank, LANES), 1)
    level = 1
    parents = jnp.where(lane == row + rank, 1.0, 0.0)
    while level < group:
        below = children(parents, 0)
        level *= 2
        parents = below[:, (level // group) * LANES : (level // group + 1) * LANES]
    chain_ref[:, LANES : 2 * LANES] = parents
    while level < leaf_count:
        for index in range(level // group, 2 * level // group):
            lanes = slice(index * LANES, (index + 1) * LANES)
            chain_ref[:, index * tile : (index + 1) * tile] = children(chain_ref[:, lanes], index)
        level *= 2
    for copy in copies[1:]:
        copy.wait()
    step = group * width
    root = jnp.zeros((columns, rank), F32)
    for index in range(leaf_count // group):
        spots = slice(index * step, (index + 1) * step)
        start = (leaf_count // group + index) * LANES
        high, low = halves(bases_ref[:, spots])
        basis = split_dot(
            dot_nn, chain_ref[:, start : start + LANES],
            spread_bases(high, group), spread_bases(low, group),
        )
        high, low = halves(basis)
        high_ref[:, spots] = high
        low_ref[:, spots] = low
        dens = dens_ref[:, spots]
        root += dot_nt(dens, high) + dot_nt(dens, low)
    root = jnp.concatenate([root, jnp.zeros((columns, LANES - rank), F32)], axis=1)
    high = root.astype(BF16).astype(F32)
    rest = root - high
    middle = rest.astype(BF16).astype(F32)
    last = (rest - middle).astype(BF16).astype(F32)
    packed = high + pltpu.roll(middle, rank, 1) + pltpu.roll(last, 2 * rank, 1)
    root_ref[...] = packed.astype(BF16)


def select_kernel(
    faces, far_groups, send_vmem, dens_ref, root_ref, *refs,
):
    other_refs = refs[: far_groups - 1]
    out_refs = refs[far_groups - 1 : -2]
    send_ref, sems = refs[-2:]
    copies = fetch([(send_vmem, send_ref)], sems)
    device = lax.axis_index("leaf")
    columns = dens_ref.shape[0]
    cap = send_ref.shape[1]
    copies[0].wait()
    for (directions, stride), out_ref in zip(faces, out_refs):
        direction = directions[0]
        if len(directions) > 1:
            direction = direction + device // stride % 2
        for place in range(cap):
            leaf = jnp.maximum(send_ref[direction, place, device], 0)
            for part, panel_ref in enumerate((dens_ref, *other_refs)):
                row = (place * far_groups + part) * columns
                out_ref[row : row + columns, :] = panel_ref[
                    :, pl.ds(pl.multiple_of(leaf * LANES, LANES), LANES)
                ]
        for row in range(cap * far_groups * columns, out_ref.shape[0], columns):
            out_ref[row : row + columns, :] = root_ref[...]


def near_kernel(
    faces, far_groups, share, *refs,
):
    source_vmems, refs = refs[:share], refs[share:]
    dens_ref, refs = refs[0], refs[1:]
    other_refs, refs = refs[: far_groups - 1], refs[far_groups - 1 :]
    got_refs, refs = refs[: len(faces)], refs[len(faces) :]
    block_hbm, refs = refs[0], refs[1:]
    mate_refs, refs = refs[: share - 1], refs[share - 1 :]
    refs = refs[1:]
    out_refs, refs = refs[:far_groups], refs[far_groups:]
    source_refs, refs = refs[:share], refs[share:]
    sum_refs, refs = refs[: far_groups - 1], refs[far_groups - 1 :]
    peak_refs, refs = refs[: far_groups - 1], refs[far_groups - 1 :]
    block_ref, buffer_ref, small_sems, sems = refs
    columns, points = dens_ref.shape
    leaf_count, near_count, width, _ = block_ref.shape
    chunk_count = sems.shape[0]
    chunk = leaf_count // chunk_count
    copies = fetch(list(zip(source_vmems, source_refs)), small_sems)
    block_copies = fetch(
        [
            (block_hbm.at[pl.ds(index * chunk, chunk)], block_ref.at[pl.ds(index * chunk, chunk)])
            for index in range(chunk_count)
        ],
        sems,
    )
    cap = (buffer_ref.shape[0] - leaf_count) // len(FACE_SIGNS)
    for (directions, _), got_ref in zip(faces, got_refs):
        for direction in directions:
            for place in range(cap):
                row = place * far_groups * columns
                buffer_ref[leaf_count + direction * cap + place] = got_ref[
                    row : row + far_groups * columns, :
                ]
    for part, panel_ref in enumerate((dens_ref, *other_refs)):
        rows = slice(part * columns, (part + 1) * columns)
        for leaf in range(leaf_count):
            buffer_ref[leaf, rows, :] = panel_ref[:, leaf * width : (leaf + 1) * width]
    for copy in copies:
        copy.wait()
    tables = list(zip(source_refs[1:], mate_refs)) + [(source_refs[0], block_ref)]
    own_ref, sent_refs = out_refs[0], out_refs[1:]
    targets = (own_ref, *sum_refs)
    for turn, (source_ref, blocks_ref) in enumerate(tables):
        for leaf in range(leaf_count):
            if blocks_ref is block_ref and leaf % chunk == 0:
                block_copies[leaf // chunk].wait()
            panels = [buffer_ref[source_ref[block, leaf]] for block in range(near_count)]
            blocks = [blocks_ref[leaf, block] for block in range(near_count)]
            total = dot_nt(jnp.concatenate(panels, axis=1), jnp.concatenate(blocks, axis=1))
            lanes = slice(leaf * width, (leaf + 1) * width)
            for part, target_ref in enumerate(targets):
                term = total[part * columns : (part + 1) * columns]
                if turn:
                    term = target_ref[:, lanes] + term
                target_ref[:, lanes] = term
                if part and turn == share - 1:
                    peak_refs[part - 1][leaf : leaf + 1, :] = jnp.max(
                        jnp.abs(term), axis=0, keepdims=True
                    )
    for sum_ref, peak_ref, sent_ref in zip(sum_refs, peak_refs, sent_refs):
        power = jnp.floor(jnp.log2(jnp.maximum(peak_ref[...], 2.0**-100))) + 1.0
        factor = STEPS * jnp.exp2(-power)
        for leaf in range(leaf_count):
            lanes = slice(leaf * width, (leaf + 1) * width)
            steps = sum_ref[:, lanes] * factor[leaf : leaf + 1, :]
            sent_ref[:, lanes] = jnp.floor(steps + 0.5).astype(jnp.int32).astype(jnp.int16)
        power = power.astype(jnp.int32).astype(jnp.int16)
        for first in range(0, leaf_count, columns):
            spot = points + first // columns * width
            sent_ref[:, spot : spot + width] = power[first : first + columns]


def coupled(leaves, far_ref, coupling_ref, turned_ref):
    far_count, rank = coupling_ref.shape[1:3]
    columns = turned_ref.shape[1] // 2
    group = LANES // rank
    parts = []
    for leaf in leaves:
        maps = jnp.concatenate([coupling_ref[leaf, j] for j in range(far_count)], axis=1)
        maps = jnp.concatenate(halves(maps), axis=0)
        picked = jnp.concatenate(
            [
                turned_ref[pl.ds(pl.multiple_of(far_ref[j, leaf] * rank, rank), rank), :]
                for j in range(far_count)
            ],
            axis=0,
        )
        out = dot_nn(maps, picked)
        parts.append(out[:rank] + out[rank:])
        if len(parts) == group:
            turned = jnp.concatenate(parts, axis=0).T
            yield turned[:columns] + turned[columns:]
            parts = []


def couple_kernel(
    far_hbm, coupling_hbm, dens_ref, bases_ref,
    table_ref, coupling_ref, turned_ref, out_ref, far_ref, sems, chunk_sems,
):
    copies = fetch([(far_hbm, far_ref), (far_hbm, table_ref)], sems)
    chunk_count = chunk_sems.shape[0]
    chunk = coupling_ref.shape[0] // chunk_count
    chunks = [pl.ds(index * chunk, chunk) for index in range(chunk_count)]
    block_copies = fetch([(coupling_hbm.at[c], coupling_ref.at[c]) for c in chunks], chunk_sems)
    columns, points = dens_ref.shape
    leaf_count, _, rank = coupling_ref.shape[:3]
    width = points // leaf_count
    upper = lax.broadcasted_iota(jnp.int32, (rank, 2 * columns), 1) < columns
    for leaf in range(leaf_count):
        spots = slice(leaf * width, (leaf + 1) * width)
        rows = jnp.concatenate(halves(bases_ref[:, spots]), axis=0)
        dens = dens_ref[:, spots]
        twice = dot_nt(rows, jnp.concatenate([dens, dens], axis=0))
        high, low = halves(twice[:rank] + twice[rank:])
        turned_ref[leaf * rank : (leaf + 1) * rank, :] = jnp.where(
            upper, high.astype(F32), low.astype(F32)
        ).astype(BF16)
    for copy in copies:
        copy.wait()
    done = out_ref.shape[1] // rank
    for index in range(chunk_count):
        block_copies[index].wait()
        leaves = range(index * chunk, min((index + 1) * chunk, done))
        for turn, field in enumerate(coupled(leaves, far_ref, coupling_ref, turned_ref)):
            spot = index * chunk * rank + turn * LANES
            out_ref[:, spot : spot + LANES] = field


def project_kernel(
    table_ref, coupling_ref, turned_ref, first_ref, bases_ref, near_ref, out_ref, far_ref, sems,
):
    copies = fetch([(table_ref, far_ref)], sems)
    rank, points = bases_ref.shape
    leaf_count = coupling_ref.shape[0]
    group = LANES // rank
    step = group * points // leaf_count

    def project(index, field):
        spots = slice(index * step, (index + 1) * step)
        high, low = halves(bases_ref[:, spots])
        out_ref[:, spots] = near_ref[:, spots] + split_dot(
            dot_nn, field, spread_bases(high, group), spread_bases(low, group)
        )

    done = first_ref.shape[1] // LANES
    for index in range(done):
        project(index, first_ref[:, index * LANES : (index + 1) * LANES])
    copies[0].wait()
    leaves = range(done * group, leaf_count)
    for index, field in enumerate(coupled(leaves, far_ref, coupling_ref, turned_ref)):
        project(done + index, field)


def far_kernel(
    roots, leaf_count, upper_ref, cross_ref, high_ref, low_ref, term_ref, *refs,
):
    root_refs, refs = refs[: len(roots)], refs[len(roots) :]
    sent_refs, (out_hbm, sum_ref, tile_ref, tree_ref, sems) = refs[:-5], refs[-5:]
    device = lax.axis_index("leaf")
    columns, points = sum_ref.shape
    width = points // leaf_count
    factors = []
    for sent_ref in sent_refs:
        powers = [
            sent_ref[:, points + first // columns * width :][:, :width]
            for first in range(0, leaf_count, columns)
        ]
        power = jnp.concatenate([p.astype(jnp.int32).astype(F32) for p in powers], axis=0)
        factors.append(jnp.exp2(power) * (1.0 / STEPS))
    rank = upper_ref.shape[1]
    device_count = upper_ref.shape[0] // 2
    for tiles, root_ref in zip(roots, root_refs):
        if tiles is None:
            for index in range(device_count):
                tile_ref[index] = root_ref[index]
        else:
            for turn, row in tiles:
                tile_ref[device ^ turn] = root_ref[row : row + columns, :]
    zero = jnp.zeros((LANES - 3 * rank, rank), BF16)

    def lifted(child):
        if child >= device_count:
            high, low = (
                jnp.concatenate([half] * 3 + [zero], axis=0) for half in halves(upper_ref[child])
            )
            tile = tile_ref[child - device_count]
            return dot_nn(tile, high) + dot_nn(tile, low)
        return split_dot(dot_nn, tree_ref[child], *halves(upper_ref[child]))

    level = device_count // 2
    while level >= 4:
        for node in range(level, 2 * level):
            tree_ref[node] = lifted(2 * node) + lifted(2 * node + 1)
        level //= 2
    lane = lax.broadcasted_iota(jnp.int32, (LANES, rank), 0)
    column = lax.broadcasted_iota(jnp.int32, (LANES, rank), 1)
    gather = jnp.where((lane % rank == column) & (lane < 3 * rank), 1.0, 0.0).astype(BF16)
    field = None
    level = 4
    while level <= device_count:
        place = device // (device_count // level)
        node = level + place
        third = jnp.where(place % 2 == 0, place + 3, place - 3)
        total = None
        for slot, other in enumerate((place - 2, place + 2, third)):
            inside = (other >= 0) & (other < level)
            other = jnp.clip(other, 0, level - 1)
            if level == device_count:
                value = dot_nn(tile_ref[other], gather)
            else:
                value = tree_ref[level + other]
            value = jnp.where(inside, value, 0.0)
            term = split_dot(dot_nt, value, *halves(cross_ref[node, slot]))
            total = term if total is None else total + term
        if field is not None:
            total = total + split_dot(dot_nt, field, *halves(upper_ref[node]))
        field = total
        level *= 2
    chunk_count = sems.shape[0]
    step = points // chunk_count
    copies = []
    for index in range(chunk_count):
        spots = slice(index * step, (index + 1) * step)
        total = term_ref[:, spots] + split_dot(
            dot_nn, field, high_ref[:, spots], low_ref[:, spots]
        )
        for sent_ref, factor in zip(sent_refs, factors):
            steps = sent_ref[:, spots].astype(jnp.int32).astype(F32)
            leaves = range(index * leaf_count // chunk_count, (index + 1) * leaf_count // chunk_count)
            scale = jnp.concatenate([factor[leaf : leaf + 1] for leaf in leaves], axis=1)
            total = total + steps * scale
        sum_ref[:, spots] = total
        copies += fetch(
            [(sum_ref.at[:, pl.ds(index * step, step)], out_hbm.at[:, pl.ds(index * step, step)])],
            sems.at[pl.ds(index, 1)],
        )
    for copy in copies:
        copy.wait()


def hbm(value):
    return pltpu.with_memory_space_constraint(value, pltpu.HBM)


def hint(micros):
    return pl.CostEstimate(flops=0, bytes_accessed=int(micros * 3.69e6), transcendentals=0)


def local(
    densities,
    bases,
    near_blocks,
    near_src,
    send_leaf,
    far_src,
    leaf_coupling,
    local_transfer,
    upper_transfer,
    up_coupling,
):
    leaf_devices = lax.axis_size("leaf")
    far_groups = lax.axis_size("far")
    share = lax.axis_size("mate")
    side = cube_side(leaf_devices)
    offsets = face_offsets(leaf_devices)
    columns, points = densities.shape
    leaf_count, near_count, width, _ = near_blocks.shape
    rank = bases.shape[0]
    cap = send_leaf.shape[2]
    node_count = local_transfer.shape[1]
    params = pltpu.CompilerParams(vmem_limit_bytes=16 * 2**20)
    dma = pltpu.SemaphoreType.DMA

    def rotated(value, axis, shift):
        count = lax.axis_size(axis)
        return lax.ppermute(value, axis, [(i, (i - shift) % count) for i in range(count)])

    def crossed(value, turn):
        return lax.ppermute(value, "leaf", [(i, i ^ turn) for i in range(leaf_devices)])

    sources = near_src.T
    others = [rotated(densities, "far", part) for part in range(1, far_groups)]
    all_sources = [sources] + [rotated(sources, "mate", part) for part in range(1, share)]
    send = send_leaf.transpose(1, 2, 0)
    dens, basis, send, sources, high, low, root = pl.pallas_call(
        up_kernel,
        out_shape=[
            jax.ShapeDtypeStruct(densities.shape, BF16),
            jax.ShapeDtypeStruct(bases.shape, F32),
            jax.ShapeDtypeStruct(send.shape, jnp.int32),
            jax.ShapeDtypeStruct(sources.shape, jnp.int32),
            jax.ShapeDtypeStruct((rank, points), BF16),
            jax.ShapeDtypeStruct((rank, points), BF16),
            jax.ShapeDtypeStruct((columns, LANES), BF16),
        ],
        in_specs=[HBM] * 5,
        out_specs=[VMEM] * 7,
        scratch_shapes=[
            pltpu.VMEM((rank, rank, node_count), F32),
            pltpu.VMEM((node_count * rank, LANES), F32),
            pltpu.VMEM((rank, node_count * rank), F32),
            dma((5,)),
        ],
        compiler_params=params,
        cost_estimate=hint(3.5),
        name="up",
    )(
        hbm(densities), hbm(bases), hbm(local_transfer[0].transpose(1, 2, 0)), hbm(send),
        hbm(sources),
    )
    all_sources[0] = sources

    beside = crossed(root, 1) if side == 2 else None
    later_blocks, others, all_sources, root = lax.optimization_barrier(
        (near_blocks, others, all_sources, root)
    )
    mate_blocks = [rotated(later_blocks, "mate", part) for part in range(1, share)]

    if side == 2:
        faces = [((2 * axis, 2 * axis + 1), 2**axis) for axis in range(3)]
    else:
        faces = [((direction,), offset) for direction, offset in enumerate(offsets)]
    chunks = [(cap * far_groups + (1 if place else 3)) * columns for place in range(len(faces))]
    outgoing = pl.pallas_call(
        functools.partial(select_kernel, faces, far_groups),
        out_shape=[jax.ShapeDtypeStruct((chunk, LANES), BF16) for chunk in chunks],
        in_specs=[VMEM] * (2 + far_groups),
        out_specs=[VMEM] * len(faces),
        scratch_shapes=[
            pltpu.SMEM(send.shape, jnp.int32),
            dma((1,)),
        ],
        compiler_params=params,
        cost_estimate=hint(1),
        name="select",
    )(send, dens, root, *others)
    outgoing, dens = lax.optimization_barrier((outgoing, dens))
    far_table = far_src.T
    first_leaves = leaf_count // 2
    *coupling, leaf_local = pl.pallas_call(
        couple_kernel,
        out_shape=[
            jax.ShapeDtypeStruct(far_table.shape, jnp.int32),
            jax.ShapeDtypeStruct(leaf_coupling.shape, F32),
            jax.ShapeDtypeStruct((leaf_count * rank, 2 * columns), BF16),
            jax.ShapeDtypeStruct((columns, first_leaves * rank), F32),
        ],
        in_specs=[HBM] * 2 + [VMEM] * 2,
        out_specs=[VMEM] * 4,
        scratch_shapes=[pltpu.SMEM(far_table.shape, jnp.int32), dma((2,)), dma((4,))],
        compiler_params=params,
        cost_estimate=hint(2),
        name="couple",
    )(hbm(far_table), hbm(leaf_coupling), dens, basis)
    tail = cap * far_groups * columns
    if side == 2:
        payloads = [outgoing[0]] + [
            jnp.concatenate([value, beside], axis=0) for value in outgoing[1:]
        ]
        arrived = [crossed(value, stride) for (_, stride), value in zip(faces, payloads)]
        first, second, third = (stride for _, stride in faces)
        far_pair = crossed(arrived[2][tail:], second)
        roots = [([(0, 0)], root), ([(first, 0)], beside)]
        for stride, value, row in (
            (second, arrived[1], tail),
            (third, arrived[2], tail),
            (second ^ third, far_pair, 0),
        ):
            roots.append(([(stride, row), (stride ^ first, row + columns)], value))
    else:
        arrived = [shifted(value, "leaf", stride) for (_, stride), value in zip(faces, outgoing)]
        roots = [(None, lax.all_gather(root, "leaf", axis=0))]

    slots = leaf_count + len(offsets) * cap
    tables = -(-leaf_count // columns) * width
    partials = pl.pallas_call(
        functools.partial(near_kernel, faces, far_groups, share),
        out_shape=[jax.ShapeDtypeStruct((columns, points), F32)]
        + [jax.ShapeDtypeStruct((columns, points + tables), jnp.int16)] * (far_groups - 1),
        in_specs=[VMEM] * (share + far_groups + len(faces))
        + [HBM]
        + [VMEM] * share,
        out_specs=[VMEM] * far_groups,
        scratch_shapes=[pltpu.SMEM(sources.shape, jnp.int32)] * share
        + [pltpu.VMEM((columns, points), F32)] * (far_groups - 1)
        + [pltpu.VMEM((leaf_count, width), F32)] * (far_groups - 1)
        + [
            pltpu.VMEM(near_blocks.shape, BF16),
            pltpu.VMEM((slots, far_groups * columns, width), BF16),
            dma((share,)),
            dma((4,)),
        ],
        compiler_params=params,
        cost_estimate=hint(3),
        name="near",
    )(
        *all_sources, dens, *others, *arrived, hbm(near_blocks), *mate_blocks, leaf_local,
    )
    received = [rotated(partials[part], "far", -part) for part in range(1, far_groups)]
    partial = pl.pallas_call(
        project_kernel,
        out_shape=jax.ShapeDtypeStruct((columns, points), F32),
        in_specs=[VMEM] * 6,
        out_specs=VMEM,
        scratch_shapes=[pltpu.SMEM(far_table.shape, jnp.int32), dma((1,))],
        compiler_params=params,
        cost_estimate=hint(1.5),
        name="project",
    )(*coupling, leaf_local, basis, partials[0])
    return pl.pallas_call(
        functools.partial(far_kernel, [tiles for tiles, _ in roots], leaf_count),
        out_shape=jax.ShapeDtypeStruct((columns, points), F32),
        in_specs=[VMEM] * (5 + len(roots) + len(received)),
        out_specs=HBM,
        scratch_shapes=[
            pltpu.VMEM((columns, points), F32),
            pltpu.VMEM((leaf_devices, columns, LANES), BF16),
            pltpu.VMEM((2 * leaf_devices, columns, rank), F32),
            dma((8,)),
        ],
        compiler_params=params,
        cost_estimate=hint(1.5),
        name="far",
    )(upper_transfer, up_coupling, high, low, partial, *[value for _, value in roots], *received)


def solution(mesh):
    leaf_devices, rhs_devices = mesh.shape["leaf"], mesh.shape["rhs"]
    share = 2 if rhs_devices % 2 == 0 else 1
    split = Mesh(
        mesh.devices.reshape(leaf_devices, rhs_devices // share, share), ("leaf", "far", "mate")
    )
    rhs = ("far", "mate")
    in_specs = (
        P(rhs, "leaf"),
        P(None, "leaf"),
        P("leaf", rhs, None, None),
        P("leaf", rhs),
        P(),
        P("leaf", None),
        P("leaf", None, None, None),
        P("leaf", None, None, None),
        P(),
        P(),
    )
    return jax.shard_map(
        local, mesh=split, in_specs=in_specs, out_specs=P(rhs, "leaf"), check_vma=False
    )
```

```python
import functools

import jax
import jax.numpy as jnp
from jax import lax
from jax.experimental import pallas as pl
from jax.experimental.pallas import tpu as pltpu
from jax.sharding import Mesh
from jax.sharding import PartitionSpec as P

FACE_SIGNS = ((1, 0), (-1, 0), (1, 1), (-1, 1), (1, 2), (-1, 2))
F32 = jnp.float32
BF16 = jnp.bfloat16
LANES = 128
STEPS = 32000.0
VMEM = pl.BlockSpec(memory_space=pltpu.VMEM)
HBM = pl.BlockSpec(memory_space=pltpu.HBM)
SMEM = pl.BlockSpec(memory_space=pltpu.SMEM)


def cube_side(device_count):
    return max((edge_len for edge_len in range(1, 65) if edge_len**3 <= device_count))


def face_offsets(device_count):
    side_len = cube_side(device_count)
    return [face_sign * side_len**axis_pos for face_sign, axis_pos in FACE_SIGNS]


def shifted(value, axis, steps):
    count = lax.axis_size(axis)
    first, last = (max(0, -steps), min(count, count - steps))
    return lax.ppermute(value, axis, [(source, source + steps) for source in range(first, last)])


def halves(value):
    high = value.astype(BF16)
    return high, (value - high.astype(F32)).astype(BF16)


def dot_nn(left, right):
    return lax.dot_general(left, right, (((1,), (0,)), ((), ())), preferred_element_type=F32)


def dot_nt(left, right):
    return lax.dot_general(left, right, (((1,), (1,)), ((), ())), preferred_element_type=F32)


def split_dot(dot, rows, right_high, right_low):
    count = rows.shape[0]
    high, low = halves(rows)
    both = jnp.concatenate([high, low], axis=0)
    out = dot(both, right_high) + dot(both, right_low)
    return out[:count] + out[count:]


def spread_bases(block, group):
    rank, lanes = block.shape
    width = lanes // group
    zero = jnp.zeros((rank, width), block.dtype)
    rows = []
    for slot in range(group):
        pieces = [zero] * group
        pieces[slot] = block[:, slot * width : (slot + 1) * width]
        rows.append(jnp.concatenate(pieces, axis=1))
    return jnp.concatenate(rows, axis=0)


def fetch(pairs, sems):
    copies = []
    for index, (source, target) in enumerate(pairs):
        copy = pltpu.make_async_copy(source, target, sems.at[index])
        copy.start()
        copies.append(copy)
    return copies


def up_kernel(
    dens_hbm, bases_hbm, maps_hbm, send_hbm, source_hbm,
    dens_ref, bases_ref, send_ref, source_ref, high_ref, low_ref, root_ref,
    maps_ref, spread_ref, chain_ref, sems,
):
    copies = fetch(
        [
            (maps_hbm, maps_ref),
            (bases_hbm, bases_ref),
            (dens_hbm, dens_ref),
            (send_hbm, send_ref),
            (source_hbm, source_ref),
        ],
        sems,
    )
    columns, points = dens_ref.shape
    rank, _, node_count = maps_ref.shape
    group = LANES // rank
    leaf_count = node_count // 2
    width = points // leaf_count
    copies[0].wait()
    node = lax.broadcasted_iota(jnp.int32, (node_count, LANES), 0)
    block = lax.broadcasted_iota(jnp.int32, (node_count, LANES), 1) // rank
    parent = node // 2 % group
    for first in range(0, rank, group):
        slab = maps_ref[first : first + group].reshape(group * rank, node_count).T
        turned = [slab] + [pltpu.roll(slab, turn * rank, 1) for turn in range(1, group)]
        for row in range(group):
            placed = jnp.zeros_like(slab)
            for place in range(group):
                here = (parent == place) & (block == place)
                placed = jnp.where(here, turned[(place - row) % group], placed)
            spread_ref[pl.ds(first + row, node_count, stride=rank), :] = placed
    tile = 2 * group * rank

    def children(parents, index):
        high, low = halves(spread_ref[index * tile : (index + 1) * tile, :])
        return split_dot(dot_nt, parents, high, low)

    row = lax.broadcasted_iota(jnp.int32, (rank, LANES), 0)
    lane = lax.broadcasted_iota(jnp.int32, (rank, LANES), 1)
    level = 1
    parents = jnp.where(lane == row + rank, 1.0, 0.0)
    while level < group:
        below = children(parents, 0)
        level *= 2
        parents = below[:, (level // group) * LANES : (level // group + 1) * LANES]
    chain_ref[:, LANES : 2 * LANES] = parents
    while level < leaf_count:
        for index in range(level // group, 2 * level // group):
            lanes = slice(index * LANES, (index + 1) * LANES)
            chain_ref[:, index * tile : (index + 1) * tile] = children(chain_ref[:, lanes], index)
        level *= 2
    for copy in copies[1:]:
        copy.wait()
    step = group * width
    root = jnp.zeros((columns, rank), F32)
    for index in range(leaf_count // group):
        spots = slice(index * step, (index + 1) * step)
        start = (leaf_count // group + index) * LANES
        high, low = halves(bases_ref[:, spots])
        basis = split_dot(
            dot_nn, chain_ref[:, start : start + LANES],
            spread_bases(high, group), spread_bases(low, group),
        )
        high, low = halves(basis)
        high_ref[:, spots] = high
        low_ref[:, spots] = low
        dens = dens_ref[:, spots]
        root += dot_nt(dens, high) + dot_nt(dens, low)
    root = jnp.concatenate([root, jnp.zeros((columns, LANES - rank), F32)], axis=1)
    high = root.astype(BF16).astype(F32)
    rest = root - high
    middle = rest.astype(BF16).astype(F32)
    last = (rest - middle).astype(BF16).astype(F32)
    packed = high + pltpu.roll(middle, rank, 1) + pltpu.roll(last, 2 * rank, 1)
    root_ref[...] = packed.astype(BF16)


def select_kernel(
    faces, far_groups, send_vmem, dens_ref, root_ref, *refs,
):
    other_refs = refs[: far_groups - 1]
    out_refs = refs[far_groups - 1 : -2]
    send_ref, sems = refs[-2:]
    copies = fetch([(send_vmem, send_ref)], sems)
    device = lax.axis_index("leaf")
    columns = dens_ref.shape[0]
    cap = send_ref.shape[1]
    copies[0].wait()
    for (directions, stride), out_ref in zip(faces, out_refs):
        direction = directions[0]
        if len(directions) > 1:
            direction = direction + device // stride % 2
        for place in range(cap):
            leaf = jnp.maximum(send_ref[direction, place, device], 0)
            for part, panel_ref in enumerate((dens_ref, *other_refs)):
                row = (place * far_groups + part) * columns
                out_ref[row : row + columns, :] = panel_ref[
                    :, pl.ds(pl.multiple_of(leaf * LANES, LANES), LANES)
                ]
        for row in range(cap * far_groups * columns, out_ref.shape[0], columns):
            out_ref[row : row + columns, :] = root_ref[...]


def near_kernel(
    faces, far_groups, share, *refs,
):
    source_vmems, refs = refs[:share], refs[share:]
    dens_ref, refs = refs[0], refs[1:]
    other_refs, refs = refs[: far_groups - 1], refs[far_groups - 1 :]
    got_refs, refs = refs[: len(faces)], refs[len(faces) :]
    block_hbm, refs = refs[0], refs[1:]
    mate_refs, refs = refs[: share - 1], refs[share - 1 :]
    refs = refs[1:]
    out_refs, refs = refs[:far_groups], refs[far_groups:]
    source_refs, refs = refs[:share], refs[share:]
    sum_refs, refs = refs[: far_groups - 1], refs[far_groups - 1 :]
    peak_refs, refs = refs[: far_groups - 1], refs[far_groups - 1 :]
    block_ref, buffer_ref, small_sems, sems = refs
    columns, points = dens_ref.shape
    leaf_count, near_count, width, _ = block_ref.shape
    chunk_count = sems.shape[0]
    chunk = leaf_count // chunk_count
    copies = fetch(list(zip(source_vmems, source_refs)), small_sems)
    block_copies = fetch(
        [
            (block_hbm.at[pl.ds(index * chunk, chunk)], block_ref.at[pl.ds(index * chunk, chunk)])
            for index in range(chunk_count)
        ],
        sems,
    )
    cap = (buffer_ref.shape[0] - leaf_count) // len(FACE_SIGNS)
    for (directions, _), got_ref in zip(faces, got_refs):
        for direction in directions:
            for place in range(cap):
                row = place * far_groups * columns
                buffer_ref[leaf_count + direction * cap + place] = got_ref[
                    row : row + far_groups * columns, :
                ]
    for part, panel_ref in enumerate((dens_ref, *other_refs)):
        rows = slice(part * columns, (part + 1) * columns)
        for leaf in range(leaf_count):
            buffer_ref[leaf, rows, :] = panel_ref[:, leaf * width : (leaf + 1) * width]
    for copy in copies:
        copy.wait()
    tables = list(zip(source_refs[1:], mate_refs)) + [(source_refs[0], block_ref)]
    own_ref, sent_refs = out_refs[0], out_refs[1:]
    targets = (own_ref, *sum_refs)
    for turn, (source_ref, blocks_ref) in enumerate(tables):
        for leaf in range(leaf_count):
            if blocks_ref is block_ref and leaf % chunk == 0:
                block_copies[leaf // chunk].wait()
            panels = [buffer_ref[source_ref[block, leaf]] for block in range(near_count)]
            blocks = [blocks_ref[leaf, block] for block in range(near_count)]
            total = dot_nt(jnp.concatenate(panels, axis=1), jnp.concatenate(blocks, axis=1))
            lanes = slice(leaf * width, (leaf + 1) * width)
            for part, target_ref in enumerate(targets):
                term = total[part * columns : (part + 1) * columns]
                if turn:
                    term = target_ref[:, lanes] + term
                target_ref[:, lanes] = term
                if part and turn == share - 1:
                    peak_refs[part - 1][leaf : leaf + 1, :] = jnp.max(
                        jnp.abs(term), axis=0, keepdims=True
                    )
    for sum_ref, peak_ref, sent_ref in zip(sum_refs, peak_refs, sent_refs):
        power = jnp.floor(jnp.log2(jnp.maximum(peak_ref[...], 2.0**-100))) + 1.0
        factor = STEPS * jnp.exp2(-power)
        for leaf in range(leaf_count):
            lanes = slice(leaf * width, (leaf + 1) * width)
            steps = sum_ref[:, lanes] * factor[leaf : leaf + 1, :]
            sent_ref[:, lanes] = jnp.floor(steps + 0.5).astype(jnp.int32).astype(jnp.int16)
        power = power.astype(jnp.int32).astype(jnp.int16)
        for first in range(0, leaf_count, columns):
            spot = points + first // columns * width
            sent_ref[:, spot : spot + width] = power[first : first + columns]


def coupled(leaves, far_ref, coupling_ref, turned_ref):
    far_count, rank = coupling_ref.shape[1:3]
    columns = turned_ref.shape[1] // 2
    group = LANES // rank
    parts = []
    for leaf in leaves:
        maps = jnp.concatenate([coupling_ref[leaf, j] for j in range(far_count)], axis=1)
        maps = jnp.concatenate(halves(maps), axis=0)
        picked = jnp.concatenate(
            [
                turned_ref[pl.ds(pl.multiple_of(far_ref[j, leaf] * rank, rank), rank), :]
                for j in range(far_count)
            ],
            axis=0,
        )
        out = dot_nn(maps, picked)
        parts.append(out[:rank] + out[rank:])
        if len(parts) == group:
            turned = jnp.concatenate(parts, axis=0).T
            yield turned[:columns] + turned[columns:]
            parts = []


def couple_kernel(
    far_hbm, coupling_hbm, dens_ref, bases_ref,
    table_ref, coupling_ref, turned_ref, out_ref, far_ref, sems, chunk_sems,
):
    copies = fetch([(far_hbm, far_ref), (far_hbm, table_ref)], sems)
    chunk_count = chunk_sems.shape[0]
    chunk = coupling_ref.shape[0] // chunk_count
    chunks = [pl.ds(index * chunk, chunk) for index in range(chunk_count)]
    block_copies = fetch([(coupling_hbm.at[c], coupling_ref.at[c]) for c in chunks], chunk_sems)
    columns, points = dens_ref.shape
    leaf_count, _, rank = coupling_ref.shape[:3]
    width = points // leaf_count
    upper = lax.broadcasted_iota(jnp.int32, (rank, 2 * columns), 1) < columns
    for leaf in range(leaf_count):
        spots = slice(leaf * width, (leaf + 1) * width)
        rows = jnp.concatenate(halves(bases_ref[:, spots]), axis=0)
        dens = dens_ref[:, spots]
        twice = dot_nt(rows, jnp.concatenate([dens, dens], axis=0))
        high, low = halves(twice[:rank] + twice[rank:])
        turned_ref[leaf * rank : (leaf + 1) * rank, :] = jnp.where(
            upper, high.astype(F32), low.astype(F32)
        ).astype(BF16)
    for copy in copies:
        copy.wait()
    done = out_ref.shape[1] // rank
    for index in range(chunk_count):
        block_copies[index].wait()
        leaves = range(index * chunk, min((index + 1) * chunk, done))
        for turn, field in enumerate(coupled(leaves, far_ref, coupling_ref, turned_ref)):
            spot = index * chunk * rank + turn * LANES
            out_ref[:, spot : spot + LANES] = field


def project_kernel(
    table_ref, coupling_ref, turned_ref, first_ref, bases_ref, near_ref, out_ref, far_ref, sems,
):
    copies = fetch([(table_ref, far_ref)], sems)
    rank, points = bases_ref.shape
    leaf_count = coupling_ref.shape[0]
    group = LANES // rank
    step = group * points // leaf_count

    def project(index, field):
        spots = slice(index * step, (index + 1) * step)
        high, low = halves(bases_ref[:, spots])
        out_ref[:, spots] = near_ref[:, spots] + split_dot(
            dot_nn, field, spread_bases(high, group), spread_bases(low, group)
        )

    done = first_ref.shape[1] // LANES
    for index in range(done):
        project(index, first_ref[:, index * LANES : (index + 1) * LANES])
    copies[0].wait()
    leaves = range(done * group, leaf_count)
    for index, field in enumerate(coupled(leaves, far_ref, coupling_ref, turned_ref)):
        project(done + index, field)


def far_kernel(
    roots, leaf_count, upper_ref, cross_ref, high_ref, low_ref, term_ref, *refs,
):
    root_refs, refs = refs[: len(roots)], refs[len(roots) :]
    sent_refs, (out_hbm, sum_ref, tile_ref, tree_ref, sems) = refs[:-5], refs[-5:]
    device = lax.axis_index("leaf")
    columns, points = sum_ref.shape
    width = points // leaf_count
    factors = []
    for sent_ref in sent_refs:
        powers = [
            sent_ref[:, points + first // columns * width :][:, :width]
            for first in range(0, leaf_count, columns)
        ]
        power = jnp.concatenate([p.astype(jnp.int32).astype(F32) for p in powers], axis=0)
        factors.append(jnp.exp2(power) * (1.0 / STEPS))
    rank = upper_ref.shape[1]
    device_count = upper_ref.shape[0] // 2
    for tiles, root_ref in zip(roots, root_refs):
        if tiles is None:
            for index in range(device_count):
                tile_ref[index] = root_ref[index]
        else:
            for turn, row in tiles:
                tile_ref[device ^ turn] = root_ref[row : row + columns, :]
    zero = jnp.zeros((LANES - 3 * rank, rank), BF16)

    def lifted(child):
        if child >= device_count:
            high, low = (
                jnp.concatenate([half] * 3 + [zero], axis=0) for half in halves(upper_ref[child])
            )
            tile = tile_ref[child - device_count]
            return dot_nn(tile, high) + dot_nn(tile, low)
        return split_dot(dot_nn, tree_ref[child], *halves(upper_ref[child]))

    level = device_count // 2
    while level >= 4:
        for node in range(level, 2 * level):
            tree_ref[node] = lifted(2 * node) + lifted(2 * node + 1)
        level //= 2
    lane = lax.broadcasted_iota(jnp.int32, (LANES, rank), 0)
    column = lax.broadcasted_iota(jnp.int32, (LANES, rank), 1)
    gather = jnp.where((lane % rank == column) & (lane < 3 * rank), 1.0, 0.0).astype(BF16)
    field = None
    level = 4
    while level <= device_count:
        place = device // (device_count // level)
        node = level + place
        third = jnp.where(place % 2 == 0, place + 3, place - 3)
        total = None
        for slot, other in enumerate((place - 2, place + 2, third)):
            inside = (other >= 0) & (other < level)
            other = jnp.clip(other, 0, level - 1)
            if level == device_count:
                value = dot_nn(tile_ref[other], gather)
            else:
                value = tree_ref[level + other]
            value = jnp.where(inside, value, 0.0)
            term = split_dot(dot_nt, value, *halves(cross_ref[node, slot]))
            total = term if total is None else total + term
        if field is not None:
            total = total + split_dot(dot_nt, field, *halves(upper_ref[node]))
        field = total
        level *= 2
    chunk_count = sems.shape[0]
    step = points // chunk_count
    copies = []
    for index in range(chunk_count):
        spots = slice(index * step, (index + 1) * step)
        total = term_ref[:, spots] + split_dot(
            dot_nn, field, high_ref[:, spots], low_ref[:, spots]
        )
        for sent_ref, factor in zip(sent_refs, factors):
            steps = sent_ref[:, spots].astype(jnp.int32).astype(F32)
            leaves = range(index * leaf_count // chunk_count, (index + 1) * leaf_count // chunk_count)
            scale = jnp.concatenate([factor[leaf : leaf + 1] for leaf in leaves], axis=1)
            total = total + steps * scale
        sum_ref[:, spots] = total
        copies += fetch(
            [(sum_ref.at[:, pl.ds(index * step, step)], out_hbm.at[:, pl.ds(index * step, step)])],
            sems.at[pl.ds(index, 1)],
        )
    for copy in copies:
        copy.wait()


def hbm(value):
    return pltpu.with_memory_space_constraint(value, pltpu.HBM)


def hint(micros):
    return pl.CostEstimate(flops=0, bytes_accessed=int(micros * 3.69e6), transcendentals=0)


def local(
    densities,
    bases,
    near_blocks,
    near_src,
    send_leaf,
    far_src,
    leaf_coupling,
    local_transfer,
    upper_transfer,
    up_coupling,
):
    leaf_devices = lax.axis_size("leaf")
    far_groups = lax.axis_size("far")
    share = lax.axis_size("mate")
    side = cube_side(leaf_devices)
    offsets = face_offsets(leaf_devices)
    columns, points = densities.shape
    leaf_count, near_count, width, _ = near_blocks.shape
    rank = bases.shape[0]
    cap = send_leaf.shape[2]
    node_count = local_transfer.shape[1]
    params = pltpu.CompilerParams(vmem_limit_bytes=16 * 2**20)
    dma = pltpu.SemaphoreType.DMA

    def rotated(value, axis, shift):
        count = lax.axis_size(axis)
        return lax.ppermute(value, axis, [(i, (i - shift) % count) for i in range(count)])

    def crossed(value, turn):
        return lax.ppermute(value, "leaf", [(i, i ^ turn) for i in range(leaf_devices)])

    sources = near_src.T
    others = [rotated(densities, "far", part) for part in range(1, far_groups)]
    all_sources = [sources] + [rotated(sources, "mate", part) for part in range(1, share)]
    send = send_leaf.transpose(1, 2, 0)
    dens, basis, send, sources, high, low, root = pl.pallas_call(
        up_kernel,
        out_shape=[
            jax.ShapeDtypeStruct(densities.shape, BF16),
            jax.ShapeDtypeStruct(bases.shape, F32),
            jax.ShapeDtypeStruct(send.shape, jnp.int32),
            jax.ShapeDtypeStruct(sources.shape, jnp.int32),
            jax.ShapeDtypeStruct((rank, points), BF16),
            jax.ShapeDtypeStruct((rank, points), BF16),
            jax.ShapeDtypeStruct((columns, LANES), BF16),
        ],
        in_specs=[HBM] * 5,
        out_specs=[VMEM] * 7,
        scratch_shapes=[
            pltpu.VMEM((rank, rank, node_count), F32),
            pltpu.VMEM((node_count * rank, LANES), F32),
            pltpu.VMEM((rank, node_count * rank), F32),
            dma((5,)),
        ],
        compiler_params=params,
        cost_estimate=hint(3.5),
        name="up",
    )(
        hbm(densities), hbm(bases), hbm(local_transfer[0].transpose(1, 2, 0)), hbm(send),
        hbm(sources),
    )
    all_sources[0] = sources

    later_blocks, others, all_sources, root = lax.optimization_barrier(
        (near_blocks, others, all_sources, root)
    )
    mate_blocks = [rotated(later_blocks, "mate", part) for part in range(1, share)]

    if side == 2:
        faces = [((2 * axis, 2 * axis + 1), 2**axis) for axis in (2, 0, 1)]
    else:
        faces = [((direction,), offset) for direction, offset in enumerate(offsets)]
    chunks = [(cap * far_groups + (1 if place else 3)) * columns for place in range(len(faces))]
    outgoing = pl.pallas_call(
        functools.partial(select_kernel, faces, far_groups),
        out_shape=[jax.ShapeDtypeStruct((chunk, LANES), BF16) for chunk in chunks],
        in_specs=[VMEM] * (2 + far_groups),
        out_specs=[VMEM] * len(faces),
        scratch_shapes=[
            pltpu.SMEM(send.shape, jnp.int32),
            dma((1,)),
        ],
        compiler_params=params,
        cost_estimate=hint(1),
        name="select",
    )(send, dens, root, *others)
    outgoing, dens = lax.optimization_barrier((outgoing, dens))
    far_table = far_src.T
    first_leaves = leaf_count // 4
    *coupling, leaf_local = pl.pallas_call(
        couple_kernel,
        out_shape=[
            jax.ShapeDtypeStruct(far_table.shape, jnp.int32),
            jax.ShapeDtypeStruct(leaf_coupling.shape, F32),
            jax.ShapeDtypeStruct((leaf_count * rank, 2 * columns), BF16),
            jax.ShapeDtypeStruct((columns, first_leaves * rank), F32),
        ],
        in_specs=[HBM] * 2 + [VMEM] * 2,
        out_specs=[VMEM] * 4,
        scratch_shapes=[pltpu.SMEM(far_table.shape, jnp.int32), dma((2,)), dma((4,))],
        compiler_params=params,
        cost_estimate=hint(2),
        name="couple",
    )(hbm(far_table), hbm(leaf_coupling), dens, basis)
    tail = cap * far_groups * columns
    if side == 2:
        arrived = [crossed(value, stride) for (_, stride), value in zip(faces, outgoing)]
        far_one, near_one, near_two = (value[tail : tail + columns] for value in arrived)
        later_two, leaf_local = lax.optimization_barrier((arrived[2], leaf_local))
        third = crossed(later_two[-4 * columns :], 1)[-columns:]
        rest = crossed(jnp.concatenate([near_one, near_two, third], axis=0), 4)
        roots = [([(0, 0)], root), ([(3, 0)], third)]
        roots += [([(stride, tail)], value) for (_, stride), value in zip(faces, arrived)]
        roots.append(([(turn + 4, (turn - 1) * columns) for turn in (1, 2, 3)], rest))
    else:
        arrived = [shifted(value, "leaf", stride) for (_, stride), value in zip(faces, outgoing)]
        roots = [(None, lax.all_gather(root, "leaf", axis=0))]

    slots = leaf_count + len(offsets) * cap
    tables = -(-leaf_count // columns) * width
    partials = pl.pallas_call(
        functools.partial(near_kernel, faces, far_groups, share),
        out_shape=[jax.ShapeDtypeStruct((columns, points), F32)]
        + [jax.ShapeDtypeStruct((columns, points + tables), jnp.int16)] * (far_groups - 1),
        in_specs=[VMEM] * (share + far_groups + len(faces))
        + [HBM]
        + [VMEM] * share,
        out_specs=[VMEM] * far_groups,
        scratch_shapes=[pltpu.SMEM(sources.shape, jnp.int32)] * share
        + [pltpu.VMEM((columns, points), F32)] * (far_groups - 1)
        + [pltpu.VMEM((leaf_count, width), F32)] * (far_groups - 1)
        + [
            pltpu.VMEM(near_blocks.shape, BF16),
            pltpu.VMEM((slots, far_groups * columns, width), BF16),
            dma((share,)),
            dma((4,)),
        ],
        compiler_params=params,
        cost_estimate=hint(3),
        name="near",
    )(
        *all_sources, dens, *others, *arrived, hbm(near_blocks), *mate_blocks, leaf_local,
    )
    received = [rotated(partials[part], "far", -part) for part in range(1, far_groups)]
    partial = pl.pallas_call(
        project_kernel,
        out_shape=jax.ShapeDtypeStruct((columns, points), F32),
        in_specs=[VMEM] * 6,
        out_specs=VMEM,
        scratch_shapes=[pltpu.SMEM(far_table.shape, jnp.int32), dma((1,))],
        compiler_params=params,
        cost_estimate=hint(1.5),
        name="project",
    )(*coupling, leaf_local, basis, partials[0])
    return pl.pallas_call(
        functools.partial(far_kernel, [tiles for tiles, _ in roots], leaf_count),
        out_shape=jax.ShapeDtypeStruct((columns, points), F32),
        in_specs=[VMEM] * (5 + len(roots) + len(received)),
        out_specs=HBM,
        scratch_shapes=[
            pltpu.VMEM((columns, points), F32),
            pltpu.VMEM((leaf_devices, columns, LANES), BF16),
            pltpu.VMEM((2 * leaf_devices, columns, rank), F32),
            dma((8,)),
        ],
        compiler_params=params,
        cost_estimate=hint(1.5),
        name="far",
    )(upper_transfer, up_coupling, high, low, partial, *[value for _, value in roots], *received)


def solution(mesh):
    leaf_devices, rhs_devices = mesh.shape["leaf"], mesh.shape["rhs"]
    share = 2 if rhs_devices % 2 == 0 else 1
    split = Mesh(
        mesh.devices.reshape(leaf_devices, rhs_devices // share, share), ("leaf", "far", "mate")
    )
    rhs = ("far", "mate")
    in_specs = (
        P(rhs, "leaf"),
        P(None, "leaf"),
        P("leaf", rhs, None, None),
        P("leaf", rhs),
        P(),
        P("leaf", None),
        P("leaf", None, None, None),
        P("leaf", None, None, None),
        P(),
        P(),
    )
    return jax.shard_map(
        local, mesh=split, in_specs=in_specs, out_specs=P(rhs, "leaf"), check_vma=False
    )
```

```python
import functools

import jax
import jax.numpy as jnp
from jax import lax
from jax.experimental import pallas as pl
from jax.experimental.pallas import tpu as pltpu
from jax.sharding import Mesh
from jax.sharding import PartitionSpec as P

FACE_SIGNS = ((1, 0), (-1, 0), (1, 1), (-1, 1), (1, 2), (-1, 2))
F32 = jnp.float32
BF16 = jnp.bfloat16
LANES = 128
STEPS = 32000.0
VMEM = pl.BlockSpec(memory_space=pltpu.VMEM)
HBM = pl.BlockSpec(memory_space=pltpu.HBM)
SMEM = pl.BlockSpec(memory_space=pltpu.SMEM)


def cube_side(device_count):
    return max((edge_len for edge_len in range(1, 65) if edge_len**3 <= device_count))


def face_offsets(device_count):
    side_len = cube_side(device_count)
    return [face_sign * side_len**axis_pos for face_sign, axis_pos in FACE_SIGNS]


def shifted(value, axis, steps):
    count = lax.axis_size(axis)
    first, last = (max(0, -steps), min(count, count - steps))
    return lax.ppermute(value, axis, [(source, source + steps) for source in range(first, last)])


def halves(value):
    high = value.astype(BF16)
    return high, (value - high.astype(F32)).astype(BF16)


def dot_nn(left, right):
    return lax.dot_general(left, right, (((1,), (0,)), ((), ())), preferred_element_type=F32)


def dot_nt(left, right):
    return lax.dot_general(left, right, (((1,), (1,)), ((), ())), preferred_element_type=F32)


def split_dot(dot, rows, right_high, right_low):
    count = rows.shape[0]
    high, low = halves(rows)
    both = jnp.concatenate([high, low], axis=0)
    out = dot(both, right_high) + dot(both, right_low)
    return out[:count] + out[count:]


def spread_bases(block, group):
    rank, lanes = block.shape
    width = lanes // group
    zero = jnp.zeros((rank, width), block.dtype)
    rows = []
    for slot in range(group):
        pieces = [zero] * group
        pieces[slot] = block[:, slot * width : (slot + 1) * width]
        rows.append(jnp.concatenate(pieces, axis=1))
    return jnp.concatenate(rows, axis=0)


def fetch(pairs, sems):
    copies = []
    for index, (source, target) in enumerate(pairs):
        copy = pltpu.make_async_copy(source, target, sems.at[index])
        copy.start()
        copies.append(copy)
    return copies


def up_kernel(
    maps_hbm, bases_hbm, *refs,
):
    count = (len(refs) - 8) // 2
    hbm_refs, bases_ref, vmem_refs = refs[:count], refs[count], refs[count + 1 : 2 * count + 1]
    high_ref, low_ref, root_ref, maps_ref, spread_ref, chain_ref, sems = refs[2 * count + 1 :]
    dens_ref = vmem_refs[0]
    copies = fetch(
        [(maps_hbm, maps_ref), (bases_hbm, bases_ref), *zip(hbm_refs, vmem_refs)], sems
    )
    columns, points = dens_ref.shape
    rank, _, node_count = maps_ref.shape
    group = LANES // rank
    leaf_count = node_count // 2
    width = points // leaf_count
    copies[0].wait()
    node = lax.broadcasted_iota(jnp.int32, (node_count, LANES), 0)
    block = lax.broadcasted_iota(jnp.int32, (node_count, LANES), 1) // rank
    parent = node // 2 % group
    for first in range(0, rank, group):
        slab = maps_ref[first : first + group].reshape(group * rank, node_count).T
        turned = [slab] + [pltpu.roll(slab, turn * rank, 1) for turn in range(1, group)]
        for row in range(group):
            placed = jnp.zeros_like(slab)
            for place in range(group):
                here = (parent == place) & (block == place)
                placed = jnp.where(here, turned[(place - row) % group], placed)
            spread_ref[pl.ds(first + row, node_count, stride=rank), :] = placed
    tile = 2 * group * rank

    def children(parents, index):
        high, low = halves(spread_ref[index * tile : (index + 1) * tile, :])
        return split_dot(dot_nt, parents, high, low)

    row = lax.broadcasted_iota(jnp.int32, (rank, LANES), 0)
    lane = lax.broadcasted_iota(jnp.int32, (rank, LANES), 1)
    level = 1
    parents = jnp.where(lane == row + rank, 1.0, 0.0)
    while level < group:
        below = children(parents, 0)
        level *= 2
        parents = below[:, (level // group) * LANES : (level // group + 1) * LANES]
    chain_ref[:, LANES : 2 * LANES] = parents
    while level < leaf_count:
        for index in range(level // group, 2 * level // group):
            lanes = slice(index * LANES, (index + 1) * LANES)
            chain_ref[:, index * tile : (index + 1) * tile] = children(chain_ref[:, lanes], index)
        level *= 2
    copies[1].wait()
    copies[2].wait()
    step = group * width
    root = jnp.zeros((columns, rank), F32)
    for index in range(leaf_count // group):
        spots = slice(index * step, (index + 1) * step)
        start = (leaf_count // group + index) * LANES
        high, low = halves(bases_ref[:, spots])
        basis = split_dot(
            dot_nn, chain_ref[:, start : start + LANES],
            spread_bases(high, group), spread_bases(low, group),
        )
        high, low = halves(basis)
        high_ref[:, spots] = high
        low_ref[:, spots] = low
        dens = dens_ref[:, spots]
        root += dot_nt(dens, high) + dot_nt(dens, low)
    root = jnp.concatenate([root, jnp.zeros((columns, LANES - rank), F32)], axis=1)
    high = root.astype(BF16).astype(F32)
    rest = root - high
    middle = rest.astype(BF16).astype(F32)
    last = (rest - middle).astype(BF16).astype(F32)
    packed = high + pltpu.roll(middle, rank, 1) + pltpu.roll(last, 2 * rank, 1)
    root_ref[...] = packed.astype(BF16)
    for copy in copies[3:]:
        copy.wait()


def select_kernel(
    faces, far_groups, send_vmem, dens_ref, root_ref, *refs,
):
    other_refs = refs[: far_groups - 1]
    out_refs = refs[far_groups - 1 : -2]
    send_ref, sems = refs[-2:]
    copies = fetch([(send_vmem, send_ref)], sems)
    device = lax.axis_index("leaf")
    columns = dens_ref.shape[0]
    cap = send_ref.shape[1]
    copies[0].wait()
    for (directions, stride), out_ref in zip(faces, out_refs):
        direction = directions[0]
        if len(directions) > 1:
            direction = direction + device // stride % 2
        for place in range(cap):
            leaf = jnp.maximum(send_ref[direction, place, device], 0)
            for part, panel_ref in enumerate((dens_ref, *other_refs)):
                row = (place * far_groups + part) * columns
                out_ref[row : row + columns, :] = panel_ref[
                    :, pl.ds(pl.multiple_of(leaf * LANES, LANES), LANES)
                ]
        for row in range(cap * far_groups * columns, out_ref.shape[0], columns):
            out_ref[row : row + columns, :] = root_ref[...]


def near_kernel(
    faces, far_groups, share, *refs,
):
    source_vmems, refs = refs[:share], refs[share:]
    dens_ref, refs = refs[0], refs[1:]
    other_refs, refs = refs[: far_groups - 1], refs[far_groups - 1 :]
    got_refs, refs = refs[: len(faces)], refs[len(faces) :]
    block_ref, refs = refs[0], refs[1:]
    mate_refs, refs = refs[: share - 1], refs[share - 1 :]
    refs = refs[1:]
    out_refs, refs = refs[:far_groups], refs[far_groups:]
    source_refs, refs = refs[:share], refs[share:]
    sum_refs, refs = refs[: far_groups - 1], refs[far_groups - 1 :]
    peak_refs, refs = refs[: far_groups - 1], refs[far_groups - 1 :]
    buffer_ref, sems = refs
    columns, points = dens_ref.shape
    leaf_count, near_count, width, _ = block_ref.shape
    copies = fetch(list(zip(source_vmems, source_refs)), sems)
    cap = (buffer_ref.shape[0] - leaf_count) // len(FACE_SIGNS)
    for (directions, _), got_ref in zip(faces, got_refs):
        for direction in directions:
            for place in range(cap):
                row = place * far_groups * columns
                buffer_ref[leaf_count + direction * cap + place] = got_ref[
                    row : row + far_groups * columns, :
                ]
    for part, panel_ref in enumerate((dens_ref, *other_refs)):
        rows = slice(part * columns, (part + 1) * columns)
        for leaf in range(leaf_count):
            buffer_ref[leaf, rows, :] = panel_ref[:, leaf * width : (leaf + 1) * width]
    for copy in copies:
        copy.wait()
    tables = list(zip(source_refs[1:], mate_refs)) + [(source_refs[0], block_ref)]
    own_ref, sent_refs = out_refs[0], out_refs[1:]
    targets = (own_ref, *sum_refs)
    for turn, (source_ref, blocks_ref) in enumerate(tables):
        for leaf in range(leaf_count):
            panels = [buffer_ref[source_ref[block, leaf]] for block in range(near_count)]
            blocks = [blocks_ref[leaf, block] for block in range(near_count)]
            total = dot_nt(jnp.concatenate(panels, axis=1), jnp.concatenate(blocks, axis=1))
            lanes = slice(leaf * width, (leaf + 1) * width)
            for part, target_ref in enumerate(targets):
                term = total[part * columns : (part + 1) * columns]
                if turn:
                    term = target_ref[:, lanes] + term
                target_ref[:, lanes] = term
                if part and turn == share - 1:
                    peak_refs[part - 1][leaf : leaf + 1, :] = jnp.max(
                        jnp.abs(term), axis=0, keepdims=True
                    )
    for sum_ref, peak_ref, sent_ref in zip(sum_refs, peak_refs, sent_refs):
        power = jnp.floor(jnp.log2(jnp.maximum(peak_ref[...], 2.0**-100))) + 1.0
        factor = STEPS * jnp.exp2(-power)
        for leaf in range(leaf_count):
            lanes = slice(leaf * width, (leaf + 1) * width)
            steps = sum_ref[:, lanes] * factor[leaf : leaf + 1, :]
            sent_ref[:, lanes] = jnp.floor(steps + 0.5).astype(jnp.int32).astype(jnp.int16)
        power = power.astype(jnp.int32).astype(jnp.int16)
        for first in range(0, leaf_count, columns):
            spot = points + first // columns * width
            sent_ref[:, spot : spot + width] = power[first : first + columns]


def coupled(leaves, far_ref, coupling_ref, turned_ref):
    far_count, rank = coupling_ref.shape[1:3]
    columns = turned_ref.shape[1] // 2
    group = LANES // rank
    parts = []
    for leaf in leaves:
        maps = jnp.concatenate([coupling_ref[leaf, j] for j in range(far_count)], axis=1)
        maps = jnp.concatenate(halves(maps), axis=0)
        picked = jnp.concatenate(
            [
                turned_ref[pl.ds(pl.multiple_of(far_ref[j, leaf] * rank, rank), rank), :]
                for j in range(far_count)
            ],
            axis=0,
        )
        out = dot_nn(maps, picked)
        parts.append(out[:rank] + out[rank:])
        if len(parts) == group:
            turned = jnp.concatenate(parts, axis=0).T
            yield turned[:columns] + turned[columns:]
            parts = []


def couple_kernel(
    table_ref, coupling_ref, dens_ref, bases_ref, turned_ref, out_ref, far_ref, sems,
):
    copies = fetch([(table_ref, far_ref)], sems)
    columns, points = dens_ref.shape
    leaf_count, _, rank = coupling_ref.shape[:3]
    width = points // leaf_count
    upper = lax.broadcasted_iota(jnp.int32, (rank, 2 * columns), 1) < columns
    for leaf in range(leaf_count):
        spots = slice(leaf * width, (leaf + 1) * width)
        rows = jnp.concatenate(halves(bases_ref[:, spots]), axis=0)
        dens = dens_ref[:, spots]
        twice = dot_nt(rows, jnp.concatenate([dens, dens], axis=0))
        high, low = halves(twice[:rank] + twice[rank:])
        turned_ref[leaf * rank : (leaf + 1) * rank, :] = jnp.where(
            upper, high.astype(F32), low.astype(F32)
        ).astype(BF16)
    copies[0].wait()
    leaves = range(out_ref.shape[1] // rank)
    for index, field in enumerate(coupled(leaves, far_ref, coupling_ref, turned_ref)):
        out_ref[:, index * LANES : (index + 1) * LANES] = field


def project_kernel(
    table_ref, coupling_ref, turned_ref, first_ref, bases_ref, near_ref, out_ref, far_ref, sems,
):
    copies = fetch([(table_ref, far_ref)], sems)
    rank, points = bases_ref.shape
    leaf_count = coupling_ref.shape[0]
    group = LANES // rank
    step = group * points // leaf_count

    def project(index, field):
        spots = slice(index * step, (index + 1) * step)
        high, low = halves(bases_ref[:, spots])
        out_ref[:, spots] = near_ref[:, spots] + split_dot(
            dot_nn, field, spread_bases(high, group), spread_bases(low, group)
        )

    done = first_ref.shape[1] // LANES
    for index in range(done):
        project(index, first_ref[:, index * LANES : (index + 1) * LANES])
    copies[0].wait()
    leaves = range(done * group, leaf_count)
    for index, field in enumerate(coupled(leaves, far_ref, coupling_ref, turned_ref)):
        project(done + index, field)


def far_kernel(
    roots, leaf_count, upper_ref, cross_ref, high_ref, low_ref, term_ref, *refs,
):
    root_refs, refs = refs[: len(roots)], refs[len(roots) :]
    sent_refs, (out_hbm, sum_ref, tile_ref, tree_ref, sems) = refs[:-5], refs[-5:]
    device = lax.axis_index("leaf")
    columns, points = sum_ref.shape
    width = points // leaf_count
    factors = []
    for sent_ref in sent_refs:
        powers = [
            sent_ref[:, points + first // columns * width :][:, :width]
            for first in range(0, leaf_count, columns)
        ]
        power = jnp.concatenate([p.astype(jnp.int32).astype(F32) for p in powers], axis=0)
        factors.append(jnp.exp2(power) * (1.0 / STEPS))
    rank = upper_ref.shape[1]
    device_count = upper_ref.shape[0] // 2
    for tiles, root_ref in zip(roots, root_refs):
        if tiles is None:
            for index in range(device_count):
                tile_ref[index] = root_ref[index]
        else:
            for turn, row in tiles:
                tile_ref[device ^ turn] = root_ref[row : row + columns, :]
    zero = jnp.zeros((LANES - 3 * rank, rank), BF16)

    def lifted(child):
        if child >= device_count:
            high, low = (
                jnp.concatenate([half] * 3 + [zero], axis=0) for half in halves(upper_ref[child])
            )
            tile = tile_ref[child - device_count]
            return dot_nn(tile, high) + dot_nn(tile, low)
        return split_dot(dot_nn, tree_ref[child], *halves(upper_ref[child]))

    level = device_count // 2
    while level >= 4:
        for node in range(level, 2 * level):
            tree_ref[node] = lifted(2 * node) + lifted(2 * node + 1)
        level //= 2
    lane = lax.broadcasted_iota(jnp.int32, (LANES, rank), 0)
    column = lax.broadcasted_iota(jnp.int32, (LANES, rank), 1)
    gather = jnp.where((lane % rank == column) & (lane < 3 * rank), 1.0, 0.0).astype(BF16)
    field = None
    level = 4
    while level <= device_count:
        place = device // (device_count // level)
        node = level + place
        third = jnp.where(place % 2 == 0, place + 3, place - 3)
        total = None
        for slot, other in enumerate((place - 2, place + 2, third)):
            inside = (other >= 0) & (other < level)
            other = jnp.clip(other, 0, level - 1)
            if level == device_count:
                value = dot_nn(tile_ref[other], gather)
            else:
                value = tree_ref[level + other]
            value = jnp.where(inside, value, 0.0)
            term = split_dot(dot_nt, value, *halves(cross_ref[node, slot]))
            total = term if total is None else total + term
        if field is not None:
            total = total + split_dot(dot_nt, field, *halves(upper_ref[node]))
        field = total
        level *= 2
    chunk_count = sems.shape[0]
    step = points // chunk_count
    copies = []
    for index in range(chunk_count):
        spots = slice(index * step, (index + 1) * step)
        total = term_ref[:, spots] + split_dot(
            dot_nn, field, high_ref[:, spots], low_ref[:, spots]
        )
        for sent_ref, factor in zip(sent_refs, factors):
            steps = sent_ref[:, spots].astype(jnp.int32).astype(F32)
            leaves = range(index * leaf_count // chunk_count, (index + 1) * leaf_count // chunk_count)
            scale = jnp.concatenate([factor[leaf : leaf + 1] for leaf in leaves], axis=1)
            total = total + steps * scale
        sum_ref[:, spots] = total
        copies += fetch(
            [(sum_ref.at[:, pl.ds(index * step, step)], out_hbm.at[:, pl.ds(index * step, step)])],
            sems.at[pl.ds(index, 1)],
        )
    for copy in copies:
        copy.wait()


def hbm(value):
    return pltpu.with_memory_space_constraint(value, pltpu.HBM)


def hint(micros):
    return pl.CostEstimate(flops=0, bytes_accessed=int(micros * 3.69e6), transcendentals=0)


def local(
    densities,
    bases,
    near_blocks,
    near_src,
    send_leaf,
    far_src,
    leaf_coupling,
    local_transfer,
    upper_transfer,
    up_coupling,
):
    leaf_devices = lax.axis_size("leaf")
    far_groups = lax.axis_size("far")
    share = lax.axis_size("mate")
    side = cube_side(leaf_devices)
    offsets = face_offsets(leaf_devices)
    columns, points = densities.shape
    leaf_count, near_count, width, _ = near_blocks.shape
    rank = bases.shape[0]
    cap = send_leaf.shape[2]
    node_count = local_transfer.shape[1]
    params = pltpu.CompilerParams(vmem_limit_bytes=16 * 2**20)
    dma = pltpu.SemaphoreType.DMA

    def rotated(value, axis, shift):
        count = lax.axis_size(axis)
        return lax.ppermute(value, axis, [(i, (i - shift) % count) for i in range(count)])

    def crossed(value, turn):
        return lax.ppermute(value, "leaf", [(i, i ^ turn) for i in range(leaf_devices)])

    sources = near_src.T
    others = [rotated(densities, "far", part) for part in range(1, far_groups)]
    all_sources = [sources] + [rotated(sources, "mate", part) for part in range(1, share)]
    send = send_leaf.transpose(1, 2, 0)
    moved = [densities, send, sources, far_src.T, leaf_coupling, near_blocks]
    basis, dens, send, sources, far_table, coupling, blocks, high, low, root = pl.pallas_call(
        up_kernel,
        out_shape=[jax.ShapeDtypeStruct(value.shape, value.dtype) for value in (bases, *moved)]
        + [
            jax.ShapeDtypeStruct((rank, points), BF16),
            jax.ShapeDtypeStruct((rank, points), BF16),
            jax.ShapeDtypeStruct((columns, LANES), BF16),
        ],
        in_specs=[HBM] * (2 + len(moved)),
        out_specs=[VMEM] * (4 + len(moved)),
        scratch_shapes=[
            pltpu.VMEM((rank, rank, node_count), F32),
            pltpu.VMEM((node_count * rank, LANES), F32),
            pltpu.VMEM((rank, node_count * rank), F32),
            dma((2 + len(moved),)),
        ],
        compiler_params=params,
        cost_estimate=hint(3.5),
        name="up",
    )(hbm(local_transfer[0].transpose(1, 2, 0)), hbm(bases), *map(hbm, moved))
    all_sources[0] = sources

    later_blocks, others, all_sources, root = lax.optimization_barrier(
        (blocks, others, all_sources, root)
    )
    mate_blocks = [rotated(later_blocks, "mate", part) for part in range(1, share)]

    if side == 2:
        faces = [((2 * axis, 2 * axis + 1), 2**axis) for axis in (2, 0, 1)]
    else:
        faces = [((direction,), offset) for direction, offset in enumerate(offsets)]
    chunks = [(cap * far_groups + (1 if place else 3)) * columns for place in range(len(faces))]
    outgoing = pl.pallas_call(
        functools.partial(select_kernel, faces, far_groups),
        out_shape=[jax.ShapeDtypeStruct((chunk, LANES), BF16) for chunk in chunks],
        in_specs=[VMEM] * (2 + far_groups),
        out_specs=[VMEM] * len(faces),
        scratch_shapes=[
            pltpu.SMEM(send.shape, jnp.int32),
            dma((1,)),
        ],
        compiler_params=params,
        cost_estimate=hint(1),
        name="select",
    )(send, dens, root, *others)
    outgoing, dens = lax.optimization_barrier((outgoing, dens))
    first_leaves = LANES // rank
    turned, leaf_local = pl.pallas_call(
        couple_kernel,
        out_shape=[
            jax.ShapeDtypeStruct((leaf_count * rank, 2 * columns), BF16),
            jax.ShapeDtypeStruct((columns, first_leaves * rank), F32),
        ],
        in_specs=[VMEM] * 4,
        out_specs=[VMEM] * 2,
        scratch_shapes=[pltpu.SMEM(far_table.shape, jnp.int32), dma((1,))],
        compiler_params=params,
        cost_estimate=hint(2),
        name="couple",
    )(far_table, coupling, dens, basis)
    tail = cap * far_groups * columns
    if side == 2:
        arrived = [crossed(value, stride) for (_, stride), value in zip(faces, outgoing)]
        far_one, near_one, _ = (value[tail : tail + columns] for value in arrived)
        later, leaf_local = lax.optimization_barrier((arrived[0][-4 * columns :], leaf_local))
        across = crossed(later, 1)
        held = jnp.concatenate([near_one, far_one, across[-columns:]], axis=0)
        beside = crossed(held, 2)
        roots = [([(0, 0)], root), ([(5, 3 * columns)], across)]
        roots += [([(stride, tail)], value) for (_, stride), value in zip(faces, arrived)]
        roots.append(([(3, 0), (6, columns), (7, 2 * columns)], beside))
    else:
        arrived = [shifted(value, "leaf", stride) for (_, stride), value in zip(faces, outgoing)]
        roots = [(None, lax.all_gather(root, "leaf", axis=0))]

    slots = leaf_count + len(offsets) * cap
    tables = -(-leaf_count // columns) * width
    partials = pl.pallas_call(
        functools.partial(near_kernel, faces, far_groups, share),
        out_shape=[jax.ShapeDtypeStruct((columns, points), F32)]
        + [jax.ShapeDtypeStruct((columns, points + tables), jnp.int16)] * (far_groups - 1),
        in_specs=[VMEM] * (2 * share + far_groups + len(faces) + 1),
        out_specs=[VMEM] * far_groups,
        scratch_shapes=[pltpu.SMEM(sources.shape, jnp.int32)] * share
        + [pltpu.VMEM((columns, points), F32)] * (far_groups - 1)
        + [pltpu.VMEM((leaf_count, width), F32)] * (far_groups - 1)
        + [
            pltpu.VMEM((slots, far_groups * columns, width), BF16),
            dma((share,)),
        ],
        compiler_params=params,
        cost_estimate=hint(3),
        name="near",
    )(
        *all_sources, dens, *others, *arrived, blocks, *mate_blocks, leaf_local,
    )
    received = [rotated(partials[part], "far", -part) for part in range(1, far_groups)]
    partial = pl.pallas_call(
        project_kernel,
        out_shape=jax.ShapeDtypeStruct((columns, points), F32),
        in_specs=[VMEM] * 6,
        out_specs=VMEM,
        scratch_shapes=[pltpu.SMEM(far_table.shape, jnp.int32), dma((1,))],
        compiler_params=params,
        cost_estimate=hint(1.5),
        name="project",
    )(far_table, coupling, turned, leaf_local, basis, partials[0])
    return pl.pallas_call(
        functools.partial(far_kernel, [tiles for tiles, _ in roots], leaf_count),
        out_shape=jax.ShapeDtypeStruct((columns, points), F32),
        in_specs=[VMEM] * (5 + len(roots) + len(received)),
        out_specs=HBM,
        scratch_shapes=[
            pltpu.VMEM((columns, points), F32),
            pltpu.VMEM((leaf_devices, columns, LANES), BF16),
            pltpu.VMEM((2 * leaf_devices, columns, rank), F32),
            dma((8,)),
        ],
        compiler_params=params,
        cost_estimate=hint(1.5),
        name="far",
    )(upper_transfer, up_coupling, high, low, partial, *[value for _, value in roots], *received)


def solution(mesh):
    leaf_devices, rhs_devices = mesh.shape["leaf"], mesh.shape["rhs"]
    share = 2 if rhs_devices % 2 == 0 else 1
    split = Mesh(
        mesh.devices.reshape(leaf_devices, rhs_devices // share, share), ("leaf", "far", "mate")
    )
    rhs = ("far", "mate")
    in_specs = (
        P(rhs, "leaf"),
        P(None, "leaf"),
        P("leaf", rhs, None, None),
        P("leaf", rhs),
        P(),
        P("leaf", None),
        P("leaf", None, None, None),
        P("leaf", None, None, None),
        P(),
        P(),
    )
    return jax.shard_map(
        local, mesh=split, in_specs=in_specs, out_specs=P(rhs, "leaf"), check_vma=False
    )
```

```python
import functools

import jax
import jax.numpy as jnp
from jax import lax
from jax.experimental import pallas as pl
from jax.experimental.pallas import tpu as pltpu
from jax.sharding import Mesh
from jax.sharding import PartitionSpec as P

FACE_SIGNS = ((1, 0), (-1, 0), (1, 1), (-1, 1), (1, 2), (-1, 2))
F32 = jnp.float32
BF16 = jnp.bfloat16
LANES = 128
STEPS = 32000.0
VMEM = pl.BlockSpec(memory_space=pltpu.VMEM)
HBM = pl.BlockSpec(memory_space=pltpu.HBM)
SMEM = pl.BlockSpec(memory_space=pltpu.SMEM)


def cube_side(device_count):
    return max((edge_len for edge_len in range(1, 65) if edge_len**3 <= device_count))


def face_offsets(device_count):
    side_len = cube_side(device_count)
    return [face_sign * side_len**axis_pos for face_sign, axis_pos in FACE_SIGNS]


def shifted(value, axis, steps):
    count = lax.axis_size(axis)
    first, last = (max(0, -steps), min(count, count - steps))
    return lax.ppermute(value, axis, [(source, source + steps) for source in range(first, last)])


def halves(value):
    high = value.astype(BF16)
    return high, (value - high.astype(F32)).astype(BF16)


def dot_nn(left, right):
    return lax.dot_general(left, right, (((1,), (0,)), ((), ())), preferred_element_type=F32)


def dot_nt(left, right):
    return lax.dot_general(left, right, (((1,), (1,)), ((), ())), preferred_element_type=F32)


def split_dot(dot, rows, right_high, right_low):
    count = rows.shape[0]
    high, low = halves(rows)
    both = jnp.concatenate([high, low], axis=0)
    out = dot(both, right_high) + dot(both, right_low)
    return out[:count] + out[count:]


def spread_bases(block, group):
    rank, lanes = block.shape
    width = lanes // group
    zero = jnp.zeros((rank, width), block.dtype)
    rows = []
    for slot in range(group):
        pieces = [zero] * group
        pieces[slot] = block[:, slot * width : (slot + 1) * width]
        rows.append(jnp.concatenate(pieces, axis=1))
    return jnp.concatenate(rows, axis=0)


def fetch(pairs, sems):
    copies = []
    for index, (source, target) in enumerate(pairs):
        copy = pltpu.make_async_copy(source, target, sems.at[index])
        copy.start()
        copies.append(copy)
    return copies


def up_kernel(
    maps_hbm, bases_hbm, *refs,
):
    count = (len(refs) - 8) // 2
    hbm_refs, bases_ref, vmem_refs = refs[:count], refs[count], refs[count + 1 : 2 * count + 1]
    high_ref, low_ref, root_ref, maps_ref, spread_ref, chain_ref, sems = refs[2 * count + 1 :]
    dens_ref = vmem_refs[0]
    copies = fetch(
        [(maps_hbm, maps_ref), (bases_hbm, bases_ref), *zip(hbm_refs, vmem_refs)], sems
    )
    columns, points = dens_ref.shape
    rank, _, node_count = maps_ref.shape
    group = LANES // rank
    leaf_count = node_count // 2
    width = points // leaf_count
    copies[0].wait()
    node = lax.broadcasted_iota(jnp.int32, (node_count, LANES), 0)
    block = lax.broadcasted_iota(jnp.int32, (node_count, LANES), 1) // rank
    parent = node // 2 % group
    for first in range(0, rank, group):
        slab = maps_ref[first : first + group].reshape(group * rank, node_count).T
        turned = [slab] + [pltpu.roll(slab, turn * rank, 1) for turn in range(1, group)]
        for row in range(group):
            placed = jnp.zeros_like(slab)
            for place in range(group):
                here = (parent == place) & (block == place)
                placed = jnp.where(here, turned[(place - row) % group], placed)
            spread_ref[pl.ds(first + row, node_count, stride=rank), :] = placed
    tile = 2 * group * rank

    def children(parents, index):
        high, low = halves(spread_ref[index * tile : (index + 1) * tile, :])
        return split_dot(dot_nt, parents, high, low)

    row = lax.broadcasted_iota(jnp.int32, (rank, LANES), 0)
    lane = lax.broadcasted_iota(jnp.int32, (rank, LANES), 1)
    level = 1
    parents = jnp.where(lane == row + rank, 1.0, 0.0)
    while level < group:
        below = children(parents, 0)
        level *= 2
        parents = below[:, (level // group) * LANES : (level // group + 1) * LANES]
    chain_ref[:, LANES : 2 * LANES] = parents
    while level < leaf_count:
        for index in range(level // group, 2 * level // group):
            lanes = slice(index * LANES, (index + 1) * LANES)
            chain_ref[:, index * tile : (index + 1) * tile] = children(chain_ref[:, lanes], index)
        level *= 2
    copies[1].wait()
    copies[2].wait()
    step = group * width
    root = jnp.zeros((columns, rank), F32)
    for index in range(leaf_count // group):
        spots = slice(index * step, (index + 1) * step)
        start = (leaf_count // group + index) * LANES
        high, low = halves(bases_ref[:, spots])
        basis = split_dot(
            dot_nn, chain_ref[:, start : start + LANES],
            spread_bases(high, group), spread_bases(low, group),
        )
        high, low = halves(basis)
        high_ref[:, spots] = high
        low_ref[:, spots] = low
        dens = dens_ref[:, spots]
        root += dot_nt(dens, high) + dot_nt(dens, low)
    root = jnp.concatenate([root, jnp.zeros((columns, LANES - rank), F32)], axis=1)
    high = root.astype(BF16).astype(F32)
    rest = root - high
    middle = rest.astype(BF16).astype(F32)
    last = (rest - middle).astype(BF16).astype(F32)
    packed = high + pltpu.roll(middle, rank, 1) + pltpu.roll(last, 2 * rank, 1)
    root_ref[...] = packed.astype(BF16)
    for copy in copies[3:]:
        copy.wait()


def select_kernel(
    faces, far_groups, send_ref, dens_ref, root_ref, *refs,
):
    other_refs, out_refs = refs[: far_groups - 1], refs[far_groups - 1 :]
    device = lax.axis_index("leaf")
    columns = dens_ref.shape[0]
    cap, device_count = send_ref.shape[1:]
    own = lax.broadcasted_iota(jnp.int32, (cap, device_count), 1) == device
    for (directions, stride), out_ref in zip(faces, out_refs):
        table = send_ref[directions[0]]
        if len(directions) > 1:
            table = jnp.where(device // stride % 2 == 0, table, send_ref[directions[1]])
        picks = jnp.max(jnp.where(own, table.astype(F32), 0.0), axis=1, keepdims=True)
        for place in range(cap):
            leaf = picks[place, 0].astype(jnp.int32)
            for part, panel_ref in enumerate((dens_ref, *other_refs)):
                row = (place * far_groups + part) * columns
                out_ref[row : row + columns, :] = panel_ref[
                    :, pl.ds(pl.multiple_of(leaf * LANES, LANES), LANES)
                ]
        out_ref[cap * far_groups * columns :, :] = root_ref[...]


def near_kernel(
    faces, far_groups, share, *refs,
):
    source_vmems, refs = refs[:share], refs[share:]
    dens_ref, refs = refs[0], refs[1:]
    other_refs, refs = refs[: far_groups - 1], refs[far_groups - 1 :]
    got_refs, refs = refs[: len(faces)], refs[len(faces) :]
    block_ref, refs = refs[0], refs[1:]
    mate_refs, refs = refs[: share - 1], refs[share - 1 :]
    refs = refs[1:]
    out_refs, refs = refs[:far_groups], refs[far_groups:]
    source_refs, refs = refs[:share], refs[share:]
    sum_refs, refs = refs[: far_groups - 1], refs[far_groups - 1 :]
    peak_refs, refs = refs[: far_groups - 1], refs[far_groups - 1 :]
    buffer_ref, sems = refs
    columns, points = dens_ref.shape
    leaf_count, near_count, width, _ = block_ref.shape
    copies = fetch(list(zip(source_vmems, source_refs)), sems)
    cap = (buffer_ref.shape[0] - leaf_count) // len(FACE_SIGNS)
    for (directions, _), got_ref in zip(faces, got_refs):
        for direction in directions:
            for place in range(cap):
                row = place * far_groups * columns
                buffer_ref[leaf_count + direction * cap + place] = got_ref[
                    row : row + far_groups * columns, :
                ]
    for part, panel_ref in enumerate((dens_ref, *other_refs)):
        rows = slice(part * columns, (part + 1) * columns)
        for leaf in range(leaf_count):
            buffer_ref[leaf, rows, :] = panel_ref[:, leaf * width : (leaf + 1) * width]
    for copy in copies:
        copy.wait()
    tables = list(zip(source_refs[1:], mate_refs)) + [(source_refs[0], block_ref)]
    own_ref, sent_refs = out_refs[0], out_refs[1:]
    targets = (own_ref, *sum_refs)
    for turn, (source_ref, blocks_ref) in enumerate(tables):
        for leaf in range(leaf_count):
            panels = [buffer_ref[source_ref[block, leaf]] for block in range(near_count)]
            blocks = [blocks_ref[leaf, block] for block in range(near_count)]
            total = dot_nt(jnp.concatenate(panels, axis=1), jnp.concatenate(blocks, axis=1))
            lanes = slice(leaf * width, (leaf + 1) * width)
            for part, target_ref in enumerate(targets):
                term = total[part * columns : (part + 1) * columns]
                if turn:
                    term = target_ref[:, lanes] + term
                target_ref[:, lanes] = term
                if part and turn == share - 1:
                    peak_refs[part - 1][leaf : leaf + 1, :] = jnp.max(
                        jnp.abs(term), axis=0, keepdims=True
                    )
    for sum_ref, peak_ref, sent_ref in zip(sum_refs, peak_refs, sent_refs):
        power = jnp.floor(jnp.log2(jnp.maximum(peak_ref[...], 2.0**-100))) + 1.0
        factor = STEPS * jnp.exp2(-power)
        for leaf in range(leaf_count):
            lanes = slice(leaf * width, (leaf + 1) * width)
            steps = sum_ref[:, lanes] * factor[leaf : leaf + 1, :]
            sent_ref[:, lanes] = jnp.floor(steps + 0.5).astype(jnp.int32).astype(jnp.int16)
        power = power.astype(jnp.int32).astype(jnp.int16)
        for first in range(0, leaf_count, columns):
            spot = points + first // columns * width
            sent_ref[:, spot : spot + width] = power[first : first + columns]


def coupled(leaves, far_ref, coupling_ref, turned_ref):
    far_count, rank = coupling_ref.shape[1:3]
    columns = turned_ref.shape[1] // 2
    group = LANES // rank
    parts = []
    for leaf in leaves:
        maps = jnp.concatenate([coupling_ref[leaf, j] for j in range(far_count)], axis=1)
        maps = jnp.concatenate(halves(maps), axis=0)
        picked = jnp.concatenate(
            [
                turned_ref[pl.ds(pl.multiple_of(far_ref[j, leaf] * rank, rank), rank), :]
                for j in range(far_count)
            ],
            axis=0,
        )
        out = dot_nn(maps, picked)
        parts.append(out[:rank] + out[rank:])
        if len(parts) == group:
            turned = jnp.concatenate(parts, axis=0).T
            yield turned[:columns] + turned[columns:]
            parts = []


def couple_kernel(
    table_ref, coupling_ref, dens_ref, bases_ref, turned_ref, out_ref, far_ref, sems,
):
    copies = fetch([(table_ref, far_ref)], sems)
    columns, points = dens_ref.shape
    leaf_count, _, rank = coupling_ref.shape[:3]
    width = points // leaf_count
    upper = lax.broadcasted_iota(jnp.int32, (rank, 2 * columns), 1) < columns
    for leaf in range(leaf_count):
        spots = slice(leaf * width, (leaf + 1) * width)
        rows = jnp.concatenate(halves(bases_ref[:, spots]), axis=0)
        dens = dens_ref[:, spots]
        twice = dot_nt(rows, jnp.concatenate([dens, dens], axis=0))
        high, low = halves(twice[:rank] + twice[rank:])
        turned_ref[leaf * rank : (leaf + 1) * rank, :] = jnp.where(
            upper, high.astype(F32), low.astype(F32)
        ).astype(BF16)
    copies[0].wait()
    leaves = range(out_ref.shape[1] // rank)
    for index, field in enumerate(coupled(leaves, far_ref, coupling_ref, turned_ref)):
        out_ref[:, index * LANES : (index + 1) * LANES] = field


def project_kernel(
    table_ref, coupling_ref, turned_ref, first_ref, bases_ref, near_ref, out_ref, far_ref, sems,
):
    copies = fetch([(table_ref, far_ref)], sems)
    rank, points = bases_ref.shape
    leaf_count = coupling_ref.shape[0]
    group = LANES // rank
    step = group * points // leaf_count

    def project(index, field):
        spots = slice(index * step, (index + 1) * step)
        high, low = halves(bases_ref[:, spots])
        out_ref[:, spots] = near_ref[:, spots] + split_dot(
            dot_nn, field, spread_bases(high, group), spread_bases(low, group)
        )

    done = first_ref.shape[1] // LANES
    for index in range(done):
        project(index, first_ref[:, index * LANES : (index + 1) * LANES])
    copies[0].wait()
    leaves = range(done * group, leaf_count)
    for index, field in enumerate(coupled(leaves, far_ref, coupling_ref, turned_ref)):
        project(done + index, field)


def far_kernel(
    roots, leaf_count, upper_ref, cross_ref, high_ref, low_ref, term_ref, *refs,
):
    root_refs, refs = refs[: len(roots)], refs[len(roots) :]
    sent_refs, (out_hbm, sum_ref, tile_ref, tree_ref, sems) = refs[:-5], refs[-5:]
    device = lax.axis_index("leaf")
    columns, points = sum_ref.shape
    width = points // leaf_count
    factors = []
    for sent_ref in sent_refs:
        powers = [
            sent_ref[:, points + first // columns * width :][:, :width]
            for first in range(0, leaf_count, columns)
        ]
        power = jnp.concatenate([p.astype(jnp.int32).astype(F32) for p in powers], axis=0)
        factors.append(jnp.exp2(power) * (1.0 / STEPS))
    rank = upper_ref.shape[1]
    device_count = upper_ref.shape[0] // 2
    for tiles, root_ref in zip(roots, root_refs):
        if tiles is None:
            for index in range(device_count):
                tile_ref[index] = root_ref[index]
        else:
            for turn, row in tiles:
                tile_ref[device ^ turn] = root_ref[row : row + columns, :]
    zero = jnp.zeros((LANES - 3 * rank, rank), BF16)

    def lifted(child):
        if child >= device_count:
            high, low = (
                jnp.concatenate([half] * 3 + [zero], axis=0) for half in halves(upper_ref[child])
            )
            tile = tile_ref[child - device_count]
            return dot_nn(tile, high) + dot_nn(tile, low)
        return split_dot(dot_nn, tree_ref[child], *halves(upper_ref[child]))

    level = device_count // 2
    while level >= 4:
        for node in range(level, 2 * level):
            tree_ref[node] = lifted(2 * node) + lifted(2 * node + 1)
        level //= 2
    lane = lax.broadcasted_iota(jnp.int32, (LANES, rank), 0)
    column = lax.broadcasted_iota(jnp.int32, (LANES, rank), 1)
    gather = jnp.where((lane % rank == column) & (lane < 3 * rank), 1.0, 0.0).astype(BF16)
    field = None
    level = 4
    while level <= device_count:
        place = device // (device_count // level)
        node = level + place
        third = jnp.where(place % 2 == 0, place + 3, place - 3)
        total = None
        for slot, other in enumerate((place - 2, place + 2, third)):
            inside = (other >= 0) & (other < level)
            other = jnp.clip(other, 0, level - 1)
            if level == device_count:
                value = dot_nn(tile_ref[other], gather)
            else:
                value = tree_ref[level + other]
            value = jnp.where(inside, value, 0.0)
            term = split_dot(dot_nt, value, *halves(cross_ref[node, slot]))
            total = term if total is None else total + term
        if field is not None:
            total = total + split_dot(dot_nt, field, *halves(upper_ref[node]))
        field = total
        level *= 2
    chunk_count = sems.shape[0]
    step = points // chunk_count
    copies = []
    for index in range(chunk_count):
        spots = slice(index * step, (index + 1) * step)
        total = term_ref[:, spots] + split_dot(
            dot_nn, field, high_ref[:, spots], low_ref[:, spots]
        )
        for sent_ref, factor in zip(sent_refs, factors):
            steps = sent_ref[:, spots].astype(jnp.int32).astype(F32)
            leaves = range(index * leaf_count // chunk_count, (index + 1) * leaf_count // chunk_count)
            scale = jnp.concatenate([factor[leaf : leaf + 1] for leaf in leaves], axis=1)
            total = total + steps * scale
        sum_ref[:, spots] = total
        copies += fetch(
            [(sum_ref.at[:, pl.ds(index * step, step)], out_hbm.at[:, pl.ds(index * step, step)])],
            sems.at[pl.ds(index, 1)],
        )
    for copy in copies:
        copy.wait()


def hbm(value):
    return pltpu.with_memory_space_constraint(value, pltpu.HBM)


def hint(micros):
    return pl.CostEstimate(flops=0, bytes_accessed=int(micros * 3.69e6), transcendentals=0)


def local(
    densities,
    bases,
    near_blocks,
    near_src,
    send_leaf,
    far_src,
    leaf_coupling,
    local_transfer,
    upper_transfer,
    up_coupling,
):
    leaf_devices = lax.axis_size("leaf")
    far_groups = lax.axis_size("far")
    share = lax.axis_size("mate")
    side = cube_side(leaf_devices)
    offsets = face_offsets(leaf_devices)
    columns, points = densities.shape
    leaf_count, near_count, width, _ = near_blocks.shape
    rank = bases.shape[0]
    cap = send_leaf.shape[2]
    node_count = local_transfer.shape[1]
    params = pltpu.CompilerParams(vmem_limit_bytes=16 * 2**20)
    dma = pltpu.SemaphoreType.DMA

    def rotated(value, axis, shift):
        count = lax.axis_size(axis)
        return lax.ppermute(value, axis, [(i, (i - shift) % count) for i in range(count)])

    def crossed(value, turn):
        return lax.ppermute(value, "leaf", [(i, i ^ turn) for i in range(leaf_devices)])

    sources = near_src.T
    others = [rotated(densities, "far", part) for part in range(1, far_groups)]
    all_sources = [sources] + [rotated(sources, "mate", part) for part in range(1, share)]
    send = send_leaf.transpose(1, 2, 0)
    moved = [densities, send, sources, far_src.T, leaf_coupling, near_blocks]
    basis, dens, send, sources, far_table, coupling, blocks, high, low, root = pl.pallas_call(
        up_kernel,
        out_shape=[jax.ShapeDtypeStruct(value.shape, value.dtype) for value in (bases, *moved)]
        + [
            jax.ShapeDtypeStruct((rank, points), BF16),
            jax.ShapeDtypeStruct((rank, points), BF16),
            jax.ShapeDtypeStruct((columns, LANES), BF16),
        ],
        in_specs=[HBM] * (2 + len(moved)),
        out_specs=[VMEM] * (4 + len(moved)),
        scratch_shapes=[
            pltpu.VMEM((rank, rank, node_count), F32),
            pltpu.VMEM((node_count * rank, LANES), F32),
            pltpu.VMEM((rank, node_count * rank), F32),
            dma((2 + len(moved),)),
        ],
        compiler_params=params,
        cost_estimate=hint(3.5),
        name="up",
    )(hbm(local_transfer[0].transpose(1, 2, 0)), hbm(bases), *map(hbm, moved))
    all_sources[0] = sources

    later_blocks, others, all_sources, root = lax.optimization_barrier(
        (blocks, others, all_sources, root)
    )
    mate_blocks = [rotated(later_blocks, "mate", part) for part in range(1, share)]

    if side == 2:
        faces = [((2 * axis, 2 * axis + 1), 2**axis) for axis in (2, 0, 1)]
    else:
        faces = [((direction,), offset) for direction, offset in enumerate(offsets)]
    chunk = (cap * far_groups + 1) * columns
    outgoing = pl.pallas_call(
        functools.partial(select_kernel, faces, far_groups),
        out_shape=[jax.ShapeDtypeStruct((chunk, LANES), BF16)] * len(faces),
        in_specs=[VMEM] * (2 + far_groups),
        out_specs=[VMEM] * len(faces),
        compiler_params=params,
        cost_estimate=hint(1),
        name="select",
    )(send, dens, root, *others)
    outgoing, dens = lax.optimization_barrier((outgoing, dens))
    first_leaves = leaf_count // 2
    turned, leaf_local = pl.pallas_call(
        couple_kernel,
        out_shape=[
            jax.ShapeDtypeStruct((leaf_count * rank, 2 * columns), BF16),
            jax.ShapeDtypeStruct((columns, first_leaves * rank), F32),
        ],
        in_specs=[VMEM] * 4,
        out_specs=[VMEM] * 2,
        scratch_shapes=[pltpu.SMEM(far_table.shape, jnp.int32), dma((1,))],
        compiler_params=params,
        cost_estimate=hint(2),
        name="couple",
    )(far_table, coupling, dens, basis)
    tail = cap * far_groups * columns
    if side == 2:
        arrived = [crossed(value, stride) for (_, stride), value in zip(faces, outgoing)]
        far_one, near_one, _ = (value[tail : tail + columns] for value in arrived)
        later, leaf_local = lax.optimization_barrier((arrived[0][-4 * columns :], leaf_local))
        across = crossed(later, 1)
        held = jnp.concatenate([near_one, far_one, across[-columns:]], axis=0)
        beside = crossed(held, 2)
        roots = [([(0, 0)], root), ([(5, 3 * columns)], across)]
        roots += [([(stride, tail)], value) for (_, stride), value in zip(faces, arrived)]
        roots.append(([(3, 0), (6, columns), (7, 2 * columns)], beside))
    else:
        arrived = [shifted(value, "leaf", stride) for (_, stride), value in zip(faces, outgoing)]
        roots = [(None, lax.all_gather(root, "leaf", axis=0))]

    slots = leaf_count + len(offsets) * cap
    tables = -(-leaf_count // columns) * width
    partials = pl.pallas_call(
        functools.partial(near_kernel, faces, far_groups, share),
        out_shape=[jax.ShapeDtypeStruct((columns, points), F32)]
        + [jax.ShapeDtypeStruct((columns, points + tables), jnp.int16)] * (far_groups - 1),
        in_specs=[VMEM] * (2 * share + far_groups + len(faces) + 1),
        out_specs=[VMEM] * far_groups,
        scratch_shapes=[pltpu.SMEM(sources.shape, jnp.int32)] * share
        + [pltpu.VMEM((columns, points), F32)] * (far_groups - 1)
        + [pltpu.VMEM((leaf_count, width), F32)] * (far_groups - 1)
        + [
            pltpu.VMEM((slots, far_groups * columns, width), BF16),
            dma((share,)),
        ],
        compiler_params=params,
        cost_estimate=hint(3),
        name="near",
    )(
        *all_sources, dens, *others, *arrived, blocks, *mate_blocks, leaf_local,
    )
    received = [rotated(partials[part], "far", -part) for part in range(1, far_groups)]
    partial = pl.pallas_call(
        project_kernel,
        out_shape=jax.ShapeDtypeStruct((columns, points), F32),
        in_specs=[VMEM] * 6,
        out_specs=VMEM,
        scratch_shapes=[pltpu.SMEM(far_table.shape, jnp.int32), dma((1,))],
        compiler_params=params,
        cost_estimate=hint(1.5),
        name="project",
    )(far_table, coupling, turned, leaf_local, basis, partials[0])
    return pl.pallas_call(
        functools.partial(far_kernel, [tiles for tiles, _ in roots], leaf_count),
        out_shape=jax.ShapeDtypeStruct((columns, points), F32),
        in_specs=[VMEM] * (5 + len(roots) + len(received)),
        out_specs=HBM,
        scratch_shapes=[
            pltpu.VMEM((columns, points), F32),
            pltpu.VMEM((leaf_devices, columns, LANES), BF16),
            pltpu.VMEM((2 * leaf_devices, columns, rank), F32),
            dma((8,)),
        ],
        compiler_params=params,
        cost_estimate=hint(1.5),
        name="far",
    )(upper_transfer, up_coupling, high, low, partial, *[value for _, value in roots], *received)


def solution(mesh):
    leaf_devices, rhs_devices = mesh.shape["leaf"], mesh.shape["rhs"]
    share = 2 if rhs_devices % 2 == 0 else 1
    split = Mesh(
        mesh.devices.reshape(leaf_devices, rhs_devices // share, share), ("leaf", "far", "mate")
    )
    rhs = ("far", "mate")
    in_specs = (
        P(rhs, "leaf"),
        P(None, "leaf"),
        P("leaf", rhs, None, None),
        P("leaf", rhs),
        P(),
        P("leaf", None),
        P("leaf", None, None, None),
        P("leaf", None, None, None),
        P(),
        P(),
    )
    return jax.shard_map(
        local, mesh=split, in_specs=in_specs, out_specs=P(rhs, "leaf"), check_vma=False
    )
```

```python
import functools

import jax
import jax.numpy as jnp
from jax import lax
from jax.experimental import pallas as pl
from jax.experimental.pallas import tpu as pltpu
from jax.sharding import Mesh
from jax.sharding import PartitionSpec as P

FACE_SIGNS = ((1, 0), (-1, 0), (1, 1), (-1, 1), (1, 2), (-1, 2))
F32 = jnp.float32
BF16 = jnp.bfloat16
LANES = 128
STEPS = 32000.0
VMEM = pl.BlockSpec(memory_space=pltpu.VMEM)
HBM = pl.BlockSpec(memory_space=pltpu.HBM)


def cube_side(device_count):
    return max((edge_len for edge_len in range(1, 65) if edge_len**3 <= device_count))


def face_offsets(device_count):
    side_len = cube_side(device_count)
    return [face_sign * side_len**axis_pos for face_sign, axis_pos in FACE_SIGNS]


def shifted(value, axis, steps):
    count = lax.axis_size(axis)
    first, last = (max(0, -steps), min(count, count - steps))
    return lax.ppermute(value, axis, [(source, source + steps) for source in range(first, last)])


def halves(value):
    high = value.astype(BF16)
    return high, (value - high.astype(F32)).astype(BF16)


def dot_nn(left, right):
    return lax.dot_general(left, right, (((1,), (0,)), ((), ())), preferred_element_type=F32)


def dot_nt(left, right):
    return lax.dot_general(left, right, (((1,), (1,)), ((), ())), preferred_element_type=F32)


def split_dot(dot, rows, right_high, right_low):
    count = rows.shape[0]
    high, low = halves(rows)
    both = jnp.concatenate([high, low], axis=0)
    out = dot(both, right_high) + dot(both, right_low)
    return out[:count] + out[count:]


def spread_bases(block, group):
    rank, lanes = block.shape
    width = lanes // group
    zero = jnp.zeros((rank, width), block.dtype)
    rows = []
    for slot in range(group):
        pieces = [zero] * group
        pieces[slot] = block[:, slot * width : (slot + 1) * width]
        rows.append(jnp.concatenate(pieces, axis=1))
    return jnp.concatenate(rows, axis=0)


def packed_words(table):
    words = []
    for first in range(0, table.shape[0], 4):
        word = table[first : first + 1]
        for row in range(first + 1, min(first + 4, table.shape[0])):
            word = word + (table[row : row + 1] << (8 * (row - first)))
        words.append(word)
    return words


def unpacked(words, count, place):
    values = [word[0, place] for word in words]
    return [(values[row // 4] >> (8 * (row % 4))) & 255 for row in range(count)]


def fetch(pairs, sems):
    copies = []
    for index, (source, target) in enumerate(pairs):
        copy = pltpu.make_async_copy(source, target, sems.at[index])
        copy.start()
        copies.append(copy)
    return copies


def up_kernel(
    maps_hbm, bases_hbm, *refs,
):
    count = (len(refs) - 8) // 2
    hbm_refs, bases_ref, vmem_refs = refs[:count], refs[count], refs[count + 1 : 2 * count + 1]
    high_ref, low_ref, root_ref, maps_ref, spread_ref, chain_ref, sems = refs[2 * count + 1 :]
    dens_ref = vmem_refs[0]
    copies = fetch(
        [(maps_hbm, maps_ref), (bases_hbm, bases_ref), *zip(hbm_refs, vmem_refs)], sems
    )
    columns, points = dens_ref.shape
    rank, _, node_count = maps_ref.shape
    group = LANES // rank
    leaf_count = node_count // 2
    width = points // leaf_count
    copies[0].wait()
    node = lax.broadcasted_iota(jnp.int32, (node_count, LANES), 0)
    block = lax.broadcasted_iota(jnp.int32, (node_count, LANES), 1) // rank
    parent = node // 2 % group
    for first in range(0, rank, group):
        slab = maps_ref[first : first + group].reshape(group * rank, node_count).T
        turned = [slab] + [pltpu.roll(slab, turn * rank, 1) for turn in range(1, group)]
        for row in range(group):
            placed = jnp.zeros_like(slab)
            for place in range(group):
                here = (parent == place) & (block == place)
                placed = jnp.where(here, turned[(place - row) % group], placed)
            spread_ref[pl.ds(first + row, node_count, stride=rank), :] = placed
    tile = 2 * group * rank

    def children(parents, index):
        high, low = halves(spread_ref[index * tile : (index + 1) * tile, :])
        return split_dot(dot_nt, parents, high, low)

    row = lax.broadcasted_iota(jnp.int32, (rank, LANES), 0)
    lane = lax.broadcasted_iota(jnp.int32, (rank, LANES), 1)
    level = 1
    parents = jnp.where(lane == row + rank, 1.0, 0.0)
    while level < group:
        below = children(parents, 0)
        level *= 2
        parents = below[:, (level // group) * LANES : (level // group + 1) * LANES]
    chain_ref[:, LANES : 2 * LANES] = parents
    while level < leaf_count:
        for index in range(level // group, 2 * level // group):
            lanes = slice(index * LANES, (index + 1) * LANES)
            chain_ref[:, index * tile : (index + 1) * tile] = children(chain_ref[:, lanes], index)
        level *= 2
    copies[1].wait()
    copies[2].wait()
    step = group * width
    root = jnp.zeros((columns, rank), F32)
    for index in range(leaf_count // group):
        spots = slice(index * step, (index + 1) * step)
        start = (leaf_count // group + index) * LANES
        high, low = halves(bases_ref[:, spots])
        basis = split_dot(
            dot_nn, chain_ref[:, start : start + LANES],
            spread_bases(high, group), spread_bases(low, group),
        )
        high, low = halves(basis)
        high_ref[:, spots] = high
        low_ref[:, spots] = low
        dens = dens_ref[:, spots]
        root += dot_nt(dens, high) + dot_nt(dens, low)
    root = jnp.concatenate([root, jnp.zeros((columns, LANES - rank), F32)], axis=1)
    high = root.astype(BF16).astype(F32)
    rest = root - high
    middle = rest.astype(BF16).astype(F32)
    last = (rest - middle).astype(BF16).astype(F32)
    packed = high + pltpu.roll(middle, rank, 1) + pltpu.roll(last, 2 * rank, 1)
    root_ref[...] = packed.astype(BF16)
    for copy in copies[3:]:
        copy.wait()


def select_kernel(
    faces, far_groups, send_ref, dens_ref, root_ref, *refs,
):
    other_refs, out_refs = refs[: far_groups - 1], refs[far_groups - 1 :]
    device = lax.axis_index("leaf")
    columns = dens_ref.shape[0]
    cap, device_count = send_ref.shape[1:]
    own = lax.broadcasted_iota(jnp.int32, (cap, device_count), 1) == device
    for (directions, stride), out_ref in zip(faces, out_refs):
        table = send_ref[directions[0]]
        if len(directions) > 1:
            table = jnp.where(device // stride % 2 == 0, table, send_ref[directions[1]])
        picks = jnp.max(jnp.where(own, table.astype(F32), 0.0), axis=1, keepdims=True)
        for place in range(cap):
            leaf = picks[place, 0].astype(jnp.int32)
            for part, panel_ref in enumerate((dens_ref, *other_refs)):
                row = (place * far_groups + part) * columns
                out_ref[row : row + columns, :] = panel_ref[
                    :, pl.ds(pl.multiple_of(leaf * LANES, LANES), LANES)
                ]
        out_ref[cap * far_groups * columns :, :] = root_ref[...]


def near_kernel(
    faces, far_groups, share, *refs,
):
    source_refs, refs = refs[:share], refs[share:]
    dens_ref, refs = refs[0], refs[1:]
    other_refs, refs = refs[: far_groups - 1], refs[far_groups - 1 :]
    got_refs, refs = refs[: len(faces)], refs[len(faces) :]
    block_ref, refs = refs[0], refs[1:]
    mate_refs, refs = refs[: share - 1], refs[share - 1 :]
    refs = refs[1:]
    out_refs, refs = refs[:far_groups], refs[far_groups:]
    sum_refs, refs = refs[: far_groups - 1], refs[far_groups - 1 :]
    peak_refs, refs = refs[: far_groups - 1], refs[far_groups - 1 :]
    (buffer_ref,) = refs
    columns, points = dens_ref.shape
    leaf_count, near_count, width, _ = block_ref.shape
    cap = (buffer_ref.shape[0] - leaf_count) // len(FACE_SIGNS)
    for (directions, _), got_ref in zip(faces, got_refs):
        for direction in directions:
            for place in range(cap):
                row = place * far_groups * columns
                buffer_ref[leaf_count + direction * cap + place] = got_ref[
                    row : row + far_groups * columns, :
                ]
    for part, panel_ref in enumerate((dens_ref, *other_refs)):
        rows = slice(part * columns, (part + 1) * columns)
        for leaf in range(leaf_count):
            buffer_ref[leaf, rows, :] = panel_ref[:, leaf * width : (leaf + 1) * width]
    tables = list(zip(source_refs[1:], mate_refs)) + [(source_refs[0], block_ref)]
    own_ref, sent_refs = out_refs[0], out_refs[1:]
    targets = (own_ref, *sum_refs)
    for turn, (source_ref, blocks_ref) in enumerate(tables):
        words = packed_words(source_ref[...])
        for leaf in range(leaf_count):
            panels = [buffer_ref[slot] for slot in unpacked(words, near_count, leaf)]
            blocks = [blocks_ref[leaf, block] for block in range(near_count)]
            total = dot_nt(jnp.concatenate(panels, axis=1), jnp.concatenate(blocks, axis=1))
            lanes = slice(leaf * width, (leaf + 1) * width)
            for part, target_ref in enumerate(targets):
                term = total[part * columns : (part + 1) * columns]
                if turn:
                    term = target_ref[:, lanes] + term
                target_ref[:, lanes] = term
                if part and turn == share - 1:
                    peak_refs[part - 1][leaf : leaf + 1, :] = jnp.max(
                        jnp.abs(term), axis=0, keepdims=True
                    )
    for sum_ref, peak_ref, sent_ref in zip(sum_refs, peak_refs, sent_refs):
        power = jnp.floor(jnp.log2(jnp.maximum(peak_ref[...], 2.0**-100))) + 1.0
        factor = STEPS * jnp.exp2(-power)
        for leaf in range(leaf_count):
            lanes = slice(leaf * width, (leaf + 1) * width)
            steps = sum_ref[:, lanes] * factor[leaf : leaf + 1, :]
            sent_ref[:, lanes] = jnp.floor(steps + 0.5).astype(jnp.int32).astype(jnp.int16)
        power = power.astype(jnp.int32).astype(jnp.int16)
        for first in range(0, leaf_count, columns):
            spot = points + first // columns * width
            sent_ref[:, spot : spot + width] = power[first : first + columns]


def coupled(leaves, table_ref, coupling_ref, turned_ref):
    far_count, rank = coupling_ref.shape[1:3]
    columns = turned_ref.shape[1] // 2
    group = LANES // rank
    words = packed_words(table_ref[...])
    parts = []
    for leaf in leaves:
        maps = jnp.concatenate([coupling_ref[leaf, j] for j in range(far_count)], axis=1)
        maps = jnp.concatenate(halves(maps), axis=0)
        picked = jnp.concatenate(
            [
                turned_ref[pl.ds(pl.multiple_of(source * rank, rank), rank), :]
                for source in unpacked(words, far_count, leaf)
            ],
            axis=0,
        )
        out = dot_nn(maps, picked)
        parts.append(out[:rank] + out[rank:])
        if len(parts) == group:
            turned = jnp.concatenate(parts, axis=0).T
            yield turned[:columns] + turned[columns:]
            parts = []


def couple_kernel(
    table_ref, coupling_ref, dens_ref, bases_ref, turned_ref, out_ref,
):
    columns, points = dens_ref.shape
    leaf_count, _, rank = coupling_ref.shape[:3]
    width = points // leaf_count
    upper = lax.broadcasted_iota(jnp.int32, (rank, 2 * columns), 1) < columns
    for leaf in range(leaf_count):
        spots = slice(leaf * width, (leaf + 1) * width)
        rows = jnp.concatenate(halves(bases_ref[:, spots]), axis=0)
        dens = dens_ref[:, spots]
        twice = dot_nt(rows, jnp.concatenate([dens, dens], axis=0))
        high, low = halves(twice[:rank] + twice[rank:])
        turned_ref[leaf * rank : (leaf + 1) * rank, :] = jnp.where(
            upper, high.astype(F32), low.astype(F32)
        ).astype(BF16)
    leaves = range(out_ref.shape[1] // rank)
    for index, field in enumerate(coupled(leaves, table_ref, coupling_ref, turned_ref)):
        out_ref[:, index * LANES : (index + 1) * LANES] = field


def project_kernel(
    table_ref, coupling_ref, turned_ref, first_ref, bases_ref, near_ref, out_ref,
):
    rank, points = bases_ref.shape
    leaf_count = coupling_ref.shape[0]
    group = LANES // rank
    step = group * points // leaf_count

    def project(index, field):
        spots = slice(index * step, (index + 1) * step)
        high, low = halves(bases_ref[:, spots])
        out_ref[:, spots] = near_ref[:, spots] + split_dot(
            dot_nn, field, spread_bases(high, group), spread_bases(low, group)
        )

    done = first_ref.shape[1] // LANES
    for index in range(done):
        project(index, first_ref[:, index * LANES : (index + 1) * LANES])
    leaves = range(done * group, leaf_count)
    for index, field in enumerate(coupled(leaves, table_ref, coupling_ref, turned_ref)):
        project(done + index, field)


def far_kernel(
    roots, upper_ref, cross_ref, high_ref, low_ref, term_ref, *refs,
):
    root_refs, refs = refs[: len(roots)], refs[len(roots) :]
    out_ref, tile_ref, tree_ref = refs
    device = lax.axis_index("leaf")
    columns, points = out_ref.shape
    rank = upper_ref.shape[1]
    device_count = upper_ref.shape[0] // 2
    for tiles, root_ref in zip(roots, root_refs):
        if tiles is None:
            for index in range(device_count):
                tile_ref[index] = root_ref[index]
        else:
            for turn, row in tiles:
                tile_ref[device ^ turn] = root_ref[row : row + columns, :]
    zero = jnp.zeros((LANES - 3 * rank, rank), BF16)

    def lifted(child):
        if child >= device_count:
            high, low = (
                jnp.concatenate([half] * 3 + [zero], axis=0) for half in halves(upper_ref[child])
            )
            tile = tile_ref[child - device_count]
            return dot_nn(tile, high) + dot_nn(tile, low)
        return split_dot(dot_nn, tree_ref[child], *halves(upper_ref[child]))

    level = device_count // 2
    while level >= 4:
        for node in range(level, 2 * level):
            tree_ref[node] = lifted(2 * node) + lifted(2 * node + 1)
        level //= 2
    lane = lax.broadcasted_iota(jnp.int32, (LANES, rank), 0)
    column = lax.broadcasted_iota(jnp.int32, (LANES, rank), 1)
    gather = jnp.where((lane % rank == column) & (lane < 3 * rank), 1.0, 0.0).astype(BF16)
    field = None
    level = 4
    while level <= device_count:
        place = device // (device_count // level)
        node = level + place
        third = jnp.where(place % 2 == 0, place + 3, place - 3)
        total = None
        for slot, other in enumerate((place - 2, place + 2, third)):
            inside = (other >= 0) & (other < level)
            other = jnp.clip(other, 0, level - 1)
            if level == device_count:
                value = dot_nn(tile_ref[other], gather)
            else:
                value = tree_ref[level + other]
            value = jnp.where(inside, value, 0.0)
            term = split_dot(dot_nt, value, *halves(cross_ref[node, slot]))
            total = term if total is None else total + term
        if field is not None:
            total = total + split_dot(dot_nt, field, *halves(upper_ref[node]))
        field = total
        level *= 2
    step = 4 * LANES
    for first in range(0, points, step):
        spots = slice(first, first + step)
        out_ref[:, spots] = term_ref[:, spots] + split_dot(
            dot_nn, field, high_ref[:, spots], low_ref[:, spots]
        )


def add_kernel(leaf_count, term_ref, *refs):
    sent_refs, (out_hbm, sum_ref, sems) = refs[:-3], refs[-3:]
    columns, points = sum_ref.shape
    width = points // leaf_count
    factors = []
    for sent_ref in sent_refs:
        powers = [
            sent_ref[:, points + first // columns * width :][:, :width]
            for first in range(0, leaf_count, columns)
        ]
        power = jnp.concatenate([p.astype(jnp.int32).astype(F32) for p in powers], axis=0)
        factors.append(jnp.exp2(power) * (1.0 / STEPS))
    chunk_count = sems.shape[0]
    step = points // chunk_count
    copies = []
    for index in range(chunk_count):
        spots = slice(index * step, (index + 1) * step)
        total = term_ref[:, spots]
        for sent_ref, factor in zip(sent_refs, factors):
            steps = sent_ref[:, spots].astype(jnp.int32).astype(F32)
            leaves = range(index * leaf_count // chunk_count, (index + 1) * leaf_count // chunk_count)
            scale = jnp.concatenate([factor[leaf : leaf + 1] for leaf in leaves], axis=1)
            total = total + steps * scale
        sum_ref[:, spots] = total
        copies += fetch(
            [(sum_ref.at[:, pl.ds(index * step, step)], out_hbm.at[:, pl.ds(index * step, step)])],
            sems.at[pl.ds(index, 1)],
        )
    for copy in copies:
        copy.wait()


def hbm(value):
    return pltpu.with_memory_space_constraint(value, pltpu.HBM)


def hint(micros):
    return pl.CostEstimate(flops=0, bytes_accessed=int(micros * 3.69e6), transcendentals=0)


def local(
    densities,
    bases,
    near_blocks,
    near_src,
    send_leaf,
    far_src,
    leaf_coupling,
    local_transfer,
    upper_transfer,
    up_coupling,
):
    leaf_devices = lax.axis_size("leaf")
    far_groups = lax.axis_size("far")
    share = lax.axis_size("mate")
    side = cube_side(leaf_devices)
    offsets = face_offsets(leaf_devices)
    columns, points = densities.shape
    leaf_count, near_count, width, _ = near_blocks.shape
    rank = bases.shape[0]
    cap = send_leaf.shape[2]
    node_count = local_transfer.shape[1]
    params = pltpu.CompilerParams(vmem_limit_bytes=16 * 2**20)
    dma = pltpu.SemaphoreType.DMA

    def rotated(value, axis, shift):
        count = lax.axis_size(axis)
        return lax.ppermute(value, axis, [(i, (i - shift) % count) for i in range(count)])

    def crossed(value, turn):
        return lax.ppermute(value, "leaf", [(i, i ^ turn) for i in range(leaf_devices)])

    sources = near_src.T
    others = [rotated(densities, "far", part) for part in range(1, far_groups)]
    all_sources = [sources] + [rotated(sources, "mate", part) for part in range(1, share)]
    send = send_leaf.transpose(1, 2, 0)
    moved = [densities, send, sources, far_src.T, leaf_coupling, near_blocks]
    basis, dens, send, sources, far_table, coupling, blocks, high, low, root = pl.pallas_call(
        up_kernel,
        out_shape=[jax.ShapeDtypeStruct(value.shape, value.dtype) for value in (bases, *moved)]
        + [
            jax.ShapeDtypeStruct((rank, points), BF16),
            jax.ShapeDtypeStruct((rank, points), BF16),
            jax.ShapeDtypeStruct((columns, LANES), BF16),
        ],
        in_specs=[HBM] * (2 + len(moved)),
        out_specs=[VMEM] * (4 + len(moved)),
        scratch_shapes=[
            pltpu.VMEM((rank, rank, node_count), F32),
            pltpu.VMEM((node_count * rank, LANES), F32),
            pltpu.VMEM((rank, node_count * rank), F32),
            dma((2 + len(moved),)),
        ],
        compiler_params=params,
        cost_estimate=hint(3.5),
        name="up",
    )(hbm(local_transfer[0].transpose(1, 2, 0)), hbm(bases), *map(hbm, moved))
    all_sources[0] = sources

    later_blocks, others, all_sources, root = lax.optimization_barrier(
        (blocks, others, all_sources, root)
    )
    mate_blocks = [rotated(later_blocks, "mate", part) for part in range(1, share)]

    if side == 2:
        faces = [((2 * axis, 2 * axis + 1), 2**axis) for axis in (2, 0, 1)]
    else:
        faces = [((direction,), offset) for direction, offset in enumerate(offsets)]
    chunk = (cap * far_groups + 1) * columns
    outgoing = pl.pallas_call(
        functools.partial(select_kernel, faces, far_groups),
        out_shape=[jax.ShapeDtypeStruct((chunk, LANES), BF16)] * len(faces),
        in_specs=[VMEM] * (2 + far_groups),
        out_specs=[VMEM] * len(faces),
        compiler_params=params,
        cost_estimate=hint(1),
        name="select",
    )(send, dens, root, *others)
    outgoing, dens = lax.optimization_barrier((outgoing, dens))
    first_leaves = leaf_count // 2
    turned, leaf_local = pl.pallas_call(
        couple_kernel,
        out_shape=[
            jax.ShapeDtypeStruct((leaf_count * rank, 2 * columns), BF16),
            jax.ShapeDtypeStruct((columns, first_leaves * rank), F32),
        ],
        in_specs=[VMEM] * 4,
        out_specs=[VMEM] * 2,
        compiler_params=params,
        cost_estimate=hint(2),
        name="couple",
    )(far_table, coupling, dens, basis)
    tail = cap * far_groups * columns
    if side == 2:
        arrived = [crossed(value, stride) for (_, stride), value in zip(faces, outgoing)]
        far_one, near_one, _ = (value[tail : tail + columns] for value in arrived)
        later, leaf_local = lax.optimization_barrier((arrived[0][-4 * columns :], leaf_local))
        across = crossed(later, 1)
        held = jnp.concatenate([near_one, far_one, across[-columns:]], axis=0)
        beside = crossed(held, 2)
        roots = [([(0, 0)], root), ([(5, 3 * columns)], across)]
        roots += [([(stride, tail)], value) for (_, stride), value in zip(faces, arrived)]
        roots.append(([(3, 0), (6, columns), (7, 2 * columns)], beside))
    else:
        arrived = [shifted(value, "leaf", stride) for (_, stride), value in zip(faces, outgoing)]
        roots = [(None, lax.all_gather(root, "leaf", axis=0))]

    slots = leaf_count + len(offsets) * cap
    tables = -(-leaf_count // columns) * width
    partials = pl.pallas_call(
        functools.partial(near_kernel, faces, far_groups, share),
        out_shape=[jax.ShapeDtypeStruct((columns, points), F32)]
        + [jax.ShapeDtypeStruct((columns, points + tables), jnp.int16)] * (far_groups - 1),
        in_specs=[VMEM] * (2 * share + far_groups + len(faces) + 1),
        out_specs=[VMEM] * far_groups,
        scratch_shapes=[pltpu.VMEM((columns, points), F32)] * (far_groups - 1)
        + [pltpu.VMEM((leaf_count, width), F32)] * (far_groups - 1)
        + [
            pltpu.VMEM((slots, far_groups * columns, width), BF16),
        ],
        compiler_params=params,
        cost_estimate=hint(3),
        name="near",
    )(
        *all_sources, dens, *others, *arrived, blocks, *mate_blocks, leaf_local,
    )
    received = [rotated(partials[part], "far", -part) for part in range(1, far_groups)]
    partial = pl.pallas_call(
        project_kernel,
        out_shape=jax.ShapeDtypeStruct((columns, points), F32),
        in_specs=[VMEM] * 6,
        out_specs=VMEM,
        compiler_params=params,
        cost_estimate=hint(1.5),
        name="project",
    )(far_table, coupling, turned, leaf_local, basis, partials[0])
    total = pl.pallas_call(
        functools.partial(far_kernel, [tiles for tiles, _ in roots]),
        out_shape=jax.ShapeDtypeStruct((columns, points), F32),
        in_specs=[VMEM] * (5 + len(roots)),
        out_specs=VMEM,
        scratch_shapes=[
            pltpu.VMEM((leaf_devices, columns, LANES), BF16),
            pltpu.VMEM((2 * leaf_devices, columns, rank), F32),
        ],
        compiler_params=params,
        cost_estimate=hint(1),
        name="far",
    )(upper_transfer, up_coupling, high, low, partial, *[value for _, value in roots])
    return pl.pallas_call(
        functools.partial(add_kernel, leaf_count),
        out_shape=jax.ShapeDtypeStruct((columns, points), F32),
        in_specs=[VMEM] * (1 + len(received)),
        out_specs=HBM,
        scratch_shapes=[pltpu.VMEM((columns, points), F32), dma((4,))],
        compiler_params=params,
        cost_estimate=hint(0.5),
        name="add",
    )(total, *received)


def solution(mesh):
    leaf_devices, rhs_devices = mesh.shape["leaf"], mesh.shape["rhs"]
    share = 2 if rhs_devices % 2 == 0 else 1
    split = Mesh(
        mesh.devices.reshape(leaf_devices, rhs_devices // share, share), ("leaf", "far", "mate")
    )
    rhs = ("far", "mate")
    in_specs = (
        P(rhs, "leaf"),
        P(None, "leaf"),
        P("leaf", rhs, None, None),
        P("leaf", rhs),
        P(),
        P("leaf", None),
        P("leaf", None, None, None),
        P("leaf", None, None, None),
        P(),
        P(),
    )
    return jax.shard_map(
        local, mesh=split, in_specs=in_specs, out_specs=P(rhs, "leaf"), check_vma=False
    )
```

```python
import functools

import jax
import jax.numpy as jnp
from jax import lax
from jax.experimental import pallas as pl
from jax.experimental.pallas import tpu as pltpu
from jax.sharding import Mesh
from jax.sharding import PartitionSpec as P

FACE_SIGNS = ((1, 0), (-1, 0), (1, 1), (-1, 1), (1, 2), (-1, 2))
F32 = jnp.float32
BF16 = jnp.bfloat16
LANES = 128
STEPS = 32000.0
VMEM = pl.BlockSpec(memory_space=pltpu.VMEM)
HBM = pl.BlockSpec(memory_space=pltpu.HBM)


def cube_side(device_count):
    return max((edge_len for edge_len in range(1, 65) if edge_len**3 <= device_count))


def face_offsets(device_count):
    side_len = cube_side(device_count)
    return [face_sign * side_len**axis_pos for face_sign, axis_pos in FACE_SIGNS]


def shifted(value, axis, steps):
    count = lax.axis_size(axis)
    first, last = (max(0, -steps), min(count, count - steps))
    return lax.ppermute(value, axis, [(source, source + steps) for source in range(first, last)])


def halves(value):
    high = value.astype(BF16)
    return high, (value - high.astype(F32)).astype(BF16)


def dot_nn(left, right):
    return lax.dot_general(left, right, (((1,), (0,)), ((), ())), preferred_element_type=F32)


def dot_nt(left, right):
    return lax.dot_general(left, right, (((1,), (1,)), ((), ())), preferred_element_type=F32)


def split_dot(dot, rows, right_high, right_low):
    count = rows.shape[0]
    high, low = halves(rows)
    both = jnp.concatenate([high, low], axis=0)
    out = dot(both, right_high) + dot(both, right_low)
    return out[:count] + out[count:]


def spread_bases(block, group):
    rank, lanes = block.shape
    width = lanes // group
    zero = jnp.zeros((rank, width), block.dtype)
    rows = []
    for slot in range(group):
        pieces = [zero] * group
        pieces[slot] = block[:, slot * width : (slot + 1) * width]
        rows.append(jnp.concatenate(pieces, axis=1))
    return jnp.concatenate(rows, axis=0)


def packed_words(table):
    words = []
    for first in range(0, table.shape[0], 4):
        word = table[first : first + 1]
        for row in range(first + 1, min(first + 4, table.shape[0])):
            word = word + (table[row : row + 1] << (8 * (row - first)))
        words.append(word)
    return words


def unpacked(words, count, place):
    values = [word[0, place] for word in words]
    return [(values[row // 4] >> (8 * (row % 4))) & 255 for row in range(count)]


def fetch(pairs, sems):
    copies = []
    for index, (source, target) in enumerate(pairs):
        copy = pltpu.make_async_copy(source, target, sems.at[index])
        copy.start()
        copies.append(copy)
    return copies


def up_kernel(
    maps_hbm, bases_hbm, *refs,
):
    count = (len(refs) - 8) // 2
    hbm_refs, bases_ref, vmem_refs = refs[:count], refs[count], refs[count + 1 : 2 * count + 1]
    high_ref, low_ref, root_ref, maps_ref, spread_ref, chain_ref, sems = refs[2 * count + 1 :]
    dens_ref = vmem_refs[0]
    copies = fetch(
        [(maps_hbm, maps_ref), (bases_hbm, bases_ref), *zip(hbm_refs, vmem_refs)], sems
    )
    columns, points = dens_ref.shape
    rank, _, node_count = maps_ref.shape
    group = LANES // rank
    leaf_count = node_count // 2
    width = points // leaf_count
    copies[0].wait()
    node = lax.broadcasted_iota(jnp.int32, (node_count, LANES), 0)
    block = lax.broadcasted_iota(jnp.int32, (node_count, LANES), 1) // rank
    parent = node // 2 % group
    for first in range(0, rank, group):
        slab = maps_ref[first : first + group].reshape(group * rank, node_count).T
        turned = [slab] + [pltpu.roll(slab, turn * rank, 1) for turn in range(1, group)]
        for row in range(group):
            placed = jnp.zeros_like(slab)
            for place in range(group):
                here = (parent == place) & (block == place)
                placed = jnp.where(here, turned[(place - row) % group], placed)
            spread_ref[pl.ds(first + row, node_count, stride=rank), :] = placed
    tile = 2 * group * rank

    def children(parents, index):
        high, low = halves(spread_ref[index * tile : (index + 1) * tile, :])
        return split_dot(dot_nt, parents, high, low)

    row = lax.broadcasted_iota(jnp.int32, (rank, LANES), 0)
    lane = lax.broadcasted_iota(jnp.int32, (rank, LANES), 1)
    level = 1
    parents = jnp.where(lane == row + rank, 1.0, 0.0)
    while level < group:
        below = children(parents, 0)
        level *= 2
        parents = below[:, (level // group) * LANES : (level // group + 1) * LANES]
    chain_ref[:, LANES : 2 * LANES] = parents
    while level < leaf_count:
        for index in range(level // group, 2 * level // group):
            lanes = slice(index * LANES, (index + 1) * LANES)
            chain_ref[:, index * tile : (index + 1) * tile] = children(chain_ref[:, lanes], index)
        level *= 2
    copies[1].wait()
    copies[2].wait()
    step = group * width
    root = jnp.zeros((columns, rank), F32)
    for index in range(leaf_count // group):
        spots = slice(index * step, (index + 1) * step)
        start = (leaf_count // group + index) * LANES
        high, low = halves(bases_ref[:, spots])
        basis = split_dot(
            dot_nn, chain_ref[:, start : start + LANES],
            spread_bases(high, group), spread_bases(low, group),
        )
        high, low = halves(basis)
        high_ref[:, spots] = high
        low_ref[:, spots] = low
        dens = dens_ref[:, spots]
        root += dot_nt(dens, high) + dot_nt(dens, low)
    root = jnp.concatenate([root, jnp.zeros((columns, LANES - rank), F32)], axis=1)
    high = root.astype(BF16).astype(F32)
    rest = root - high
    middle = rest.astype(BF16).astype(F32)
    last = (rest - middle).astype(BF16).astype(F32)
    packed = high + pltpu.roll(middle, rank, 1) + pltpu.roll(last, 2 * rank, 1)
    root_ref[...] = packed.astype(BF16)
    for copy in copies[3:]:
        copy.wait()


def select_kernel(
    faces, far_groups, send_ref, dens_ref, root_ref, *refs,
):
    other_refs, out_refs = refs[: far_groups - 1], refs[far_groups - 1 :]
    device = lax.axis_index("leaf")
    columns = dens_ref.shape[0]
    cap, device_count = send_ref.shape[1:]
    own = lax.broadcasted_iota(jnp.int32, (cap, device_count), 1) == device
    for (directions, stride), out_ref in zip(faces, out_refs):
        table = send_ref[directions[0]]
        if len(directions) > 1:
            table = jnp.where(device // stride % 2 == 0, table, send_ref[directions[1]])
        picks = jnp.max(jnp.where(own, table.astype(F32), 0.0), axis=1, keepdims=True)
        for place in range(cap):
            leaf = picks[place, 0].astype(jnp.int32)
            for part, panel_ref in enumerate((dens_ref, *other_refs)):
                row = (place * far_groups + part) * columns
                out_ref[row : row + columns, :] = panel_ref[
                    :, pl.ds(pl.multiple_of(leaf * LANES, LANES), LANES)
                ]
        out_ref[cap * far_groups * columns :, :] = root_ref[...]


def near_kernel(
    faces, far_groups, share, *refs,
):
    source_refs, refs = refs[:share], refs[share:]
    dens_ref, refs = refs[0], refs[1:]
    other_refs, refs = refs[: far_groups - 1], refs[far_groups - 1 :]
    got_refs, refs = refs[: len(faces)], refs[len(faces) :]
    block_ref, refs = refs[0], refs[1:]
    mate_refs, refs = refs[: share - 1], refs[share - 1 :]
    refs = refs[2:]
    out_refs, refs = refs[:far_groups], refs[far_groups:]
    sum_refs, refs = refs[: far_groups - 1], refs[far_groups - 1 :]
    peak_refs, refs = refs[: far_groups - 1], refs[far_groups - 1 :]
    (buffer_ref,) = refs
    columns, points = dens_ref.shape
    leaf_count, near_count, width, _ = block_ref.shape
    cap = (buffer_ref.shape[0] - leaf_count) // len(FACE_SIGNS)
    for (directions, _), got_ref in zip(faces, got_refs):
        for direction in directions:
            for place in range(cap):
                row = place * far_groups * columns
                buffer_ref[leaf_count + direction * cap + place] = got_ref[
                    row : row + far_groups * columns, :
                ]
    for part, panel_ref in enumerate((dens_ref, *other_refs)):
        rows = slice(part * columns, (part + 1) * columns)
        for leaf in range(leaf_count):
            buffer_ref[leaf, rows, :] = panel_ref[:, leaf * width : (leaf + 1) * width]
    words = [packed_words(source_ref[...]) for source_ref in source_refs]
    own_ref, sent_refs = out_refs[0], out_refs[1:]
    targets = (own_ref, *sum_refs)
    for leaf in range(leaf_count):
        panels, blocks = [], []
        for word, blocks_ref in zip(words, (block_ref, *mate_refs)):
            panels += [buffer_ref[slot] for slot in unpacked(word, near_count, leaf)]
            blocks += [blocks_ref[leaf, block] for block in range(near_count)]
        total = dot_nt(jnp.concatenate(panels, axis=1), jnp.concatenate(blocks, axis=1))
        lanes = slice(leaf * width, (leaf + 1) * width)
        for part, target_ref in enumerate(targets):
            term = total[part * columns : (part + 1) * columns]
            target_ref[:, lanes] = term
            if part:
                peak_refs[part - 1][leaf : leaf + 1, :] = jnp.max(
                    jnp.abs(term), axis=0, keepdims=True
                )
    for sum_ref, peak_ref, sent_ref in zip(sum_refs, peak_refs, sent_refs):
        power = jnp.floor(jnp.log2(jnp.maximum(peak_ref[...], 2.0**-100))) + 1.0
        factor = STEPS * jnp.exp2(-power)
        for leaf in range(leaf_count):
            lanes = slice(leaf * width, (leaf + 1) * width)
            steps = sum_ref[:, lanes] * factor[leaf : leaf + 1, :]
            sent_ref[:, lanes] = jnp.floor(steps + 0.5).astype(jnp.int32).astype(jnp.int16)
        power = power.astype(jnp.int32).astype(jnp.int16)
        for first in range(0, leaf_count, columns):
            spot = points + first // columns * width
            sent_ref[:, spot : spot + width] = power[first : first + columns]


def coupled(leaves, table_ref, coupling_ref, turned_ref):
    far_count, rank = coupling_ref.shape[1:3]
    columns = turned_ref.shape[1] // 2
    group = LANES // rank
    words = packed_words(table_ref[...])
    parts = []
    for leaf in leaves:
        maps = jnp.concatenate([coupling_ref[leaf, j] for j in range(far_count)], axis=1)
        maps = jnp.concatenate(halves(maps), axis=0)
        picked = jnp.concatenate(
            [
                turned_ref[pl.ds(pl.multiple_of(source * rank, rank), rank), :]
                for source in unpacked(words, far_count, leaf)
            ],
            axis=0,
        )
        out = dot_nn(maps, picked)
        parts.append(out[:rank] + out[rank:])
        if len(parts) == group:
            turned = jnp.concatenate(parts, axis=0).T
            yield turned[:columns] + turned[columns:]
            parts = []


def couple_kernel(
    table_ref, coupling_ref, dens_ref, bases_ref, turned_ref, out_ref,
):
    columns, points = dens_ref.shape
    leaf_count, _, rank = coupling_ref.shape[:3]
    width = points // leaf_count
    upper = lax.broadcasted_iota(jnp.int32, (rank, 2 * columns), 1) < columns
    for leaf in range(leaf_count):
        spots = slice(leaf * width, (leaf + 1) * width)
        rows = jnp.concatenate(halves(bases_ref[:, spots]), axis=0)
        dens = dens_ref[:, spots]
        twice = dot_nt(rows, jnp.concatenate([dens, dens], axis=0))
        high, low = halves(twice[:rank] + twice[rank:])
        turned_ref[leaf * rank : (leaf + 1) * rank, :] = jnp.where(
            upper, high.astype(F32), low.astype(F32)
        ).astype(BF16)
    leaves = range(out_ref.shape[1] // rank)
    for index, field in enumerate(coupled(leaves, table_ref, coupling_ref, turned_ref)):
        out_ref[:, index * LANES : (index + 1) * LANES] = field


def project_kernel(
    table_ref, coupling_ref, turned_ref, first_ref, bases_ref, near_ref, out_ref,
):
    rank, points = bases_ref.shape
    leaf_count = coupling_ref.shape[0]
    group = LANES // rank
    step = group * points // leaf_count

    def project(index, field):
        spots = slice(index * step, (index + 1) * step)
        high, low = halves(bases_ref[:, spots])
        out_ref[:, spots] = near_ref[:, spots] + split_dot(
            dot_nn, field, spread_bases(high, group), spread_bases(low, group)
        )

    done = first_ref.shape[1] // LANES
    for index in range(done):
        project(index, first_ref[:, index * LANES : (index + 1) * LANES])
    leaves = range(done * group, leaf_count)
    for index, field in enumerate(coupled(leaves, table_ref, coupling_ref, turned_ref)):
        project(done + index, field)


def paths_kernel(turns, exchanged, upper_ref, cross_ref, high_ref, low_ref, map_ref):
    device = lax.axis_index("leaf")
    rank = upper_ref.shape[1]
    device_count = upper_ref.shape[0] // 2
    downs = {device_count: None}
    level = device_count
    while level > 4:
        node = level + device // (device_count // level)
        below = downs[level]
        matrix = upper_ref[node]
        downs[level // 2] = matrix if below is None else split_dot(dot_nn, below, *halves(matrix))
        level //= 2
    for level in sorted(downs):
        place = device // (device_count // level)
        for index in range(level):
            if level == 4:
                map_ref[level + index] = jnp.zeros((rank, rank), F32)
            else:
                above = map_ref[(level + index) // 2]
                map_ref[level + index] = split_dot(
                    dot_nt, above, *halves(upper_ref[level + index])
                )
        third = jnp.where(place % 2 == 0, place + 3, place - 3)
        for slot, other in enumerate((place - 2, place + 2, third)):
            inside = (other >= 0) & (other < level)
            matrix = cross_ref[level + place, slot]
            if downs[level] is not None:
                matrix = split_dot(dot_nn, downs[level], *halves(matrix))
            node = level + jnp.clip(other, 0, level - 1)
            map_ref[node] = map_ref[node] + jnp.where(inside, matrix, 0.0)
    zero = jnp.zeros((rank, LANES - 3 * rank), F32)
    for place, turn in enumerate(turns):
        matrix = map_ref[device_count + (device ^ turn if exchanged else turn)]
        matrix = jnp.concatenate([matrix] * 3 + [zero], axis=1)
        high, low = halves(matrix)
        high_ref[:, place * LANES : (place + 1) * LANES] = high
        low_ref[:, place * LANES : (place + 1) * LANES] = low


def far_kernel(
    tiles, path_high_ref, path_low_ref, high_ref, low_ref, term_ref, *refs,
):
    root_refs, out_ref = refs[:-1], refs[-1]
    columns, points = out_ref.shape
    pieces = []
    for rows, root_ref in zip(tiles, root_refs):
        pieces += [root_ref[row : row + columns, :] for row in rows]
    roots = jnp.concatenate(pieces, axis=1)
    field = dot_nt(roots, path_high_ref[...]) + dot_nt(roots, path_low_ref[...])
    step = 4 * LANES
    for first in range(0, points, step):
        spots = slice(first, first + step)
        out_ref[:, spots] = term_ref[:, spots] + split_dot(
            dot_nn, field, high_ref[:, spots], low_ref[:, spots]
        )


def add_kernel(leaf_count, term_ref, *refs):
    sent_refs, (out_hbm, sum_ref, sems) = refs[:-3], refs[-3:]
    columns, points = sum_ref.shape
    width = points // leaf_count
    factors = []
    for sent_ref in sent_refs:
        powers = [
            sent_ref[:, points + first // columns * width :][:, :width]
            for first in range(0, leaf_count, columns)
        ]
        power = jnp.concatenate([p.astype(jnp.int32).astype(F32) for p in powers], axis=0)
        factors.append(jnp.exp2(power) * (1.0 / STEPS))
    chunk_count = sems.shape[0]
    step = points // chunk_count
    copies = []
    for index in range(chunk_count):
        spots = slice(index * step, (index + 1) * step)
        total = term_ref[:, spots]
        for sent_ref, factor in zip(sent_refs, factors):
            steps = sent_ref[:, spots].astype(jnp.int32).astype(F32)
            leaves = range(index * leaf_count // chunk_count, (index + 1) * leaf_count // chunk_count)
            scale = jnp.concatenate([factor[leaf : leaf + 1] for leaf in leaves], axis=1)
            total = total + steps * scale
        sum_ref[:, spots] = total
        copies += fetch(
            [(sum_ref.at[:, pl.ds(index * step, step)], out_hbm.at[:, pl.ds(index * step, step)])],
            sems.at[pl.ds(index, 1)],
        )
    for copy in copies:
        copy.wait()


def hbm(value):
    return pltpu.with_memory_space_constraint(value, pltpu.HBM)


def hint(micros):
    return pl.CostEstimate(flops=0, bytes_accessed=int(micros * 3.69e6), transcendentals=0)


def local(
    densities,
    bases,
    near_blocks,
    near_src,
    send_leaf,
    far_src,
    leaf_coupling,
    local_transfer,
    upper_transfer,
    up_coupling,
):
    leaf_devices = lax.axis_size("leaf")
    far_groups = lax.axis_size("far")
    share = lax.axis_size("mate")
    side = cube_side(leaf_devices)
    offsets = face_offsets(leaf_devices)
    columns, points = densities.shape
    leaf_count, near_count, width, _ = near_blocks.shape
    rank = bases.shape[0]
    cap = send_leaf.shape[2]
    node_count = local_transfer.shape[1]
    params = pltpu.CompilerParams(vmem_limit_bytes=16 * 2**20)
    dma = pltpu.SemaphoreType.DMA

    def rotated(value, axis, shift):
        count = lax.axis_size(axis)
        return lax.ppermute(value, axis, [(i, (i - shift) % count) for i in range(count)])

    def crossed(value, turn):
        return lax.ppermute(value, "leaf", [(i, i ^ turn) for i in range(leaf_devices)])

    sources = near_src.T
    others = [rotated(densities, "far", part) for part in range(1, far_groups)]
    all_sources = [sources] + [rotated(sources, "mate", part) for part in range(1, share)]
    send = send_leaf.transpose(1, 2, 0)
    moved = [
        densities, send, sources, far_src.T, upper_transfer, up_coupling, leaf_coupling, near_blocks,
    ]
    (
        basis, dens, send, sources, far_table, upper, cross, coupling, blocks, high, low, root,
    ) = pl.pallas_call(
        up_kernel,
        out_shape=[jax.ShapeDtypeStruct(value.shape, value.dtype) for value in (bases, *moved)]
        + [
            jax.ShapeDtypeStruct((rank, points), BF16),
            jax.ShapeDtypeStruct((rank, points), BF16),
            jax.ShapeDtypeStruct((columns, LANES), BF16),
        ],
        in_specs=[HBM] * (2 + len(moved)),
        out_specs=[VMEM] * (4 + len(moved)),
        scratch_shapes=[
            pltpu.VMEM((rank, rank, node_count), F32),
            pltpu.VMEM((node_count * rank, LANES), F32),
            pltpu.VMEM((rank, node_count * rank), F32),
            dma((2 + len(moved),)),
        ],
        compiler_params=params,
        cost_estimate=hint(3.5),
        name="up",
    )(hbm(local_transfer[0].transpose(1, 2, 0)), hbm(bases), *map(hbm, moved))
    all_sources[0] = sources

    later_blocks, others, all_sources, root = lax.optimization_barrier(
        (blocks, others, all_sources, root)
    )
    mate_blocks = [rotated(later_blocks, "mate", part) for part in range(1, share)]

    if side == 2:
        faces = [((2 * axis, 2 * axis + 1), 2**axis) for axis in (2, 0, 1)]
    else:
        faces = [((direction,), offset) for direction, offset in enumerate(offsets)]
    chunk = (cap * far_groups + 1) * columns
    outgoing = pl.pallas_call(
        functools.partial(select_kernel, faces, far_groups),
        out_shape=[jax.ShapeDtypeStruct((chunk, LANES), BF16)] * len(faces),
        in_specs=[VMEM] * (2 + far_groups),
        out_specs=[VMEM] * len(faces),
        compiler_params=params,
        cost_estimate=hint(1),
        name="select",
    )(send, dens, root, *others)
    outgoing, dens = lax.optimization_barrier((outgoing, dens))
    first_leaves = leaf_count // 2
    turned, leaf_local = pl.pallas_call(
        couple_kernel,
        out_shape=[
            jax.ShapeDtypeStruct((leaf_count * rank, 2 * columns), BF16),
            jax.ShapeDtypeStruct((columns, first_leaves * rank), F32),
        ],
        in_specs=[VMEM] * 4,
        out_specs=[VMEM] * 2,
        compiler_params=params,
        cost_estimate=hint(2),
        name="couple",
    )(far_table, coupling, dens, basis)
    tail = cap * far_groups * columns
    if side == 2:
        arrived = [crossed(value, stride) for (_, stride), value in zip(faces, outgoing)]
        far_one, _, near_two = (value[tail : tail + columns] for value in arrived)
        later, leaf_local = lax.optimization_barrier((arrived[0][-4 * columns :], leaf_local))
        across = crossed(later, 2)
        held = jnp.concatenate([near_two, far_one, across[-columns:]], axis=0)
        beside = crossed(held, 1)
        turns = [0] + [stride for _, stride in faces] + [6, 3, 5, 7]
        roots = [([0], root)] + [([tail], value) for value in arrived]
        roots += [([3 * columns], across), ([0, columns, 2 * columns], beside)]
    else:
        arrived = [shifted(value, "leaf", stride) for (_, stride), value in zip(faces, outgoing)]
        turns = list(range(leaf_devices))
        everyone = lax.all_gather(root, "leaf", axis=0, tiled=True)
        roots = [([turn * columns for turn in turns], everyone)]
    paths = pl.pallas_call(
        functools.partial(paths_kernel, turns, side == 2),
        out_shape=[jax.ShapeDtypeStruct((rank, leaf_devices * LANES), BF16)] * 2,
        in_specs=[VMEM] * 2,
        out_specs=[VMEM] * 2,
        scratch_shapes=[pltpu.VMEM((2 * leaf_devices, rank, rank), F32)],
        compiler_params=params,
        cost_estimate=hint(0.7),
        name="paths",
    )(upper, cross)

    slots = leaf_count + len(offsets) * cap
    tables = -(-leaf_count // columns) * width
    partials = pl.pallas_call(
        functools.partial(near_kernel, faces, far_groups, share),
        out_shape=[jax.ShapeDtypeStruct((columns, points), F32)]
        + [jax.ShapeDtypeStruct((columns, points + tables), jnp.int16)] * (far_groups - 1),
        in_specs=[VMEM] * (2 * share + far_groups + len(faces) + 2),
        out_specs=[VMEM] * far_groups,
        scratch_shapes=[pltpu.VMEM((columns, points), F32)] * (far_groups - 1)
        + [pltpu.VMEM((leaf_count, width), F32)] * (far_groups - 1)
        + [
            pltpu.VMEM((slots, far_groups * columns, width), BF16),
        ],
        compiler_params=params,
        cost_estimate=hint(3),
        name="near",
    )(
        *all_sources, dens, *others, *arrived, blocks, *mate_blocks, leaf_local, paths[0],
    )
    received = [rotated(partials[part], "far", -part) for part in range(1, far_groups)]
    partial = pl.pallas_call(
        project_kernel,
        out_shape=jax.ShapeDtypeStruct((columns, points), F32),
        in_specs=[VMEM] * 6,
        out_specs=VMEM,
        compiler_params=params,
        cost_estimate=hint(1.5),
        name="project",
    )(far_table, coupling, turned, leaf_local, basis, partials[0])
    total = pl.pallas_call(
        functools.partial(far_kernel, [rows for rows, _ in roots]),
        out_shape=jax.ShapeDtypeStruct((columns, points), F32),
        in_specs=[VMEM] * (5 + len(roots)),
        out_specs=VMEM,
        compiler_params=params,
        cost_estimate=hint(0.6),
        name="far",
    )(*paths, high, low, partial, *[value for _, value in roots])
    return pl.pallas_call(
        functools.partial(add_kernel, leaf_count),
        out_shape=jax.ShapeDtypeStruct((columns, points), F32),
        in_specs=[VMEM] * (1 + len(received)),
        out_specs=HBM,
        scratch_shapes=[pltpu.VMEM((columns, points), F32), dma((4,))],
        compiler_params=params,
        cost_estimate=hint(0.5),
        name="add",
    )(total, *received)


def solution(mesh):
    leaf_devices, rhs_devices = mesh.shape["leaf"], mesh.shape["rhs"]
    share = 2 if rhs_devices % 2 == 0 else 1
    split = Mesh(
        mesh.devices.reshape(leaf_devices, rhs_devices // share, share), ("leaf", "far", "mate")
    )
    rhs = ("far", "mate")
    in_specs = (
        P(rhs, "leaf"),
        P(None, "leaf"),
        P("leaf", rhs, None, None),
        P("leaf", rhs),
        P(),
        P("leaf", None),
        P("leaf", None, None, None),
        P("leaf", None, None, None),
        P(),
        P(),
    )
    return jax.shard_map(
        local, mesh=split, in_specs=in_specs, out_specs=P(rhs, "leaf"), check_vma=False
    )
```

```python
import functools

import jax
import jax.numpy as jnp
from jax import lax
from jax.experimental import pallas as pl
from jax.experimental.pallas import tpu as pltpu
from jax.sharding import Mesh
from jax.sharding import PartitionSpec as P

FACE_SIGNS = ((1, 0), (-1, 0), (1, 1), (-1, 1), (1, 2), (-1, 2))
F32 = jnp.float32
BF16 = jnp.bfloat16
LANES = 128
STEPS = 32000.0
VMEM = pl.BlockSpec(memory_space=pltpu.VMEM)
HBM = pl.BlockSpec(memory_space=pltpu.HBM)


def cube_side(device_count):
    return max((edge_len for edge_len in range(1, 65) if edge_len**3 <= device_count))


def face_offsets(device_count):
    side_len = cube_side(device_count)
    return [face_sign * side_len**axis_pos for face_sign, axis_pos in FACE_SIGNS]


def shifted(value, axis, steps):
    count = lax.axis_size(axis)
    first, last = (max(0, -steps), min(count, count - steps))
    return lax.ppermute(value, axis, [(source, source + steps) for source in range(first, last)])


def halves(value):
    high = value.astype(BF16)
    return high, (value - high.astype(F32)).astype(BF16)


def dot_nn(left, right):
    return lax.dot_general(left, right, (((1,), (0,)), ((), ())), preferred_element_type=F32)


def dot_nt(left, right):
    return lax.dot_general(left, right, (((1,), (1,)), ((), ())), preferred_element_type=F32)


def split_dot(dot, rows, right_high, right_low):
    count = rows.shape[0]
    high, low = halves(rows)
    both = jnp.concatenate([high, low], axis=0)
    out = dot(both, right_high) + dot(both, right_low)
    return out[:count] + out[count:]


def spread_bases(block, group):
    rank, lanes = block.shape
    width = lanes // group
    zero = jnp.zeros((rank, width), block.dtype)
    rows = []
    for slot in range(group):
        pieces = [zero] * group
        pieces[slot] = block[:, slot * width : (slot + 1) * width]
        rows.append(jnp.concatenate(pieces, axis=1))
    return jnp.concatenate(rows, axis=0)


def packed_words(table):
    words = []
    for first in range(0, table.shape[0], 4):
        word = table[first : first + 1]
        for row in range(first + 1, min(first + 4, table.shape[0])):
            word = word + (table[row : row + 1] << (8 * (row - first)))
        words.append(word)
    return words


def unpacked(words, count, place):
    values = [word[0, place] for word in words]
    return [(values[row // 4] >> (8 * (row % 4))) & 255 for row in range(count)]


def fetch(pairs, sems):
    copies = []
    for index, (source, target) in enumerate(pairs):
        copy = pltpu.make_async_copy(source, target, sems.at[index])
        copy.start()
        copies.append(copy)
    return copies


def up_kernel(
    maps_hbm, bases_hbm, *refs,
):
    count = (len(refs) - 8) // 2
    hbm_refs, bases_ref, vmem_refs = refs[:count], refs[count], refs[count + 1 : 2 * count + 1]
    high_ref, low_ref, root_ref, maps_ref, spread_ref, chain_ref, sems = refs[2 * count + 1 :]
    dens_ref = vmem_refs[0]
    copies = fetch(
        [(maps_hbm, maps_ref), (bases_hbm, bases_ref), *zip(hbm_refs, vmem_refs)], sems
    )
    columns, points = dens_ref.shape
    rank, _, node_count = maps_ref.shape
    group = LANES // rank
    leaf_count = node_count // 2
    width = points // leaf_count
    copies[0].wait()
    node = lax.broadcasted_iota(jnp.int32, (node_count, LANES), 0)
    block = lax.broadcasted_iota(jnp.int32, (node_count, LANES), 1) // rank
    parent = node // 2 % group
    for first in range(0, rank, group):
        slab = maps_ref[first : first + group].reshape(group * rank, node_count).T
        turned = [slab] + [pltpu.roll(slab, turn * rank, 1) for turn in range(1, group)]
        for row in range(group):
            placed = jnp.zeros_like(slab)
            for place in range(group):
                here = (parent == place) & (block == place)
                placed = jnp.where(here, turned[(place - row) % group], placed)
            spread_ref[pl.ds(first + row, node_count, stride=rank), :] = placed
    tile = 2 * group * rank

    def children(parents, index):
        high, low = halves(spread_ref[index * tile : (index + 1) * tile, :])
        return split_dot(dot_nt, parents, high, low)

    row = lax.broadcasted_iota(jnp.int32, (rank, LANES), 0)
    lane = lax.broadcasted_iota(jnp.int32, (rank, LANES), 1)
    level = 1
    parents = jnp.where(lane == row + rank, 1.0, 0.0)
    while level < group:
        below = children(parents, 0)
        level *= 2
        parents = below[:, (level // group) * LANES : (level // group + 1) * LANES]
    chain_ref[:, LANES : 2 * LANES] = parents
    while level < leaf_count:
        for index in range(level // group, 2 * level // group):
            lanes = slice(index * LANES, (index + 1) * LANES)
            chain_ref[:, index * tile : (index + 1) * tile] = children(chain_ref[:, lanes], index)
        level *= 2
    copies[1].wait()
    copies[2].wait()
    step = group * width
    root = jnp.zeros((columns, rank), F32)
    for index in range(leaf_count // group):
        spots = slice(index * step, (index + 1) * step)
        start = (leaf_count // group + index) * LANES
        high, low = halves(bases_ref[:, spots])
        basis = split_dot(
            dot_nn, chain_ref[:, start : start + LANES],
            spread_bases(high, group), spread_bases(low, group),
        )
        high, low = halves(basis)
        high_ref[:, spots] = high
        low_ref[:, spots] = low
        dens = dens_ref[:, spots]
        root += dot_nt(dens, high) + dot_nt(dens, low)
    root = jnp.concatenate([root, jnp.zeros((columns, LANES - rank), F32)], axis=1)
    high = root.astype(BF16).astype(F32)
    rest = root - high
    middle = rest.astype(BF16).astype(F32)
    last = (rest - middle).astype(BF16).astype(F32)
    packed = high + pltpu.roll(middle, rank, 1) + pltpu.roll(last, 2 * rank, 1)
    root_ref[...] = packed.astype(BF16)
    for copy in copies[3:]:
        copy.wait()


def select_kernel(
    faces, far_groups, send_ref, dens_ref, root_ref, *refs,
):
    other_refs, out_refs = refs[: far_groups - 1], refs[far_groups - 1 :]
    device = lax.axis_index("leaf")
    columns = dens_ref.shape[0]
    cap, device_count = send_ref.shape[1:]
    own = lax.broadcasted_iota(jnp.int32, (cap, device_count), 1) == device
    for (directions, stride), out_ref in zip(faces, out_refs):
        table = send_ref[directions[0]]
        if len(directions) > 1:
            table = jnp.where(device // stride % 2 == 0, table, send_ref[directions[1]])
        picks = jnp.max(jnp.where(own, table.astype(F32), 0.0), axis=1, keepdims=True)
        for place in range(cap):
            leaf = picks[place, 0].astype(jnp.int32)
            for part, panel_ref in enumerate((dens_ref, *other_refs)):
                row = (place * far_groups + part) * columns
                out_ref[row : row + columns, :] = panel_ref[
                    :, pl.ds(pl.multiple_of(leaf * LANES, LANES), LANES)
                ]
        out_ref[cap * far_groups * columns :, :] = root_ref[...]


def near_kernel(
    faces, far_groups, share, *refs,
):
    source_refs, refs = refs[:share], refs[share:]
    dens_ref, refs = refs[0], refs[1:]
    other_refs, refs = refs[: far_groups - 1], refs[far_groups - 1 :]
    got_refs, refs = refs[: len(faces)], refs[len(faces) :]
    block_ref, refs = refs[0], refs[1:]
    mate_refs, refs = refs[: share - 1], refs[share - 1 :]
    refs = refs[1:]
    out_refs, refs = refs[:far_groups], refs[far_groups:]
    power_refs, refs = refs[: far_groups - 1], refs[far_groups - 1 :]
    (buffer_ref,) = refs
    columns, points = dens_ref.shape
    leaf_count, near_count, width, _ = block_ref.shape
    cap = (buffer_ref.shape[0] - leaf_count) // len(FACE_SIGNS)
    for (directions, _), got_ref in zip(faces, got_refs):
        for direction in directions:
            for place in range(cap):
                row = place * far_groups * columns
                buffer_ref[leaf_count + direction * cap + place] = got_ref[
                    row : row + far_groups * columns, :
                ]
    for part, panel_ref in enumerate((dens_ref, *other_refs)):
        rows = slice(part * columns, (part + 1) * columns)
        for leaf in range(leaf_count):
            buffer_ref[leaf, rows, :] = panel_ref[:, leaf * width : (leaf + 1) * width]
    words = [packed_words(source_ref[...]) for source_ref in source_refs]
    own_ref, sent_refs = out_refs[0], out_refs[1:]
    for leaf in range(leaf_count):
        panels, blocks = [], []
        for word, blocks_ref in zip(words, (block_ref, *mate_refs)):
            panels += [buffer_ref[slot] for slot in unpacked(word, near_count, leaf)]
            blocks += [blocks_ref[leaf, block] for block in range(near_count)]
        total = dot_nt(jnp.concatenate(panels, axis=1), jnp.concatenate(blocks, axis=1))
        lanes = slice(leaf * width, (leaf + 1) * width)
        own_ref[:, lanes] = total[:columns]
        for part, (sent_ref, power_ref) in enumerate(zip(sent_refs, power_refs), 1):
            term = total[part * columns : (part + 1) * columns]
            peak = jnp.max(jnp.abs(term), axis=0, keepdims=True)
            power = jnp.floor(jnp.log2(jnp.maximum(peak, 2.0**-100))) + 1.0
            steps = jnp.floor(term * (STEPS * jnp.exp2(-power)) + 0.5)
            sent_ref[:, lanes] = steps.astype(jnp.int32).astype(jnp.int16)
            power_ref[leaf : leaf + 1, :] = power
    for sent_ref, power_ref in zip(sent_refs, power_refs):
        power = power_ref[...].astype(jnp.int32).astype(jnp.int16)
        for first in range(0, leaf_count, columns):
            spot = points + first // columns * width
            sent_ref[:, spot : spot + width] = power[first : first + columns]


def coupled(leaves, table_ref, coupling_ref, turned_ref):
    far_count, rank = coupling_ref.shape[1:3]
    columns = turned_ref.shape[1] // 2
    group = LANES // rank
    words = packed_words(table_ref[...])
    parts = []
    for leaf in leaves:
        maps = jnp.concatenate([coupling_ref[leaf, j] for j in range(far_count)], axis=1)
        maps = jnp.concatenate(halves(maps), axis=0)
        picked = jnp.concatenate(
            [
                turned_ref[pl.ds(pl.multiple_of(source * rank, rank), rank), :]
                for source in unpacked(words, far_count, leaf)
            ],
            axis=0,
        )
        out = dot_nn(maps, picked)
        parts.append(out[:rank] + out[rank:])
        if len(parts) == group:
            turned = jnp.concatenate(parts, axis=0).T
            yield turned[:columns] + turned[columns:]
            parts = []


def couple_kernel(
    table_ref, coupling_ref, dens_ref, bases_ref, turned_ref, out_ref,
):
    columns, points = dens_ref.shape
    leaf_count, _, rank = coupling_ref.shape[:3]
    width = points // leaf_count
    upper = lax.broadcasted_iota(jnp.int32, (rank, 2 * columns), 1) < columns
    for leaf in range(leaf_count):
        spots = slice(leaf * width, (leaf + 1) * width)
        rows = jnp.concatenate(halves(bases_ref[:, spots]), axis=0)
        dens = dens_ref[:, spots]
        twice = dot_nt(rows, jnp.concatenate([dens, dens], axis=0))
        high, low = halves(twice[:rank] + twice[rank:])
        turned_ref[leaf * rank : (leaf + 1) * rank, :] = jnp.where(
            upper, high.astype(F32), low.astype(F32)
        ).astype(BF16)
    leaves = range(out_ref.shape[1] // rank)
    for index, field in enumerate(coupled(leaves, table_ref, coupling_ref, turned_ref)):
        out_ref[:, index * LANES : (index + 1) * LANES] = field


def project_kernel(
    table_ref, coupling_ref, turned_ref, first_ref, bases_ref, near_ref, out_ref,
):
    rank, points = bases_ref.shape
    leaf_count = coupling_ref.shape[0]
    group = LANES // rank
    step = group * points // leaf_count

    def project(index, field):
        spots = slice(index * step, (index + 1) * step)
        high, low = halves(bases_ref[:, spots])
        out_ref[:, spots] = near_ref[:, spots] + split_dot(
            dot_nn, field, spread_bases(high, group), spread_bases(low, group)
        )

    done = first_ref.shape[1] // LANES
    for index in range(done):
        project(index, first_ref[:, index * LANES : (index + 1) * LANES])
    leaves = range(done * group, leaf_count)
    for index, field in enumerate(coupled(leaves, table_ref, coupling_ref, turned_ref)):
        project(done + index, field)


def paths_kernel(turns, exchanged, upper_ref, cross_ref, high_ref, low_ref, map_ref):
    device = lax.axis_index("leaf")
    rank = upper_ref.shape[1]
    device_count = upper_ref.shape[0] // 2
    downs = {device_count: None}
    level = device_count
    while level > 4:
        node = level + device // (device_count // level)
        below = downs[level]
        matrix = upper_ref[node]
        downs[level // 2] = matrix if below is None else split_dot(dot_nn, below, *halves(matrix))
        level //= 2
    for level in sorted(downs):
        place = device // (device_count // level)
        for index in range(level):
            if level == 4:
                map_ref[level + index] = jnp.zeros((rank, rank), F32)
            else:
                above = map_ref[(level + index) // 2]
                map_ref[level + index] = split_dot(
                    dot_nt, above, *halves(upper_ref[level + index])
                )
        third = jnp.where(place % 2 == 0, place + 3, place - 3)
        for slot, other in enumerate((place - 2, place + 2, third)):
            inside = (other >= 0) & (other < level)
            matrix = cross_ref[level + place, slot]
            if downs[level] is not None:
                matrix = split_dot(dot_nn, downs[level], *halves(matrix))
            node = level + jnp.clip(other, 0, level - 1)
            map_ref[node] = map_ref[node] + jnp.where(inside, matrix, 0.0)
    zero = jnp.zeros((rank, LANES - 3 * rank), F32)
    for place, turn in enumerate(turns):
        matrix = map_ref[device_count + (device ^ turn if exchanged else turn)]
        matrix = jnp.concatenate([matrix] * 3 + [zero], axis=1)
        high, low = halves(matrix)
        high_ref[:, place * LANES : (place + 1) * LANES] = high
        low_ref[:, place * LANES : (place + 1) * LANES] = low


def far_kernel(
    tiles, path_high_ref, path_low_ref, high_ref, low_ref, term_ref, *refs,
):
    root_refs, out_ref = refs[:-1], refs[-1]
    columns, points = out_ref.shape
    pieces = []
    for rows, root_ref in zip(tiles, root_refs):
        pieces += [root_ref[row : row + columns, :] for row in rows]
    roots = jnp.concatenate(pieces, axis=1)
    field = dot_nt(roots, path_high_ref[...]) + dot_nt(roots, path_low_ref[...])
    step = 4 * LANES
    for first in range(0, points, step):
        spots = slice(first, first + step)
        out_ref[:, spots] = term_ref[:, spots] + split_dot(
            dot_nn, field, high_ref[:, spots], low_ref[:, spots]
        )


def add_kernel(leaf_count, term_ref, *refs):
    sent_refs, (out_hbm, sum_ref, sems) = refs[:-3], refs[-3:]
    columns, points = sum_ref.shape
    width = points // leaf_count
    factors = []
    for sent_ref in sent_refs:
        powers = [
            sent_ref[:, points + first // columns * width :][:, :width]
            for first in range(0, leaf_count, columns)
        ]
        power = jnp.concatenate([p.astype(jnp.int32).astype(F32) for p in powers], axis=0)
        factors.append(jnp.exp2(power) * (1.0 / STEPS))
    chunk_count = sems.shape[0]
    step = points // chunk_count
    copies = []
    for index in range(chunk_count):
        spots = slice(index * step, (index + 1) * step)
        total = term_ref[:, spots]
        for sent_ref, factor in zip(sent_refs, factors):
            steps = sent_ref[:, spots].astype(jnp.int32).astype(F32)
            leaves = range(index * leaf_count // chunk_count, (index + 1) * leaf_count // chunk_count)
            scale = jnp.concatenate([factor[leaf : leaf + 1] for leaf in leaves], axis=1)
            total = total + steps * scale
        sum_ref[:, spots] = total
        copies += fetch(
            [(sum_ref.at[:, pl.ds(index * step, step)], out_hbm.at[:, pl.ds(index * step, step)])],
            sems.at[pl.ds(index, 1)],
        )
    for copy in copies:
        copy.wait()


def hbm(value):
    return pltpu.with_memory_space_constraint(value, pltpu.HBM)


def hint(micros):
    return pl.CostEstimate(flops=0, bytes_accessed=int(micros * 3.69e6), transcendentals=0)


def local(
    densities,
    bases,
    near_blocks,
    near_src,
    send_leaf,
    far_src,
    leaf_coupling,
    local_transfer,
    upper_transfer,
    up_coupling,
):
    leaf_devices = lax.axis_size("leaf")
    far_groups = lax.axis_size("far")
    share = lax.axis_size("mate")
    side = cube_side(leaf_devices)
    offsets = face_offsets(leaf_devices)
    columns, points = densities.shape
    leaf_count, near_count, width, _ = near_blocks.shape
    rank = bases.shape[0]
    cap = send_leaf.shape[2]
    node_count = local_transfer.shape[1]
    params = pltpu.CompilerParams(vmem_limit_bytes=16 * 2**20)
    dma = pltpu.SemaphoreType.DMA

    def rotated(value, axis, shift):
        count = lax.axis_size(axis)
        return lax.ppermute(value, axis, [(i, (i - shift) % count) for i in range(count)])

    def crossed(value, turn):
        return lax.ppermute(value, "leaf", [(i, i ^ turn) for i in range(leaf_devices)])

    sources = near_src.T
    others = [rotated(densities, "far", part) for part in range(1, far_groups)]
    all_sources = [sources] + [rotated(sources, "mate", part) for part in range(1, share)]
    send = send_leaf.transpose(1, 2, 0)
    moved = [
        densities, send, sources, far_src.T, upper_transfer, up_coupling, leaf_coupling, near_blocks,
    ]
    (
        basis, dens, send, sources, far_table, upper, cross, coupling, blocks, high, low, root,
    ) = pl.pallas_call(
        up_kernel,
        out_shape=[jax.ShapeDtypeStruct(value.shape, value.dtype) for value in (bases, *moved)]
        + [
            jax.ShapeDtypeStruct((rank, points), BF16),
            jax.ShapeDtypeStruct((rank, points), BF16),
            jax.ShapeDtypeStruct((columns, LANES), BF16),
        ],
        in_specs=[HBM] * (2 + len(moved)),
        out_specs=[VMEM] * (4 + len(moved)),
        scratch_shapes=[
            pltpu.VMEM((rank, rank, node_count), F32),
            pltpu.VMEM((node_count * rank, LANES), F32),
            pltpu.VMEM((rank, node_count * rank), F32),
            dma((2 + len(moved),)),
        ],
        compiler_params=params,
        cost_estimate=hint(3.5),
        name="up",
    )(hbm(local_transfer[0].transpose(1, 2, 0)), hbm(bases), *map(hbm, moved))
    all_sources[0] = sources

    later_blocks, others, all_sources, root = lax.optimization_barrier(
        (blocks, others, all_sources, root)
    )
    mate_blocks = [rotated(later_blocks, "mate", part) for part in range(1, share)]

    if side == 2:
        faces = [((2 * axis, 2 * axis + 1), 2**axis) for axis in (2, 0, 1)]
    else:
        faces = [((direction,), offset) for direction, offset in enumerate(offsets)]
    chunk = (cap * far_groups + 1) * columns
    outgoing = pl.pallas_call(
        functools.partial(select_kernel, faces, far_groups),
        out_shape=[jax.ShapeDtypeStruct((chunk, LANES), BF16)] * len(faces),
        in_specs=[VMEM] * (2 + far_groups),
        out_specs=[VMEM] * len(faces),
        compiler_params=params,
        cost_estimate=hint(1),
        name="select",
    )(send, dens, root, *others)
    outgoing, dens = lax.optimization_barrier((outgoing, dens))
    first_leaves = leaf_count // 2
    turned, leaf_local = pl.pallas_call(
        couple_kernel,
        out_shape=[
            jax.ShapeDtypeStruct((leaf_count * rank, 2 * columns), BF16),
            jax.ShapeDtypeStruct((columns, first_leaves * rank), F32),
        ],
        in_specs=[VMEM] * 4,
        out_specs=[VMEM] * 2,
        compiler_params=params,
        cost_estimate=hint(2),
        name="couple",
    )(far_table, coupling, dens, basis)
    tail = cap * far_groups * columns
    if side == 2:
        arrived = [crossed(value, stride) for (_, stride), value in zip(faces, outgoing)]
        far_one, _, near_two = (value[tail : tail + columns] for value in arrived)
        later, leaf_local = lax.optimization_barrier((arrived[0][-4 * columns :], leaf_local))
        across = crossed(later, 2)
        held = jnp.concatenate([near_two, far_one, across[-columns:]], axis=0)
        beside = crossed(held, 1)
        turns = [0] + [stride for _, stride in faces] + [6, 3, 5, 7]
        roots = [([0], root)] + [([tail], value) for value in arrived]
        roots += [([3 * columns], across), ([0, columns, 2 * columns], beside)]
    else:
        arrived = [shifted(value, "leaf", stride) for (_, stride), value in zip(faces, outgoing)]
        turns = list(range(leaf_devices))
        everyone = lax.all_gather(root, "leaf", axis=0, tiled=True)
        roots = [([turn * columns for turn in turns], everyone)]
    slots = leaf_count + len(offsets) * cap
    tables = -(-leaf_count // columns) * width
    partials = pl.pallas_call(
        functools.partial(near_kernel, faces, far_groups, share),
        out_shape=[jax.ShapeDtypeStruct((columns, points), F32)]
        + [jax.ShapeDtypeStruct((columns, points + tables), jnp.int16)] * (far_groups - 1),
        in_specs=[VMEM] * (2 * share + far_groups + len(faces) + 1),
        out_specs=[VMEM] * far_groups,
        scratch_shapes=[pltpu.VMEM((leaf_count, width), F32)] * (far_groups - 1)
        + [
            pltpu.VMEM((slots, far_groups * columns, width), BF16),
        ],
        compiler_params=params,
        cost_estimate=hint(3),
        name="near",
    )(
        *all_sources, dens, *others, *arrived, blocks, *mate_blocks, leaf_local,
    )
    upper, cross, near_own = lax.optimization_barrier((upper, cross, partials[0]))
    paths = pl.pallas_call(
        functools.partial(paths_kernel, turns, side == 2),
        out_shape=[jax.ShapeDtypeStruct((rank, leaf_devices * LANES), BF16)] * 2,
        in_specs=[VMEM] * 2,
        out_specs=[VMEM] * 2,
        scratch_shapes=[pltpu.VMEM((2 * leaf_devices, rank, rank), F32)],
        compiler_params=params,
        cost_estimate=hint(0.7),
        name="paths",
    )(upper, cross)
    received = [rotated(partials[part], "far", -part) for part in range(1, far_groups)]
    partial = pl.pallas_call(
        project_kernel,
        out_shape=jax.ShapeDtypeStruct((columns, points), F32),
        in_specs=[VMEM] * 6,
        out_specs=VMEM,
        compiler_params=params,
        cost_estimate=hint(1.5),
        name="project",
    )(far_table, coupling, turned, leaf_local, basis, near_own)
    total = pl.pallas_call(
        functools.partial(far_kernel, [rows for rows, _ in roots]),
        out_shape=jax.ShapeDtypeStruct((columns, points), F32),
        in_specs=[VMEM] * (5 + len(roots)),
        out_specs=VMEM,
        compiler_params=params,
        cost_estimate=hint(0.6),
        name="far",
    )(*paths, high, low, partial, *[value for _, value in roots])
    return pl.pallas_call(
        functools.partial(add_kernel, leaf_count),
        out_shape=jax.ShapeDtypeStruct((columns, points), F32),
        in_specs=[VMEM] * (1 + len(received)),
        out_specs=HBM,
        scratch_shapes=[pltpu.VMEM((columns, points), F32), dma((4,))],
        compiler_params=params,
        cost_estimate=hint(0.5),
        name="add",
    )(total, *received)


def solution(mesh):
    leaf_devices, rhs_devices = mesh.shape["leaf"], mesh.shape["rhs"]
    share = 2 if rhs_devices % 2 == 0 else 1
    split = Mesh(
        mesh.devices.reshape(leaf_devices, rhs_devices // share, share), ("leaf", "far", "mate")
    )
    rhs = ("far", "mate")
    in_specs = (
        P(rhs, "leaf"),
        P(None, "leaf"),
        P("leaf", rhs, None, None),
        P("leaf", rhs),
        P(),
        P("leaf", None),
        P("leaf", None, None, None),
        P("leaf", None, None, None),
        P(),
        P(),
    )
    return jax.shard_map(
        local, mesh=split, in_specs=in_specs, out_specs=P(rhs, "leaf"), check_vma=False
    )
```

```python
import functools

import jax
import jax.numpy as jnp
from jax import lax
from jax.experimental import pallas as pl
from jax.experimental.pallas import tpu as pltpu
from jax.sharding import Mesh
from jax.sharding import PartitionSpec as P

FACE_SIGNS = ((1, 0), (-1, 0), (1, 1), (-1, 1), (1, 2), (-1, 2))
F32 = jnp.float32
BF16 = jnp.bfloat16
LANES = 128
STEPS = 32000.0
VMEM = pl.BlockSpec(memory_space=pltpu.VMEM)
HBM = pl.BlockSpec(memory_space=pltpu.HBM)


def cube_side(device_count):
    return max((edge_len for edge_len in range(1, 65) if edge_len**3 <= device_count))


def face_offsets(device_count):
    side_len = cube_side(device_count)
    return [face_sign * side_len**axis_pos for face_sign, axis_pos in FACE_SIGNS]


def shifted(value, axis, steps):
    count = lax.axis_size(axis)
    first, last = (max(0, -steps), min(count, count - steps))
    return lax.ppermute(value, axis, [(source, source + steps) for source in range(first, last)])


def halves(value):
    high = value.astype(BF16)
    return high, (value - high.astype(F32)).astype(BF16)


def dot_nn(left, right):
    return lax.dot_general(left, right, (((1,), (0,)), ((), ())), preferred_element_type=F32)


def dot_nt(left, right):
    return lax.dot_general(left, right, (((1,), (1,)), ((), ())), preferred_element_type=F32)


def split_dot(dot, rows, right_high, right_low):
    count = rows.shape[0]
    high, low = halves(rows)
    both = jnp.concatenate([high, low], axis=0)
    out = dot(both, right_high) + dot(both, right_low)
    return out[:count] + out[count:]


def spread_bases(block, group):
    rank, lanes = block.shape
    width = lanes // group
    zero = jnp.zeros((rank, width), block.dtype)
    rows = []
    for slot in range(group):
        pieces = [zero] * group
        pieces[slot] = block[:, slot * width : (slot + 1) * width]
        rows.append(jnp.concatenate(pieces, axis=1))
    return jnp.concatenate(rows, axis=0)


def packed_words(table):
    words = []
    for first in range(0, table.shape[0], 4):
        word = table[first : first + 1]
        for row in range(first + 1, min(first + 4, table.shape[0])):
            word = word + (table[row : row + 1] << (8 * (row - first)))
        words.append(word)
    return words


def unpacked(words, count, place):
    values = [word[0, place] for word in words]
    return [(values[row // 4] >> (8 * (row % 4))) & 255 for row in range(count)]


def fetch(pairs, sems):
    copies = []
    for index, (source, target) in enumerate(pairs):
        copy = pltpu.make_async_copy(source, target, sems.at[index])
        copy.start()
        copies.append(copy)
    return copies


def up_kernel(
    maps_hbm, bases_hbm, *refs,
):
    count = (len(refs) - 8) // 2
    hbm_refs, bases_ref, vmem_refs = refs[:count], refs[count], refs[count + 1 : 2 * count + 1]
    high_ref, low_ref, root_ref, maps_ref, spread_ref, chain_ref, sems = refs[2 * count + 1 :]
    dens_ref = vmem_refs[0]
    copies = fetch(
        [(maps_hbm, maps_ref), (bases_hbm, bases_ref), *zip(hbm_refs, vmem_refs)], sems
    )
    columns, points = dens_ref.shape
    rank, _, node_count = maps_ref.shape
    group = LANES // rank
    leaf_count = node_count // 2
    width = points // leaf_count
    copies[0].wait()
    node = lax.broadcasted_iota(jnp.int32, (node_count, LANES), 0)
    block = lax.broadcasted_iota(jnp.int32, (node_count, LANES), 1) // rank
    parent = node // 2 % group
    for first in range(0, rank, group):
        slab = maps_ref[first : first + group].reshape(group * rank, node_count).T
        turned = [slab] + [pltpu.roll(slab, turn * rank, 1) for turn in range(1, group)]
        for row in range(group):
            placed = jnp.zeros_like(slab)
            for place in range(group):
                here = (parent == place) & (block == place)
                placed = jnp.where(here, turned[(place - row) % group], placed)
            spread_ref[pl.ds(first + row, node_count, stride=rank), :] = placed
    tile = 2 * group * rank

    def children(parents, index):
        high, low = halves(spread_ref[index * tile : (index + 1) * tile, :])
        return split_dot(dot_nt, parents, high, low)

    row = lax.broadcasted_iota(jnp.int32, (rank, LANES), 0)
    lane = lax.broadcasted_iota(jnp.int32, (rank, LANES), 1)
    level = 1
    parents = jnp.where(lane == row + rank, 1.0, 0.0)
    while level < group:
        below = children(parents, 0)
        level *= 2
        parents = below[:, (level // group) * LANES : (level // group + 1) * LANES]
    chain_ref[:, LANES : 2 * LANES] = parents
    while level < leaf_count:
        for index in range(level // group, 2 * level // group):
            lanes = slice(index * LANES, (index + 1) * LANES)
            chain_ref[:, index * tile : (index + 1) * tile] = children(chain_ref[:, lanes], index)
        level *= 2
    copies[1].wait()
    copies[2].wait()
    step = group * width
    root = jnp.zeros((columns, rank), F32)
    for index in range(leaf_count // group):
        spots = slice(index * step, (index + 1) * step)
        start = (leaf_count // group + index) * LANES
        high, low = halves(bases_ref[:, spots])
        basis = split_dot(
            dot_nn, chain_ref[:, start : start + LANES],
            spread_bases(high, group), spread_bases(low, group),
        )
        high, low = halves(basis)
        high_ref[:, spots] = high
        low_ref[:, spots] = low
        dens = dens_ref[:, spots]
        root += dot_nt(dens, high) + dot_nt(dens, low)
    root = jnp.concatenate([root, jnp.zeros((columns, LANES - rank), F32)], axis=1)
    high = root.astype(BF16).astype(F32)
    rest = root - high
    middle = rest.astype(BF16).astype(F32)
    last = (rest - middle).astype(BF16).astype(F32)
    packed = high + pltpu.roll(middle, rank, 1) + pltpu.roll(last, 2 * rank, 1)
    root_ref[...] = packed.astype(BF16)
    for copy in copies[3:]:
        copy.wait()


def select_kernel(
    faces, far_groups, send_ref, dens_ref, root_ref, *refs,
):
    other_refs, out_refs = refs[: far_groups - 1], refs[far_groups - 1 :]
    device = lax.axis_index("leaf")
    columns = dens_ref.shape[0]
    cap, device_count = send_ref.shape[1:]
    own = lax.broadcasted_iota(jnp.int32, (cap, device_count), 1) == device
    for (directions, stride), out_ref in zip(faces, out_refs):
        table = send_ref[directions[0]]
        if len(directions) > 1:
            table = jnp.where(device // stride % 2 == 0, table, send_ref[directions[1]])
        picks = jnp.max(jnp.where(own, table.astype(F32), 0.0), axis=1, keepdims=True)
        for place in range(cap):
            leaf = picks[place, 0].astype(jnp.int32)
            for part, panel_ref in enumerate((dens_ref, *other_refs)):
                row = (place * far_groups + part) * columns
                out_ref[row : row + columns, :] = panel_ref[
                    :, pl.ds(pl.multiple_of(leaf * LANES, LANES), LANES)
                ]
        out_ref[cap * far_groups * columns :, :] = root_ref[...]


def near_kernel(
    faces, far_groups, share, *refs,
):
    source_refs, refs = refs[:share], refs[share:]
    dens_ref, refs = refs[0], refs[1:]
    other_refs, refs = refs[: far_groups - 1], refs[far_groups - 1 :]
    got_refs, refs = refs[: len(faces)], refs[len(faces) :]
    block_ref, refs = refs[0], refs[1:]
    mate_refs, refs = refs[: share - 1], refs[share - 1 :]
    refs = refs[1:]
    out_refs, refs = refs[:far_groups], refs[far_groups:]
    power_refs, refs = refs[: far_groups - 1], refs[far_groups - 1 :]
    (buffer_ref,) = refs
    columns, points = dens_ref.shape
    leaf_count, near_count, width, _ = block_ref.shape
    cap = (buffer_ref.shape[0] - leaf_count) // len(FACE_SIGNS)
    for (directions, _), got_ref in zip(faces, got_refs):
        for direction in directions:
            for place in range(cap):
                row = place * far_groups * columns
                buffer_ref[leaf_count + direction * cap + place] = got_ref[
                    row : row + far_groups * columns, :
                ]
    for part, panel_ref in enumerate((dens_ref, *other_refs)):
        rows = slice(part * columns, (part + 1) * columns)
        for leaf in range(leaf_count):
            buffer_ref[leaf, rows, :] = panel_ref[:, leaf * width : (leaf + 1) * width]
    words = [packed_words(source_ref[...]) for source_ref in source_refs]
    own_ref, sent_refs = out_refs[0], out_refs[1:]
    for leaf in range(leaf_count):
        panels, blocks = [], []
        for word, blocks_ref in zip(words, (block_ref, *mate_refs)):
            panels += [buffer_ref[slot] for slot in unpacked(word, near_count, leaf)]
            blocks += [blocks_ref[leaf, block] for block in range(near_count)]
        total = dot_nt(jnp.concatenate(blocks, axis=1), jnp.concatenate(panels, axis=1)).T
        lanes = slice(leaf * width, (leaf + 1) * width)
        own_ref[:, lanes] = total[:columns]
        for part, (sent_ref, power_ref) in enumerate(zip(sent_refs, power_refs), 1):
            term = total[part * columns : (part + 1) * columns]
            peak = jnp.max(jnp.abs(term), axis=0, keepdims=True)
            power = jnp.floor(jnp.log2(jnp.maximum(peak, 2.0**-100))) + 1.0
            steps = jnp.floor(term * (STEPS * jnp.exp2(-power)) + 0.5)
            sent_ref[:, lanes] = steps.astype(jnp.int32).astype(jnp.int16)
            power_ref[leaf : leaf + 1, :] = power
    for sent_ref, power_ref in zip(sent_refs, power_refs):
        power = power_ref[...].astype(jnp.int32).astype(jnp.int16)
        for first in range(0, leaf_count, columns):
            spot = points + first // columns * width
            sent_ref[:, spot : spot + width] = power[first : first + columns]


def coupled(leaves, table_ref, coupling_ref, turned_ref):
    far_count, rank = coupling_ref.shape[1:3]
    columns = turned_ref.shape[1] // 2
    group = LANES // rank
    words = packed_words(table_ref[...])
    parts = []
    for leaf in leaves:
        maps = jnp.concatenate([coupling_ref[leaf, j] for j in range(far_count)], axis=1)
        maps = jnp.concatenate(halves(maps), axis=0)
        picked = jnp.concatenate(
            [
                turned_ref[pl.ds(pl.multiple_of(source * rank, rank), rank), :]
                for source in unpacked(words, far_count, leaf)
            ],
            axis=0,
        )
        out = dot_nn(maps, picked)
        parts.append(out[:rank] + out[rank:])
        if len(parts) == group:
            turned = jnp.concatenate(parts, axis=0).T
            yield turned[:columns] + turned[columns:]
            parts = []


def couple_kernel(
    table_ref, coupling_ref, dens_ref, bases_ref, turned_ref, out_ref,
):
    columns, points = dens_ref.shape
    leaf_count, _, rank = coupling_ref.shape[:3]
    width = points // leaf_count
    upper = lax.broadcasted_iota(jnp.int32, (rank, 2 * columns), 1) < columns
    for leaf in range(leaf_count):
        spots = slice(leaf * width, (leaf + 1) * width)
        rows = jnp.concatenate(halves(bases_ref[:, spots]), axis=0)
        dens = dens_ref[:, spots]
        twice = dot_nt(rows, jnp.concatenate([dens, dens], axis=0))
        high, low = halves(twice[:rank] + twice[rank:])
        turned_ref[leaf * rank : (leaf + 1) * rank, :] = jnp.where(
            upper, high.astype(F32), low.astype(F32)
        ).astype(BF16)
    leaves = range(out_ref.shape[1] // rank)
    for index, field in enumerate(coupled(leaves, table_ref, coupling_ref, turned_ref)):
        out_ref[:, index * LANES : (index + 1) * LANES] = field


def project_kernel(
    table_ref, coupling_ref, turned_ref, first_ref, bases_ref, near_ref, out_ref,
):
    rank, points = bases_ref.shape
    leaf_count = coupling_ref.shape[0]
    group = LANES // rank
    step = group * points // leaf_count

    def project(index, field):
        spots = slice(index * step, (index + 1) * step)
        high, low = halves(bases_ref[:, spots])
        out_ref[:, spots] = near_ref[:, spots] + split_dot(
            dot_nn, field, spread_bases(high, group), spread_bases(low, group)
        )

    done = first_ref.shape[1] // LANES
    for index in range(done):
        project(index, first_ref[:, index * LANES : (index + 1) * LANES])
    leaves = range(done * group, leaf_count)
    for index, field in enumerate(coupled(leaves, table_ref, coupling_ref, turned_ref)):
        project(done + index, field)


def paths_kernel(turns, exchanged, upper_ref, cross_ref, high_ref, low_ref, map_ref):
    device = lax.axis_index("leaf")
    rank = upper_ref.shape[1]
    device_count = upper_ref.shape[0] // 2
    downs = {device_count: None}
    level = device_count
    while level > 4:
        node = level + device // (device_count // level)
        below = downs[level]
        matrix = upper_ref[node]
        downs[level // 2] = matrix if below is None else split_dot(dot_nn, below, *halves(matrix))
        level //= 2
    for level in sorted(downs):
        place = device // (device_count // level)
        for index in range(level):
            if level == 4:
                map_ref[level + index] = jnp.zeros((rank, rank), F32)
            else:
                above = map_ref[(level + index) // 2]
                map_ref[level + index] = split_dot(
                    dot_nt, above, *halves(upper_ref[level + index])
                )
        third = jnp.where(place % 2 == 0, place + 3, place - 3)
        for slot, other in enumerate((place - 2, place + 2, third)):
            inside = (other >= 0) & (other < level)
            matrix = cross_ref[level + place, slot]
            if downs[level] is not None:
                matrix = split_dot(dot_nn, downs[level], *halves(matrix))
            node = level + jnp.clip(other, 0, level - 1)
            map_ref[node] = map_ref[node] + jnp.where(inside, matrix, 0.0)
    zero = jnp.zeros((rank, LANES - 3 * rank), F32)
    for place, turn in enumerate(turns):
        matrix = map_ref[device_count + (device ^ turn if exchanged else turn)]
        matrix = jnp.concatenate([matrix] * 3 + [zero], axis=1)
        high, low = halves(matrix)
        high_ref[:, place * LANES : (place + 1) * LANES] = high
        low_ref[:, place * LANES : (place + 1) * LANES] = low


def far_kernel(
    tiles, path_high_ref, path_low_ref, high_ref, low_ref, term_ref, *refs,
):
    root_refs, out_ref = refs[:-1], refs[-1]
    columns, points = out_ref.shape
    pieces = []
    for rows, root_ref in zip(tiles, root_refs):
        pieces += [root_ref[row : row + columns, :] for row in rows]
    roots = jnp.concatenate(pieces, axis=1)
    field = dot_nt(roots, path_high_ref[...]) + dot_nt(roots, path_low_ref[...])
    step = 4 * LANES
    for first in range(0, points, step):
        spots = slice(first, first + step)
        out_ref[:, spots] = term_ref[:, spots] + split_dot(
            dot_nn, field, high_ref[:, spots], low_ref[:, spots]
        )


def add_kernel(leaf_count, term_ref, *refs):
    sent_refs, (out_hbm, sum_ref, sems) = refs[:-3], refs[-3:]
    columns, points = sum_ref.shape
    width = points // leaf_count
    factors = []
    for sent_ref in sent_refs:
        powers = [
            sent_ref[:, points + first // columns * width :][:, :width]
            for first in range(0, leaf_count, columns)
        ]
        power = jnp.concatenate([p.astype(jnp.int32).astype(F32) for p in powers], axis=0)
        factors.append(jnp.exp2(power) * (1.0 / STEPS))
    chunk_count = sems.shape[0]
    step = points // chunk_count
    copies = []
    for index in range(chunk_count):
        spots = slice(index * step, (index + 1) * step)
        total = term_ref[:, spots]
        for sent_ref, factor in zip(sent_refs, factors):
            steps = sent_ref[:, spots].astype(jnp.int32).astype(F32)
            leaves = range(index * leaf_count // chunk_count, (index + 1) * leaf_count // chunk_count)
            scale = jnp.concatenate([factor[leaf : leaf + 1] for leaf in leaves], axis=1)
            total = total + steps * scale
        sum_ref[:, spots] = total
        copies += fetch(
            [(sum_ref.at[:, pl.ds(index * step, step)], out_hbm.at[:, pl.ds(index * step, step)])],
            sems.at[pl.ds(index, 1)],
        )
    for copy in copies:
        copy.wait()


def hbm(value):
    return pltpu.with_memory_space_constraint(value, pltpu.HBM)


def hint(micros):
    return pl.CostEstimate(flops=0, bytes_accessed=int(micros * 3.69e6), transcendentals=0)


def local(
    densities,
    bases,
    near_blocks,
    near_src,
    send_leaf,
    far_src,
    leaf_coupling,
    local_transfer,
    upper_transfer,
    up_coupling,
):
    leaf_devices = lax.axis_size("leaf")
    far_groups = lax.axis_size("far")
    share = lax.axis_size("mate")
    side = cube_side(leaf_devices)
    offsets = face_offsets(leaf_devices)
    columns, points = densities.shape
    leaf_count, near_count, width, _ = near_blocks.shape
    rank = bases.shape[0]
    cap = send_leaf.shape[2]
    node_count = local_transfer.shape[1]
    params = pltpu.CompilerParams(vmem_limit_bytes=16 * 2**20)
    dma = pltpu.SemaphoreType.DMA

    def rotated(value, axis, shift):
        count = lax.axis_size(axis)
        return lax.ppermute(value, axis, [(i, (i - shift) % count) for i in range(count)])

    def crossed(value, turn):
        return lax.ppermute(value, "leaf", [(i, i ^ turn) for i in range(leaf_devices)])

    sources = near_src.T
    others = [rotated(densities, "far", part) for part in range(1, far_groups)]
    all_sources = [sources] + [rotated(sources, "mate", part) for part in range(1, share)]
    send = send_leaf.transpose(1, 2, 0)
    moved = [
        densities, send, sources, far_src.T, upper_transfer, up_coupling, leaf_coupling, near_blocks,
    ]
    (
        basis, dens, send, sources, far_table, upper, cross, coupling, blocks, high, low, root,
    ) = pl.pallas_call(
        up_kernel,
        out_shape=[jax.ShapeDtypeStruct(value.shape, value.dtype) for value in (bases, *moved)]
        + [
            jax.ShapeDtypeStruct((rank, points), BF16),
            jax.ShapeDtypeStruct((rank, points), BF16),
            jax.ShapeDtypeStruct((columns, LANES), BF16),
        ],
        in_specs=[HBM] * (2 + len(moved)),
        out_specs=[VMEM] * (4 + len(moved)),
        scratch_shapes=[
            pltpu.VMEM((rank, rank, node_count), F32),
            pltpu.VMEM((node_count * rank, LANES), F32),
            pltpu.VMEM((rank, node_count * rank), F32),
            dma((2 + len(moved),)),
        ],
        compiler_params=params,
        cost_estimate=hint(3.5),
        name="up",
    )(hbm(local_transfer[0].transpose(1, 2, 0)), hbm(bases), *map(hbm, moved))
    all_sources[0] = sources

    later_blocks, others, all_sources, root = lax.optimization_barrier(
        (blocks, others, all_sources, root)
    )
    mate_blocks = [rotated(later_blocks, "mate", part) for part in range(1, share)]

    if side == 2:
        faces = [((2 * axis, 2 * axis + 1), 2**axis) for axis in (2, 0, 1)]
    else:
        faces = [((direction,), offset) for direction, offset in enumerate(offsets)]
    chunk = (cap * far_groups + 1) * columns
    outgoing = pl.pallas_call(
        functools.partial(select_kernel, faces, far_groups),
        out_shape=[jax.ShapeDtypeStruct((chunk, LANES), BF16)] * len(faces),
        in_specs=[VMEM] * (2 + far_groups),
        out_specs=[VMEM] * len(faces),
        compiler_params=params,
        cost_estimate=hint(1),
        name="select",
    )(send, dens, root, *others)
    outgoing, dens = lax.optimization_barrier((outgoing, dens))
    first_leaves = leaf_count // 2
    turned, leaf_local = pl.pallas_call(
        couple_kernel,
        out_shape=[
            jax.ShapeDtypeStruct((leaf_count * rank, 2 * columns), BF16),
            jax.ShapeDtypeStruct((columns, first_leaves * rank), F32),
        ],
        in_specs=[VMEM] * 4,
        out_specs=[VMEM] * 2,
        compiler_params=params,
        cost_estimate=hint(2),
        name="couple",
    )(far_table, coupling, dens, basis)
    tail = cap * far_groups * columns
    if side == 2:
        arrived = [crossed(value, stride) for (_, stride), value in zip(faces, outgoing)]
        far_one, _, near_two = (value[tail : tail + columns] for value in arrived)
        later, leaf_local = lax.optimization_barrier((arrived[0][-4 * columns :], leaf_local))
        across = crossed(later, 2)
        held = jnp.concatenate([near_two, far_one, across[-columns:]], axis=0)
        beside = crossed(held, 1)
        turns = [0] + [stride for _, stride in faces] + [6, 3, 5, 7]
        roots = [([0], root)] + [([tail], value) for value in arrived]
        roots += [([3 * columns], across), ([0, columns, 2 * columns], beside)]
    else:
        arrived = [shifted(value, "leaf", stride) for (_, stride), value in zip(faces, outgoing)]
        turns = list(range(leaf_devices))
        everyone = lax.all_gather(root, "leaf", axis=0, tiled=True)
        roots = [([turn * columns for turn in turns], everyone)]
    slots = leaf_count + len(offsets) * cap
    tables = -(-leaf_count // columns) * width
    partials = pl.pallas_call(
        functools.partial(near_kernel, faces, far_groups, share),
        out_shape=[jax.ShapeDtypeStruct((columns, points), F32)]
        + [jax.ShapeDtypeStruct((columns, points + tables), jnp.int16)] * (far_groups - 1),
        in_specs=[VMEM] * (2 * share + far_groups + len(faces) + 1),
        out_specs=[VMEM] * far_groups,
        scratch_shapes=[pltpu.VMEM((leaf_count, width), F32)] * (far_groups - 1)
        + [
            pltpu.VMEM((slots, far_groups * columns, width), BF16),
        ],
        compiler_params=params,
        cost_estimate=hint(3),
        name="near",
    )(
        *all_sources, dens, *others, *arrived, blocks, *mate_blocks, leaf_local,
    )
    upper, cross, near_own = lax.optimization_barrier((upper, cross, partials[0]))
    paths = pl.pallas_call(
        functools.partial(paths_kernel, turns, side == 2),
        out_shape=[jax.ShapeDtypeStruct((rank, leaf_devices * LANES), BF16)] * 2,
        in_specs=[VMEM] * 2,
        out_specs=[VMEM] * 2,
        scratch_shapes=[pltpu.VMEM((2 * leaf_devices, rank, rank), F32)],
        compiler_params=params,
        cost_estimate=hint(0.7),
        name="paths",
    )(upper, cross)
    received = [rotated(partials[part], "far", -part) for part in range(1, far_groups)]
    partial = pl.pallas_call(
        project_kernel,
        out_shape=jax.ShapeDtypeStruct((columns, points), F32),
        in_specs=[VMEM] * 6,
        out_specs=VMEM,
        compiler_params=params,
        cost_estimate=hint(1.5),
        name="project",
    )(far_table, coupling, turned, leaf_local, basis, near_own)
    total = pl.pallas_call(
        functools.partial(far_kernel, [rows for rows, _ in roots]),
        out_shape=jax.ShapeDtypeStruct((columns, points), F32),
        in_specs=[VMEM] * (5 + len(roots)),
        out_specs=VMEM,
        compiler_params=params,
        cost_estimate=hint(0.6),
        name="far",
    )(*paths, high, low, partial, *[value for _, value in roots])
    return pl.pallas_call(
        functools.partial(add_kernel, leaf_count),
        out_shape=jax.ShapeDtypeStruct((columns, points), F32),
        in_specs=[VMEM] * (1 + len(received)),
        out_specs=HBM,
        scratch_shapes=[pltpu.VMEM((columns, points), F32), dma((4,))],
        compiler_params=params,
        cost_estimate=hint(0.5),
        name="add",
    )(total, *received)


def solution(mesh):
    leaf_devices, rhs_devices = mesh.shape["leaf"], mesh.shape["rhs"]
    share = 2 if rhs_devices % 2 == 0 else 1
    split = Mesh(
        mesh.devices.reshape(leaf_devices, rhs_devices // share, share), ("leaf", "far", "mate")
    )
    rhs = ("far", "mate")
    in_specs = (
        P(rhs, "leaf"),
        P(None, "leaf"),
        P("leaf", rhs, None, None),
        P("leaf", rhs),
        P(),
        P("leaf", None),
        P("leaf", None, None, None),
        P("leaf", None, None, None),
        P(),
        P(),
    )
    return jax.shard_map(
        local, mesh=split, in_specs=in_specs, out_specs=P(rhs, "leaf"), check_vma=False
    )
```

```python
import functools

import jax
import jax.numpy as jnp
from jax import lax
from jax.experimental import pallas as pl
from jax.experimental.pallas import tpu as pltpu
from jax.sharding import Mesh
from jax.sharding import PartitionSpec as P

FACE_SIGNS = ((1, 0), (-1, 0), (1, 1), (-1, 1), (1, 2), (-1, 2))
F32 = jnp.float32
BF16 = jnp.bfloat16
LANES = 128
STEPS = 32000.0
VMEM = pl.BlockSpec(memory_space=pltpu.VMEM)
HBM = pl.BlockSpec(memory_space=pltpu.HBM)


def cube_side(device_count):
    return max((edge_len for edge_len in range(1, 65) if edge_len**3 <= device_count))


def face_offsets(device_count):
    side_len = cube_side(device_count)
    return [face_sign * side_len**axis_pos for face_sign, axis_pos in FACE_SIGNS]


def shifted(value, axis, steps):
    count = lax.axis_size(axis)
    first, last = (max(0, -steps), min(count, count - steps))
    return lax.ppermute(value, axis, [(source, source + steps) for source in range(first, last)])


def halves(value):
    high = value.astype(BF16)
    return high, (value - high.astype(F32)).astype(BF16)


def dot_nn(left, right):
    return lax.dot_general(left, right, (((1,), (0,)), ((), ())), preferred_element_type=F32)


def dot_nt(left, right):
    return lax.dot_general(left, right, (((1,), (1,)), ((), ())), preferred_element_type=F32)


def split_dot(dot, rows, right_high, right_low):
    count = rows.shape[0]
    high, low = halves(rows)
    both = jnp.concatenate([high, low], axis=0)
    out = dot(both, right_high) + dot(both, right_low)
    return out[:count] + out[count:]


def spread_bases(block, group):
    rank, lanes = block.shape
    width = lanes // group
    zero = jnp.zeros((rank, width), block.dtype)
    rows = []
    for slot in range(group):
        pieces = [zero] * group
        pieces[slot] = block[:, slot * width : (slot + 1) * width]
        rows.append(jnp.concatenate(pieces, axis=1))
    return jnp.concatenate(rows, axis=0)


def packed_words(table):
    words = []
    for first in range(0, table.shape[0], 4):
        word = table[first : first + 1]
        for row in range(first + 1, min(first + 4, table.shape[0])):
            word = word + (table[row : row + 1] << (8 * (row - first)))
        words.append(word)
    return words


def unpacked(words, count, place):
    values = [word[0, place] for word in words]
    return [(values[row // 4] >> (8 * (row % 4))) & 255 for row in range(count)]


def fetch(pairs, sems):
    copies = []
    for index, (source, target) in enumerate(pairs):
        copy = pltpu.make_async_copy(source, target, sems.at[index])
        copy.start()
        copies.append(copy)
    return copies


def up_kernel(
    maps_hbm, bases_hbm, *refs,
):
    count = (len(refs) - 8) // 2
    hbm_refs, bases_ref, vmem_refs = refs[:count], refs[count], refs[count + 1 : 2 * count + 1]
    high_ref, low_ref, root_ref, maps_ref, spread_ref, chain_ref, sems = refs[2 * count + 1 :]
    dens_ref = vmem_refs[0]
    copies = fetch(
        [(maps_hbm, maps_ref), (bases_hbm, bases_ref), *zip(hbm_refs, vmem_refs)], sems
    )
    columns, points = dens_ref.shape
    rank, _, node_count = maps_ref.shape
    group = LANES // rank
    leaf_count = node_count // 2
    width = points // leaf_count
    copies[0].wait()
    node = lax.broadcasted_iota(jnp.int32, (node_count, LANES), 0)
    block = lax.broadcasted_iota(jnp.int32, (node_count, LANES), 1) // rank
    parent = node // 2 % group
    for first in range(0, rank, group):
        slab = maps_ref[first : first + group].reshape(group * rank, node_count).T
        turned = [slab] + [pltpu.roll(slab, turn * rank, 1) for turn in range(1, group)]
        for row in range(group):
            placed = jnp.zeros_like(slab)
            for place in range(group):
                here = (parent == place) & (block == place)
                placed = jnp.where(here, turned[(place - row) % group], placed)
            spread_ref[pl.ds(first + row, node_count, stride=rank), :] = placed
    tile = 2 * group * rank

    def children(parents, index):
        high, low = halves(spread_ref[index * tile : (index + 1) * tile, :])
        return split_dot(dot_nt, parents, high, low)

    row = lax.broadcasted_iota(jnp.int32, (rank, LANES), 0)
    lane = lax.broadcasted_iota(jnp.int32, (rank, LANES), 1)
    level = 1
    parents = jnp.where(lane == row + rank, 1.0, 0.0)
    while level < group:
        below = children(parents, 0)
        level *= 2
        parents = below[:, (level // group) * LANES : (level // group + 1) * LANES]
    chain_ref[:, LANES : 2 * LANES] = parents
    while level < leaf_count:
        for index in range(level // group, 2 * level // group):
            lanes = slice(index * LANES, (index + 1) * LANES)
            chain_ref[:, index * tile : (index + 1) * tile] = children(chain_ref[:, lanes], index)
        level *= 2
    copies[1].wait()
    copies[2].wait()
    step = group * width
    root = jnp.zeros((columns, rank), F32)
    for index in range(leaf_count // group):
        spots = slice(index * step, (index + 1) * step)
        start = (leaf_count // group + index) * LANES
        high, low = halves(bases_ref[:, spots])
        basis = split_dot(
            dot_nn, chain_ref[:, start : start + LANES],
            spread_bases(high, group), spread_bases(low, group),
        )
        high, low = halves(basis)
        high_ref[:, spots] = high
        low_ref[:, spots] = low
        dens = dens_ref[:, spots]
        root += dot_nt(dens, high) + dot_nt(dens, low)
    root = jnp.concatenate([root, jnp.zeros((columns, LANES - rank), F32)], axis=1)
    high = root.astype(BF16).astype(F32)
    rest = root - high
    middle = rest.astype(BF16).astype(F32)
    last = (rest - middle).astype(BF16).astype(F32)
    packed = high + pltpu.roll(middle, rank, 1) + pltpu.roll(last, 2 * rank, 1)
    root_ref[...] = packed.astype(BF16)
    for copy in copies[3:]:
        copy.wait()


def select_kernel(
    faces, far_groups, send_ref, dens_ref, root_ref, *refs,
):
    other_refs, out_refs = refs[: far_groups - 1], refs[far_groups - 1 :]
    device = lax.axis_index("leaf")
    columns = dens_ref.shape[0]
    cap, device_count = send_ref.shape[1:]
    own = lax.broadcasted_iota(jnp.int32, (cap, device_count), 1) == device
    for (directions, stride), out_ref in zip(faces, out_refs):
        table = send_ref[directions[0]]
        if len(directions) > 1:
            table = jnp.where(device // stride % 2 == 0, table, send_ref[directions[1]])
        picks = jnp.max(jnp.where(own, table.astype(F32), 0.0), axis=1, keepdims=True)
        for place in range(cap):
            leaf = picks[place, 0].astype(jnp.int32)
            for part, panel_ref in enumerate((dens_ref, *other_refs)):
                row = (place * far_groups + part) * columns
                out_ref[row : row + columns, :] = panel_ref[
                    :, pl.ds(pl.multiple_of(leaf * LANES, LANES), LANES)
                ]
        out_ref[cap * far_groups * columns :, :] = root_ref[...]


def near_kernel(
    faces, far_groups, share, *refs,
):
    source_refs, refs = refs[:share], refs[share:]
    dens_ref, refs = refs[0], refs[1:]
    other_refs, refs = refs[: far_groups - 1], refs[far_groups - 1 :]
    got_refs, refs = refs[: len(faces)], refs[len(faces) :]
    block_ref, refs = refs[0], refs[1:]
    mate_refs, refs = refs[: share - 1], refs[share - 1 :]
    refs = refs[1:]
    out_refs, refs = refs[:far_groups], refs[far_groups:]
    power_refs, refs = refs[: far_groups - 1], refs[far_groups - 1 :]
    smem_refs, (buffer_ref, sems) = refs[:share], refs[share:]
    columns, points = dens_ref.shape
    leaf_count, near_count, width, _ = block_ref.shape
    copies = fetch([(source_ref, smem) for source_ref, smem in zip(source_refs, smem_refs)], sems)
    cap = (buffer_ref.shape[0] - leaf_count) // len(FACE_SIGNS)
    for (directions, _), got_ref in zip(faces, got_refs):
        for direction in directions:
            for place in range(cap):
                row = place * far_groups * columns
                buffer_ref[leaf_count + direction * cap + place] = got_ref[
                    row : row + far_groups * columns, :
                ]
    for part, panel_ref in enumerate((dens_ref, *other_refs)):
        rows = slice(part * columns, (part + 1) * columns)
        for leaf in range(leaf_count):
            buffer_ref[leaf, rows, :] = panel_ref[:, leaf * width : (leaf + 1) * width]
    words = packed_words(jnp.concatenate([source_ref[...] for source_ref in source_refs], axis=0))
    early = 3 * leaf_count // 8
    own_ref, sent_refs = out_refs[0], out_refs[1:]
    for leaf in range(leaf_count):
        if leaf < early:
            slots = unpacked(words, near_count * share, leaf)
        else:
            if leaf == early:
                for copy in copies:
                    copy.wait()
            slots = [smem[block, leaf] for smem in smem_refs for block in range(near_count)]
        panels = [buffer_ref[slot] for slot in slots]
        blocks = [
            blocks_ref[leaf, block]
            for blocks_ref in (block_ref, *mate_refs)
            for block in range(near_count)
        ]
        total = dot_nt(jnp.concatenate(panels, axis=1), jnp.concatenate(blocks, axis=1))
        lanes = slice(leaf * width, (leaf + 1) * width)
        own_ref[:, lanes] = total[:columns]
        for part, (sent_ref, power_ref) in enumerate(zip(sent_refs, power_refs), 1):
            term = total[part * columns : (part + 1) * columns]
            peak = jnp.max(jnp.abs(term), axis=0, keepdims=True)
            power = jnp.floor(jnp.log2(jnp.maximum(peak, 2.0**-100))) + 1.0
            steps = jnp.floor(term * (STEPS * jnp.exp2(-power)) + 0.5)
            sent_ref[:, lanes] = steps.astype(jnp.int32).astype(jnp.int16)
            power_ref[leaf : leaf + 1, :] = power
    for sent_ref, power_ref in zip(sent_refs, power_refs):
        power = power_ref[...].astype(jnp.int32).astype(jnp.int16)
        for first in range(0, leaf_count, columns):
            spot = points + first // columns * width
            sent_ref[:, spot : spot + width] = power[first : first + columns]


def coupled(leaves, table_ref, coupling_ref, turned_ref):
    far_count, rank = coupling_ref.shape[1:3]
    columns = turned_ref.shape[1] // 2
    group = LANES // rank
    words = packed_words(table_ref[...])
    parts = []
    for leaf in leaves:
        maps = jnp.concatenate([coupling_ref[leaf, j] for j in range(far_count)], axis=1)
        maps = jnp.concatenate(halves(maps), axis=0)
        picked = jnp.concatenate(
            [
                turned_ref[pl.ds(pl.multiple_of(source * rank, rank), rank), :]
                for source in unpacked(words, far_count, leaf)
            ],
            axis=0,
        )
        out = dot_nn(maps, picked)
        parts.append(out[:rank] + out[rank:])
        if len(parts) == group:
            turned = jnp.concatenate(parts, axis=0).T
            yield turned[:columns] + turned[columns:]
            parts = []


def couple_kernel(
    table_ref, coupling_ref, dens_ref, bases_ref, turned_ref, out_ref,
):
    columns, points = dens_ref.shape
    leaf_count, _, rank = coupling_ref.shape[:3]
    width = points // leaf_count
    upper = lax.broadcasted_iota(jnp.int32, (rank, 2 * columns), 1) < columns
    for leaf in range(leaf_count):
        spots = slice(leaf * width, (leaf + 1) * width)
        rows = jnp.concatenate(halves(bases_ref[:, spots]), axis=0)
        dens = dens_ref[:, spots]
        twice = dot_nt(rows, jnp.concatenate([dens, dens], axis=0))
        high, low = halves(twice[:rank] + twice[rank:])
        turned_ref[leaf * rank : (leaf + 1) * rank, :] = jnp.where(
            upper, high.astype(F32), low.astype(F32)
        ).astype(BF16)
    leaves = range(out_ref.shape[1] // rank)
    for index, field in enumerate(coupled(leaves, table_ref, coupling_ref, turned_ref)):
        out_ref[:, index * LANES : (index + 1) * LANES] = field


def project_kernel(
    table_ref, coupling_ref, turned_ref, first_ref, bases_ref, near_ref, out_ref,
):
    rank, points = bases_ref.shape
    leaf_count = coupling_ref.shape[0]
    group = LANES // rank
    step = group * points // leaf_count

    def project(index, field):
        spots = slice(index * step, (index + 1) * step)
        high, low = halves(bases_ref[:, spots])
        out_ref[:, spots] = near_ref[:, spots] + split_dot(
            dot_nn, field, spread_bases(high, group), spread_bases(low, group)
        )

    done = first_ref.shape[1] // LANES
    for index in range(done):
        project(index, first_ref[:, index * LANES : (index + 1) * LANES])
    leaves = range(done * group, leaf_count)
    for index, field in enumerate(coupled(leaves, table_ref, coupling_ref, turned_ref)):
        project(done + index, field)


def paths_kernel(turns, exchanged, upper_ref, cross_ref, high_ref, low_ref, map_ref):
    device = lax.axis_index("leaf")
    rank = upper_ref.shape[1]
    device_count = upper_ref.shape[0] // 2
    downs = {device_count: None}
    level = device_count
    while level > 4:
        node = level + device // (device_count // level)
        below = downs[level]
        matrix = upper_ref[node]
        downs[level // 2] = matrix if below is None else split_dot(dot_nn, below, *halves(matrix))
        level //= 2
    for level in sorted(downs):
        place = device // (device_count // level)
        for index in range(level):
            if level == 4:
                map_ref[level + index] = jnp.zeros((rank, rank), F32)
            else:
                above = map_ref[(level + index) // 2]
                map_ref[level + index] = split_dot(
                    dot_nt, above, *halves(upper_ref[level + index])
                )
        third = jnp.where(place % 2 == 0, place + 3, place - 3)
        for slot, other in enumerate((place - 2, place + 2, third)):
            inside = (other >= 0) & (other < level)
            matrix = cross_ref[level + place, slot]
            if downs[level] is not None:
                matrix = split_dot(dot_nn, downs[level], *halves(matrix))
            node = level + jnp.clip(other, 0, level - 1)
            map_ref[node] = map_ref[node] + jnp.where(inside, matrix, 0.0)
    zero = jnp.zeros((rank, LANES - 3 * rank), F32)
    for place, turn in enumerate(turns):
        matrix = map_ref[device_count + (device ^ turn if exchanged else turn)]
        matrix = jnp.concatenate([matrix] * 3 + [zero], axis=1)
        high, low = halves(matrix)
        high_ref[:, place * LANES : (place + 1) * LANES] = high
        low_ref[:, place * LANES : (place + 1) * LANES] = low


def far_kernel(
    tiles, path_high_ref, path_low_ref, high_ref, low_ref, term_ref, *refs,
):
    root_refs, out_ref = refs[:-1], refs[-1]
    columns, points = out_ref.shape
    pieces = []
    for rows, root_ref in zip(tiles, root_refs):
        pieces += [root_ref[row : row + columns, :] for row in rows]
    roots = jnp.concatenate(pieces, axis=1)
    field = dot_nt(roots, path_high_ref[...]) + dot_nt(roots, path_low_ref[...])
    step = 4 * LANES
    for first in range(0, points, step):
        spots = slice(first, first + step)
        out_ref[:, spots] = term_ref[:, spots] + split_dot(
            dot_nn, field, high_ref[:, spots], low_ref[:, spots]
        )


def add_kernel(leaf_count, term_ref, *refs):
    sent_refs, (out_hbm, sum_ref, sems) = refs[:-3], refs[-3:]
    columns, points = sum_ref.shape
    width = points // leaf_count
    factors = []
    for sent_ref in sent_refs:
        powers = [
            sent_ref[:, points + first // columns * width :][:, :width]
            for first in range(0, leaf_count, columns)
        ]
        power = jnp.concatenate([p.astype(jnp.int32).astype(F32) for p in powers], axis=0)
        factors.append(jnp.exp2(power) * (1.0 / STEPS))
    chunk_count = sems.shape[0]
    step = points // chunk_count
    copies = []
    for index in range(chunk_count):
        spots = slice(index * step, (index + 1) * step)
        total = term_ref[:, spots]
        for sent_ref, factor in zip(sent_refs, factors):
            steps = sent_ref[:, spots].astype(jnp.int32).astype(F32)
            leaves = range(index * leaf_count // chunk_count, (index + 1) * leaf_count // chunk_count)
            scale = jnp.concatenate([factor[leaf : leaf + 1] for leaf in leaves], axis=1)
            total = total + steps * scale
        sum_ref[:, spots] = total
        copies += fetch(
            [(sum_ref.at[:, pl.ds(index * step, step)], out_hbm.at[:, pl.ds(index * step, step)])],
            sems.at[pl.ds(index, 1)],
        )
    for copy in copies:
        copy.wait()


def hbm(value):
    return pltpu.with_memory_space_constraint(value, pltpu.HBM)


def hint(micros):
    return pl.CostEstimate(flops=0, bytes_accessed=int(micros * 3.69e6), transcendentals=0)


def local(
    densities,
    bases,
    near_blocks,
    near_src,
    send_leaf,
    far_src,
    leaf_coupling,
    local_transfer,
    upper_transfer,
    up_coupling,
):
    leaf_devices = lax.axis_size("leaf")
    far_groups = lax.axis_size("far")
    share = lax.axis_size("mate")
    side = cube_side(leaf_devices)
    offsets = face_offsets(leaf_devices)
    columns, points = densities.shape
    leaf_count, near_count, width, _ = near_blocks.shape
    rank = bases.shape[0]
    cap = send_leaf.shape[2]
    node_count = local_transfer.shape[1]
    params = pltpu.CompilerParams(vmem_limit_bytes=16 * 2**20)
    dma = pltpu.SemaphoreType.DMA

    def rotated(value, axis, shift):
        count = lax.axis_size(axis)
        return lax.ppermute(value, axis, [(i, (i - shift) % count) for i in range(count)])

    def crossed(value, turn):
        return lax.ppermute(value, "leaf", [(i, i ^ turn) for i in range(leaf_devices)])

    sources = near_src.T
    others = [rotated(densities, "far", part) for part in range(1, far_groups)]
    all_sources = [sources] + [rotated(sources, "mate", part) for part in range(1, share)]
    send = send_leaf.transpose(1, 2, 0)
    moved = [
        densities, send, sources, far_src.T, upper_transfer, up_coupling, leaf_coupling, near_blocks,
    ]
    (
        basis, dens, send, sources, far_table, upper, cross, coupling, blocks, high, low, root,
    ) = pl.pallas_call(
        up_kernel,
        out_shape=[jax.ShapeDtypeStruct(value.shape, value.dtype) for value in (bases, *moved)]
        + [
            jax.ShapeDtypeStruct((rank, points), BF16),
            jax.ShapeDtypeStruct((rank, points), BF16),
            jax.ShapeDtypeStruct((columns, LANES), BF16),
        ],
        in_specs=[HBM] * (2 + len(moved)),
        out_specs=[VMEM] * (4 + len(moved)),
        scratch_shapes=[
            pltpu.VMEM((rank, rank, node_count), F32),
            pltpu.VMEM((node_count * rank, LANES), F32),
            pltpu.VMEM((rank, node_count * rank), F32),
            dma((2 + len(moved),)),
        ],
        compiler_params=params,
        cost_estimate=hint(3.5),
        name="up",
    )(hbm(local_transfer[0].transpose(1, 2, 0)), hbm(bases), *map(hbm, moved))
    all_sources[0] = sources

    later_blocks, others, all_sources, root = lax.optimization_barrier(
        (blocks, others, all_sources, root)
    )
    mate_blocks = [rotated(later_blocks, "mate", part) for part in range(1, share)]

    if side == 2:
        faces = [((2 * axis, 2 * axis + 1), 2**axis) for axis in (2, 0, 1)]
    else:
        faces = [((direction,), offset) for direction, offset in enumerate(offsets)]
    chunk = (cap * far_groups + 1) * columns
    outgoing = pl.pallas_call(
        functools.partial(select_kernel, faces, far_groups),
        out_shape=[jax.ShapeDtypeStruct((chunk, LANES), BF16)] * len(faces),
        in_specs=[VMEM] * (2 + far_groups),
        out_specs=[VMEM] * len(faces),
        compiler_params=params,
        cost_estimate=hint(1),
        name="select",
    )(send, dens, root, *others)
    outgoing, dens = lax.optimization_barrier((outgoing, dens))
    first_leaves = leaf_count // 2
    turned, leaf_local = pl.pallas_call(
        couple_kernel,
        out_shape=[
            jax.ShapeDtypeStruct((leaf_count * rank, 2 * columns), BF16),
            jax.ShapeDtypeStruct((columns, first_leaves * rank), F32),
        ],
        in_specs=[VMEM] * 4,
        out_specs=[VMEM] * 2,
        compiler_params=params,
        cost_estimate=hint(2),
        name="couple",
    )(far_table, coupling, dens, basis)
    tail = cap * far_groups * columns
    if side == 2:
        arrived = [crossed(value, stride) for (_, stride), value in zip(faces, outgoing)]
        far_one, _, near_two = (value[tail : tail + columns] for value in arrived)
        later, leaf_local = lax.optimization_barrier((arrived[0][-4 * columns :], leaf_local))
        across = crossed(later, 2)
        held = jnp.concatenate([near_two, far_one, across[-columns:]], axis=0)
        beside = crossed(held, 1)
        turns = [0] + [stride for _, stride in faces] + [6, 3, 5, 7]
        roots = [([0], root)] + [([tail], value) for value in arrived]
        roots += [([3 * columns], across), ([0, columns, 2 * columns], beside)]
    else:
        arrived = [shifted(value, "leaf", stride) for (_, stride), value in zip(faces, outgoing)]
        turns = list(range(leaf_devices))
        everyone = lax.all_gather(root, "leaf", axis=0, tiled=True)
        roots = [([turn * columns for turn in turns], everyone)]
    slots = leaf_count + len(offsets) * cap
    tables = -(-leaf_count // columns) * width
    partials = pl.pallas_call(
        functools.partial(near_kernel, faces, far_groups, share),
        out_shape=[jax.ShapeDtypeStruct((columns, points), F32)]
        + [jax.ShapeDtypeStruct((columns, points + tables), jnp.int16)] * (far_groups - 1),
        in_specs=[VMEM] * (2 * share + far_groups + len(faces) + 1),
        out_specs=[VMEM] * far_groups,
        scratch_shapes=[pltpu.VMEM((leaf_count, width), F32)] * (far_groups - 1)
        + [pltpu.SMEM(sources.shape, jnp.int32)] * share
        + [pltpu.VMEM((slots, far_groups * columns, width), BF16), dma((share,))],
        compiler_params=params,
        cost_estimate=hint(3),
        name="near",
    )(
        *all_sources, dens, *others, *arrived, blocks, *mate_blocks, leaf_local,
    )
    upper, cross, near_own = lax.optimization_barrier((upper, cross, partials[0]))
    paths = pl.pallas_call(
        functools.partial(paths_kernel, turns, side == 2),
        out_shape=[jax.ShapeDtypeStruct((rank, leaf_devices * LANES), BF16)] * 2,
        in_specs=[VMEM] * 2,
        out_specs=[VMEM] * 2,
        scratch_shapes=[pltpu.VMEM((2 * leaf_devices, rank, rank), F32)],
        compiler_params=params,
        cost_estimate=hint(0.7),
        name="paths",
    )(upper, cross)
    received = [rotated(partials[part], "far", -part) for part in range(1, far_groups)]
    partial = pl.pallas_call(
        project_kernel,
        out_shape=jax.ShapeDtypeStruct((columns, points), F32),
        in_specs=[VMEM] * 6,
        out_specs=VMEM,
        compiler_params=params,
        cost_estimate=hint(1.5),
        name="project",
    )(far_table, coupling, turned, leaf_local, basis, near_own)
    total = pl.pallas_call(
        functools.partial(far_kernel, [rows for rows, _ in roots]),
        out_shape=jax.ShapeDtypeStruct((columns, points), F32),
        in_specs=[VMEM] * (5 + len(roots)),
        out_specs=VMEM,
        compiler_params=params,
        cost_estimate=hint(0.6),
        name="far",
    )(*paths, high, low, partial, *[value for _, value in roots])
    return pl.pallas_call(
        functools.partial(add_kernel, leaf_count),
        out_shape=jax.ShapeDtypeStruct((columns, points), F32),
        in_specs=[VMEM] * (1 + len(received)),
        out_specs=HBM,
        scratch_shapes=[pltpu.VMEM((columns, points), F32), dma((4,))],
        compiler_params=params,
        cost_estimate=hint(0.5),
        name="add",
    )(total, *received)


def solution(mesh):
    leaf_devices, rhs_devices = mesh.shape["leaf"], mesh.shape["rhs"]
    share = 2 if rhs_devices % 2 == 0 else 1
    split = Mesh(
        mesh.devices.reshape(leaf_devices, rhs_devices // share, share), ("leaf", "far", "mate")
    )
    rhs = ("far", "mate")
    in_specs = (
        P(rhs, "leaf"),
        P(None, "leaf"),
        P("leaf", rhs, None, None),
        P("leaf", rhs),
        P(),
        P("leaf", None),
        P("leaf", None, None, None),
        P("leaf", None, None, None),
        P(),
        P(),
    )
    return jax.shard_map(
        local, mesh=split, in_specs=in_specs, out_specs=P(rhs, "leaf"), check_vma=False
    )
```

```python
import functools

import jax
import jax.numpy as jnp
from jax import lax
from jax.experimental import pallas as pl
from jax.experimental.pallas import tpu as pltpu
from jax.sharding import Mesh
from jax.sharding import PartitionSpec as P

FACE_SIGNS = ((1, 0), (-1, 0), (1, 1), (-1, 1), (1, 2), (-1, 2))
F32 = jnp.float32
BF16 = jnp.bfloat16
LANES = 128
STEPS = 32000.0
VMEM = pl.BlockSpec(memory_space=pltpu.VMEM)
HBM = pl.BlockSpec(memory_space=pltpu.HBM)


def cube_side(device_count):
    return max((edge_len for edge_len in range(1, 65) if edge_len**3 <= device_count))


def face_offsets(device_count):
    side_len = cube_side(device_count)
    return [face_sign * side_len**axis_pos for face_sign, axis_pos in FACE_SIGNS]


def shifted(value, axis, steps):
    count = lax.axis_size(axis)
    first, last = (max(0, -steps), min(count, count - steps))
    return lax.ppermute(value, axis, [(source, source + steps) for source in range(first, last)])


def halves(value):
    high = value.astype(BF16)
    return high, (value - high.astype(F32)).astype(BF16)


def dot_nn(left, right):
    return lax.dot_general(left, right, (((1,), (0,)), ((), ())), preferred_element_type=F32)


def dot_nt(left, right):
    return lax.dot_general(left, right, (((1,), (1,)), ((), ())), preferred_element_type=F32)


def split_dot(dot, rows, right_high, right_low):
    count = rows.shape[0]
    high, low = halves(rows)
    both = jnp.concatenate([high, low], axis=0)
    out = dot(both, right_high) + dot(both, right_low)
    return out[:count] + out[count:]


def spread_bases(block, group):
    rank, lanes = block.shape
    width = lanes // group
    zero = jnp.zeros((rank, width), block.dtype)
    rows = []
    for slot in range(group):
        pieces = [zero] * group
        pieces[slot] = block[:, slot * width : (slot + 1) * width]
        rows.append(jnp.concatenate(pieces, axis=1))
    return jnp.concatenate(rows, axis=0)


def packed_words(table):
    words = []
    for first in range(0, table.shape[0], 4):
        word = table[first : first + 1]
        for row in range(first + 1, min(first + 4, table.shape[0])):
            word = word + (table[row : row + 1] << (8 * (row - first)))
        words.append(word)
    return words


def unpacked(words, count, place):
    values = [word[0, place] for word in words]
    return [(values[row // 4] >> (8 * (row % 4))) & 255 for row in range(count)]


def fetch(pairs, sems):
    copies = []
    for index, (source, target) in enumerate(pairs):
        copy = pltpu.make_async_copy(source, target, sems.at[index])
        copy.start()
        copies.append(copy)
    return copies


def up_kernel(
    maps_hbm, bases_hbm, *refs,
):
    count = (len(refs) - 7) // 2
    hbm_refs, bases_ref, vmem_refs = refs[:count], refs[count], refs[count + 1 : 2 * count + 1]
    halves_ref, root_ref, maps_ref, spread_ref, chain_ref, sems = refs[2 * count + 1 :]
    dens_ref = vmem_refs[0]
    copies = fetch(
        [(maps_hbm, maps_ref), (bases_hbm, bases_ref), *zip(hbm_refs, vmem_refs)], sems
    )
    columns, points = dens_ref.shape
    rank, _, node_count = maps_ref.shape
    group = LANES // rank
    leaf_count = node_count // 2
    width = points // leaf_count
    copies[0].wait()
    node = lax.broadcasted_iota(jnp.int32, (node_count, LANES), 0)
    block = lax.broadcasted_iota(jnp.int32, (node_count, LANES), 1) // rank
    parent = node // 2 % group
    for first in range(0, rank, group):
        slab = maps_ref[first : first + group].reshape(group * rank, node_count).T
        turned = [slab] + [pltpu.roll(slab, turn * rank, 1) for turn in range(1, group)]
        for row in range(group):
            placed = jnp.zeros_like(slab)
            for place in range(group):
                here = (parent == place) & (block == place)
                placed = jnp.where(here, turned[(place - row) % group], placed)
            spread_ref[pl.ds(first + row, node_count, stride=rank), :] = placed
    tile = 2 * group * rank

    def children(parents, index):
        high, low = halves(spread_ref[index * tile : (index + 1) * tile, :])
        return split_dot(dot_nt, parents, high, low)

    row = lax.broadcasted_iota(jnp.int32, (rank, LANES), 0)
    lane = lax.broadcasted_iota(jnp.int32, (rank, LANES), 1)
    level = 1
    parents = jnp.where(lane == row + rank, 1.0, 0.0)
    while level < group:
        below = children(parents, 0)
        level *= 2
        parents = below[:, (level // group) * LANES : (level // group + 1) * LANES]
    chain_ref[:, LANES : 2 * LANES] = parents
    while level < leaf_count:
        for index in range(level // group, 2 * level // group):
            lanes = slice(index * LANES, (index + 1) * LANES)
            chain_ref[:, index * tile : (index + 1) * tile] = children(chain_ref[:, lanes], index)
        level *= 2
    copies[1].wait()
    copies[2].wait()
    step = group * width
    root = jnp.zeros((columns, rank), F32)
    for index in range(leaf_count // group):
        spots = slice(index * step, (index + 1) * step)
        start = (leaf_count // group + index) * LANES
        high, low = halves(bases_ref[:, spots])
        basis = split_dot(
            dot_nn, chain_ref[:, start : start + LANES],
            spread_bases(high, group), spread_bases(low, group),
        )
        high, low = halves(basis)
        halves_ref[:rank, spots] = high
        halves_ref[rank:, spots] = low
        dens = dens_ref[:, spots]
        root += dot_nt(dens, high) + dot_nt(dens, low)
    root = jnp.concatenate([root, jnp.zeros((columns, LANES - rank), F32)], axis=1)
    high = root.astype(BF16).astype(F32)
    rest = root - high
    middle = rest.astype(BF16).astype(F32)
    last = (rest - middle).astype(BF16).astype(F32)
    packed = high + pltpu.roll(middle, rank, 1) + pltpu.roll(last, 2 * rank, 1)
    root_ref[...] = packed.astype(BF16)
    for copy in copies[3:]:
        copy.wait()


def select_kernel(
    faces, far_groups, send_ref, dens_ref, root_ref, *refs,
):
    other_refs, out_refs = refs[: far_groups - 1], refs[far_groups - 1 :]
    device = lax.axis_index("leaf")
    columns = dens_ref.shape[0]
    cap, device_count = send_ref.shape[1:]
    own = lax.broadcasted_iota(jnp.int32, (cap, device_count), 1) == device
    for (directions, stride), out_ref in zip(faces, out_refs):
        table = send_ref[directions[0]]
        if len(directions) > 1:
            table = jnp.where(device // stride % 2 == 0, table, send_ref[directions[1]])
        picks = jnp.max(jnp.where(own, table.astype(F32), 0.0), axis=1, keepdims=True)
        for place in range(cap):
            leaf = picks[place, 0].astype(jnp.int32)
            for part, panel_ref in enumerate((dens_ref, *other_refs)):
                row = (place * far_groups + part) * columns
                out_ref[row : row + columns, :] = panel_ref[
                    :, pl.ds(pl.multiple_of(leaf * LANES, LANES), LANES)
                ]
        out_ref[cap * far_groups * columns :, :] = root_ref[...]


def near_kernel(
    faces, far_groups, share, *refs,
):
    source_refs, refs = refs[:share], refs[share:]
    dens_ref, refs = refs[0], refs[1:]
    other_refs, refs = refs[: far_groups - 1], refs[far_groups - 1 :]
    got_refs, refs = refs[: len(faces)], refs[len(faces) :]
    block_ref, refs = refs[0], refs[1:]
    mate_refs, refs = refs[: share - 1], refs[share - 1 :]
    refs = refs[1:]
    out_refs, refs = refs[:far_groups], refs[far_groups:]
    power_refs, refs = refs[: far_groups - 1], refs[far_groups - 1 :]
    (buffer_ref,) = refs
    columns, points = dens_ref.shape
    leaf_count, near_count, width, _ = block_ref.shape
    cap = (buffer_ref.shape[0] - leaf_count) // len(FACE_SIGNS)
    for (directions, _), got_ref in zip(faces, got_refs):
        for direction in directions:
            for place in range(cap):
                row = place * far_groups * columns
                buffer_ref[leaf_count + direction * cap + place] = got_ref[
                    row : row + far_groups * columns, :
                ]
    for part, panel_ref in enumerate((dens_ref, *other_refs)):
        rows = slice(part * columns, (part + 1) * columns)
        for leaf in range(leaf_count):
            buffer_ref[leaf, rows, :] = panel_ref[:, leaf * width : (leaf + 1) * width]
    words = packed_words(jnp.concatenate([source_ref[...] for source_ref in source_refs], axis=0))
    own_ref, sent_refs = out_refs[0], out_refs[1:]
    for leaf in range(leaf_count):
        panels = [buffer_ref[slot] for slot in unpacked(words, near_count * share, leaf)]
        blocks = [
            blocks_ref[leaf, block]
            for blocks_ref in (block_ref, *mate_refs)
            for block in range(near_count)
        ]
        total = dot_nt(jnp.concatenate(panels, axis=1), jnp.concatenate(blocks, axis=1))
        lanes = slice(leaf * width, (leaf + 1) * width)
        own_ref[:, lanes] = total[:columns]
        for part, (sent_ref, power_ref) in enumerate(zip(sent_refs, power_refs), 1):
            term = total[part * columns : (part + 1) * columns]
            peak = jnp.max(jnp.abs(term), axis=0, keepdims=True)
            power = jnp.floor(jnp.log2(jnp.maximum(peak, 2.0**-100))) + 1.0
            steps = jnp.floor(term * (STEPS * jnp.exp2(-power)) + 0.5)
            sent_ref[:, lanes] = steps.astype(jnp.int32).astype(jnp.int16)
            power_ref[leaf : leaf + 1, :] = power
    for sent_ref, power_ref in zip(sent_refs, power_refs):
        power = power_ref[...].astype(jnp.int32).astype(jnp.int16)
        for first in range(0, leaf_count, columns):
            spot = points + first // columns * width
            sent_ref[:, spot : spot + width] = power[first : first + columns]


def coupled(leaves, table_ref, coupling_ref, turned_ref):
    far_count, rank = coupling_ref.shape[1:3]
    columns = turned_ref.shape[1] // 2
    group = LANES // rank
    words = packed_words(table_ref[...])
    parts = []
    for leaf in leaves:
        maps = jnp.concatenate([coupling_ref[leaf, j] for j in range(far_count)], axis=1)
        maps = jnp.concatenate(halves(maps), axis=0)
        picked = jnp.concatenate(
            [
                turned_ref[pl.ds(pl.multiple_of(source * rank, rank), rank), :]
                for source in unpacked(words, far_count, leaf)
            ],
            axis=0,
        )
        out = dot_nn(maps, picked)
        parts.append(out[:rank] + out[rank:])
        if len(parts) == group:
            turned = jnp.concatenate(parts, axis=0).T
            yield turned[:columns] + turned[columns:]
            parts = []


def couple_kernel(
    table_ref, coupling_ref, dens_ref, bases_ref, turned_ref, out_ref,
):
    columns, points = dens_ref.shape
    leaf_count, _, rank = coupling_ref.shape[:3]
    width = points // leaf_count
    upper = lax.broadcasted_iota(jnp.int32, (rank, 2 * columns), 1) < columns
    for leaf in range(leaf_count):
        spots = slice(leaf * width, (leaf + 1) * width)
        rows = jnp.concatenate(halves(bases_ref[:, spots]), axis=0)
        dens = dens_ref[:, spots]
        twice = dot_nt(rows, jnp.concatenate([dens, dens], axis=0))
        high, low = halves(twice[:rank] + twice[rank:])
        turned_ref[leaf * rank : (leaf + 1) * rank, :] = jnp.where(
            upper, high.astype(F32), low.astype(F32)
        ).astype(BF16)
    leaves = range(out_ref.shape[1] // rank)
    for index, field in enumerate(coupled(leaves, table_ref, coupling_ref, turned_ref)):
        out_ref[:, index * LANES : (index + 1) * LANES] = field


def project_kernel(
    table_ref, coupling_ref, turned_ref, first_ref, bases_ref, near_ref, out_ref,
):
    rank, points = bases_ref.shape
    leaf_count = coupling_ref.shape[0]
    group = LANES // rank
    step = group * points // leaf_count

    def project(index, field):
        spots = slice(index * step, (index + 1) * step)
        high, low = halves(bases_ref[:, spots])
        out_ref[:, spots] = near_ref[:, spots] + split_dot(
            dot_nn, field, spread_bases(high, group), spread_bases(low, group)
        )

    done = first_ref.shape[1] // LANES
    for index in range(done):
        project(index, first_ref[:, index * LANES : (index + 1) * LANES])
    leaves = range(done * group, leaf_count)
    for index, field in enumerate(coupled(leaves, table_ref, coupling_ref, turned_ref)):
        project(done + index, field)


def paths_kernel(turns, exchanged, upper_ref, cross_ref, high_ref, low_ref, map_ref):
    device = lax.axis_index("leaf")
    rank = upper_ref.shape[1]
    device_count = upper_ref.shape[0] // 2
    downs = {device_count: None}
    level = device_count
    while level > 4:
        node = level + device // (device_count // level)
        below = downs[level]
        matrix = upper_ref[node]
        downs[level // 2] = matrix if below is None else split_dot(dot_nn, below, *halves(matrix))
        level //= 2
    for level in sorted(downs):
        place = device // (device_count // level)
        for index in range(level):
            if level == 4:
                map_ref[level + index] = jnp.zeros((rank, rank), F32)
            else:
                above = map_ref[(level + index) // 2]
                map_ref[level + index] = split_dot(
                    dot_nt, above, *halves(upper_ref[level + index])
                )
        third = jnp.where(place % 2 == 0, place + 3, place - 3)
        for slot, other in enumerate((place - 2, place + 2, third)):
            inside = (other >= 0) & (other < level)
            matrix = cross_ref[level + place, slot]
            if downs[level] is not None:
                matrix = split_dot(dot_nn, downs[level], *halves(matrix))
            node = level + jnp.clip(other, 0, level - 1)
            map_ref[node] = map_ref[node] + jnp.where(inside, matrix, 0.0)
    zero = jnp.zeros((rank, LANES - 3 * rank), F32)
    for place, turn in enumerate(turns):
        matrix = map_ref[device_count + (device ^ turn if exchanged else turn)]
        matrix = jnp.concatenate([matrix] * 3 + [zero], axis=1)
        high, low = halves(matrix)
        high_ref[:, place * LANES : (place + 1) * LANES] = high
        low_ref[:, place * LANES : (place + 1) * LANES] = low


def far_kernel(
    tiles, path_high_ref, path_low_ref, halves_ref, term_ref, *refs,
):
    root_refs, out_ref = refs[:-1], refs[-1]
    columns, points = out_ref.shape
    pieces = []
    for rows, root_ref in zip(tiles, root_refs):
        pieces += [root_ref[row : row + columns, :] for row in rows]
    roots = jnp.concatenate(pieces, axis=1)
    field = dot_nt(roots, path_high_ref[...]) + dot_nt(roots, path_low_ref[...])
    rows = jnp.concatenate(halves(field), axis=0)
    rows = jnp.concatenate([rows, rows], axis=1)
    step = 4 * LANES
    for first in range(0, points, step):
        spots = slice(first, first + step)
        out = dot_nn(rows, halves_ref[:, spots])
        out_ref[:, spots] = term_ref[:, spots] + (out[:columns] + out[columns:])


def add_kernel(leaf_count, term_ref, *refs):
    sent_refs, (out_hbm, sum_ref, sems) = refs[:-3], refs[-3:]
    columns, points = sum_ref.shape
    width = points // leaf_count
    factors = []
    for sent_ref in sent_refs:
        powers = [
            sent_ref[:, points + first // columns * width :][:, :width]
            for first in range(0, leaf_count, columns)
        ]
        power = jnp.concatenate([p.astype(jnp.int32).astype(F32) for p in powers], axis=0)
        factors.append(jnp.exp2(power) * (1.0 / STEPS))
    chunk_count = sems.shape[0]
    step = points // chunk_count
    copies = []
    for index in range(chunk_count):
        spots = slice(index * step, (index + 1) * step)
        total = term_ref[:, spots]
        for sent_ref, factor in zip(sent_refs, factors):
            steps = sent_ref[:, spots].astype(jnp.int32).astype(F32)
            leaves = range(index * leaf_count // chunk_count, (index + 1) * leaf_count // chunk_count)
            scale = jnp.concatenate([factor[leaf : leaf + 1] for leaf in leaves], axis=1)
            total = total + steps * scale
        sum_ref[:, spots] = total
        copies += fetch(
            [(sum_ref.at[:, pl.ds(index * step, step)], out_hbm.at[:, pl.ds(index * step, step)])],
            sems.at[pl.ds(index, 1)],
        )
    for copy in copies:
        copy.wait()


def hbm(value):
    return pltpu.with_memory_space_constraint(value, pltpu.HBM)


def hint(micros):
    return pl.CostEstimate(flops=0, bytes_accessed=int(micros * 3.69e6), transcendentals=0)


def local(
    densities,
    bases,
    near_blocks,
    near_src,
    send_leaf,
    far_src,
    leaf_coupling,
    local_transfer,
    upper_transfer,
    up_coupling,
):
    leaf_devices = lax.axis_size("leaf")
    far_groups = lax.axis_size("far")
    share = lax.axis_size("mate")
    side = cube_side(leaf_devices)
    offsets = face_offsets(leaf_devices)
    columns, points = densities.shape
    leaf_count, near_count, width, _ = near_blocks.shape
    rank = bases.shape[0]
    cap = send_leaf.shape[2]
    node_count = local_transfer.shape[1]
    params = pltpu.CompilerParams(vmem_limit_bytes=16 * 2**20)
    dma = pltpu.SemaphoreType.DMA

    def rotated(value, axis, shift):
        count = lax.axis_size(axis)
        return lax.ppermute(value, axis, [(i, (i - shift) % count) for i in range(count)])

    def crossed(value, turn):
        return lax.ppermute(value, "leaf", [(i, i ^ turn) for i in range(leaf_devices)])

    sources = near_src.T
    others = [rotated(densities, "far", part) for part in range(1, far_groups)]
    all_sources = [sources] + [rotated(sources, "mate", part) for part in range(1, share)]
    send = send_leaf.transpose(1, 2, 0)
    moved = [
        densities, send, sources, far_src.T, upper_transfer, up_coupling, leaf_coupling, near_blocks,
    ]
    (
        basis, dens, send, sources, far_table, upper, cross, coupling, blocks, subtree, root,
    ) = pl.pallas_call(
        up_kernel,
        out_shape=[jax.ShapeDtypeStruct(value.shape, value.dtype) for value in (bases, *moved)]
        + [
            jax.ShapeDtypeStruct((2 * rank, points), BF16),
            jax.ShapeDtypeStruct((columns, LANES), BF16),
        ],
        in_specs=[HBM] * (2 + len(moved)),
        out_specs=[VMEM] * (3 + len(moved)),
        scratch_shapes=[
            pltpu.VMEM((rank, rank, node_count), F32),
            pltpu.VMEM((node_count * rank, LANES), F32),
            pltpu.VMEM((rank, node_count * rank), F32),
            dma((2 + len(moved),)),
        ],
        compiler_params=params,
        cost_estimate=hint(3.5),
        name="up",
    )(hbm(local_transfer[0].transpose(1, 2, 0)), hbm(bases), *map(hbm, moved))
    all_sources[0] = sources

    later_blocks, others, all_sources, root = lax.optimization_barrier(
        (blocks, others, all_sources, root)
    )
    mate_blocks = [rotated(later_blocks, "mate", part) for part in range(1, share)]

    if side == 2:
        faces = [((2 * axis, 2 * axis + 1), 2**axis) for axis in (2, 1, 0)]
    else:
        faces = [((direction,), offset) for direction, offset in enumerate(offsets)]
    chunk = (cap * far_groups + 1) * columns
    outgoing = pl.pallas_call(
        functools.partial(select_kernel, faces, far_groups),
        out_shape=[jax.ShapeDtypeStruct((chunk, LANES), BF16)] * len(faces),
        in_specs=[VMEM] * (2 + far_groups),
        out_specs=[VMEM] * len(faces),
        compiler_params=params,
        cost_estimate=hint(1),
        name="select",
    )(send, dens, root, *others)
    outgoing, dens = lax.optimization_barrier((outgoing, dens))
    first_leaves = leaf_count // 2
    turned, leaf_local = pl.pallas_call(
        couple_kernel,
        out_shape=[
            jax.ShapeDtypeStruct((leaf_count * rank, 2 * columns), BF16),
            jax.ShapeDtypeStruct((columns, first_leaves * rank), F32),
        ],
        in_specs=[VMEM] * 4,
        out_specs=[VMEM] * 2,
        compiler_params=params,
        cost_estimate=hint(2),
        name="couple",
    )(far_table, coupling, dens, basis)
    tail = cap * far_groups * columns
    if side == 2:
        arrived = [crossed(value, stride) for (_, stride), value in zip(faces, outgoing)]
        far_one, near_two, _ = (value[tail : tail + columns] for value in arrived)
        later, leaf_local = lax.optimization_barrier((arrived[0][-4 * columns :], leaf_local))
        across = crossed(later, 2)
        held = jnp.concatenate([near_two, far_one, across[-columns:]], axis=0)
        beside = crossed(held, 1)
        turns = [0] + [stride for _, stride in faces] + [6, 3, 5, 7]
        roots = [([0], root)] + [([tail], value) for value in arrived]
        roots += [([3 * columns], across), ([0, columns, 2 * columns], beside)]
    else:
        arrived = [shifted(value, "leaf", stride) for (_, stride), value in zip(faces, outgoing)]
        turns = list(range(leaf_devices))
        everyone = lax.all_gather(root, "leaf", axis=0, tiled=True)
        roots = [([turn * columns for turn in turns], everyone)]
    slots = leaf_count + len(offsets) * cap
    tables = -(-leaf_count // columns) * width
    partials = pl.pallas_call(
        functools.partial(near_kernel, faces, far_groups, share),
        out_shape=[jax.ShapeDtypeStruct((columns, points), F32)]
        + [jax.ShapeDtypeStruct((columns, points + tables), jnp.int16)] * (far_groups - 1),
        in_specs=[VMEM] * (2 * share + far_groups + len(faces) + 1),
        out_specs=[VMEM] * far_groups,
        scratch_shapes=[pltpu.VMEM((leaf_count, width), F32)] * (far_groups - 1)
        + [
            pltpu.VMEM((slots, far_groups * columns, width), BF16),
        ],
        compiler_params=params,
        cost_estimate=hint(3),
        name="near",
    )(
        *all_sources, dens, *others, *arrived, blocks, *mate_blocks, leaf_local,
    )
    upper, cross, near_own = lax.optimization_barrier((upper, cross, partials[0]))
    paths = pl.pallas_call(
        functools.partial(paths_kernel, turns, side == 2),
        out_shape=[jax.ShapeDtypeStruct((rank, leaf_devices * LANES), BF16)] * 2,
        in_specs=[VMEM] * 2,
        out_specs=[VMEM] * 2,
        scratch_shapes=[pltpu.VMEM((2 * leaf_devices, rank, rank), F32)],
        compiler_params=params,
        cost_estimate=hint(0.7),
        name="paths",
    )(upper, cross)
    received = [rotated(partials[part], "far", -part) for part in range(1, far_groups)]
    partial = pl.pallas_call(
        project_kernel,
        out_shape=jax.ShapeDtypeStruct((columns, points), F32),
        in_specs=[VMEM] * 6,
        out_specs=VMEM,
        compiler_params=params,
        cost_estimate=hint(1.5),
        name="project",
    )(far_table, coupling, turned, leaf_local, basis, near_own)
    total = pl.pallas_call(
        functools.partial(far_kernel, [rows for rows, _ in roots]),
        out_shape=jax.ShapeDtypeStruct((columns, points), F32),
        in_specs=[VMEM] * (4 + len(roots)),
        out_specs=VMEM,
        compiler_params=params,
        cost_estimate=hint(0.6),
        name="far",
    )(*paths, subtree, partial, *[value for _, value in roots])
    return pl.pallas_call(
        functools.partial(add_kernel, leaf_count),
        out_shape=jax.ShapeDtypeStruct((columns, points), F32),
        in_specs=[VMEM] * (1 + len(received)),
        out_specs=HBM,
        scratch_shapes=[pltpu.VMEM((columns, points), F32), dma((4,))],
        compiler_params=params,
        cost_estimate=hint(0.5),
        name="add",
    )(total, *received)


def solution(mesh):
    leaf_devices, rhs_devices = mesh.shape["leaf"], mesh.shape["rhs"]
    share = 2 if rhs_devices % 2 == 0 else 1
    split = Mesh(
        mesh.devices.reshape(leaf_devices, rhs_devices // share, share), ("leaf", "far", "mate")
    )
    rhs = ("far", "mate")
    in_specs = (
        P(rhs, "leaf"),
        P(None, "leaf"),
        P("leaf", rhs, None, None),
        P("leaf", rhs),
        P(),
        P("leaf", None),
        P("leaf", None, None, None),
        P("leaf", None, None, None),
        P(),
        P(),
    )
    return jax.shard_map(
        local, mesh=split, in_specs=in_specs, out_specs=P(rhs, "leaf"), check_vma=False
    )
```

```python
import functools

import jax
import jax.numpy as jnp
from jax import lax
from jax.experimental import pallas as pl
from jax.experimental.pallas import tpu as pltpu
from jax.sharding import Mesh
from jax.sharding import PartitionSpec as P

FACE_SIGNS = ((1, 0), (-1, 0), (1, 1), (-1, 1), (1, 2), (-1, 2))
F32 = jnp.float32
BF16 = jnp.bfloat16
LANES = 128
STEPS = 32000.0
VMEM = pl.BlockSpec(memory_space=pltpu.VMEM)
HBM = pl.BlockSpec(memory_space=pltpu.HBM)


def cube_side(device_count):
    return max((edge_len for edge_len in range(1, 65) if edge_len**3 <= device_count))


def face_offsets(device_count):
    side_len = cube_side(device_count)
    return [face_sign * side_len**axis_pos for face_sign, axis_pos in FACE_SIGNS]


def shifted(value, axis, steps):
    count = lax.axis_size(axis)
    first, last = (max(0, -steps), min(count, count - steps))
    return lax.ppermute(value, axis, [(source, source + steps) for source in range(first, last)])


def halves(value):
    high = value.astype(BF16)
    return high, (value - high.astype(F32)).astype(BF16)


def dot_nn(left, right):
    return lax.dot_general(left, right, (((1,), (0,)), ((), ())), preferred_element_type=F32)


def dot_nt(left, right):
    return lax.dot_general(left, right, (((1,), (1,)), ((), ())), preferred_element_type=F32)


def split_dot(dot, rows, right_high, right_low):
    count = rows.shape[0]
    high, low = halves(rows)
    both = jnp.concatenate([high, low], axis=0)
    out = dot(both, right_high) + dot(both, right_low)
    return out[:count] + out[count:]


def spread_bases(block, group):
    rank, lanes = block.shape
    width = lanes // group
    zero = jnp.zeros((rank, width), block.dtype)
    rows = []
    for slot in range(group):
        pieces = [zero] * group
        pieces[slot] = block[:, slot * width : (slot + 1) * width]
        rows.append(jnp.concatenate(pieces, axis=1))
    return jnp.concatenate(rows, axis=0)


def packed_words(table):
    words = []
    for first in range(0, table.shape[0], 4):
        word = table[first : first + 1]
        for row in range(first + 1, min(first + 4, table.shape[0])):
            word = word + (table[row : row + 1] << (8 * (row - first)))
        words.append(word)
    return words


def unpacked(words, count, place):
    values = [word[0, place] for word in words]
    return [(values[row // 4] >> (8 * (row % 4))) & 255 for row in range(count)]


def fetch(pairs, sems):
    copies = []
    for index, (source, target) in enumerate(pairs):
        copy = pltpu.make_async_copy(source, target, sems.at[index])
        copy.start()
        copies.append(copy)
    return copies


def up_kernel(
    maps_hbm, bases_hbm, *refs,
):
    count = (len(refs) - 7) // 2
    hbm_refs, bases_ref, vmem_refs = refs[:count], refs[count], refs[count + 1 : 2 * count + 1]
    halves_ref, root_ref, maps_ref, spread_ref, chain_ref, sems = refs[2 * count + 1 :]
    dens_ref = vmem_refs[0]
    copies = fetch(
        [(maps_hbm, maps_ref), (bases_hbm, bases_ref), *zip(hbm_refs, vmem_refs)], sems
    )
    columns, points = dens_ref.shape
    rank, _, node_count = maps_ref.shape
    group = LANES // rank
    leaf_count = node_count // 2
    width = points // leaf_count
    copies[0].wait()
    node = lax.broadcasted_iota(jnp.int32, (node_count, LANES), 0)
    block = lax.broadcasted_iota(jnp.int32, (node_count, LANES), 1) // rank
    parent = node // 2 % group
    for first in range(0, rank, group):
        slab = maps_ref[first : first + group].reshape(group * rank, node_count).T
        turned = [slab] + [pltpu.roll(slab, turn * rank, 1) for turn in range(1, group)]
        for row in range(group):
            placed = jnp.zeros_like(slab)
            for place in range(group):
                here = (parent == place) & (block == place)
                placed = jnp.where(here, turned[(place - row) % group], placed)
            spread_ref[pl.ds(first + row, node_count, stride=rank), :] = placed
    tile = 2 * group * rank

    def children(parents, index):
        high, low = halves(spread_ref[index * tile : (index + 1) * tile, :])
        return split_dot(dot_nt, parents, high, low)

    row = lax.broadcasted_iota(jnp.int32, (rank, LANES), 0)
    lane = lax.broadcasted_iota(jnp.int32, (rank, LANES), 1)
    level = 1
    parents = jnp.where(lane == row + rank, 1.0, 0.0)
    while level < group:
        below = children(parents, 0)
        level *= 2
        parents = below[:, (level // group) * LANES : (level // group + 1) * LANES]
    chain_ref[:, LANES : 2 * LANES] = parents
    while level < leaf_count:
        for index in range(level // group, 2 * level // group):
            lanes = slice(index * LANES, (index + 1) * LANES)
            chain_ref[:, index * tile : (index + 1) * tile] = children(chain_ref[:, lanes], index)
        level *= 2
    copies[1].wait()
    copies[2].wait()
    step = group * width
    root = jnp.zeros((columns, rank), F32)
    for index in range(leaf_count // group):
        spots = slice(index * step, (index + 1) * step)
        start = (leaf_count // group + index) * LANES
        high, low = halves(bases_ref[:, spots])
        basis = split_dot(
            dot_nn, chain_ref[:, start : start + LANES],
            spread_bases(high, group), spread_bases(low, group),
        )
        high, low = halves(basis)
        halves_ref[:rank, spots] = high
        halves_ref[rank:, spots] = low
        dens = dens_ref[:, spots]
        root += dot_nt(dens, high) + dot_nt(dens, low)
    root = jnp.concatenate([root, jnp.zeros((columns, LANES - rank), F32)], axis=1)
    high = root.astype(BF16).astype(F32)
    rest = root - high
    middle = rest.astype(BF16).astype(F32)
    last = (rest - middle).astype(BF16).astype(F32)
    packed = high + pltpu.roll(middle, rank, 1) + pltpu.roll(last, 2 * rank, 1)
    root_ref[...] = packed.astype(BF16)
    for copy in copies[3:]:
        copy.wait()


def select_kernel(
    faces, far_groups, send_ref, dens_ref, root_ref, *refs,
):
    other_refs, out_refs = refs[: far_groups - 1], refs[far_groups - 1 :]
    device = lax.axis_index("leaf")
    columns = dens_ref.shape[0]
    cap, device_count = send_ref.shape[1:]
    own = lax.broadcasted_iota(jnp.int32, (cap, device_count), 1) == device
    for (directions, stride), out_ref in zip(faces, out_refs):
        table = send_ref[directions[0]]
        if len(directions) > 1:
            table = jnp.where(device // stride % 2 == 0, table, send_ref[directions[1]])
        picks = jnp.max(jnp.where(own, table.astype(F32), 0.0), axis=1, keepdims=True)
        for place in range(cap):
            leaf = picks[place, 0].astype(jnp.int32)
            for part, panel_ref in enumerate((dens_ref, *other_refs)):
                row = (place * far_groups + part) * columns
                out_ref[row : row + columns, :] = panel_ref[
                    :, pl.ds(pl.multiple_of(leaf * LANES, LANES), LANES)
                ]
        out_ref[cap * far_groups * columns :, :] = root_ref[...]


def near_kernel(
    faces, far_groups, share, *refs,
):
    source_refs, refs = refs[:share], refs[share:]
    dens_ref, refs = refs[0], refs[1:]
    other_refs, refs = refs[: far_groups - 1], refs[far_groups - 1 :]
    got_refs, refs = refs[: len(faces)], refs[len(faces) :]
    block_ref, refs = refs[0], refs[1:]
    mate_refs, refs = refs[: share - 1], refs[share - 1 :]
    refs = refs[1:]
    out_refs, refs = refs[:far_groups], refs[far_groups:]
    power_refs, refs = refs[: far_groups - 1], refs[far_groups - 1 :]
    (buffer_ref,) = refs
    columns, points = dens_ref.shape
    leaf_count, near_count, width, _ = block_ref.shape
    cap = (buffer_ref.shape[0] - leaf_count) // len(FACE_SIGNS)
    for (directions, _), got_ref in zip(faces, got_refs):
        for direction in directions:
            for place in range(cap):
                row = place * far_groups * columns
                buffer_ref[leaf_count + direction * cap + place] = got_ref[
                    row : row + far_groups * columns, :
                ]
    for part, panel_ref in enumerate((dens_ref, *other_refs)):
        rows = slice(part * columns, (part + 1) * columns)
        for leaf in range(leaf_count):
            buffer_ref[leaf, rows, :] = panel_ref[:, leaf * width : (leaf + 1) * width]
    words = packed_words(jnp.concatenate([source_ref[...] for source_ref in source_refs], axis=0))
    own_ref, sent_refs = out_refs[0], out_refs[1:]
    for leaf in range(leaf_count):
        panels = [buffer_ref[slot] for slot in unpacked(words, near_count * share, leaf)]
        blocks = [
            blocks_ref[leaf, block]
            for blocks_ref in (block_ref, *mate_refs)
            for block in range(near_count)
        ]
        panels, blocks = jnp.concatenate(panels, axis=1), jnp.concatenate(blocks, axis=1)
        total = dot_nt(panels, blocks) if leaf % 2 else dot_nt(blocks, panels).T
        lanes = slice(leaf * width, (leaf + 1) * width)
        own_ref[:, lanes] = total[:columns]
        for part, (sent_ref, power_ref) in enumerate(zip(sent_refs, power_refs), 1):
            term = total[part * columns : (part + 1) * columns]
            peak = jnp.max(jnp.abs(term), axis=0, keepdims=True)
            power = jnp.floor(jnp.log2(jnp.maximum(peak, 2.0**-100))) + 1.0
            steps = jnp.floor(term * (STEPS * jnp.exp2(-power)) + 0.5)
            sent_ref[:, lanes] = steps.astype(jnp.int32).astype(jnp.int16)
            power_ref[leaf : leaf + 1, :] = power
    for sent_ref, power_ref in zip(sent_refs, power_refs):
        power = power_ref[...].astype(jnp.int32).astype(jnp.int16)
        for first in range(0, leaf_count, columns):
            spot = points + first // columns * width
            sent_ref[:, spot : spot + width] = power[first : first + columns]


def coupled(leaves, table_ref, coupling_ref, turned_ref):
    far_count, rank = coupling_ref.shape[1:3]
    columns = turned_ref.shape[1] // 2
    group = LANES // rank
    words = packed_words(table_ref[...])
    parts = []
    for leaf in leaves:
        maps = jnp.concatenate([coupling_ref[leaf, j] for j in range(far_count)], axis=1)
        maps = jnp.concatenate(halves(maps), axis=0)
        picked = jnp.concatenate(
            [
                turned_ref[pl.ds(pl.multiple_of(source * rank, rank), rank), :]
                for source in unpacked(words, far_count, leaf)
            ],
            axis=0,
        )
        out = dot_nn(maps, picked)
        parts.append(out[:rank] + out[rank:])
        if len(parts) == group:
            turned = jnp.concatenate(parts, axis=0).T
            yield turned[:columns] + turned[columns:]
            parts = []


def couple_kernel(
    table_ref, coupling_ref, dens_ref, bases_ref, turned_ref, out_ref,
):
    columns, points = dens_ref.shape
    leaf_count, _, rank = coupling_ref.shape[:3]
    width = points // leaf_count
    upper = lax.broadcasted_iota(jnp.int32, (rank, 2 * columns), 1) < columns
    for leaf in range(leaf_count):
        spots = slice(leaf * width, (leaf + 1) * width)
        rows = jnp.concatenate(halves(bases_ref[:, spots]), axis=0)
        dens = dens_ref[:, spots]
        twice = dot_nt(rows, jnp.concatenate([dens, dens], axis=0))
        high, low = halves(twice[:rank] + twice[rank:])
        turned_ref[leaf * rank : (leaf + 1) * rank, :] = jnp.where(
            upper, high.astype(F32), low.astype(F32)
        ).astype(BF16)
    leaves = range(out_ref.shape[1] // rank)
    for index, field in enumerate(coupled(leaves, table_ref, coupling_ref, turned_ref)):
        out_ref[:, index * LANES : (index + 1) * LANES] = field


def project_kernel(
    table_ref, coupling_ref, turned_ref, first_ref, bases_ref, near_ref, out_ref,
):
    rank, points = bases_ref.shape
    leaf_count = coupling_ref.shape[0]
    group = LANES // rank
    step = group * points // leaf_count

    def project(index, field):
        spots = slice(index * step, (index + 1) * step)
        high, low = halves(bases_ref[:, spots])
        out_ref[:, spots] = near_ref[:, spots] + split_dot(
            dot_nn, field, spread_bases(high, group), spread_bases(low, group)
        )

    done = first_ref.shape[1] // LANES
    for index in range(done):
        project(index, first_ref[:, index * LANES : (index + 1) * LANES])
    leaves = range(done * group, leaf_count)
    for index, field in enumerate(coupled(leaves, table_ref, coupling_ref, turned_ref)):
        project(done + index, field)


def paths_kernel(turns, exchanged, upper_ref, cross_ref, high_ref, low_ref, map_ref):
    device = lax.axis_index("leaf")
    rank = upper_ref.shape[1]
    device_count = upper_ref.shape[0] // 2
    downs = {device_count: None}
    level = device_count
    while level > 4:
        node = level + device // (device_count // level)
        below = downs[level]
        matrix = upper_ref[node]
        downs[level // 2] = matrix if below is None else split_dot(dot_nn, below, *halves(matrix))
        level //= 2
    for level in sorted(downs):
        place = device // (device_count // level)
        for index in range(level):
            if level == 4:
                map_ref[level + index] = jnp.zeros((rank, rank), F32)
            else:
                above = map_ref[(level + index) // 2]
                map_ref[level + index] = split_dot(
                    dot_nt, above, *halves(upper_ref[level + index])
                )
        third = jnp.where(place % 2 == 0, place + 3, place - 3)
        for slot, other in enumerate((place - 2, place + 2, third)):
            inside = (other >= 0) & (other < level)
            matrix = cross_ref[level + place, slot]
            if downs[level] is not None:
                matrix = split_dot(dot_nn, downs[level], *halves(matrix))
            node = level + jnp.clip(other, 0, level - 1)
            map_ref[node] = map_ref[node] + jnp.where(inside, matrix, 0.0)
    zero = jnp.zeros((rank, LANES - 3 * rank), F32)
    for place, turn in enumerate(turns):
        matrix = map_ref[device_count + (device ^ turn if exchanged else turn)]
        matrix = jnp.concatenate([matrix] * 3 + [zero], axis=1)
        high, low = halves(matrix)
        high_ref[:, place * LANES : (place + 1) * LANES] = high
        low_ref[:, place * LANES : (place + 1) * LANES] = low


def far_kernel(
    tiles, path_high_ref, path_low_ref, halves_ref, term_ref, *refs,
):
    root_refs, out_ref = refs[:-1], refs[-1]
    columns, points = out_ref.shape
    pieces = []
    for rows, root_ref in zip(tiles, root_refs):
        pieces += [root_ref[row : row + columns, :] for row in rows]
    roots = jnp.concatenate(pieces, axis=1)
    field = dot_nt(roots, path_high_ref[...]) + dot_nt(roots, path_low_ref[...])
    rows = jnp.concatenate(halves(field), axis=0)
    rows = jnp.concatenate([rows, rows], axis=1)
    step = 4 * LANES
    for first in range(0, points, step):
        spots = slice(first, first + step)
        out = dot_nn(rows, halves_ref[:, spots])
        out_ref[:, spots] = term_ref[:, spots] + (out[:columns] + out[columns:])


def add_kernel(leaf_count, term_ref, *refs):
    sent_refs, (out_hbm, sum_ref, sems) = refs[:-3], refs[-3:]
    columns, points = sum_ref.shape
    width = points // leaf_count
    factors = []
    for sent_ref in sent_refs:
        powers = [
            sent_ref[:, points + first // columns * width :][:, :width]
            for first in range(0, leaf_count, columns)
        ]
        power = jnp.concatenate([p.astype(jnp.int32).astype(F32) for p in powers], axis=0)
        factors.append(jnp.exp2(power) * (1.0 / STEPS))
    chunk_count = sems.shape[0]
    step = points // chunk_count
    copies = []
    for index in range(chunk_count):
        spots = slice(index * step, (index + 1) * step)
        total = term_ref[:, spots]
        for sent_ref, factor in zip(sent_refs, factors):
            steps = sent_ref[:, spots].astype(jnp.int32).astype(F32)
            leaves = range(index * leaf_count // chunk_count, (index + 1) * leaf_count // chunk_count)
            scale = jnp.concatenate([factor[leaf : leaf + 1] for leaf in leaves], axis=1)
            total = total + steps * scale
        sum_ref[:, spots] = total
        copies += fetch(
            [(sum_ref.at[:, pl.ds(index * step, step)], out_hbm.at[:, pl.ds(index * step, step)])],
            sems.at[pl.ds(index, 1)],
        )
    for copy in copies:
        copy.wait()


def hbm(value):
    return pltpu.with_memory_space_constraint(value, pltpu.HBM)


def hint(micros):
    return pl.CostEstimate(flops=0, bytes_accessed=int(micros * 3.69e6), transcendentals=0)


def local(
    densities,
    bases,
    near_blocks,
    near_src,
    send_leaf,
    far_src,
    leaf_coupling,
    local_transfer,
    upper_transfer,
    up_coupling,
):
    leaf_devices = lax.axis_size("leaf")
    far_groups = lax.axis_size("far")
    share = lax.axis_size("mate")
    side = cube_side(leaf_devices)
    offsets = face_offsets(leaf_devices)
    columns, points = densities.shape
    leaf_count, near_count, width, _ = near_blocks.shape
    rank = bases.shape[0]
    cap = send_leaf.shape[2]
    node_count = local_transfer.shape[1]
    params = pltpu.CompilerParams(vmem_limit_bytes=16 * 2**20)
    dma = pltpu.SemaphoreType.DMA

    def rotated(value, axis, shift):
        count = lax.axis_size(axis)
        return lax.ppermute(value, axis, [(i, (i - shift) % count) for i in range(count)])

    def crossed(value, turn):
        return lax.ppermute(value, "leaf", [(i, i ^ turn) for i in range(leaf_devices)])

    sources = near_src.T
    others = [rotated(densities, "far", part) for part in range(1, far_groups)]
    all_sources = [sources] + [rotated(sources, "mate", part) for part in range(1, share)]
    send = send_leaf.transpose(1, 2, 0)
    moved = [
        densities, send, sources, far_src.T, upper_transfer, up_coupling, leaf_coupling, near_blocks,
    ]
    (
        basis, dens, send, sources, far_table, upper, cross, coupling, blocks, subtree, root,
    ) = pl.pallas_call(
        up_kernel,
        out_shape=[jax.ShapeDtypeStruct(value.shape, value.dtype) for value in (bases, *moved)]
        + [
            jax.ShapeDtypeStruct((2 * rank, points), BF16),
            jax.ShapeDtypeStruct((columns, LANES), BF16),
        ],
        in_specs=[HBM] * (2 + len(moved)),
        out_specs=[VMEM] * (3 + len(moved)),
        scratch_shapes=[
            pltpu.VMEM((rank, rank, node_count), F32),
            pltpu.VMEM((node_count * rank, LANES), F32),
            pltpu.VMEM((rank, node_count * rank), F32),
            dma((2 + len(moved),)),
        ],
        compiler_params=params,
        cost_estimate=hint(3.5),
        name="up",
    )(hbm(local_transfer[0].transpose(1, 2, 0)), hbm(bases), *map(hbm, moved))
    all_sources[0] = sources

    later_blocks, others, all_sources, root = lax.optimization_barrier(
        (blocks, others, all_sources, root)
    )
    mate_blocks = [rotated(later_blocks, "mate", part) for part in range(1, share)]

    if side == 2:
        faces = [((2 * axis, 2 * axis + 1), 2**axis) for axis in (2, 1, 0)]
    else:
        faces = [((direction,), offset) for direction, offset in enumerate(offsets)]
    chunk = (cap * far_groups + 1) * columns
    outgoing = pl.pallas_call(
        functools.partial(select_kernel, faces, far_groups),
        out_shape=[jax.ShapeDtypeStruct((chunk, LANES), BF16)] * len(faces),
        in_specs=[VMEM] * (2 + far_groups),
        out_specs=[VMEM] * len(faces),
        compiler_params=params,
        cost_estimate=hint(1),
        name="select",
    )(send, dens, root, *others)
    outgoing, dens = lax.optimization_barrier((outgoing, dens))
    first_leaves = leaf_count // 2
    turned, leaf_local = pl.pallas_call(
        couple_kernel,
        out_shape=[
            jax.ShapeDtypeStruct((leaf_count * rank, 2 * columns), BF16),
            jax.ShapeDtypeStruct((columns, first_leaves * rank), F32),
        ],
        in_specs=[VMEM] * 4,
        out_specs=[VMEM] * 2,
        compiler_params=params,
        cost_estimate=hint(2),
        name="couple",
    )(far_table, coupling, dens, basis)
    tail = cap * far_groups * columns
    if side == 2:
        arrived = [crossed(value, stride) for (_, stride), value in zip(faces, outgoing)]
        far_one, near_two, _ = (value[tail : tail + columns] for value in arrived)
        later, leaf_local = lax.optimization_barrier((arrived[0][-4 * columns :], leaf_local))
        across = crossed(later, 2)
        held = jnp.concatenate([near_two, far_one, across[-columns:]], axis=0)
        beside = crossed(held, 1)
        turns = [0] + [stride for _, stride in faces] + [6, 3, 5, 7]
        roots = [([0], root)] + [([tail], value) for value in arrived]
        roots += [([3 * columns], across), ([0, columns, 2 * columns], beside)]
    else:
        arrived = [shifted(value, "leaf", stride) for (_, stride), value in zip(faces, outgoing)]
        turns = list(range(leaf_devices))
        everyone = lax.all_gather(root, "leaf", axis=0, tiled=True)
        roots = [([turn * columns for turn in turns], everyone)]
    slots = leaf_count + len(offsets) * cap
    tables = -(-leaf_count // columns) * width
    partials = pl.pallas_call(
        functools.partial(near_kernel, faces, far_groups, share),
        out_shape=[jax.ShapeDtypeStruct((columns, points), F32)]
        + [jax.ShapeDtypeStruct((columns, points + tables), jnp.int16)] * (far_groups - 1),
        in_specs=[VMEM] * (2 * share + far_groups + len(faces) + 1),
        out_specs=[VMEM] * far_groups,
        scratch_shapes=[pltpu.VMEM((leaf_count, width), F32)] * (far_groups - 1)
        + [
            pltpu.VMEM((slots, far_groups * columns, width), BF16),
        ],
        compiler_params=params,
        cost_estimate=hint(3),
        name="near",
    )(
        *all_sources, dens, *others, *arrived, blocks, *mate_blocks, leaf_local,
    )
    upper, cross, near_own = lax.optimization_barrier((upper, cross, partials[0]))
    paths = pl.pallas_call(
        functools.partial(paths_kernel, turns, side == 2),
        out_shape=[jax.ShapeDtypeStruct((rank, leaf_devices * LANES), BF16)] * 2,
        in_specs=[VMEM] * 2,
        out_specs=[VMEM] * 2,
        scratch_shapes=[pltpu.VMEM((2 * leaf_devices, rank, rank), F32)],
        compiler_params=params,
        cost_estimate=hint(0.7),
        name="paths",
    )(upper, cross)
    received = [rotated(partials[part], "far", -part) for part in range(1, far_groups)]
    partial = pl.pallas_call(
        project_kernel,
        out_shape=jax.ShapeDtypeStruct((columns, points), F32),
        in_specs=[VMEM] * 6,
        out_specs=VMEM,
        compiler_params=params,
        cost_estimate=hint(1.5),
        name="project",
    )(far_table, coupling, turned, leaf_local, basis, near_own)
    total = pl.pallas_call(
        functools.partial(far_kernel, [rows for rows, _ in roots]),
        out_shape=jax.ShapeDtypeStruct((columns, points), F32),
        in_specs=[VMEM] * (4 + len(roots)),
        out_specs=VMEM,
        compiler_params=params,
        cost_estimate=hint(0.6),
        name="far",
    )(*paths, subtree, partial, *[value for _, value in roots])
    return pl.pallas_call(
        functools.partial(add_kernel, leaf_count),
        out_shape=jax.ShapeDtypeStruct((columns, points), F32),
        in_specs=[VMEM] * (1 + len(received)),
        out_specs=HBM,
        scratch_shapes=[pltpu.VMEM((columns, points), F32), dma((4,))],
        compiler_params=params,
        cost_estimate=hint(0.5),
        name="add",
    )(total, *received)


def solution(mesh):
    leaf_devices, rhs_devices = mesh.shape["leaf"], mesh.shape["rhs"]
    share = 2 if rhs_devices % 2 == 0 else 1
    split = Mesh(
        mesh.devices.reshape(leaf_devices, rhs_devices // share, share), ("leaf", "far", "mate")
    )
    rhs = ("far", "mate")
    in_specs = (
        P(rhs, "leaf"),
        P(None, "leaf"),
        P("leaf", rhs, None, None),
        P("leaf", rhs),
        P(),
        P("leaf", None),
        P("leaf", None, None, None),
        P("leaf", None, None, None),
        P(),
        P(),
    )
    return jax.shard_map(
        local, mesh=split, in_specs=in_specs, out_specs=P(rhs, "leaf"), check_vma=False
    )
```

```python
import functools

import jax
import jax.numpy as jnp
from jax import lax
from jax.experimental import pallas as pl
from jax.experimental.pallas import tpu as pltpu
from jax.sharding import Mesh
from jax.sharding import PartitionSpec as P

FACE_SIGNS = ((1, 0), (-1, 0), (1, 1), (-1, 1), (1, 2), (-1, 2))
F32 = jnp.float32
BF16 = jnp.bfloat16
LANES = 128
STEPS = 32000.0
VMEM = pl.BlockSpec(memory_space=pltpu.VMEM)
HBM = pl.BlockSpec(memory_space=pltpu.HBM)


def cube_side(device_count):
    return max((edge_len for edge_len in range(1, 65) if edge_len**3 <= device_count))


def face_offsets(device_count):
    side_len = cube_side(device_count)
    return [face_sign * side_len**axis_pos for face_sign, axis_pos in FACE_SIGNS]


def shifted(value, axis, steps):
    count = lax.axis_size(axis)
    first, last = (max(0, -steps), min(count, count - steps))
    return lax.ppermute(value, axis, [(source, source + steps) for source in range(first, last)])


def halves(value):
    high = value.astype(BF16)
    return high, (value - high.astype(F32)).astype(BF16)


def dot_nn(left, right):
    return lax.dot_general(left, right, (((1,), (0,)), ((), ())), preferred_element_type=F32)


def dot_nt(left, right):
    return lax.dot_general(left, right, (((1,), (1,)), ((), ())), preferred_element_type=F32)


def split_dot(dot, rows, right_high, right_low):
    count = rows.shape[0]
    high, low = halves(rows)
    both = jnp.concatenate([high, low], axis=0)
    out = dot(both, right_high) + dot(both, right_low)
    return out[:count] + out[count:]


def spread_bases(block, group):
    rank, lanes = block.shape
    width = lanes // group
    zero = jnp.zeros((rank, width), block.dtype)
    rows = []
    for slot in range(group):
        pieces = [zero] * group
        pieces[slot] = block[:, slot * width : (slot + 1) * width]
        rows.append(jnp.concatenate(pieces, axis=1))
    return jnp.concatenate(rows, axis=0)


def packed_words(table):
    words = []
    for first in range(0, table.shape[0], 4):
        word = table[first : first + 1]
        for row in range(first + 1, min(first + 4, table.shape[0])):
            word = word + (table[row : row + 1] << (8 * (row - first)))
        words.append(word)
    return words


def unpacked(words, count, place):
    values = [word[0, place] for word in words]
    return [(values[row // 4] >> (8 * (row % 4))) & 255 for row in range(count)]


def fetch(pairs, sems):
    copies = []
    for index, (source, target) in enumerate(pairs):
        copy = pltpu.make_async_copy(source, target, sems.at[index])
        copy.start()
        copies.append(copy)
    return copies


def up_kernel(
    maps_hbm, bases_hbm, *refs,
):
    count = (len(refs) - 7) // 2
    hbm_refs, bases_ref, vmem_refs = refs[:count], refs[count], refs[count + 1 : 2 * count + 1]
    halves_ref, root_ref, maps_ref, spread_ref, chain_ref, sems = refs[2 * count + 1 :]
    dens_ref = vmem_refs[0]
    copies = fetch(
        [(maps_hbm, maps_ref), (bases_hbm, bases_ref), *zip(hbm_refs, vmem_refs)], sems
    )
    columns, points = dens_ref.shape
    rank, _, node_count = maps_ref.shape
    group = LANES // rank
    leaf_count = node_count // 2
    width = points // leaf_count
    copies[0].wait()
    node = lax.broadcasted_iota(jnp.int32, (node_count, LANES), 0)
    block = lax.broadcasted_iota(jnp.int32, (node_count, LANES), 1) // rank
    parent = node // 2 % group
    for first in range(0, rank, group):
        slab = maps_ref[first : first + group].reshape(group * rank, node_count).T
        turned = [slab] + [pltpu.roll(slab, turn * rank, 1) for turn in range(1, group)]
        for row in range(group):
            placed = jnp.zeros_like(slab)
            for place in range(group):
                here = (parent == place) & (block == place)
                placed = jnp.where(here, turned[(place - row) % group], placed)
            spread_ref[pl.ds(first + row, node_count, stride=rank), :] = placed
    tile = 2 * group * rank

    def children(parents, index):
        high, low = halves(spread_ref[index * tile : (index + 1) * tile, :])
        return split_dot(dot_nt, parents, high, low)

    row = lax.broadcasted_iota(jnp.int32, (rank, LANES), 0)
    lane = lax.broadcasted_iota(jnp.int32, (rank, LANES), 1)
    level = 1
    parents = jnp.where(lane == row + rank, 1.0, 0.0)
    while level < group:
        below = children(parents, 0)
        level *= 2
        parents = below[:, (level // group) * LANES : (level // group + 1) * LANES]
    chain_ref[:, LANES : 2 * LANES] = parents
    while level < leaf_count:
        for index in range(level // group, 2 * level // group):
            lanes = slice(index * LANES, (index + 1) * LANES)
            chain_ref[:, index * tile : (index + 1) * tile] = children(chain_ref[:, lanes], index)
        level *= 2
    copies[1].wait()
    copies[2].wait()
    step = group * width
    root = jnp.zeros((columns, rank), F32)
    for index in range(leaf_count // group):
        spots = slice(index * step, (index + 1) * step)
        start = (leaf_count // group + index) * LANES
        high, low = halves(bases_ref[:, spots])
        basis = split_dot(
            dot_nn, chain_ref[:, start : start + LANES],
            spread_bases(high, group), spread_bases(low, group),
        )
        high, low = halves(basis)
        halves_ref[:rank, spots] = high
        halves_ref[rank:, spots] = low
        dens = dens_ref[:, spots]
        root += dot_nt(dens, high) + dot_nt(dens, low)
    root = jnp.concatenate([root, jnp.zeros((columns, LANES - rank), F32)], axis=1)
    high = root.astype(BF16).astype(F32)
    rest = root - high
    middle = rest.astype(BF16).astype(F32)
    last = (rest - middle).astype(BF16).astype(F32)
    packed = high + pltpu.roll(middle, rank, 1) + pltpu.roll(last, 2 * rank, 1)
    root_ref[...] = packed.astype(BF16)
    for copy in copies[3:]:
        copy.wait()


def select_kernel(
    faces, far_groups, send_ref, dens_ref, root_ref, *refs,
):
    other_refs, out_refs = refs[: far_groups - 1], refs[far_groups - 1 :]
    device = lax.axis_index("leaf")
    columns = dens_ref.shape[0]
    cap, device_count = send_ref.shape[1:]
    own = lax.broadcasted_iota(jnp.int32, (cap, device_count), 1) == device
    for (directions, stride), out_ref in zip(faces, out_refs):
        table = send_ref[directions[0]]
        if len(directions) > 1:
            table = jnp.where(device // stride % 2 == 0, table, send_ref[directions[1]])
        picks = jnp.max(jnp.where(own, table.astype(F32), 0.0), axis=1, keepdims=True)
        for place in range(cap):
            leaf = picks[place, 0].astype(jnp.int32)
            for part, panel_ref in enumerate((dens_ref, *other_refs)):
                row = (place * far_groups + part) * columns
                out_ref[row : row + columns, :] = panel_ref[
                    :, pl.ds(pl.multiple_of(leaf * LANES, LANES), LANES)
                ]
        out_ref[cap * far_groups * columns :, :] = root_ref[...]


def near_kernel(
    faces, far_groups, share, *refs,
):
    source_refs, refs = refs[:share], refs[share:]
    dens_ref, refs = refs[0], refs[1:]
    other_refs, refs = refs[: far_groups - 1], refs[far_groups - 1 :]
    got_refs, refs = refs[: len(faces)], refs[len(faces) :]
    block_ref, refs = refs[0], refs[1:]
    mate_refs, refs = refs[: share - 1], refs[share - 1 :]
    refs = refs[1:]
    out_refs, refs = refs[:far_groups], refs[far_groups:]
    power_refs, refs = refs[: far_groups - 1], refs[far_groups - 1 :]
    (buffer_ref,) = refs
    columns, points = dens_ref.shape
    leaf_count, near_count, width, _ = block_ref.shape
    cap = (buffer_ref.shape[0] - leaf_count) // len(FACE_SIGNS)
    for (directions, _), got_ref in zip(faces, got_refs):
        for direction in directions:
            for place in range(cap):
                row = place * far_groups * columns
                buffer_ref[leaf_count + direction * cap + place] = got_ref[
                    row : row + far_groups * columns, :
                ]
    for part, panel_ref in enumerate((dens_ref, *other_refs)):
        rows = slice(part * columns, (part + 1) * columns)
        for leaf in range(leaf_count):
            buffer_ref[leaf, rows, :] = panel_ref[:, leaf * width : (leaf + 1) * width]
    words = packed_words(jnp.concatenate([source_ref[...] for source_ref in source_refs], axis=0))
    own_ref, sent_refs = out_refs[0], out_refs[1:]
    for leaf in range(leaf_count):
        panels = [buffer_ref[slot] for slot in unpacked(words, near_count * share, leaf)]
        blocks = [
            blocks_ref[leaf, block]
            for blocks_ref in (block_ref, *mate_refs)
            for block in range(near_count)
        ]
        total = dot_nt(jnp.concatenate(panels, axis=1), jnp.concatenate(blocks, axis=1))
        lanes = slice(leaf * width, (leaf + 1) * width)
        own_ref[:, lanes] = total[:columns]
        for part, (sent_ref, power_ref) in enumerate(zip(sent_refs, power_refs), 1):
            term = total[part * columns : (part + 1) * columns]
            peak = jnp.max(jnp.abs(term), axis=0, keepdims=True)
            power = jnp.floor(jnp.log2(jnp.maximum(peak, 2.0**-100))) + 1.0
            steps = jnp.floor(term * (STEPS * jnp.exp2(-power)) + 0.5)
            sent_ref[:, lanes] = steps.astype(jnp.int32).astype(jnp.int16)
            power_ref[leaf : leaf + 1, :] = power
    for sent_ref, power_ref in zip(sent_refs, power_refs):
        power = power_ref[...].astype(jnp.int32).astype(jnp.int16)
        for first in range(0, leaf_count, columns):
            spot = points + first // columns * width
            sent_ref[:, spot : spot + width] = power[first : first + columns]


def coupled(leaves, table_ref, coupling_ref, turned_ref):
    far_count, rank = coupling_ref.shape[1:3]
    columns = turned_ref.shape[1] // 2
    group = LANES // rank
    words = packed_words(table_ref[...])
    parts = []
    for leaf in leaves:
        maps = jnp.concatenate([coupling_ref[leaf, j] for j in range(far_count)], axis=1)
        maps = jnp.concatenate(halves(maps), axis=0)
        picked = jnp.concatenate(
            [
                turned_ref[pl.ds(pl.multiple_of(source * rank, rank), rank), :]
                for source in unpacked(words, far_count, leaf)
            ],
            axis=0,
        )
        out = dot_nn(maps, picked)
        parts.append(out[:rank] + out[rank:])
        if len(parts) == group:
            turned = jnp.concatenate(parts, axis=0).T
            yield turned[:columns] + turned[columns:]
            parts = []


def couple_kernel(
    table_ref, coupling_ref, dens_ref, bases_ref, turned_ref, out_ref,
):
    columns, points = dens_ref.shape
    leaf_count, _, rank = coupling_ref.shape[:3]
    width = points // leaf_count
    upper = lax.broadcasted_iota(jnp.int32, (rank, 2 * columns), 1) < columns
    for leaf in range(leaf_count):
        spots = slice(leaf * width, (leaf + 1) * width)
        rows = jnp.concatenate(halves(bases_ref[:, spots]), axis=0)
        dens = dens_ref[:, spots]
        twice = dot_nt(rows, jnp.concatenate([dens, dens], axis=0))
        high, low = halves(twice[:rank] + twice[rank:])
        turned_ref[leaf * rank : (leaf + 1) * rank, :] = jnp.where(
            upper, high.astype(F32), low.astype(F32)
        ).astype(BF16)
    leaves = range(out_ref.shape[1] // rank)
    for index, field in enumerate(coupled(leaves, table_ref, coupling_ref, turned_ref)):
        out_ref[:, index * LANES : (index + 1) * LANES] = field


def project_kernel(
    table_ref, coupling_ref, turned_ref, first_ref, bases_ref, near_ref, out_ref,
):
    rank, points = bases_ref.shape
    leaf_count = coupling_ref.shape[0]
    group = LANES // rank
    step = group * points // leaf_count

    def project(index, field):
        spots = slice(index * step, (index + 1) * step)
        high, low = halves(bases_ref[:, spots])
        out_ref[:, spots] = near_ref[:, spots] + split_dot(
            dot_nn, field, spread_bases(high, group), spread_bases(low, group)
        )

    done = first_ref.shape[1] // LANES
    for index in range(done):
        project(index, first_ref[:, index * LANES : (index + 1) * LANES])
    leaves = range(done * group, leaf_count)
    for index, field in enumerate(coupled(leaves, table_ref, coupling_ref, turned_ref)):
        project(done + index, field)


def paths_kernel(turns, exchanged, upper_ref, cross_ref, high_ref, low_ref, map_ref):
    device = lax.axis_index("leaf")
    rank = upper_ref.shape[1]
    device_count = upper_ref.shape[0] // 2
    downs = {device_count: None}
    level = device_count
    while level > 4:
        node = level + device // (device_count // level)
        below = downs[level]
        matrix = upper_ref[node]
        downs[level // 2] = matrix if below is None else split_dot(dot_nn, below, *halves(matrix))
        level //= 2
    for level in sorted(downs):
        place = device // (device_count // level)
        for index in range(level):
            if level == 4:
                map_ref[level + index] = jnp.zeros((rank, rank), F32)
            else:
                above = map_ref[(level + index) // 2]
                map_ref[level + index] = split_dot(
                    dot_nt, above, *halves(upper_ref[level + index])
                )
        third = jnp.where(place % 2 == 0, place + 3, place - 3)
        for slot, other in enumerate((place - 2, place + 2, third)):
            inside = (other >= 0) & (other < level)
            matrix = cross_ref[level + place, slot]
            if downs[level] is not None:
                matrix = split_dot(dot_nn, downs[level], *halves(matrix))
            node = level + jnp.clip(other, 0, level - 1)
            map_ref[node] = map_ref[node] + jnp.where(inside, matrix, 0.0)
    zero = jnp.zeros((rank, LANES - 3 * rank), F32)
    for place, turn in enumerate(turns):
        matrix = map_ref[device_count + (device ^ turn if exchanged else turn)]
        matrix = jnp.concatenate([matrix] * 3 + [zero], axis=1)
        high, low = halves(matrix)
        high_ref[:, place * LANES : (place + 1) * LANES] = high
        low_ref[:, place * LANES : (place + 1) * LANES] = low


def far_kernel(
    tiles, path_high_ref, path_low_ref, halves_ref, term_ref, *refs,
):
    root_refs, out_ref = refs[:-1], refs[-1]
    columns, points = out_ref.shape
    pieces = []
    for rows, root_ref in zip(tiles, root_refs):
        pieces += [root_ref[row : row + columns, :] for row in rows]
    roots = jnp.concatenate(pieces, axis=1)
    field = dot_nt(roots, path_high_ref[...]) + dot_nt(roots, path_low_ref[...])
    rows = jnp.concatenate(halves(field), axis=0)
    rows = jnp.concatenate([rows, rows], axis=1)
    step = 4 * LANES
    for first in range(0, points, step):
        spots = slice(first, first + step)
        out = dot_nn(rows, halves_ref[:, spots])
        out_ref[:, spots] = term_ref[:, spots] + (out[:columns] + out[columns:])


def add_kernel(leaf_count, term_ref, *refs):
    sent_refs, (out_hbm, sum_ref, sems) = refs[:-3], refs[-3:]
    columns, points = sum_ref.shape
    width = points // leaf_count
    factors = []
    for sent_ref in sent_refs:
        powers = [
            sent_ref[:, points + first // columns * width :][:, :width]
            for first in range(0, leaf_count, columns)
        ]
        power = jnp.concatenate([p.astype(jnp.int32).astype(F32) for p in powers], axis=0)
        factors.append(jnp.exp2(power) * (1.0 / STEPS))
    chunk_count = sems.shape[0]
    step = points // chunk_count
    copies = []
    for index in range(chunk_count):
        spots = slice(index * step, (index + 1) * step)
        total = term_ref[:, spots]
        for sent_ref, factor in zip(sent_refs, factors):
            steps = sent_ref[:, spots].astype(jnp.int32).astype(F32)
            leaves = range(index * leaf_count // chunk_count, (index + 1) * leaf_count // chunk_count)
            scale = jnp.concatenate([factor[leaf : leaf + 1] for leaf in leaves], axis=1)
            total = total + steps * scale
        sum_ref[:, spots] = total
        copies += fetch(
            [(sum_ref.at[:, pl.ds(index * step, step)], out_hbm.at[:, pl.ds(index * step, step)])],
            sems.at[pl.ds(index, 1)],
        )
    for copy in copies:
        copy.wait()


def hbm(value):
    return pltpu.with_memory_space_constraint(value, pltpu.HBM)


def hint(micros):
    return pl.CostEstimate(flops=0, bytes_accessed=int(micros * 3.69e6), transcendentals=0)


def local(
    densities,
    bases,
    near_blocks,
    near_src,
    send_leaf,
    far_src,
    leaf_coupling,
    local_transfer,
    upper_transfer,
    up_coupling,
):
    leaf_devices = lax.axis_size("leaf")
    far_groups = lax.axis_size("far")
    share = lax.axis_size("mate")
    side = cube_side(leaf_devices)
    offsets = face_offsets(leaf_devices)
    columns, points = densities.shape
    leaf_count, near_count, width, _ = near_blocks.shape
    rank = bases.shape[0]
    cap = send_leaf.shape[2]
    node_count = local_transfer.shape[1]
    params = pltpu.CompilerParams(vmem_limit_bytes=16 * 2**20)
    dma = pltpu.SemaphoreType.DMA

    def rotated(value, axis, shift):
        count = lax.axis_size(axis)
        return lax.ppermute(value, axis, [(i, (i - shift) % count) for i in range(count)])

    def crossed(value, turn):
        return lax.ppermute(value, "leaf", [(i, i ^ turn) for i in range(leaf_devices)])

    sources = near_src.T
    others = [rotated(densities, "far", part) for part in range(1, far_groups)]
    all_sources = [sources] + [rotated(sources, "mate", part) for part in range(1, share)]
    send = send_leaf.transpose(1, 2, 0)
    moved = [
        densities, send, sources, far_src.T, upper_transfer, up_coupling, leaf_coupling, near_blocks,
    ]
    (
        basis, dens, send, sources, far_table, upper, cross, coupling, blocks, subtree, root,
    ) = pl.pallas_call(
        up_kernel,
        out_shape=[jax.ShapeDtypeStruct(value.shape, value.dtype) for value in (bases, *moved)]
        + [
            jax.ShapeDtypeStruct((2 * rank, points), BF16),
            jax.ShapeDtypeStruct((columns, LANES), BF16),
        ],
        in_specs=[HBM] * (2 + len(moved)),
        out_specs=[VMEM] * (3 + len(moved)),
        scratch_shapes=[
            pltpu.VMEM((rank, rank, node_count), F32),
            pltpu.VMEM((node_count * rank, LANES), F32),
            pltpu.VMEM((rank, node_count * rank), F32),
            dma((2 + len(moved),)),
        ],
        compiler_params=params,
        cost_estimate=hint(3.5),
        name="up",
    )(hbm(local_transfer[0].transpose(1, 2, 0)), hbm(bases), *map(hbm, moved))
    all_sources[0] = sources

    later_blocks, others, all_sources, root = lax.optimization_barrier(
        (blocks, others, all_sources, root)
    )
    mate_blocks = [rotated(later_blocks, "mate", part) for part in range(1, share)]

    if side == 2:
        faces = [((2 * axis, 2 * axis + 1), 2**axis) for axis in (2, 1, 0)]
    else:
        faces = [((direction,), offset) for direction, offset in enumerate(offsets)]
    chunk = (cap * far_groups + 1) * columns
    outgoing = pl.pallas_call(
        functools.partial(select_kernel, faces, far_groups),
        out_shape=[jax.ShapeDtypeStruct((chunk, LANES), BF16)] * len(faces),
        in_specs=[VMEM] * (2 + far_groups),
        out_specs=[VMEM] * len(faces),
        compiler_params=params,
        cost_estimate=hint(1),
        name="select",
    )(send, dens, root, *others)
    outgoing, dens = lax.optimization_barrier((outgoing, dens))
    first_leaves = 3 * leaf_count // 4
    turned, leaf_local = pl.pallas_call(
        couple_kernel,
        out_shape=[
            jax.ShapeDtypeStruct((leaf_count * rank, 2 * columns), BF16),
            jax.ShapeDtypeStruct((columns, first_leaves * rank), F32),
        ],
        in_specs=[VMEM] * 4,
        out_specs=[VMEM] * 2,
        compiler_params=params,
        cost_estimate=hint(2),
        name="couple",
    )(far_table, coupling, dens, basis)
    tail = cap * far_groups * columns
    if side == 2:
        arrived = [crossed(value, stride) for (_, stride), value in zip(faces, outgoing)]
        far_one, _, near_one = (value[tail : tail + columns] for value in arrived)
        later, leaf_local = lax.optimization_barrier((arrived[0][-4 * columns :], leaf_local))
        across = crossed(later, 1)
        held = jnp.concatenate([near_one, far_one, across[-columns:]], axis=0)
        beside = crossed(held, 2)
        turns = [0] + [stride for _, stride in faces] + [5, 3, 6, 7]
        roots = [([0], root)] + [([tail], value) for value in arrived]
        roots += [([3 * columns], across), ([0, columns, 2 * columns], beside)]
    else:
        arrived = [shifted(value, "leaf", stride) for (_, stride), value in zip(faces, outgoing)]
        turns = list(range(leaf_devices))
        everyone = lax.all_gather(root, "leaf", axis=0, tiled=True)
        roots = [([turn * columns for turn in turns], everyone)]
    slots = leaf_count + len(offsets) * cap
    tables = -(-leaf_count // columns) * width
    partials = pl.pallas_call(
        functools.partial(near_kernel, faces, far_groups, share),
        out_shape=[jax.ShapeDtypeStruct((columns, points), F32)]
        + [jax.ShapeDtypeStruct((columns, points + tables), jnp.int16)] * (far_groups - 1),
        in_specs=[VMEM] * (2 * share + far_groups + len(faces) + 1),
        out_specs=[VMEM] * far_groups,
        scratch_shapes=[pltpu.VMEM((leaf_count, width), F32)] * (far_groups - 1)
        + [
            pltpu.VMEM((slots, far_groups * columns, width), BF16),
        ],
        compiler_params=params,
        cost_estimate=hint(3),
        name="near",
    )(
        *all_sources, dens, *others, *arrived, blocks, *mate_blocks, leaf_local,
    )
    upper, cross, near_own = lax.optimization_barrier((upper, cross, partials[0]))
    paths = pl.pallas_call(
        functools.partial(paths_kernel, turns, side == 2),
        out_shape=[jax.ShapeDtypeStruct((rank, leaf_devices * LANES), BF16)] * 2,
        in_specs=[VMEM] * 2,
        out_specs=[VMEM] * 2,
        scratch_shapes=[pltpu.VMEM((2 * leaf_devices, rank, rank), F32)],
        compiler_params=params,
        cost_estimate=hint(0.7),
        name="paths",
    )(upper, cross)
    received = [rotated(partials[part], "far", -part) for part in range(1, far_groups)]
    partial = pl.pallas_call(
        project_kernel,
        out_shape=jax.ShapeDtypeStruct((columns, points), F32),
        in_specs=[VMEM] * 6,
        out_specs=VMEM,
        compiler_params=params,
        cost_estimate=hint(1.5),
        name="project",
    )(far_table, coupling, turned, leaf_local, basis, near_own)
    total = pl.pallas_call(
        functools.partial(far_kernel, [rows for rows, _ in roots]),
        out_shape=jax.ShapeDtypeStruct((columns, points), F32),
        in_specs=[VMEM] * (4 + len(roots)),
        out_specs=VMEM,
        compiler_params=params,
        cost_estimate=hint(0.6),
        name="far",
    )(*paths, subtree, partial, *[value for _, value in roots])
    return pl.pallas_call(
        functools.partial(add_kernel, leaf_count),
        out_shape=jax.ShapeDtypeStruct((columns, points), F32),
        in_specs=[VMEM] * (1 + len(received)),
        out_specs=HBM,
        scratch_shapes=[pltpu.VMEM((columns, points), F32), dma((4,))],
        compiler_params=params,
        cost_estimate=hint(0.5),
        name="add",
    )(total, *received)


def solution(mesh):
    leaf_devices, rhs_devices = mesh.shape["leaf"], mesh.shape["rhs"]
    share = 2 if rhs_devices % 2 == 0 else 1
    split = Mesh(
        mesh.devices.reshape(leaf_devices, rhs_devices // share, share), ("leaf", "far", "mate")
    )
    rhs = ("far", "mate")
    in_specs = (
        P(rhs, "leaf"),
        P(None, "leaf"),
        P("leaf", rhs, None, None),
        P("leaf", rhs),
        P(),
        P("leaf", None),
        P("leaf", None, None, None),
        P("leaf", None, None, None),
        P(),
        P(),
    )
    return jax.shard_map(
        local, mesh=split, in_specs=in_specs, out_specs=P(rhs, "leaf"), check_vma=False
    )
```

```python
import functools

import jax
import jax.numpy as jnp
from jax import lax
from jax.experimental import pallas as pl
from jax.experimental.pallas import tpu as pltpu
from jax.sharding import Mesh
from jax.sharding import PartitionSpec as P

FACE_SIGNS = ((1, 0), (-1, 0), (1, 1), (-1, 1), (1, 2), (-1, 2))
F32 = jnp.float32
BF16 = jnp.bfloat16
LANES = 128
STEPS = 32000.0
VMEM = pl.BlockSpec(memory_space=pltpu.VMEM)
HBM = pl.BlockSpec(memory_space=pltpu.HBM)


def cube_side(device_count):
    return max((edge_len for edge_len in range(1, 65) if edge_len**3 <= device_count))


def face_offsets(device_count):
    side_len = cube_side(device_count)
    return [face_sign * side_len**axis_pos for face_sign, axis_pos in FACE_SIGNS]


def shifted(value, axis, steps):
    count = lax.axis_size(axis)
    first, last = (max(0, -steps), min(count, count - steps))
    return lax.ppermute(value, axis, [(source, source + steps) for source in range(first, last)])


def halves(value):
    high = value.astype(BF16)
    return high, (value - high.astype(F32)).astype(BF16)


def dot_nn(left, right):
    return lax.dot_general(left, right, (((1,), (0,)), ((), ())), preferred_element_type=F32)


def dot_nt(left, right):
    return lax.dot_general(left, right, (((1,), (1,)), ((), ())), preferred_element_type=F32)


def split_dot(dot, rows, right_high, right_low):
    count = rows.shape[0]
    high, low = halves(rows)
    both = jnp.concatenate([high, low], axis=0)
    out = dot(both, right_high) + dot(both, right_low)
    return out[:count] + out[count:]


def spread_bases(block, group):
    rank, lanes = block.shape
    width = lanes // group
    zero = jnp.zeros((rank, width), block.dtype)
    rows = []
    for slot in range(group):
        pieces = [zero] * group
        pieces[slot] = block[:, slot * width : (slot + 1) * width]
        rows.append(jnp.concatenate(pieces, axis=1))
    return jnp.concatenate(rows, axis=0)


def packed_words(table):
    words = []
    for first in range(0, table.shape[0], 4):
        word = table[first : first + 1]
        for row in range(first + 1, min(first + 4, table.shape[0])):
            word = word + (table[row : row + 1] << (8 * (row - first)))
        words.append(word)
    return words


def unpacked(words, count, place):
    values = [word[0, place] for word in words]
    return [(values[row // 4] >> (8 * (row % 4))) & 255 for row in range(count)]


def fetch(pairs, sems):
    copies = []
    for index, (source, target) in enumerate(pairs):
        copy = pltpu.make_async_copy(source, target, sems.at[index])
        copy.start()
        copies.append(copy)
    return copies


def up_kernel(
    maps_hbm, bases_hbm, *refs,
):
    count = (len(refs) - 7) // 2
    hbm_refs, bases_ref, vmem_refs = refs[:count], refs[count], refs[count + 1 : 2 * count + 1]
    halves_ref, root_ref, maps_ref, spread_ref, chain_ref, sems = refs[2 * count + 1 :]
    dens_ref = vmem_refs[0]
    copies = fetch(
        [(maps_hbm, maps_ref), (bases_hbm, bases_ref), *zip(hbm_refs, vmem_refs)], sems
    )
    columns, points = dens_ref.shape
    rank, _, node_count = maps_ref.shape
    group = LANES // rank
    leaf_count = node_count // 2
    width = points // leaf_count
    copies[0].wait()
    node = lax.broadcasted_iota(jnp.int32, (node_count, LANES), 0)
    block = lax.broadcasted_iota(jnp.int32, (node_count, LANES), 1) // rank
    parent = node // 2 % group
    for first in range(0, rank, group):
        slab = maps_ref[first : first + group].reshape(group * rank, node_count).T
        turned = [slab] + [pltpu.roll(slab, turn * rank, 1) for turn in range(1, group)]
        for row in range(group):
            placed = jnp.zeros_like(slab)
            for place in range(group):
                here = (parent == place) & (block == place)
                placed = jnp.where(here, turned[(place - row) % group], placed)
            spread_ref[pl.ds(first + row, node_count, stride=rank), :] = placed
    tile = 2 * group * rank

    def children(parents, index):
        high, low = halves(spread_ref[index * tile : (index + 1) * tile, :])
        return split_dot(dot_nt, parents, high, low)

    row = lax.broadcasted_iota(jnp.int32, (rank, LANES), 0)
    lane = lax.broadcasted_iota(jnp.int32, (rank, LANES), 1)
    level = 1
    parents = jnp.where(lane == row + rank, 1.0, 0.0)
    while level < group:
        below = children(parents, 0)
        level *= 2
        parents = below[:, (level // group) * LANES : (level // group + 1) * LANES]
    chain_ref[:, LANES : 2 * LANES] = parents
    while level < leaf_count:
        for index in range(level // group, 2 * level // group):
            lanes = slice(index * LANES, (index + 1) * LANES)
            chain_ref[:, index * tile : (index + 1) * tile] = children(chain_ref[:, lanes], index)
        level *= 2
    copies[1].wait()
    copies[2].wait()
    step = group * width
    root = jnp.zeros((columns, rank), F32)
    for index in range(leaf_count // group):
        spots = slice(index * step, (index + 1) * step)
        start = (leaf_count // group + index) * LANES
        high, low = halves(bases_ref[:, spots])
        basis = split_dot(
            dot_nn, chain_ref[:, start : start + LANES],
            spread_bases(high, group), spread_bases(low, group),
        )
        high, low = halves(basis)
        halves_ref[:rank, spots] = high
        halves_ref[rank:, spots] = low
        dens = dens_ref[:, spots]
        root += dot_nt(dens, high) + dot_nt(dens, low)
    root = jnp.concatenate([root, jnp.zeros((columns, LANES - rank), F32)], axis=1)
    high = root.astype(BF16).astype(F32)
    rest = root - high
    middle = rest.astype(BF16).astype(F32)
    last = (rest - middle).astype(BF16).astype(F32)
    packed = high + pltpu.roll(middle, rank, 1) + pltpu.roll(last, 2 * rank, 1)
    root_ref[...] = packed.astype(BF16)
    for copy in copies[3:]:
        copy.wait()


def select_kernel(
    faces, far_groups, send_ref, dens_ref, root_ref, *refs,
):
    other_refs, out_refs = refs[: far_groups - 1], refs[far_groups - 1 :]
    device = lax.axis_index("leaf")
    columns = dens_ref.shape[0]
    cap, device_count = send_ref.shape[1:]
    own = lax.broadcasted_iota(jnp.int32, (cap, device_count), 1) == device
    for (directions, stride), out_ref in zip(faces, out_refs):
        table = send_ref[directions[0]]
        if len(directions) > 1:
            table = jnp.where(device // stride % 2 == 0, table, send_ref[directions[1]])
        picks = jnp.max(jnp.where(own, table.astype(F32), 0.0), axis=1, keepdims=True)
        for place in range(cap):
            leaf = picks[place, 0].astype(jnp.int32)
            for part, panel_ref in enumerate((dens_ref, *other_refs)):
                row = (place * far_groups + part) * columns
                out_ref[row : row + columns, :] = panel_ref[
                    :, pl.ds(pl.multiple_of(leaf * LANES, LANES), LANES)
                ]
        out_ref[cap * far_groups * columns :, :] = root_ref[...]


def near_kernel(
    faces, far_groups, share, *refs,
):
    source_refs, refs = refs[:share], refs[share:]
    dens_ref, refs = refs[0], refs[1:]
    other_refs, refs = refs[: far_groups - 1], refs[far_groups - 1 :]
    got_refs, refs = refs[: len(faces)], refs[len(faces) :]
    block_ref, refs = refs[0], refs[1:]
    mate_refs, refs = refs[: share - 1], refs[share - 1 :]
    refs = refs[1:]
    out_refs, refs = refs[:far_groups], refs[far_groups:]
    power_refs, refs = refs[: far_groups - 1], refs[far_groups - 1 :]
    (buffer_ref,) = refs
    columns, points = dens_ref.shape
    leaf_count, near_count, width, _ = block_ref.shape
    cap = (buffer_ref.shape[0] - leaf_count) // len(FACE_SIGNS)
    for (directions, _), got_ref in zip(faces, got_refs):
        for direction in directions:
            for place in range(cap):
                row = place * far_groups * columns
                buffer_ref[leaf_count + direction * cap + place] = got_ref[
                    row : row + far_groups * columns, :
                ]
    for part, panel_ref in enumerate((dens_ref, *other_refs)):
        rows = slice(part * columns, (part + 1) * columns)
        for leaf in range(leaf_count):
            buffer_ref[leaf, rows, :] = panel_ref[:, leaf * width : (leaf + 1) * width]
    words = packed_words(jnp.concatenate([source_ref[...] for source_ref in source_refs], axis=0))
    own_ref, sent_refs = out_refs[0], out_refs[1:]
    for leaf in range(leaf_count):
        panels = [buffer_ref[slot] for slot in unpacked(words, near_count * share, leaf)]
        blocks = [
            blocks_ref[leaf, block]
            for blocks_ref in (block_ref, *mate_refs)
            for block in range(near_count)
        ]
        total = dot_nt(jnp.concatenate(panels, axis=1), jnp.concatenate(blocks, axis=1))
        lanes = slice(leaf * width, (leaf + 1) * width)
        own_ref[:, lanes] = total[:columns]
        for part, (sent_ref, power_ref) in enumerate(zip(sent_refs, power_refs), 1):
            term = total[part * columns : (part + 1) * columns]
            peak = jnp.max(jnp.abs(term), axis=0, keepdims=True)
            power = jnp.floor(jnp.log2(jnp.maximum(peak, 2.0**-100))) + 1.0
            steps = jnp.floor(term * (STEPS * jnp.exp2(-power)) + 0.5)
            steps = steps.astype(jnp.int32).astype(jnp.int16)
            for copy in range(sent_ref.shape[0]):
                sent_ref[copy, :, lanes] = steps
            power_ref[leaf : leaf + 1, :] = power
    for sent_ref, power_ref in zip(sent_refs, power_refs):
        power = power_ref[...].astype(jnp.int32).astype(jnp.int16)
        for first in range(0, leaf_count, columns):
            spot = points + first // columns * width
            for copy in range(sent_ref.shape[0]):
                sent_ref[copy, :, spot : spot + width] = power[first : first + columns]


def coupled(leaves, table_ref, coupling_ref, turned_ref):
    far_count, rank = coupling_ref.shape[1:3]
    columns = turned_ref.shape[1] // 2
    group = LANES // rank
    words = packed_words(table_ref[...])
    parts = []
    for leaf in leaves:
        maps = jnp.concatenate([coupling_ref[leaf, j] for j in range(far_count)], axis=1)
        maps = jnp.concatenate(halves(maps), axis=0)
        picked = jnp.concatenate(
            [
                turned_ref[pl.ds(pl.multiple_of(source * rank, rank), rank), :]
                for source in unpacked(words, far_count, leaf)
            ],
            axis=0,
        )
        out = dot_nn(maps, picked)
        parts.append(out[:rank] + out[rank:])
        if len(parts) == group:
            turned = jnp.concatenate(parts, axis=0).T
            yield turned[:columns] + turned[columns:]
            parts = []


def couple_kernel(
    table_ref, coupling_ref, dens_ref, bases_ref, turned_ref, out_ref,
):
    columns, points = dens_ref.shape
    leaf_count, _, rank = coupling_ref.shape[:3]
    width = points // leaf_count
    upper = lax.broadcasted_iota(jnp.int32, (rank, 2 * columns), 1) < columns
    for leaf in range(leaf_count):
        spots = slice(leaf * width, (leaf + 1) * width)
        rows = jnp.concatenate(halves(bases_ref[:, spots]), axis=0)
        dens = dens_ref[:, spots]
        twice = dot_nt(rows, jnp.concatenate([dens, dens], axis=0))
        high, low = halves(twice[:rank] + twice[rank:])
        turned_ref[leaf * rank : (leaf + 1) * rank, :] = jnp.where(
            upper, high.astype(F32), low.astype(F32)
        ).astype(BF16)
    leaves = range(out_ref.shape[1] // rank)
    for index, field in enumerate(coupled(leaves, table_ref, coupling_ref, turned_ref)):
        out_ref[:, index * LANES : (index + 1) * LANES] = field


def project_kernel(
    table_ref, coupling_ref, turned_ref, first_ref, bases_ref, near_ref, out_ref,
):
    rank, points = bases_ref.shape
    leaf_count = coupling_ref.shape[0]
    group = LANES // rank
    step = group * points // leaf_count

    def project(index, field):
        spots = slice(index * step, (index + 1) * step)
        high, low = halves(bases_ref[:, spots])
        out_ref[:, spots] = near_ref[:, spots] + split_dot(
            dot_nn, field, spread_bases(high, group), spread_bases(low, group)
        )

    done = first_ref.shape[1] // LANES
    for index in range(done):
        project(index, first_ref[:, index * LANES : (index + 1) * LANES])
    leaves = range(done * group, leaf_count)
    for index, field in enumerate(coupled(leaves, table_ref, coupling_ref, turned_ref)):
        project(done + index, field)


def paths_kernel(turns, exchanged, upper_ref, cross_ref, high_ref, low_ref, map_ref):
    device = lax.axis_index("leaf")
    rank = upper_ref.shape[1]
    device_count = upper_ref.shape[0] // 2
    downs = {device_count: None}
    level = device_count
    while level > 4:
        node = level + device // (device_count // level)
        below = downs[level]
        matrix = upper_ref[node]
        downs[level // 2] = matrix if below is None else split_dot(dot_nn, below, *halves(matrix))
        level //= 2
    for level in sorted(downs):
        place = device // (device_count // level)
        for index in range(level):
            if level == 4:
                map_ref[level + index] = jnp.zeros((rank, rank), F32)
            else:
                above = map_ref[(level + index) // 2]
                map_ref[level + index] = split_dot(
                    dot_nt, above, *halves(upper_ref[level + index])
                )
        third = jnp.where(place % 2 == 0, place + 3, place - 3)
        for slot, other in enumerate((place - 2, place + 2, third)):
            inside = (other >= 0) & (other < level)
            matrix = cross_ref[level + place, slot]
            if downs[level] is not None:
                matrix = split_dot(dot_nn, downs[level], *halves(matrix))
            node = level + jnp.clip(other, 0, level - 1)
            map_ref[node] = map_ref[node] + jnp.where(inside, matrix, 0.0)
    zero = jnp.zeros((rank, LANES - 3 * rank), F32)
    for place, turn in enumerate(turns):
        matrix = map_ref[device_count + (device ^ turn if exchanged else turn)]
        matrix = jnp.concatenate([matrix] * 3 + [zero], axis=1)
        high, low = halves(matrix)
        high_ref[:, place * LANES : (place + 1) * LANES] = high
        low_ref[:, place * LANES : (place + 1) * LANES] = low


def far_kernel(
    tiles, path_high_ref, path_low_ref, halves_ref, term_ref, *refs,
):
    root_refs, out_ref = refs[:-1], refs[-1]
    columns, points = out_ref.shape
    pieces = []
    for rows, root_ref in zip(tiles, root_refs):
        pieces += [root_ref[row : row + columns, :] for row in rows]
    roots = jnp.concatenate(pieces, axis=1)
    field = dot_nt(roots, path_high_ref[...]) + dot_nt(roots, path_low_ref[...])
    rows = jnp.concatenate(halves(field), axis=0)
    rows = jnp.concatenate([rows, rows], axis=1)
    step = 4 * LANES
    for first in range(0, points, step):
        spots = slice(first, first + step)
        out = dot_nn(rows, halves_ref[:, spots])
        out_ref[:, spots] = term_ref[:, spots] + (out[:columns] + out[columns:])


def add_kernel(leaf_count, term_ref, *refs):
    sent_refs, (out_hbm, sum_ref, sems) = refs[:-3], refs[-3:]
    count = len(sent_refs) + 1
    own = lax.axis_index("far")
    sent_refs = [
        sent_ref.at[lax.rem(own + count - part, count)] for part, sent_ref in enumerate(sent_refs, 1)
    ]
    columns, points = sum_ref.shape
    width = points // leaf_count
    factors = []
    for sent_ref in sent_refs:
        powers = [
            sent_ref[:, points + first // columns * width : points + first // columns * width + width]
            for first in range(0, leaf_count, columns)
        ]
        power = jnp.concatenate([p.astype(jnp.int32).astype(F32) for p in powers], axis=0)
        factors.append(jnp.exp2(power) * (1.0 / STEPS))
    chunk_count = sems.shape[0]
    step = points // chunk_count
    copies = []
    for index in range(chunk_count):
        spots = slice(index * step, (index + 1) * step)
        total = term_ref[:, spots]
        for sent_ref, factor in zip(sent_refs, factors):
            steps = sent_ref[:, spots].astype(jnp.int32).astype(F32)
            leaves = range(index * leaf_count // chunk_count, (index + 1) * leaf_count // chunk_count)
            scale = jnp.concatenate([factor[leaf : leaf + 1] for leaf in leaves], axis=1)
            total = total + steps * scale
        sum_ref[:, spots] = total
        copies += fetch(
            [(sum_ref.at[:, pl.ds(index * step, step)], out_hbm.at[:, pl.ds(index * step, step)])],
            sems.at[pl.ds(index, 1)],
        )
    for copy in copies:
        copy.wait()


def hbm(value):
    return pltpu.with_memory_space_constraint(value, pltpu.HBM)


def hint(micros):
    return pl.CostEstimate(flops=0, bytes_accessed=int(micros * 3.69e6), transcendentals=0)


def local(
    densities,
    bases,
    near_blocks,
    near_src,
    send_leaf,
    far_src,
    leaf_coupling,
    local_transfer,
    upper_transfer,
    up_coupling,
):
    leaf_devices = lax.axis_size("leaf")
    far_groups = lax.axis_size("far")
    share = lax.axis_size("mate")
    side = cube_side(leaf_devices)
    offsets = face_offsets(leaf_devices)
    columns, points = densities.shape
    leaf_count, near_count, width, _ = near_blocks.shape
    rank = bases.shape[0]
    cap = send_leaf.shape[2]
    node_count = local_transfer.shape[1]
    params = pltpu.CompilerParams(vmem_limit_bytes=16 * 2**20)
    dma = pltpu.SemaphoreType.DMA

    def rotated(value, axis, shift):
        count = lax.axis_size(axis)
        return lax.ppermute(value, axis, [(i, (i - shift) % count) for i in range(count)])

    def crossed(value, turn):
        return lax.ppermute(value, "leaf", [(i, i ^ turn) for i in range(leaf_devices)])

    sources = near_src.T
    others = [rotated(densities, "far", part) for part in range(1, far_groups)]
    all_sources = [sources] + [rotated(sources, "mate", part) for part in range(1, share)]
    send = send_leaf.transpose(1, 2, 0)
    moved = [
        densities, send, sources, far_src.T, upper_transfer, up_coupling, leaf_coupling, near_blocks,
    ]
    (
        basis, dens, send, sources, far_table, upper, cross, coupling, blocks, subtree, root,
    ) = pl.pallas_call(
        up_kernel,
        out_shape=[jax.ShapeDtypeStruct(value.shape, value.dtype) for value in (bases, *moved)]
        + [
            jax.ShapeDtypeStruct((2 * rank, points), BF16),
            jax.ShapeDtypeStruct((columns, LANES), BF16),
        ],
        in_specs=[HBM] * (2 + len(moved)),
        out_specs=[VMEM] * (3 + len(moved)),
        scratch_shapes=[
            pltpu.VMEM((rank, rank, node_count), F32),
            pltpu.VMEM((node_count * rank, LANES), F32),
            pltpu.VMEM((rank, node_count * rank), F32),
            dma((2 + len(moved),)),
        ],
        compiler_params=params,
        cost_estimate=hint(3.5),
        name="up",
    )(hbm(local_transfer[0].transpose(1, 2, 0)), hbm(bases), *map(hbm, moved))
    all_sources[0] = sources

    later_blocks, others, all_sources, root = lax.optimization_barrier(
        (blocks, others, all_sources, root)
    )
    mate_blocks = [rotated(later_blocks, "mate", part) for part in range(1, share)]

    if side == 2:
        faces = [((2 * axis, 2 * axis + 1), 2**axis) for axis in (2, 1, 0)]
    else:
        faces = [((direction,), offset) for direction, offset in enumerate(offsets)]
    chunk = (cap * far_groups + 1) * columns
    outgoing = pl.pallas_call(
        functools.partial(select_kernel, faces, far_groups),
        out_shape=[jax.ShapeDtypeStruct((chunk, LANES), BF16)] * len(faces),
        in_specs=[VMEM] * (2 + far_groups),
        out_specs=[VMEM] * len(faces),
        compiler_params=params,
        cost_estimate=hint(1),
        name="select",
    )(send, dens, root, *others)
    outgoing, dens = lax.optimization_barrier((outgoing, dens))
    first_leaves = leaf_count // 2
    turned, leaf_local = pl.pallas_call(
        couple_kernel,
        out_shape=[
            jax.ShapeDtypeStruct((leaf_count * rank, 2 * columns), BF16),
            jax.ShapeDtypeStruct((columns, first_leaves * rank), F32),
        ],
        in_specs=[VMEM] * 4,
        out_specs=[VMEM] * 2,
        compiler_params=params,
        cost_estimate=hint(2),
        name="couple",
    )(far_table, coupling, dens, basis)
    tail = cap * far_groups * columns
    if side == 2:
        arrived = [crossed(value, stride) for (_, stride), value in zip(faces, outgoing)]
        far_one, near_two, _ = (value[tail : tail + columns] for value in arrived)
        later, leaf_local = lax.optimization_barrier((arrived[0][-4 * columns :], leaf_local))
        across = crossed(later, 2)
        held = jnp.concatenate([near_two, far_one, across[-columns:]], axis=0)
        beside = crossed(held, 1)
        turns = [0] + [stride for _, stride in faces] + [6, 3, 5, 7]
        roots = [([0], root)] + [([tail], value) for value in arrived]
        roots += [([3 * columns], across), ([0, columns, 2 * columns], beside)]
    else:
        arrived = [shifted(value, "leaf", stride) for (_, stride), value in zip(faces, outgoing)]
        turns = list(range(leaf_devices))
        everyone = lax.all_gather(root, "leaf", axis=0, tiled=True)
        roots = [([turn * columns for turn in turns], everyone)]
    slots = leaf_count + len(offsets) * cap
    tables = -(-leaf_count // columns) * width
    partials = pl.pallas_call(
        functools.partial(near_kernel, faces, far_groups, share),
        out_shape=[jax.ShapeDtypeStruct((columns, points), F32)]
        + [jax.ShapeDtypeStruct((far_groups, columns, points + tables), jnp.int16)] * (far_groups - 1),
        in_specs=[VMEM] * (2 * share + far_groups + len(faces) + 1),
        out_specs=[VMEM] * far_groups,
        scratch_shapes=[pltpu.VMEM((leaf_count, width), F32)] * (far_groups - 1)
        + [
            pltpu.VMEM((slots, far_groups * columns, width), BF16),
        ],
        compiler_params=params,
        cost_estimate=hint(3),
        name="near",
    )(
        *all_sources, dens, *others, *arrived, blocks, *mate_blocks, leaf_local,
    )
    upper, cross, near_own = lax.optimization_barrier((upper, cross, partials[0]))
    paths = pl.pallas_call(
        functools.partial(paths_kernel, turns, side == 2),
        out_shape=[jax.ShapeDtypeStruct((rank, leaf_devices * LANES), BF16)] * 2,
        in_specs=[VMEM] * 2,
        out_specs=[VMEM] * 2,
        scratch_shapes=[pltpu.VMEM((2 * leaf_devices, rank, rank), F32)],
        compiler_params=params,
        cost_estimate=hint(0.7),
        name="paths",
    )(upper, cross)
    received = [
        lax.all_to_all(partials[part], "far", 0, 0, tiled=True) for part in range(1, far_groups)
    ]
    partial = pl.pallas_call(
        project_kernel,
        out_shape=jax.ShapeDtypeStruct((columns, points), F32),
        in_specs=[VMEM] * 6,
        out_specs=VMEM,
        compiler_params=params,
        cost_estimate=hint(1.5),
        name="project",
    )(far_table, coupling, turned, leaf_local, basis, near_own)
    total = pl.pallas_call(
        functools.partial(far_kernel, [rows for rows, _ in roots]),
        out_shape=jax.ShapeDtypeStruct((columns, points), F32),
        in_specs=[VMEM] * (4 + len(roots)),
        out_specs=VMEM,
        compiler_params=params,
        cost_estimate=hint(0.6),
        name="far",
    )(*paths, subtree, partial, *[value for _, value in roots])
    return pl.pallas_call(
        functools.partial(add_kernel, leaf_count),
        out_shape=jax.ShapeDtypeStruct((columns, points), F32),
        in_specs=[VMEM] * (1 + len(received)),
        out_specs=HBM,
        scratch_shapes=[pltpu.VMEM((columns, points), F32), dma((4,))],
        compiler_params=params,
        cost_estimate=hint(0.5),
        name="add",
    )(total, *received)


def solution(mesh):
    leaf_devices, rhs_devices = mesh.shape["leaf"], mesh.shape["rhs"]
    share = 2 if rhs_devices % 2 == 0 else 1
    split = Mesh(
        mesh.devices.reshape(leaf_devices, rhs_devices // share, share), ("leaf", "far", "mate")
    )
    rhs = ("far", "mate")
    in_specs = (
        P(rhs, "leaf"),
        P(None, "leaf"),
        P("leaf", rhs, None, None),
        P("leaf", rhs),
        P(),
        P("leaf", None),
        P("leaf", None, None, None),
        P("leaf", None, None, None),
        P(),
        P(),
    )
    return jax.shard_map(
        local, mesh=split, in_specs=in_specs, out_specs=P(rhs, "leaf"), check_vma=False
    )
```

```python
import functools

import jax
import jax.numpy as jnp
from jax import lax
from jax.experimental import pallas as pl
from jax.experimental.pallas import tpu as pltpu
from jax.sharding import Mesh
from jax.sharding import PartitionSpec as P

FACE_SIGNS = ((1, 0), (-1, 0), (1, 1), (-1, 1), (1, 2), (-1, 2))
F32 = jnp.float32
BF16 = jnp.bfloat16
LANES = 128
STEPS = 32000.0
VMEM = pl.BlockSpec(memory_space=pltpu.VMEM)
HBM = pl.BlockSpec(memory_space=pltpu.HBM)


def cube_side(device_count):
    return max((edge_len for edge_len in range(1, 65) if edge_len**3 <= device_count))


def face_offsets(device_count):
    side_len = cube_side(device_count)
    return [face_sign * side_len**axis_pos for face_sign, axis_pos in FACE_SIGNS]


def shifted(value, axis, steps):
    count = lax.axis_size(axis)
    first, last = (max(0, -steps), min(count, count - steps))
    return lax.ppermute(value, axis, [(source, source + steps) for source in range(first, last)])


def halves(value):
    high = value.astype(BF16)
    return high, (value - high.astype(F32)).astype(BF16)


def dot_nn(left, right):
    return lax.dot_general(left, right, (((1,), (0,)), ((), ())), preferred_element_type=F32)


def dot_nt(left, right):
    return lax.dot_general(left, right, (((1,), (1,)), ((), ())), preferred_element_type=F32)


def split_dot(dot, rows, right_high, right_low):
    count = rows.shape[0]
    high, low = halves(rows)
    both = jnp.concatenate([high, low], axis=0)
    out = dot(both, right_high) + dot(both, right_low)
    return out[:count] + out[count:]


def spread_bases(block, group):
    rank, lanes = block.shape
    width = lanes // group
    zero = jnp.zeros((rank, width), block.dtype)
    rows = []
    for slot in range(group):
        pieces = [zero] * group
        pieces[slot] = block[:, slot * width : (slot + 1) * width]
        rows.append(jnp.concatenate(pieces, axis=1))
    return jnp.concatenate(rows, axis=0)


def packed_words(table):
    words = []
    for first in range(0, table.shape[0], 4):
        word = table[first : first + 1]
        for row in range(first + 1, min(first + 4, table.shape[0])):
            word = word + (table[row : row + 1] << (8 * (row - first)))
        words.append(word)
    return words


def unpacked(words, count, place):
    values = [word[0, place] for word in words]
    return [(values[row // 4] >> (8 * (row % 4))) & 255 for row in range(count)]


def fetch(pairs, sems):
    copies = []
    for index, (source, target) in enumerate(pairs):
        copy = pltpu.make_async_copy(source, target, sems.at[index])
        copy.start()
        copies.append(copy)
    return copies


def up_kernel(
    maps_hbm, bases_hbm, *refs,
):
    count = (len(refs) - 7) // 2
    hbm_refs, bases_ref, vmem_refs = refs[:count], refs[count], refs[count + 1 : 2 * count + 1]
    halves_ref, root_ref, maps_ref, spread_ref, chain_ref, sems = refs[2 * count + 1 :]
    dens_ref, source_ref, shared_ref = vmem_refs[0], vmem_refs[2], vmem_refs[-1]
    block_rows = hbm_refs[-1].shape[0]
    vmem_refs = (*vmem_refs[:-1], shared_ref.at[pl.ds(0, block_rows)])
    copies = fetch(
        [(maps_hbm, maps_ref), (bases_hbm, bases_ref), *zip(hbm_refs, vmem_refs)], sems
    )
    columns, points = dens_ref.shape
    rank, _, node_count = maps_ref.shape
    group = LANES // rank
    leaf_count = node_count // 2
    width = points // leaf_count
    copies[0].wait()
    node = lax.broadcasted_iota(jnp.int32, (node_count, LANES), 0)
    block = lax.broadcasted_iota(jnp.int32, (node_count, LANES), 1) // rank
    parent = node // 2 % group
    for first in range(0, rank, group):
        slab = maps_ref[first : first + group].reshape(group * rank, node_count).T
        turned = [slab] + [pltpu.roll(slab, turn * rank, 1) for turn in range(1, group)]
        for row in range(group):
            placed = jnp.zeros_like(slab)
            for place in range(group):
                here = (parent == place) & (block == place)
                placed = jnp.where(here, turned[(place - row) % group], placed)
            spread_ref[pl.ds(first + row, node_count, stride=rank), :] = placed
    tile = 2 * group * rank

    def children(parents, index):
        high, low = halves(spread_ref[index * tile : (index + 1) * tile, :])
        return split_dot(dot_nt, parents, high, low)

    row = lax.broadcasted_iota(jnp.int32, (rank, LANES), 0)
    lane = lax.broadcasted_iota(jnp.int32, (rank, LANES), 1)
    level = 1
    parents = jnp.where(lane == row + rank, 1.0, 0.0)
    while level < group:
        below = children(parents, 0)
        level *= 2
        parents = below[:, (level // group) * LANES : (level // group + 1) * LANES]
    chain_ref[:, LANES : 2 * LANES] = parents
    while level < leaf_count:
        for index in range(level // group, 2 * level // group):
            lanes = slice(index * LANES, (index + 1) * LANES)
            chain_ref[:, index * tile : (index + 1) * tile] = children(chain_ref[:, lanes], index)
        level *= 2
    copies[1].wait()
    copies[2].wait()
    step = group * width
    root = jnp.zeros((columns, rank), F32)
    for index in range(leaf_count // group):
        spots = slice(index * step, (index + 1) * step)
        start = (leaf_count // group + index) * LANES
        high, low = halves(bases_ref[:, spots])
        basis = split_dot(
            dot_nn, chain_ref[:, start : start + LANES],
            spread_bases(high, group), spread_bases(low, group),
        )
        high, low = halves(basis)
        halves_ref[:rank, spots] = high
        halves_ref[rank:, spots] = low
        dens = dens_ref[:, spots]
        root += dot_nt(dens, high) + dot_nt(dens, low)
    root = jnp.concatenate([root, jnp.zeros((columns, LANES - rank), F32)], axis=1)
    high = root.astype(BF16).astype(F32)
    rest = root - high
    middle = rest.astype(BF16).astype(F32)
    last = (rest - middle).astype(BF16).astype(F32)
    packed = high + pltpu.roll(middle, rank, 1) + pltpu.roll(last, 2 * rank, 1)
    root_ref[...] = packed.astype(BF16)
    for copy in copies[3:]:
        copy.wait()
    near_count, leaf_count = source_ref.shape
    tile_rows = shared_ref.shape[0] - block_rows
    sources = jnp.concatenate(
        [source_ref[...].astype(F32), jnp.zeros((near_count, LANES - leaf_count), F32)], axis=1
    )
    sources = jnp.concatenate([sources, jnp.zeros((tile_rows - near_count, LANES), F32)], axis=0)
    shared_ref[block_rows:, :] = sources.astype(BF16)


def select_kernel(
    faces, far_groups, send_ref, dens_ref, root_ref, *refs,
):
    other_refs, out_refs = refs[: far_groups - 1], refs[far_groups - 1 :]
    device = lax.axis_index("leaf")
    columns = dens_ref.shape[0]
    cap, device_count = send_ref.shape[1:]
    own = lax.broadcasted_iota(jnp.int32, (cap, device_count), 1) == device
    for (directions, stride), out_ref in zip(faces, out_refs):
        table = send_ref[directions[0]]
        if len(directions) > 1:
            table = jnp.where(device // stride % 2 == 0, table, send_ref[directions[1]])
        picks = jnp.max(jnp.where(own, table.astype(F32), 0.0), axis=1, keepdims=True)
        for place in range(cap):
            leaf = picks[place, 0].astype(jnp.int32)
            for part, panel_ref in enumerate((dens_ref, *other_refs)):
                row = (place * far_groups + part) * columns
                out_ref[row : row + columns, :] = panel_ref[
                    :, pl.ds(pl.multiple_of(leaf * LANES, LANES), LANES)
                ]
        out_ref[cap * far_groups * columns :, :] = root_ref[...]


def near_kernel(
    faces, far_groups, share, *refs,
):
    dens_ref, refs = refs[0], refs[1:]
    other_refs, refs = refs[: far_groups - 1], refs[far_groups - 1 :]
    got_refs, refs = refs[: len(faces)], refs[len(faces) :]
    block_ref, refs = refs[0], refs[1:]
    mate_refs, refs = refs[: share - 1], refs[share - 1 :]
    refs = refs[1:]
    out_refs, refs = refs[:far_groups], refs[far_groups:]
    power_refs, refs = refs[: far_groups - 1], refs[far_groups - 1 :]
    (buffer_ref,) = refs
    columns, points = dens_ref.shape
    width = block_ref.shape[1]
    leaf_count = points // width
    block_rows = block_ref.shape[0] // width * width
    near_count = block_rows // width // leaf_count
    cap = (buffer_ref.shape[0] - leaf_count) // len(FACE_SIGNS)
    for (directions, _), got_ref in zip(faces, got_refs):
        for direction in directions:
            for place in range(cap):
                row = place * far_groups * columns
                buffer_ref[leaf_count + direction * cap + place] = got_ref[
                    row : row + far_groups * columns, :
                ]
    for part, panel_ref in enumerate((dens_ref, *other_refs)):
        rows = slice(part * columns, (part + 1) * columns)
        for leaf in range(leaf_count):
            buffer_ref[leaf, rows, :] = panel_ref[:, leaf * width : (leaf + 1) * width]
    tables = [ref[block_rows:, :].astype(F32) for ref in (block_ref, *mate_refs)]
    tables = jnp.concatenate([table[:near_count] for table in tables], axis=0)
    words = packed_words(tables.astype(jnp.int32))
    own_ref, sent_refs = out_refs[0], out_refs[1:]
    for leaf in range(leaf_count):
        panels = [buffer_ref[slot] for slot in unpacked(words, near_count * share, leaf)]
        blocks = [
            blocks_ref[(leaf * near_count + block) * width : (leaf * near_count + block + 1) * width, :]
            for blocks_ref in (block_ref, *mate_refs)
            for block in range(near_count)
        ]
        total = dot_nt(jnp.concatenate(panels, axis=1), jnp.concatenate(blocks, axis=1))
        lanes = slice(leaf * width, (leaf + 1) * width)
        own_ref[:, lanes] = total[:columns]
        for part, (sent_ref, power_ref) in enumerate(zip(sent_refs, power_refs), 1):
            term = total[part * columns : (part + 1) * columns]
            peak = jnp.max(jnp.abs(term), axis=0, keepdims=True)
            power = jnp.floor(jnp.log2(jnp.maximum(peak, 2.0**-100))) + 1.0
            steps = jnp.floor(term * (STEPS * jnp.exp2(-power)) + 0.5)
            sent_ref[:, lanes] = steps.astype(jnp.int32).astype(jnp.int16)
            power_ref[leaf : leaf + 1, :] = power
    for sent_ref, power_ref in zip(sent_refs, power_refs):
        power = power_ref[...].astype(jnp.int32).astype(jnp.int16)
        for first in range(0, leaf_count, columns):
            spot = points + first // columns * width
            sent_ref[:, spot : spot + width] = power[first : first + columns]


def coupled(leaves, table_ref, coupling_ref, turned_ref):
    far_count, rank = coupling_ref.shape[1:3]
    columns = turned_ref.shape[1] // 2
    group = LANES // rank
    words = packed_words(table_ref[...])
    parts = []
    for leaf in leaves:
        maps = jnp.concatenate([coupling_ref[leaf, j] for j in range(far_count)], axis=1)
        maps = jnp.concatenate(halves(maps), axis=0)
        picked = jnp.concatenate(
            [
                turned_ref[pl.ds(pl.multiple_of(source * rank, rank), rank), :]
                for source in unpacked(words, far_count, leaf)
            ],
            axis=0,
        )
        out = dot_nn(maps, picked)
        parts.append(out[:rank] + out[rank:])
        if len(parts) == group:
            turned = jnp.concatenate(parts, axis=0).T
            yield turned[:columns] + turned[columns:]
            parts = []


def couple_kernel(
    table_ref, coupling_ref, dens_ref, bases_ref, turned_ref, out_ref,
):
    columns, points = dens_ref.shape
    leaf_count, _, rank = coupling_ref.shape[:3]
    width = points // leaf_count
    upper = lax.broadcasted_iota(jnp.int32, (rank, 2 * columns), 1) < columns
    for leaf in range(leaf_count):
        spots = slice(leaf * width, (leaf + 1) * width)
        rows = jnp.concatenate(halves(bases_ref[:, spots]), axis=0)
        dens = dens_ref[:, spots]
        twice = dot_nt(rows, jnp.concatenate([dens, dens], axis=0))
        high, low = halves(twice[:rank] + twice[rank:])
        turned_ref[leaf * rank : (leaf + 1) * rank, :] = jnp.where(
            upper, high.astype(F32), low.astype(F32)
        ).astype(BF16)
    leaves = range(out_ref.shape[1] // rank)
    for index, field in enumerate(coupled(leaves, table_ref, coupling_ref, turned_ref)):
        out_ref[:, index * LANES : (index + 1) * LANES] = field


def project_kernel(
    table_ref, coupling_ref, turned_ref, first_ref, bases_ref, near_ref, out_ref,
):
    rank, points = bases_ref.shape
    leaf_count = coupling_ref.shape[0]
    group = LANES // rank
    step = group * points // leaf_count

    def project(index, field):
        spots = slice(index * step, (index + 1) * step)
        high, low = halves(bases_ref[:, spots])
        out_ref[:, spots] = near_ref[:, spots] + split_dot(
            dot_nn, field, spread_bases(high, group), spread_bases(low, group)
        )

    done = first_ref.shape[1] // LANES
    for index in range(done):
        project(index, first_ref[:, index * LANES : (index + 1) * LANES])
    leaves = range(done * group, leaf_count)
    for index, field in enumerate(coupled(leaves, table_ref, coupling_ref, turned_ref)):
        project(done + index, field)


def paths_kernel(turns, exchanged, upper_ref, cross_ref, high_ref, low_ref, map_ref):
    device = lax.axis_index("leaf")
    rank = upper_ref.shape[1]
    device_count = upper_ref.shape[0] // 2
    downs = {device_count: None}
    level = device_count
    while level > 4:
        node = level + device // (device_count // level)
        below = downs[level]
        matrix = upper_ref[node]
        downs[level // 2] = matrix if below is None else split_dot(dot_nn, below, *halves(matrix))
        level //= 2
    for level in sorted(downs):
        place = device // (device_count // level)
        for index in range(level):
            if level == 4:
                map_ref[level + index] = jnp.zeros((rank, rank), F32)
            else:
                above = map_ref[(level + index) // 2]
                map_ref[level + index] = split_dot(
                    dot_nt, above, *halves(upper_ref[level + index])
                )
        third = jnp.where(place % 2 == 0, place + 3, place - 3)
        for slot, other in enumerate((place - 2, place + 2, third)):
            inside = (other >= 0) & (other < level)
            matrix = cross_ref[level + place, slot]
            if downs[level] is not None:
                matrix = split_dot(dot_nn, downs[level], *halves(matrix))
            node = level + jnp.clip(other, 0, level - 1)
            map_ref[node] = map_ref[node] + jnp.where(inside, matrix, 0.0)
    zero = jnp.zeros((rank, LANES - 3 * rank), F32)
    for place, turn in enumerate(turns):
        matrix = map_ref[device_count + (device ^ turn if exchanged else turn)]
        matrix = jnp.concatenate([matrix] * 3 + [zero], axis=1)
        high, low = halves(matrix)
        high_ref[:, place * LANES : (place + 1) * LANES] = high
        low_ref[:, place * LANES : (place + 1) * LANES] = low


def far_kernel(
    tiles, path_high_ref, path_low_ref, halves_ref, term_ref, *refs,
):
    root_refs, out_ref = refs[:-1], refs[-1]
    columns, points = out_ref.shape
    pieces = []
    for rows, root_ref in zip(tiles, root_refs):
        pieces += [root_ref[row : row + columns, :] for row in rows]
    roots = jnp.concatenate(pieces, axis=1)
    field = dot_nt(roots, path_high_ref[...]) + dot_nt(roots, path_low_ref[...])
    rows = jnp.concatenate(halves(field), axis=0)
    rows = jnp.concatenate([rows, rows], axis=1)
    step = 4 * LANES
    for first in range(0, points, step):
        spots = slice(first, first + step)
        out = dot_nn(rows, halves_ref[:, spots])
        out_ref[:, spots] = term_ref[:, spots] + (out[:columns] + out[columns:])


def add_kernel(leaf_count, term_ref, *refs):
    sent_refs, (out_hbm, sum_ref, sems) = refs[:-3], refs[-3:]
    columns, points = sum_ref.shape
    width = points // leaf_count
    factors = []
    for sent_ref in sent_refs:
        powers = [
            sent_ref[:, points + first // columns * width :][:, :width]
            for first in range(0, leaf_count, columns)
        ]
        power = jnp.concatenate([p.astype(jnp.int32).astype(F32) for p in powers], axis=0)
        factors.append(jnp.exp2(power) * (1.0 / STEPS))
    chunk_count = sems.shape[0]
    step = points // chunk_count
    copies = []
    for index in range(chunk_count):
        spots = slice(index * step, (index + 1) * step)
        total = term_ref[:, spots]
        for sent_ref, factor in zip(sent_refs, factors):
            steps = sent_ref[:, spots].astype(jnp.int32).astype(F32)
            leaves = range(index * leaf_count // chunk_count, (index + 1) * leaf_count // chunk_count)
            scale = jnp.concatenate([factor[leaf : leaf + 1] for leaf in leaves], axis=1)
            total = total + steps * scale
        sum_ref[:, spots] = total
        copies += fetch(
            [(sum_ref.at[:, pl.ds(index * step, step)], out_hbm.at[:, pl.ds(index * step, step)])],
            sems.at[pl.ds(index, 1)],
        )
    for copy in copies:
        copy.wait()


def hbm(value):
    return pltpu.with_memory_space_constraint(value, pltpu.HBM)


def hint(micros):
    return pl.CostEstimate(flops=0, bytes_accessed=int(micros * 3.69e6), transcendentals=0)


def local(
    densities,
    bases,
    near_blocks,
    near_src,
    send_leaf,
    far_src,
    leaf_coupling,
    local_transfer,
    upper_transfer,
    up_coupling,
):
    leaf_devices = lax.axis_size("leaf")
    far_groups = lax.axis_size("far")
    share = lax.axis_size("mate")
    side = cube_side(leaf_devices)
    offsets = face_offsets(leaf_devices)
    columns, points = densities.shape
    leaf_count, near_count, width, _ = near_blocks.shape
    rank = bases.shape[0]
    cap = send_leaf.shape[2]
    node_count = local_transfer.shape[1]
    params = pltpu.CompilerParams(vmem_limit_bytes=16 * 2**20)
    dma = pltpu.SemaphoreType.DMA

    def rotated(value, axis, shift):
        count = lax.axis_size(axis)
        return lax.ppermute(value, axis, [(i, (i - shift) % count) for i in range(count)])

    def crossed(value, turn):
        return lax.ppermute(value, "leaf", [(i, i ^ turn) for i in range(leaf_devices)])

    sources = near_src.T
    others = [rotated(densities, "far", part) for part in range(1, far_groups)]
    send = send_leaf.transpose(1, 2, 0)
    moved = [
        densities, send, sources, far_src.T, upper_transfer, up_coupling, leaf_coupling,
        near_blocks.reshape(-1, width),
    ]
    (
        basis, dens, send, sources, far_table, upper, cross, coupling, blocks, subtree, root,
    ) = pl.pallas_call(
        up_kernel,
        out_shape=[jax.ShapeDtypeStruct(value.shape, value.dtype) for value in (bases, *moved[:-1])]
        + [jax.ShapeDtypeStruct((moved[-1].shape[0] + 16, width), BF16)]
        + [
            jax.ShapeDtypeStruct((2 * rank, points), BF16),
            jax.ShapeDtypeStruct((columns, LANES), BF16),
        ],
        in_specs=[HBM] * (2 + len(moved)),
        out_specs=[VMEM] * (3 + len(moved)),
        scratch_shapes=[
            pltpu.VMEM((rank, rank, node_count), F32),
            pltpu.VMEM((node_count * rank, LANES), F32),
            pltpu.VMEM((rank, node_count * rank), F32),
            dma((2 + len(moved),)),
        ],
        compiler_params=params,
        cost_estimate=hint(3.5),
        name="up",
    )(hbm(local_transfer[0].transpose(1, 2, 0)), hbm(bases), *map(hbm, moved))

    later_blocks, others, root = lax.optimization_barrier((blocks, others, root))
    mate_blocks = [rotated(later_blocks, "mate", part) for part in range(1, share)]

    if side == 2:
        faces = [((2 * axis, 2 * axis + 1), 2**axis) for axis in (2, 1, 0)]
    else:
        faces = [((direction,), offset) for direction, offset in enumerate(offsets)]
    chunk = (cap * far_groups + 1) * columns
    outgoing = pl.pallas_call(
        functools.partial(select_kernel, faces, far_groups),
        out_shape=[jax.ShapeDtypeStruct((chunk, LANES), BF16)] * len(faces),
        in_specs=[VMEM] * (2 + far_groups),
        out_specs=[VMEM] * len(faces),
        compiler_params=params,
        cost_estimate=hint(1),
        name="select",
    )(send, dens, root, *others)
    outgoing, dens = lax.optimization_barrier((outgoing, dens))
    first_leaves = leaf_count // 2
    turned, leaf_local = pl.pallas_call(
        couple_kernel,
        out_shape=[
            jax.ShapeDtypeStruct((leaf_count * rank, 2 * columns), BF16),
            jax.ShapeDtypeStruct((columns, first_leaves * rank), F32),
        ],
        in_specs=[VMEM] * 4,
        out_specs=[VMEM] * 2,
        compiler_params=params,
        cost_estimate=hint(2),
        name="couple",
    )(far_table, coupling, dens, basis)
    tail = cap * far_groups * columns
    if side == 2:
        arrived = [crossed(value, stride) for (_, stride), value in zip(faces, outgoing)]
        far_one, near_two, _ = (value[tail : tail + columns] for value in arrived)
        later, leaf_local = lax.optimization_barrier((arrived[0][-4 * columns :], leaf_local))
        across = crossed(later, 2)
        held = jnp.concatenate([near_two, far_one, across[-columns:]], axis=0)
        beside = crossed(held, 1)
        turns = [0] + [stride for _, stride in faces] + [6, 3, 5, 7]
        roots = [([0], root)] + [([tail], value) for value in arrived]
        roots += [([3 * columns], across), ([0, columns, 2 * columns], beside)]
    else:
        arrived = [shifted(value, "leaf", stride) for (_, stride), value in zip(faces, outgoing)]
        turns = list(range(leaf_devices))
        everyone = lax.all_gather(root, "leaf", axis=0, tiled=True)
        roots = [([turn * columns for turn in turns], everyone)]
    slots = leaf_count + len(offsets) * cap
    tables = -(-leaf_count // columns) * width
    partials = pl.pallas_call(
        functools.partial(near_kernel, faces, far_groups, share),
        out_shape=[jax.ShapeDtypeStruct((columns, points), F32)]
        + [jax.ShapeDtypeStruct((columns, points + tables), jnp.int16)] * (far_groups - 1),
        in_specs=[VMEM] * (share + far_groups + len(faces) + 1),
        out_specs=[VMEM] * far_groups,
        scratch_shapes=[pltpu.VMEM((leaf_count, width), F32)] * (far_groups - 1)
        + [
            pltpu.VMEM((slots, far_groups * columns, width), BF16),
        ],
        compiler_params=params,
        cost_estimate=hint(3),
        name="near",
    )(
        dens, *others, *arrived, blocks, *mate_blocks, leaf_local,
    )
    upper, cross, near_own = lax.optimization_barrier((upper, cross, partials[0]))
    paths = pl.pallas_call(
        functools.partial(paths_kernel, turns, side == 2),
        out_shape=[jax.ShapeDtypeStruct((rank, leaf_devices * LANES), BF16)] * 2,
        in_specs=[VMEM] * 2,
        out_specs=[VMEM] * 2,
        scratch_shapes=[pltpu.VMEM((2 * leaf_devices, rank, rank), F32)],
        compiler_params=params,
        cost_estimate=hint(0.7),
        name="paths",
    )(upper, cross)
    received = [rotated(partials[part], "far", -part) for part in range(1, far_groups)]
    partial = pl.pallas_call(
        project_kernel,
        out_shape=jax.ShapeDtypeStruct((columns, points), F32),
        in_specs=[VMEM] * 6,
        out_specs=VMEM,
        compiler_params=params,
        cost_estimate=hint(1.5),
        name="project",
    )(far_table, coupling, turned, leaf_local, basis, near_own)
    total = pl.pallas_call(
        functools.partial(far_kernel, [rows for rows, _ in roots]),
        out_shape=jax.ShapeDtypeStruct((columns, points), F32),
        in_specs=[VMEM] * (4 + len(roots)),
        out_specs=VMEM,
        compiler_params=params,
        cost_estimate=hint(0.6),
        name="far",
    )(*paths, subtree, partial, *[value for _, value in roots])
    return pl.pallas_call(
        functools.partial(add_kernel, leaf_count),
        out_shape=jax.ShapeDtypeStruct((columns, points), F32),
        in_specs=[VMEM] * (1 + len(received)),
        out_specs=HBM,
        scratch_shapes=[pltpu.VMEM((columns, points), F32), dma((4,))],
        compiler_params=params,
        cost_estimate=hint(0.5),
        name="add",
    )(total, *received)


def solution(mesh):
    leaf_devices, rhs_devices = mesh.shape["leaf"], mesh.shape["rhs"]
    share = 2 if rhs_devices % 2 == 0 else 1
    split = Mesh(
        mesh.devices.reshape(leaf_devices, rhs_devices // share, share), ("leaf", "far", "mate")
    )
    rhs = ("far", "mate")
    in_specs = (
        P(rhs, "leaf"),
        P(None, "leaf"),
        P("leaf", rhs, None, None),
        P("leaf", rhs),
        P(),
        P("leaf", None),
        P("leaf", None, None, None),
        P("leaf", None, None, None),
        P(),
        P(),
    )
    return jax.shard_map(
        local, mesh=split, in_specs=in_specs, out_specs=P(rhs, "leaf"), check_vma=False
    )
```

```python
import functools

import jax
import jax.numpy as jnp
from jax import lax
from jax.experimental import pallas as pl
from jax.experimental.pallas import tpu as pltpu
from jax.sharding import Mesh
from jax.sharding import PartitionSpec as P

FACE_SIGNS = ((1, 0), (-1, 0), (1, 1), (-1, 1), (1, 2), (-1, 2))
F32 = jnp.float32
BF16 = jnp.bfloat16
LANES = 128
STEPS = 32000.0
VMEM = pl.BlockSpec(memory_space=pltpu.VMEM)
HBM = pl.BlockSpec(memory_space=pltpu.HBM)


def cube_side(device_count):
    return max((edge_len for edge_len in range(1, 65) if edge_len**3 <= device_count))


def face_offsets(device_count):
    side_len = cube_side(device_count)
    return [face_sign * side_len**axis_pos for face_sign, axis_pos in FACE_SIGNS]


def shifted(value, axis, steps):
    count = lax.axis_size(axis)
    first, last = (max(0, -steps), min(count, count - steps))
    return lax.ppermute(value, axis, [(source, source + steps) for source in range(first, last)])


def halves(value):
    high = value.astype(BF16)
    return high, (value - high.astype(F32)).astype(BF16)


def dot_nn(left, right):
    return lax.dot_general(left, right, (((1,), (0,)), ((), ())), preferred_element_type=F32)


def dot_nt(left, right):
    return lax.dot_general(left, right, (((1,), (1,)), ((), ())), preferred_element_type=F32)


def split_dot(dot, rows, right_high, right_low):
    count = rows.shape[0]
    high, low = halves(rows)
    both = jnp.concatenate([high, low], axis=0)
    out = dot(both, right_high) + dot(both, right_low)
    return out[:count] + out[count:]


def spread_bases(block, group):
    rank, lanes = block.shape
    width = lanes // group
    zero = jnp.zeros((rank, width), block.dtype)
    rows = []
    for slot in range(group):
        pieces = [zero] * group
        pieces[slot] = block[:, slot * width : (slot + 1) * width]
        rows.append(jnp.concatenate(pieces, axis=1))
    return jnp.concatenate(rows, axis=0)


def packed_words(table):
    words = []
    for first in range(0, table.shape[0], 4):
        word = table[first : first + 1]
        for row in range(first + 1, min(first + 4, table.shape[0])):
            word = word + (table[row : row + 1] << (8 * (row - first)))
        words.append(word)
    return words


def unpacked(words, count, place):
    values = [word[0, place] for word in words]
    return [(values[row // 4] >> (8 * (row % 4))) & 255 for row in range(count)]


def fetch(pairs, sems):
    copies = []
    for index, (source, target) in enumerate(pairs):
        copy = pltpu.make_async_copy(source, target, sems.at[index])
        copy.start()
        copies.append(copy)
    return copies


def up_kernel(
    maps_hbm, bases_hbm, *refs,
):
    count = (len(refs) - 7) // 2
    hbm_refs, bases_ref, vmem_refs = refs[:count], refs[count], refs[count + 1 : 2 * count + 1]
    halves_ref, root_ref, maps_ref, spread_ref, chain_ref, sems = refs[2 * count + 1 :]
    dens_ref, source_ref, shared_ref = vmem_refs[0], vmem_refs[2], vmem_refs[-1]
    block_rows = hbm_refs[-1].shape[0]
    vmem_refs = (*vmem_refs[:-1], shared_ref.at[pl.ds(0, block_rows)])
    copies = fetch(
        [(maps_hbm, maps_ref), (bases_hbm, bases_ref), *zip(hbm_refs, vmem_refs)], sems
    )
    columns, points = dens_ref.shape
    rank, _, node_count = maps_ref.shape
    group = LANES // rank
    leaf_count = node_count // 2
    width = points // leaf_count
    copies[0].wait()
    node = lax.broadcasted_iota(jnp.int32, (node_count, LANES), 0)
    block = lax.broadcasted_iota(jnp.int32, (node_count, LANES), 1) // rank
    parent = node // 2 % group
    for first in range(0, rank, group):
        slab = maps_ref[first : first + group].reshape(group * rank, node_count).T
        turned = [slab] + [pltpu.roll(slab, turn * rank, 1) for turn in range(1, group)]
        for row in range(group):
            placed = jnp.zeros_like(slab)
            for place in range(group):
                here = (parent == place) & (block == place)
                placed = jnp.where(here, turned[(place - row) % group], placed)
            spread_ref[pl.ds(first + row, node_count, stride=rank), :] = placed
    tile = 2 * group * rank

    def children(parents, index):
        high, low = halves(spread_ref[index * tile : (index + 1) * tile, :])
        return split_dot(dot_nt, parents, high, low)

    row = lax.broadcasted_iota(jnp.int32, (rank, LANES), 0)
    lane = lax.broadcasted_iota(jnp.int32, (rank, LANES), 1)
    level = 1
    parents = jnp.where(lane == row + rank, 1.0, 0.0)
    while level < group:
        below = children(parents, 0)
        level *= 2
        parents = below[:, (level // group) * LANES : (level // group + 1) * LANES]
    chain_ref[:, LANES : 2 * LANES] = parents
    while level < leaf_count:
        for index in range(level // group, 2 * level // group):
            lanes = slice(index * LANES, (index + 1) * LANES)
            chain_ref[:, index * tile : (index + 1) * tile] = children(chain_ref[:, lanes], index)
        level *= 2
    copies[1].wait()
    copies[2].wait()
    copies[4].wait()
    near_count = source_ref.shape[0]
    tile_rows = shared_ref.shape[0] - block_rows
    sources = jnp.concatenate(
        [source_ref[...].astype(F32), jnp.zeros((near_count, LANES - leaf_count), F32)], axis=1
    )
    sources = jnp.concatenate([sources, jnp.zeros((tile_rows - near_count, LANES), F32)], axis=0)
    shared_ref[block_rows:, :] = sources.astype(BF16)
    step = group * width
    root = jnp.zeros((columns, rank), F32)
    for index in range(leaf_count // group):
        spots = slice(index * step, (index + 1) * step)
        start = (leaf_count // group + index) * LANES
        high, low = halves(bases_ref[:, spots])
        basis = split_dot(
            dot_nn, chain_ref[:, start : start + LANES],
            spread_bases(high, group), spread_bases(low, group),
        )
        high, low = halves(basis)
        halves_ref[:rank, spots] = high
        halves_ref[rank:, spots] = low
        dens = dens_ref[:, spots]
        root += dot_nt(dens, high) + dot_nt(dens, low)
    root = jnp.concatenate([root, jnp.zeros((columns, LANES - rank), F32)], axis=1)
    high = root.astype(BF16).astype(F32)
    rest = root - high
    middle = rest.astype(BF16).astype(F32)
    last = (rest - middle).astype(BF16).astype(F32)
    packed = high + pltpu.roll(middle, rank, 1) + pltpu.roll(last, 2 * rank, 1)
    root_ref[...] = packed.astype(BF16)
    copies[3].wait()
    for copy in copies[5:]:
        copy.wait()


def select_kernel(
    faces, far_groups, send_ref, dens_ref, root_ref, *refs,
):
    other_refs, out_refs = refs[: far_groups - 1], refs[far_groups - 1 :]
    device = lax.axis_index("leaf")
    columns = dens_ref.shape[0]
    cap, device_count = send_ref.shape[1:]
    own = lax.broadcasted_iota(jnp.int32, (cap, device_count), 1) == device
    for (directions, stride), out_ref in zip(faces, out_refs):
        table = send_ref[directions[0]]
        if len(directions) > 1:
            table = jnp.where(device // stride % 2 == 0, table, send_ref[directions[1]])
        picks = jnp.max(jnp.where(own, table.astype(F32), 0.0), axis=1, keepdims=True)
        for place in range(cap):
            leaf = picks[place, 0].astype(jnp.int32)
            for part, panel_ref in enumerate((dens_ref, *other_refs)):
                row = (place * far_groups + part) * columns
                out_ref[row : row + columns, :] = panel_ref[
                    :, pl.ds(pl.multiple_of(leaf * LANES, LANES), LANES)
                ]
        out_ref[cap * far_groups * columns :, :] = root_ref[...]


def near_kernel(
    faces, far_groups, share, *refs,
):
    dens_ref, refs = refs[0], refs[1:]
    other_refs, refs = refs[: far_groups - 1], refs[far_groups - 1 :]
    got_refs, refs = refs[: len(faces)], refs[len(faces) :]
    block_ref, refs = refs[0], refs[1:]
    mate_refs, refs = refs[: share - 1], refs[share - 1 :]
    refs = refs[1:]
    out_refs, refs = refs[:far_groups], refs[far_groups:]
    power_refs, refs = refs[: far_groups - 1], refs[far_groups - 1 :]
    (buffer_ref,) = refs
    columns, points = dens_ref.shape
    width = block_ref.shape[1]
    leaf_count = points // width
    block_rows = block_ref.shape[0] // width * width
    near_count = block_rows // width // leaf_count
    cap = (buffer_ref.shape[0] - leaf_count) // len(FACE_SIGNS)
    for (directions, _), got_ref in zip(faces, got_refs):
        for direction in directions:
            for place in range(cap):
                row = place * far_groups * columns
                buffer_ref[leaf_count + direction * cap + place] = got_ref[
                    row : row + far_groups * columns, :
                ]
    for part, panel_ref in enumerate((dens_ref, *other_refs)):
        rows = slice(part * columns, (part + 1) * columns)
        for leaf in range(leaf_count):
            buffer_ref[leaf, rows, :] = panel_ref[:, leaf * width : (leaf + 1) * width]
    tables = [ref[block_rows:, :].astype(F32) for ref in (block_ref, *mate_refs)]
    tables = jnp.concatenate([table[:near_count] for table in tables], axis=0)
    words = packed_words(tables.astype(jnp.int32))
    own_ref, sent_refs = out_refs[0], out_refs[1:]
    for leaf in range(leaf_count):
        panels = [buffer_ref[slot] for slot in unpacked(words, near_count * share, leaf)]
        blocks = [
            blocks_ref[(leaf * near_count + block) * width : (leaf * near_count + block + 1) * width, :]
            for blocks_ref in (block_ref, *mate_refs)
            for block in range(near_count)
        ]
        total = dot_nt(jnp.concatenate(panels, axis=1), jnp.concatenate(blocks, axis=1))
        lanes = slice(leaf * width, (leaf + 1) * width)
        own_ref[:, lanes] = total[:columns]
        for part, (sent_ref, power_ref) in enumerate(zip(sent_refs, power_refs), 1):
            term = total[part * columns : (part + 1) * columns]
            peak = jnp.max(jnp.abs(term), axis=0, keepdims=True)
            power = jnp.floor(jnp.log2(jnp.maximum(peak, 2.0**-100))) + 1.0
            steps = jnp.floor(term * (STEPS * jnp.exp2(-power)) + 0.5)
            sent_ref[:, lanes] = steps.astype(jnp.int32).astype(jnp.int16)
            power_ref[leaf : leaf + 1, :] = power
    for sent_ref, power_ref in zip(sent_refs, power_refs):
        power = power_ref[...].astype(jnp.int32).astype(jnp.int16)
        for first in range(0, leaf_count, columns):
            spot = points + first // columns * width
            sent_ref[:, spot : spot + width] = power[first : first + columns]


def coupled(leaves, table_ref, coupling_ref, turned_ref):
    far_count, rank = coupling_ref.shape[1:3]
    columns = turned_ref.shape[1] // 2
    group = LANES // rank
    words = packed_words(table_ref[...])
    parts = []
    for leaf in leaves:
        maps = jnp.concatenate([coupling_ref[leaf, j] for j in range(far_count)], axis=1)
        maps = jnp.concatenate(halves(maps), axis=0)
        picked = jnp.concatenate(
            [
                turned_ref[pl.ds(pl.multiple_of(source * rank, rank), rank), :]
                for source in unpacked(words, far_count, leaf)
            ],
            axis=0,
        )
        out = dot_nn(maps, picked)
        parts.append(out[:rank] + out[rank:])
        if len(parts) == group:
            turned = jnp.concatenate(parts, axis=0).T
            yield turned[:columns] + turned[columns:]
            parts = []


def couple_kernel(
    table_ref, coupling_ref, dens_ref, bases_ref, turned_ref, out_ref,
):
    columns, points = dens_ref.shape
    leaf_count, _, rank = coupling_ref.shape[:3]
    width = points // leaf_count
    upper = lax.broadcasted_iota(jnp.int32, (rank, 2 * columns), 1) < columns
    for leaf in range(leaf_count):
        spots = slice(leaf * width, (leaf + 1) * width)
        rows = jnp.concatenate(halves(bases_ref[:, spots]), axis=0)
        dens = dens_ref[:, spots]
        twice = dot_nt(rows, jnp.concatenate([dens, dens], axis=0))
        high, low = halves(twice[:rank] + twice[rank:])
        turned_ref[leaf * rank : (leaf + 1) * rank, :] = jnp.where(
            upper, high.astype(F32), low.astype(F32)
        ).astype(BF16)
    leaves = range(out_ref.shape[1] // rank)
    for index, field in enumerate(coupled(leaves, table_ref, coupling_ref, turned_ref)):
        out_ref[:, index * LANES : (index + 1) * LANES] = field


def project_kernel(
    table_ref, coupling_ref, turned_ref, first_ref, bases_ref, near_ref, out_ref,
):
    rank, points = bases_ref.shape
    leaf_count = coupling_ref.shape[0]
    group = LANES // rank
    step = group * points // leaf_count

    def project(index, field):
        spots = slice(index * step, (index + 1) * step)
        high, low = halves(bases_ref[:, spots])
        out_ref[:, spots] = near_ref[:, spots] + split_dot(
            dot_nn, field, spread_bases(high, group), spread_bases(low, group)
        )

    done = first_ref.shape[1] // LANES
    for index in range(done):
        project(index, first_ref[:, index * LANES : (index + 1) * LANES])
    leaves = range(done * group, leaf_count)
    for index, field in enumerate(coupled(leaves, table_ref, coupling_ref, turned_ref)):
        project(done + index, field)


def paths_kernel(turns, exchanged, upper_ref, cross_ref, high_ref, low_ref, map_ref):
    device = lax.axis_index("leaf")
    rank = upper_ref.shape[1]
    device_count = upper_ref.shape[0] // 2
    downs = {device_count: None}
    level = device_count
    while level > 4:
        node = level + device // (device_count // level)
        below = downs[level]
        matrix = upper_ref[node]
        downs[level // 2] = matrix if below is None else split_dot(dot_nn, below, *halves(matrix))
        level //= 2
    for level in sorted(downs):
        place = device // (device_count // level)
        for index in range(level):
            if level == 4:
                map_ref[level + index] = jnp.zeros((rank, rank), F32)
            else:
                above = map_ref[(level + index) // 2]
                map_ref[level + index] = split_dot(
                    dot_nt, above, *halves(upper_ref[level + index])
                )
        third = jnp.where(place % 2 == 0, place + 3, place - 3)
        for slot, other in enumerate((place - 2, place + 2, third)):
            inside = (other >= 0) & (other < level)
            matrix = cross_ref[level + place, slot]
            if downs[level] is not None:
                matrix = split_dot(dot_nn, downs[level], *halves(matrix))
            node = level + jnp.clip(other, 0, level - 1)
            map_ref[node] = map_ref[node] + jnp.where(inside, matrix, 0.0)
    zero = jnp.zeros((rank, LANES - 3 * rank), F32)
    for place, turn in enumerate(turns):
        matrix = map_ref[device_count + (device ^ turn if exchanged else turn)]
        matrix = jnp.concatenate([matrix] * 3 + [zero], axis=1)
        high, low = halves(matrix)
        high_ref[:, place * LANES : (place + 1) * LANES] = high
        low_ref[:, place * LANES : (place + 1) * LANES] = low


def far_kernel(
    tiles, path_high_ref, path_low_ref, halves_ref, term_ref, *refs,
):
    root_refs, out_ref = refs[:-1], refs[-1]
    columns, points = out_ref.shape
    pieces = []
    for rows, root_ref in zip(tiles, root_refs):
        pieces += [root_ref[row : row + columns, :] for row in rows]
    roots = jnp.concatenate(pieces, axis=1)
    field = dot_nt(roots, path_high_ref[...]) + dot_nt(roots, path_low_ref[...])
    rows = jnp.concatenate(halves(field), axis=0)
    rows = jnp.concatenate([rows, rows], axis=1)
    step = 4 * LANES
    for first in range(0, points, step):
        spots = slice(first, first + step)
        out = dot_nn(rows, halves_ref[:, spots])
        out_ref[:, spots] = term_ref[:, spots] + (out[:columns] + out[columns:])


def add_kernel(leaf_count, term_ref, *refs):
    sent_refs, (out_hbm, sum_ref, sems) = refs[:-3], refs[-3:]
    columns, points = sum_ref.shape
    width = points // leaf_count
    factors = []
    for sent_ref in sent_refs:
        powers = [
            sent_ref[:, points + first // columns * width :][:, :width]
            for first in range(0, leaf_count, columns)
        ]
        power = jnp.concatenate([p.astype(jnp.int32).astype(F32) for p in powers], axis=0)
        factors.append(jnp.exp2(power) * (1.0 / STEPS))
    chunk_count = sems.shape[0]
    step = points // chunk_count
    copies = []
    for index in range(chunk_count):
        spots = slice(index * step, (index + 1) * step)
        total = term_ref[:, spots]
        for sent_ref, factor in zip(sent_refs, factors):
            steps = sent_ref[:, spots].astype(jnp.int32).astype(F32)
            leaves = range(index * leaf_count // chunk_count, (index + 1) * leaf_count // chunk_count)
            scale = jnp.concatenate([factor[leaf : leaf + 1] for leaf in leaves], axis=1)
            total = total + steps * scale
        sum_ref[:, spots] = total
        copies += fetch(
            [(sum_ref.at[:, pl.ds(index * step, step)], out_hbm.at[:, pl.ds(index * step, step)])],
            sems.at[pl.ds(index, 1)],
        )
    for copy in copies:
        copy.wait()


def hbm(value):
    return pltpu.with_memory_space_constraint(value, pltpu.HBM)


def hint(micros):
    return pl.CostEstimate(flops=0, bytes_accessed=int(micros * 3.69e6), transcendentals=0)


def local(
    densities,
    bases,
    near_blocks,
    near_src,
    send_leaf,
    far_src,
    leaf_coupling,
    local_transfer,
    upper_transfer,
    up_coupling,
):
    leaf_devices = lax.axis_size("leaf")
    far_groups = lax.axis_size("far")
    share = lax.axis_size("mate")
    side = cube_side(leaf_devices)
    offsets = face_offsets(leaf_devices)
    columns, points = densities.shape
    leaf_count, near_count, width, _ = near_blocks.shape
    rank = bases.shape[0]
    cap = send_leaf.shape[2]
    node_count = local_transfer.shape[1]
    params = pltpu.CompilerParams(vmem_limit_bytes=16 * 2**20)
    dma = pltpu.SemaphoreType.DMA

    def rotated(value, axis, shift):
        count = lax.axis_size(axis)
        return lax.ppermute(value, axis, [(i, (i - shift) % count) for i in range(count)])

    def crossed(value, turn):
        return lax.ppermute(value, "leaf", [(i, i ^ turn) for i in range(leaf_devices)])

    sources = near_src.T
    others = [rotated(densities, "far", part) for part in range(1, far_groups)]
    send = send_leaf.transpose(1, 2, 0)
    moved = [
        densities, send, sources, far_src.T, upper_transfer, up_coupling, leaf_coupling,
        near_blocks.reshape(-1, width),
    ]
    (
        basis, dens, send, sources, far_table, upper, cross, coupling, blocks, subtree, root,
    ) = pl.pallas_call(
        up_kernel,
        out_shape=[jax.ShapeDtypeStruct(value.shape, value.dtype) for value in (bases, *moved[:-1])]
        + [jax.ShapeDtypeStruct((moved[-1].shape[0] + 16, width), BF16)]
        + [
            jax.ShapeDtypeStruct((2 * rank, points), BF16),
            jax.ShapeDtypeStruct((columns, LANES), BF16),
        ],
        in_specs=[HBM] * (2 + len(moved)),
        out_specs=[VMEM] * (3 + len(moved)),
        scratch_shapes=[
            pltpu.VMEM((rank, rank, node_count), F32),
            pltpu.VMEM((node_count * rank, LANES), F32),
            pltpu.VMEM((rank, node_count * rank), F32),
            dma((2 + len(moved),)),
        ],
        compiler_params=params,
        cost_estimate=hint(3.5),
        name="up",
    )(hbm(local_transfer[0].transpose(1, 2, 0)), hbm(bases), *map(hbm, moved))

    later_blocks, others, root = lax.optimization_barrier((blocks, others, root))
    mate_blocks = [rotated(later_blocks, "mate", part) for part in range(1, share)]

    if side == 2:
        faces = [((2 * axis, 2 * axis + 1), 2**axis) for axis in (2, 1, 0)]
    else:
        faces = [((direction,), offset) for direction, offset in enumerate(offsets)]
    chunk = (cap * far_groups + 1) * columns
    outgoing = pl.pallas_call(
        functools.partial(select_kernel, faces, far_groups),
        out_shape=[jax.ShapeDtypeStruct((chunk, LANES), BF16)] * len(faces),
        in_specs=[VMEM] * (2 + far_groups),
        out_specs=[VMEM] * len(faces),
        compiler_params=params,
        cost_estimate=hint(1),
        name="select",
    )(send, dens, root, *others)
    outgoing, dens = lax.optimization_barrier((outgoing, dens))
    first_leaves = leaf_count // 2
    turned, leaf_local = pl.pallas_call(
        couple_kernel,
        out_shape=[
            jax.ShapeDtypeStruct((leaf_count * rank, 2 * columns), BF16),
            jax.ShapeDtypeStruct((columns, first_leaves * rank), F32),
        ],
        in_specs=[VMEM] * 4,
        out_specs=[VMEM] * 2,
        compiler_params=params,
        cost_estimate=hint(2),
        name="couple",
    )(far_table, coupling, dens, basis)
    tail = cap * far_groups * columns
    if side == 2:
        arrived = [crossed(value, stride) for (_, stride), value in zip(faces, outgoing)]
        far_one, near_two, _ = (value[tail : tail + columns] for value in arrived)
        later, leaf_local = lax.optimization_barrier((arrived[0][-4 * columns :], leaf_local))
        across = crossed(later, 2)
        held = jnp.concatenate([near_two, far_one, across[-columns:]], axis=0)
        beside = crossed(held, 1)
        turns = [0] + [stride for _, stride in faces] + [6, 3, 5, 7]
        roots = [([0], root)] + [([tail], value) for value in arrived]
        roots += [([3 * columns], across), ([0, columns, 2 * columns], beside)]
    else:
        arrived = [shifted(value, "leaf", stride) for (_, stride), value in zip(faces, outgoing)]
        turns = list(range(leaf_devices))
        everyone = lax.all_gather(root, "leaf", axis=0, tiled=True)
        roots = [([turn * columns for turn in turns], everyone)]
    slots = leaf_count + len(offsets) * cap
    tables = -(-leaf_count // columns) * width
    partials = pl.pallas_call(
        functools.partial(near_kernel, faces, far_groups, share),
        out_shape=[jax.ShapeDtypeStruct((columns, points), F32)]
        + [jax.ShapeDtypeStruct((columns, points + tables), jnp.int16)] * (far_groups - 1),
        in_specs=[VMEM] * (share + far_groups + len(faces) + 1),
        out_specs=[VMEM] * far_groups,
        scratch_shapes=[pltpu.VMEM((leaf_count, width), F32)] * (far_groups - 1)
        + [
            pltpu.VMEM((slots, far_groups * columns, width), BF16),
        ],
        compiler_params=params,
        cost_estimate=hint(3),
        name="near",
    )(
        dens, *others, *arrived, blocks, *mate_blocks, leaf_local,
    )
    upper, cross, near_own = lax.optimization_barrier((upper, cross, partials[0]))
    paths = pl.pallas_call(
        functools.partial(paths_kernel, turns, side == 2),
        out_shape=[jax.ShapeDtypeStruct((rank, leaf_devices * LANES), BF16)] * 2,
        in_specs=[VMEM] * 2,
        out_specs=[VMEM] * 2,
        scratch_shapes=[pltpu.VMEM((2 * leaf_devices, rank, rank), F32)],
        compiler_params=params,
        cost_estimate=hint(0.7),
        name="paths",
    )(upper, cross)
    received = [rotated(partials[part], "far", -part) for part in range(1, far_groups)]
    partial = pl.pallas_call(
        project_kernel,
        out_shape=jax.ShapeDtypeStruct((columns, points), F32),
        in_specs=[VMEM] * 6,
        out_specs=VMEM,
        compiler_params=params,
        cost_estimate=hint(1.5),
        name="project",
    )(far_table, coupling, turned, leaf_local, basis, near_own)
    total = pl.pallas_call(
        functools.partial(far_kernel, [rows for rows, _ in roots]),
        out_shape=jax.ShapeDtypeStruct((columns, points), F32),
        in_specs=[VMEM] * (4 + len(roots)),
        out_specs=VMEM,
        compiler_params=params,
        cost_estimate=hint(0.6),
        name="far",
    )(*paths, subtree, partial, *[value for _, value in roots])
    return pl.pallas_call(
        functools.partial(add_kernel, leaf_count),
        out_shape=jax.ShapeDtypeStruct((columns, points), F32),
        in_specs=[VMEM] * (1 + len(received)),
        out_specs=HBM,
        scratch_shapes=[pltpu.VMEM((columns, points), F32), dma((4,))],
        compiler_params=params,
        cost_estimate=hint(0.5),
        name="add",
    )(total, *received)


def solution(mesh):
    leaf_devices, rhs_devices = mesh.shape["leaf"], mesh.shape["rhs"]
    share = 2 if rhs_devices % 2 == 0 else 1
    split = Mesh(
        mesh.devices.reshape(leaf_devices, rhs_devices // share, share), ("leaf", "far", "mate")
    )
    rhs = ("far", "mate")
    in_specs = (
        P(rhs, "leaf"),
        P(None, "leaf"),
        P("leaf", rhs, None, None),
        P("leaf", rhs),
        P(),
        P("leaf", None),
        P("leaf", None, None, None),
        P("leaf", None, None, None),
        P(),
        P(),
    )
    return jax.shard_map(
        local, mesh=split, in_specs=in_specs, out_specs=P(rhs, "leaf"), check_vma=False
    )
```

```python
import functools

import jax
import jax.numpy as jnp
from jax import lax
from jax.experimental import pallas as pl
from jax.experimental.pallas import tpu as pltpu
from jax.sharding import Mesh
from jax.sharding import PartitionSpec as P

FACE_SIGNS = ((1, 0), (-1, 0), (1, 1), (-1, 1), (1, 2), (-1, 2))
F32 = jnp.float32
BF16 = jnp.bfloat16
LANES = 128
STEPS = 32000.0
VMEM = pl.BlockSpec(memory_space=pltpu.VMEM)
HBM = pl.BlockSpec(memory_space=pltpu.HBM)


def cube_side(device_count):
    return max((edge_len for edge_len in range(1, 65) if edge_len**3 <= device_count))


def face_offsets(device_count):
    side_len = cube_side(device_count)
    return [face_sign * side_len**axis_pos for face_sign, axis_pos in FACE_SIGNS]


def shifted(value, axis, steps):
    count = lax.axis_size(axis)
    first, last = (max(0, -steps), min(count, count - steps))
    return lax.ppermute(value, axis, [(source, source + steps) for source in range(first, last)])


def halves(value):
    high = value.astype(BF16)
    return high, (value - high.astype(F32)).astype(BF16)


def dot_nn(left, right):
    return lax.dot_general(left, right, (((1,), (0,)), ((), ())), preferred_element_type=F32)


def dot_nt(left, right):
    return lax.dot_general(left, right, (((1,), (1,)), ((), ())), preferred_element_type=F32)


def split_dot(dot, rows, right_high, right_low):
    count = rows.shape[0]
    high, low = halves(rows)
    both = jnp.concatenate([high, low], axis=0)
    out = dot(both, right_high) + dot(both, right_low)
    return out[:count] + out[count:]


def spread_bases(block, group):
    rank, lanes = block.shape
    width = lanes // group
    zero = jnp.zeros((rank, width), block.dtype)
    rows = []
    for slot in range(group):
        pieces = [zero] * group
        pieces[slot] = block[:, slot * width : (slot + 1) * width]
        rows.append(jnp.concatenate(pieces, axis=1))
    return jnp.concatenate(rows, axis=0)


def packed_words(table):
    words = []
    for first in range(0, table.shape[0], 4):
        word = table[first : first + 1]
        for row in range(first + 1, min(first + 4, table.shape[0])):
            word = word + (table[row : row + 1] << (8 * (row - first)))
        words.append(word)
    return words


def unpacked(words, count, place):
    values = [word[0, place] for word in words]
    return [(values[row // 4] >> (8 * (row % 4))) & 255 for row in range(count)]


def fetch(pairs, sems):
    copies = []
    for index, (source, target) in enumerate(pairs):
        copy = pltpu.make_async_copy(source, target, sems.at[index])
        copy.start()
        copies.append(copy)
    return copies


def up_kernel(
    maps_hbm, bases_hbm, *refs,
):
    count = (len(refs) - 8) // 2
    hbm_refs, bases_ref, vmem_refs = refs[:count], refs[count], refs[count + 1 : 2 * count + 1]
    halves_ref, root_ref, maps_ref, spread_ref, chain_ref, sems, chunk_sems = refs[2 * count + 1 :]
    dens_ref, source_ref, shared_ref = vmem_refs[0], vmem_refs[2], vmem_refs[-1]
    block_rows = hbm_refs[-1].shape[0]
    pieces = chunk_sems.shape[0]
    pieces = [pl.ds(index * (block_rows // pieces), block_rows // pieces) for index in range(pieces)]
    copies = fetch(
        [(maps_hbm, maps_ref), (bases_hbm, bases_ref), *zip(hbm_refs[:-1], vmem_refs[:-1])], sems
    )
    copies += fetch([(hbm_refs[-1].at[piece], shared_ref.at[piece]) for piece in pieces], chunk_sems)
    columns, points = dens_ref.shape
    rank, _, node_count = maps_ref.shape
    group = LANES // rank
    leaf_count = node_count // 2
    width = points // leaf_count
    copies[0].wait()
    node = lax.broadcasted_iota(jnp.int32, (node_count, LANES), 0)
    block = lax.broadcasted_iota(jnp.int32, (node_count, LANES), 1) // rank
    parent = node // 2 % group
    for first in range(0, rank, group):
        slab = maps_ref[first : first + group].reshape(group * rank, node_count).T
        turned = [slab] + [pltpu.roll(slab, turn * rank, 1) for turn in range(1, group)]
        for row in range(group):
            placed = jnp.zeros_like(slab)
            for place in range(group):
                here = (parent == place) & (block == place)
                placed = jnp.where(here, turned[(place - row) % group], placed)
            spread_ref[pl.ds(first + row, node_count, stride=rank), :] = placed
    tile = 2 * group * rank

    def children(parents, index):
        high, low = halves(spread_ref[index * tile : (index + 1) * tile, :])
        return split_dot(dot_nt, parents, high, low)

    row = lax.broadcasted_iota(jnp.int32, (rank, LANES), 0)
    lane = lax.broadcasted_iota(jnp.int32, (rank, LANES), 1)
    level = 1
    parents = jnp.where(lane == row + rank, 1.0, 0.0)
    while level < group:
        below = children(parents, 0)
        level *= 2
        parents = below[:, (level // group) * LANES : (level // group + 1) * LANES]
    chain_ref[:, LANES : 2 * LANES] = parents
    while level < leaf_count:
        for index in range(level // group, 2 * level // group):
            lanes = slice(index * LANES, (index + 1) * LANES)
            chain_ref[:, index * tile : (index + 1) * tile] = children(chain_ref[:, lanes], index)
        level *= 2
    copies[1].wait()
    copies[2].wait()
    copies[4].wait()
    near_count = source_ref.shape[0]
    tile_rows = shared_ref.shape[0] - block_rows
    sources = jnp.concatenate(
        [source_ref[...].astype(F32), jnp.zeros((near_count, LANES - leaf_count), F32)], axis=1
    )
    sources = jnp.concatenate([sources, jnp.zeros((tile_rows - near_count, LANES), F32)], axis=0)
    shared_ref[block_rows:, :] = sources.astype(BF16)
    step = group * width
    root = jnp.zeros((columns, rank), F32)
    for index in range(leaf_count // group):
        spots = slice(index * step, (index + 1) * step)
        start = (leaf_count // group + index) * LANES
        high, low = halves(bases_ref[:, spots])
        basis = split_dot(
            dot_nn, chain_ref[:, start : start + LANES],
            spread_bases(high, group), spread_bases(low, group),
        )
        high, low = halves(basis)
        halves_ref[:rank, spots] = high
        halves_ref[rank:, spots] = low
        dens = dens_ref[:, spots]
        root += dot_nt(dens, high) + dot_nt(dens, low)
    root = jnp.concatenate([root, jnp.zeros((columns, LANES - rank), F32)], axis=1)
    high = root.astype(BF16).astype(F32)
    rest = root - high
    middle = rest.astype(BF16).astype(F32)
    last = (rest - middle).astype(BF16).astype(F32)
    packed = high + pltpu.roll(middle, rank, 1) + pltpu.roll(last, 2 * rank, 1)
    root_ref[...] = packed.astype(BF16)
    copies[3].wait()
    for copy in copies[5:]:
        copy.wait()


def select_kernel(
    faces, far_groups, send_ref, dens_ref, root_ref, *refs,
):
    other_refs, out_refs = refs[: far_groups - 1], refs[far_groups - 1 :]
    device = lax.axis_index("leaf")
    columns = dens_ref.shape[0]
    cap, device_count = send_ref.shape[1:]
    own = lax.broadcasted_iota(jnp.int32, (cap, device_count), 1) == device
    for (directions, stride), out_ref in zip(faces, out_refs):
        table = send_ref[directions[0]]
        if len(directions) > 1:
            table = jnp.where(device // stride % 2 == 0, table, send_ref[directions[1]])
        picks = jnp.max(jnp.where(own, table.astype(F32), 0.0), axis=1, keepdims=True)
        for place in range(cap):
            leaf = picks[place, 0].astype(jnp.int32)
            for part, panel_ref in enumerate((dens_ref, *other_refs)):
                row = (place * far_groups + part) * columns
                out_ref[row : row + columns, :] = panel_ref[
                    :, pl.ds(pl.multiple_of(leaf * LANES, LANES), LANES)
                ]
        out_ref[cap * far_groups * columns :, :] = root_ref[...]


def near_kernel(
    faces, far_groups, share, *refs,
):
    dens_ref, refs = refs[0], refs[1:]
    other_refs, refs = refs[: far_groups - 1], refs[far_groups - 1 :]
    got_refs, refs = refs[: len(faces)], refs[len(faces) :]
    block_ref, refs = refs[0], refs[1:]
    mate_refs, refs = refs[: share - 1], refs[share - 1 :]
    refs = refs[1:]
    out_refs, refs = refs[:far_groups], refs[far_groups:]
    power_refs, refs = refs[: far_groups - 1], refs[far_groups - 1 :]
    (buffer_ref,) = refs
    columns, points = dens_ref.shape
    width = block_ref.shape[1]
    leaf_count = points // width
    block_rows = block_ref.shape[0] // width * width
    near_count = block_rows // width // leaf_count
    cap = (buffer_ref.shape[0] - leaf_count) // len(FACE_SIGNS)
    for (directions, _), got_ref in zip(faces, got_refs):
        for direction in directions:
            for place in range(cap):
                row = place * far_groups * columns
                buffer_ref[leaf_count + direction * cap + place] = got_ref[
                    row : row + far_groups * columns, :
                ]
    for part, panel_ref in enumerate((dens_ref, *other_refs)):
        rows = slice(part * columns, (part + 1) * columns)
        for leaf in range(leaf_count):
            buffer_ref[leaf, rows, :] = panel_ref[:, leaf * width : (leaf + 1) * width]
    tables = [ref[block_rows:, :].astype(F32) for ref in (block_ref, *mate_refs)]
    tables = jnp.concatenate([table[:near_count] for table in tables], axis=0)
    words = packed_words(tables.astype(jnp.int32))
    own_ref, sent_refs = out_refs[0], out_refs[1:]
    for leaf in range(leaf_count):
        panels = [buffer_ref[slot] for slot in unpacked(words, near_count * share, leaf)]
        blocks = [
            blocks_ref[(leaf * near_count + block) * width : (leaf * near_count + block + 1) * width, :]
            for blocks_ref in (block_ref, *mate_refs)
            for block in range(near_count)
        ]
        total = dot_nt(jnp.concatenate(panels, axis=1), jnp.concatenate(blocks, axis=1))
        lanes = slice(leaf * width, (leaf + 1) * width)
        own_ref[:, lanes] = total[:columns]
        for part, (sent_ref, power_ref) in enumerate(zip(sent_refs, power_refs), 1):
            term = total[part * columns : (part + 1) * columns]
            peak = jnp.max(jnp.abs(term), axis=0, keepdims=True)
            power = jnp.floor(jnp.log2(jnp.maximum(peak, 2.0**-100))) + 1.0
            steps = jnp.floor(term * (STEPS * jnp.exp2(-power)) + 0.5)
            sent_ref[:, lanes] = steps.astype(jnp.int32).astype(jnp.int16)
            power_ref[leaf : leaf + 1, :] = power
    for sent_ref, power_ref in zip(sent_refs, power_refs):
        power = power_ref[...].astype(jnp.int32).astype(jnp.int16)
        for first in range(0, leaf_count, columns):
            spot = points + first // columns * width
            sent_ref[:, spot : spot + width] = power[first : first + columns]


def coupled(leaves, table_ref, coupling_ref, turned_ref):
    far_count, rank = coupling_ref.shape[1:3]
    columns = turned_ref.shape[1] // 2
    group = LANES // rank
    words = packed_words(table_ref[...])
    parts = []
    for leaf in leaves:
        maps = jnp.concatenate([coupling_ref[leaf, j] for j in range(far_count)], axis=1)
        maps = jnp.concatenate(halves(maps), axis=0)
        picked = jnp.concatenate(
            [
                turned_ref[pl.ds(pl.multiple_of(source * rank, rank), rank), :]
                for source in unpacked(words, far_count, leaf)
            ],
            axis=0,
        )
        out = dot_nn(maps, picked)
        parts.append(out[:rank] + out[rank:])
        if len(parts) == group:
            turned = jnp.concatenate(parts, axis=0).T
            yield turned[:columns] + turned[columns:]
            parts = []


def couple_kernel(
    table_ref, coupling_ref, dens_ref, bases_ref, turned_ref, out_ref,
):
    columns, points = dens_ref.shape
    leaf_count, _, rank = coupling_ref.shape[:3]
    width = points // leaf_count
    upper = lax.broadcasted_iota(jnp.int32, (rank, 2 * columns), 1) < columns
    for leaf in range(leaf_count):
        spots = slice(leaf * width, (leaf + 1) * width)
        rows = jnp.concatenate(halves(bases_ref[:, spots]), axis=0)
        dens = dens_ref[:, spots]
        twice = dot_nt(rows, jnp.concatenate([dens, dens], axis=0))
        high, low = halves(twice[:rank] + twice[rank:])
        turned_ref[leaf * rank : (leaf + 1) * rank, :] = jnp.where(
            upper, high.astype(F32), low.astype(F32)
        ).astype(BF16)
    leaves = range(out_ref.shape[1] // rank)
    for index, field in enumerate(coupled(leaves, table_ref, coupling_ref, turned_ref)):
        out_ref[:, index * LANES : (index + 1) * LANES] = field


def project_kernel(
    table_ref, coupling_ref, turned_ref, first_ref, bases_ref, near_ref, out_ref,
):
    rank, points = bases_ref.shape
    leaf_count = coupling_ref.shape[0]
    group = LANES // rank
    step = group * points // leaf_count

    def project(index, field):
        spots = slice(index * step, (index + 1) * step)
        high, low = halves(bases_ref[:, spots])
        out_ref[:, spots] = near_ref[:, spots] + split_dot(
            dot_nn, field, spread_bases(high, group), spread_bases(low, group)
        )

    done = first_ref.shape[1] // LANES
    for index in range(done):
        project(index, first_ref[:, index * LANES : (index + 1) * LANES])
    leaves = range(done * group, leaf_count)
    for index, field in enumerate(coupled(leaves, table_ref, coupling_ref, turned_ref)):
        project(done + index, field)


def paths_kernel(turns, exchanged, upper_ref, cross_ref, high_ref, low_ref, map_ref):
    device = lax.axis_index("leaf")
    rank = upper_ref.shape[1]
    device_count = upper_ref.shape[0] // 2
    downs = {device_count: None}
    level = device_count
    while level > 4:
        node = level + device // (device_count // level)
        below = downs[level]
        matrix = upper_ref[node]
        downs[level // 2] = matrix if below is None else split_dot(dot_nn, below, *halves(matrix))
        level //= 2
    for level in sorted(downs):
        place = device // (device_count // level)
        for index in range(level):
            if level == 4:
                map_ref[level + index] = jnp.zeros((rank, rank), F32)
            else:
                above = map_ref[(level + index) // 2]
                map_ref[level + index] = split_dot(
                    dot_nt, above, *halves(upper_ref[level + index])
                )
        third = jnp.where(place % 2 == 0, place + 3, place - 3)
        for slot, other in enumerate((place - 2, place + 2, third)):
            inside = (other >= 0) & (other < level)
            matrix = cross_ref[level + place, slot]
            if downs[level] is not None:
                matrix = split_dot(dot_nn, downs[level], *halves(matrix))
            node = level + jnp.clip(other, 0, level - 1)
            map_ref[node] = map_ref[node] + jnp.where(inside, matrix, 0.0)
    zero = jnp.zeros((rank, LANES - 3 * rank), F32)
    for place, turn in enumerate(turns):
        matrix = map_ref[device_count + (device ^ turn if exchanged else turn)]
        matrix = jnp.concatenate([matrix] * 3 + [zero], axis=1)
        high, low = halves(matrix)
        high_ref[:, place * LANES : (place + 1) * LANES] = high
        low_ref[:, place * LANES : (place + 1) * LANES] = low


def far_kernel(
    tiles, path_high_ref, path_low_ref, halves_ref, term_ref, *refs,
):
    root_refs, out_ref = refs[:-1], refs[-1]
    columns, points = out_ref.shape
    pieces = []
    for rows, root_ref in zip(tiles, root_refs):
        pieces += [root_ref[row : row + columns, :] for row in rows]
    roots = jnp.concatenate(pieces, axis=1)
    field = dot_nt(roots, path_high_ref[...]) + dot_nt(roots, path_low_ref[...])
    rows = jnp.concatenate(halves(field), axis=0)
    rows = jnp.concatenate([rows, rows], axis=1)
    step = 4 * LANES
    for first in range(0, points, step):
        spots = slice(first, first + step)
        out = dot_nn(rows, halves_ref[:, spots])
        out_ref[:, spots] = term_ref[:, spots] + (out[:columns] + out[columns:])


def add_kernel(leaf_count, term_ref, *refs):
    sent_refs, (out_hbm, sum_ref, sems) = refs[:-3], refs[-3:]
    columns, points = sum_ref.shape
    width = points // leaf_count
    factors = []
    for sent_ref in sent_refs:
        powers = [
            sent_ref[:, points + first // columns * width :][:, :width]
            for first in range(0, leaf_count, columns)
        ]
        power = jnp.concatenate([p.astype(jnp.int32).astype(F32) for p in powers], axis=0)
        factors.append(jnp.exp2(power) * (1.0 / STEPS))
    chunk_count = sems.shape[0]
    step = points // chunk_count
    copies = []
    for index in range(chunk_count):
        spots = slice(index * step, (index + 1) * step)
        total = term_ref[:, spots]
        for sent_ref, factor in zip(sent_refs, factors):
            steps = sent_ref[:, spots].astype(jnp.int32).astype(F32)
            leaves = range(index * leaf_count // chunk_count, (index + 1) * leaf_count // chunk_count)
            scale = jnp.concatenate([factor[leaf : leaf + 1] for leaf in leaves], axis=1)
            total = total + steps * scale
        sum_ref[:, spots] = total
        copies += fetch(
            [(sum_ref.at[:, pl.ds(index * step, step)], out_hbm.at[:, pl.ds(index * step, step)])],
            sems.at[pl.ds(index, 1)],
        )
    for copy in copies:
        copy.wait()


def hbm(value):
    return pltpu.with_memory_space_constraint(value, pltpu.HBM)


def hint(micros):
    return pl.CostEstimate(flops=0, bytes_accessed=int(micros * 3.69e6), transcendentals=0)


def local(
    densities,
    bases,
    near_blocks,
    near_src,
    send_leaf,
    far_src,
    leaf_coupling,
    local_transfer,
    upper_transfer,
    up_coupling,
):
    leaf_devices = lax.axis_size("leaf")
    far_groups = lax.axis_size("far")
    share = lax.axis_size("mate")
    side = cube_side(leaf_devices)
    offsets = face_offsets(leaf_devices)
    columns, points = densities.shape
    leaf_count, near_count, width, _ = near_blocks.shape
    rank = bases.shape[0]
    cap = send_leaf.shape[2]
    node_count = local_transfer.shape[1]
    params = pltpu.CompilerParams(vmem_limit_bytes=16 * 2**20)
    dma = pltpu.SemaphoreType.DMA

    def rotated(value, axis, shift):
        count = lax.axis_size(axis)
        return lax.ppermute(value, axis, [(i, (i - shift) % count) for i in range(count)])

    def crossed(value, turn):
        return lax.ppermute(value, "leaf", [(i, i ^ turn) for i in range(leaf_devices)])

    sources = near_src.T
    others = [rotated(densities, "far", part) for part in range(1, far_groups)]
    send = send_leaf.transpose(1, 2, 0)
    moved = [
        densities, send, sources, far_src.T, upper_transfer, up_coupling, leaf_coupling,
        near_blocks.reshape(-1, width),
    ]
    (
        basis, dens, send, sources, far_table, upper, cross, coupling, blocks, subtree, root,
    ) = pl.pallas_call(
        up_kernel,
        out_shape=[jax.ShapeDtypeStruct(value.shape, value.dtype) for value in (bases, *moved[:-1])]
        + [jax.ShapeDtypeStruct((moved[-1].shape[0] + 16, width), BF16)]
        + [
            jax.ShapeDtypeStruct((2 * rank, points), BF16),
            jax.ShapeDtypeStruct((columns, LANES), BF16),
        ],
        in_specs=[HBM] * (2 + len(moved)),
        out_specs=[VMEM] * (3 + len(moved)),
        scratch_shapes=[
            pltpu.VMEM((rank, rank, node_count), F32),
            pltpu.VMEM((node_count * rank, LANES), F32),
            pltpu.VMEM((rank, node_count * rank), F32),
            dma((1 + len(moved),)),
            dma((8,)),
        ],
        compiler_params=params,
        cost_estimate=hint(3.5),
        name="up",
    )(hbm(local_transfer[0].transpose(1, 2, 0)), hbm(bases), *map(hbm, moved))

    later_blocks, others, root = lax.optimization_barrier((blocks, others, root))
    mate_blocks = [rotated(later_blocks, "mate", part) for part in range(1, share)]

    if side == 2:
        faces = [((2 * axis, 2 * axis + 1), 2**axis) for axis in (2, 1, 0)]
    else:
        faces = [((direction,), offset) for direction, offset in enumerate(offsets)]
    chunk = (cap * far_groups + 1) * columns
    outgoing = pl.pallas_call(
        functools.partial(select_kernel, faces, far_groups),
        out_shape=[jax.ShapeDtypeStruct((chunk, LANES), BF16)] * len(faces),
        in_specs=[VMEM] * (2 + far_groups),
        out_specs=[VMEM] * len(faces),
        compiler_params=params,
        cost_estimate=hint(1),
        name="select",
    )(send, dens, root, *others)
    outgoing, dens = lax.optimization_barrier((outgoing, dens))
    first_leaves = leaf_count // 2
    turned, leaf_local = pl.pallas_call(
        couple_kernel,
        out_shape=[
            jax.ShapeDtypeStruct((leaf_count * rank, 2 * columns), BF16),
            jax.ShapeDtypeStruct((columns, first_leaves * rank), F32),
        ],
        in_specs=[VMEM] * 4,
        out_specs=[VMEM] * 2,
        compiler_params=params,
        cost_estimate=hint(2),
        name="couple",
    )(far_table, coupling, dens, basis)
    tail = cap * far_groups * columns
    if side == 2:
        arrived = [crossed(value, stride) for (_, stride), value in zip(faces, outgoing)]
        far_one, near_two, _ = (value[tail : tail + columns] for value in arrived)
        later, leaf_local = lax.optimization_barrier((arrived[0][-4 * columns :], leaf_local))
        across = crossed(later, 2)
        held = jnp.concatenate([near_two, far_one, across[-columns:]], axis=0)
        beside = crossed(held, 1)
        turns = [0] + [stride for _, stride in faces] + [6, 3, 5, 7]
        roots = [([0], root)] + [([tail], value) for value in arrived]
        roots += [([3 * columns], across), ([0, columns, 2 * columns], beside)]
    else:
        arrived = [shifted(value, "leaf", stride) for (_, stride), value in zip(faces, outgoing)]
        turns = list(range(leaf_devices))
        everyone = lax.all_gather(root, "leaf", axis=0, tiled=True)
        roots = [([turn * columns for turn in turns], everyone)]
    slots = leaf_count + len(offsets) * cap
    tables = -(-leaf_count // columns) * width
    partials = pl.pallas_call(
        functools.partial(near_kernel, faces, far_groups, share),
        out_shape=[jax.ShapeDtypeStruct((columns, points), F32)]
        + [jax.ShapeDtypeStruct((columns, points + tables), jnp.int16)] * (far_groups - 1),
        in_specs=[VMEM] * (share + far_groups + len(faces) + 1),
        out_specs=[VMEM] * far_groups,
        scratch_shapes=[pltpu.VMEM((leaf_count, width), F32)] * (far_groups - 1)
        + [
            pltpu.VMEM((slots, far_groups * columns, width), BF16),
        ],
        compiler_params=params,
        cost_estimate=hint(3),
        name="near",
    )(
        dens, *others, *arrived, blocks, *mate_blocks, leaf_local,
    )
    upper, cross, near_own = lax.optimization_barrier((upper, cross, partials[0]))
    paths = pl.pallas_call(
        functools.partial(paths_kernel, turns, side == 2),
        out_shape=[jax.ShapeDtypeStruct((rank, leaf_devices * LANES), BF16)] * 2,
        in_specs=[VMEM] * 2,
        out_specs=[VMEM] * 2,
        scratch_shapes=[pltpu.VMEM((2 * leaf_devices, rank, rank), F32)],
        compiler_params=params,
        cost_estimate=hint(0.7),
        name="paths",
    )(upper, cross)
    received = [rotated(partials[part], "far", -part) for part in range(1, far_groups)]
    partial = pl.pallas_call(
        project_kernel,
        out_shape=jax.ShapeDtypeStruct((columns, points), F32),
        in_specs=[VMEM] * 6,
        out_specs=VMEM,
        compiler_params=params,
        cost_estimate=hint(1.5),
        name="project",
    )(far_table, coupling, turned, leaf_local, basis, near_own)
    total = pl.pallas_call(
        functools.partial(far_kernel, [rows for rows, _ in roots]),
        out_shape=jax.ShapeDtypeStruct((columns, points), F32),
        in_specs=[VMEM] * (4 + len(roots)),
        out_specs=VMEM,
        compiler_params=params,
        cost_estimate=hint(0.6),
        name="far",
    )(*paths, subtree, partial, *[value for _, value in roots])
    return pl.pallas_call(
        functools.partial(add_kernel, leaf_count),
        out_shape=jax.ShapeDtypeStruct((columns, points), F32),
        in_specs=[VMEM] * (1 + len(received)),
        out_specs=HBM,
        scratch_shapes=[pltpu.VMEM((columns, points), F32), dma((4,))],
        compiler_params=params,
        cost_estimate=hint(0.5),
        name="add",
    )(total, *received)


def solution(mesh):
    leaf_devices, rhs_devices = mesh.shape["leaf"], mesh.shape["rhs"]
    share = 2 if rhs_devices % 2 == 0 else 1
    split = Mesh(
        mesh.devices.reshape(leaf_devices, rhs_devices // share, share), ("leaf", "far", "mate")
    )
    rhs = ("far", "mate")
    in_specs = (
        P(rhs, "leaf"),
        P(None, "leaf"),
        P("leaf", rhs, None, None),
        P("leaf", rhs),
        P(),
        P("leaf", None),
        P("leaf", None, None, None),
        P("leaf", None, None, None),
        P(),
        P(),
    )
    return jax.shard_map(
        local, mesh=split, in_specs=in_specs, out_specs=P(rhs, "leaf"), check_vma=False
    )
```

```python
import functools

import jax
import jax.numpy as jnp
from jax import lax
from jax.experimental import pallas as pl
from jax.experimental.pallas import tpu as pltpu
from jax.sharding import Mesh
from jax.sharding import PartitionSpec as P

FACE_SIGNS = ((1, 0), (-1, 0), (1, 1), (-1, 1), (1, 2), (-1, 2))
F32 = jnp.float32
BF16 = jnp.bfloat16
LANES = 128
STEPS = 32000.0
VMEM = pl.BlockSpec(memory_space=pltpu.VMEM)
HBM = pl.BlockSpec(memory_space=pltpu.HBM)


def cube_side(device_count):
    return max((edge_len for edge_len in range(1, 65) if edge_len**3 <= device_count))


def face_offsets(device_count):
    side_len = cube_side(device_count)
    return [face_sign * side_len**axis_pos for face_sign, axis_pos in FACE_SIGNS]


def shifted(value, axis, steps):
    count = lax.axis_size(axis)
    first, last = (max(0, -steps), min(count, count - steps))
    return lax.ppermute(value, axis, [(source, source + steps) for source in range(first, last)])


def halves(value):
    high = value.astype(BF16)
    return high, (value - high.astype(F32)).astype(BF16)


def dot_nn(left, right):
    return lax.dot_general(left, right, (((1,), (0,)), ((), ())), preferred_element_type=F32)


def dot_nt(left, right):
    return lax.dot_general(left, right, (((1,), (1,)), ((), ())), preferred_element_type=F32)


def split_dot(dot, rows, right_high, right_low):
    count = rows.shape[0]
    high, low = halves(rows)
    both = jnp.concatenate([high, low], axis=0)
    out = dot(both, right_high) + dot(both, right_low)
    return out[:count] + out[count:]


def spread_bases(block, group):
    rank, lanes = block.shape
    width = lanes // group
    zero = jnp.zeros((rank, width), block.dtype)
    rows = []
    for slot in range(group):
        pieces = [zero] * group
        pieces[slot] = block[:, slot * width : (slot + 1) * width]
        rows.append(jnp.concatenate(pieces, axis=1))
    return jnp.concatenate(rows, axis=0)


def packed_words(table):
    words = []
    for first in range(0, table.shape[0], 4):
        word = table[first : first + 1]
        for row in range(first + 1, min(first + 4, table.shape[0])):
            word = word + (table[row : row + 1] << (8 * (row - first)))
        words.append(word)
    return words


def unpacked(words, count, place):
    values = [word[0, place] for word in words]
    return [(values[row // 4] >> (8 * (row % 4))) & 255 for row in range(count)]


def fetch(pairs, sems):
    copies = []
    for index, (source, target) in enumerate(pairs):
        copy = pltpu.make_async_copy(source, target, sems.at[index])
        copy.start()
        copies.append(copy)
    return copies


def up_kernel(
    maps_hbm, bases_hbm, *refs,
):
    count = (len(refs) - 7) // 2
    hbm_refs, bases_ref, vmem_refs = refs[:count], refs[count], refs[count + 1 : 2 * count + 1]
    halves_ref, root_ref, maps_ref, spread_ref, chain_ref, sems = refs[2 * count + 1 :]
    dens_ref, source_ref, shared_ref = vmem_refs[0], vmem_refs[2], vmem_refs[-1]
    block_rows = hbm_refs[-1].shape[0]
    vmem_refs = (*vmem_refs[:-1], shared_ref.at[pl.ds(0, block_rows)])
    copies = fetch(
        [(maps_hbm, maps_ref), (bases_hbm, bases_ref), *zip(hbm_refs[:-2], vmem_refs[:-2])], sems
    )
    columns, points = dens_ref.shape
    rank, _, node_count = maps_ref.shape
    group = LANES // rank
    leaf_count = node_count // 2
    width = points // leaf_count
    copies[0].wait()
    copies += fetch(zip(hbm_refs[-2:], vmem_refs[-2:]), sems.at[pl.ds(count, 2)])
    node = lax.broadcasted_iota(jnp.int32, (node_count, LANES), 0)
    block = lax.broadcasted_iota(jnp.int32, (node_count, LANES), 1) // rank
    parent = node // 2 % group
    for first in range(0, rank, group):
        slab = maps_ref[first : first + group].reshape(group * rank, node_count).T
        turned = [slab] + [pltpu.roll(slab, turn * rank, 1) for turn in range(1, group)]
        for row in range(group):
            placed = jnp.zeros_like(slab)
            for place in range(group):
                here = (parent == place) & (block == place)
                placed = jnp.where(here, turned[(place - row) % group], placed)
            spread_ref[pl.ds(first + row, node_count, stride=rank), :] = placed
    tile = 2 * group * rank

    def children(parents, index):
        high, low = halves(spread_ref[index * tile : (index + 1) * tile, :])
        return split_dot(dot_nt, parents, high, low)

    row = lax.broadcasted_iota(jnp.int32, (rank, LANES), 0)
    lane = lax.broadcasted_iota(jnp.int32, (rank, LANES), 1)
    level = 1
    parents = jnp.where(lane == row + rank, 1.0, 0.0)
    while level < group:
        below = children(parents, 0)
        level *= 2
        parents = below[:, (level // group) * LANES : (level // group + 1) * LANES]
    chain_ref[:, LANES : 2 * LANES] = parents
    while level < leaf_count:
        for index in range(level // group, 2 * level // group):
            lanes = slice(index * LANES, (index + 1) * LANES)
            chain_ref[:, index * tile : (index + 1) * tile] = children(chain_ref[:, lanes], index)
        level *= 2
    copies[1].wait()
    copies[2].wait()
    copies[4].wait()
    near_count = source_ref.shape[0]
    tile_rows = shared_ref.shape[0] - block_rows
    sources = jnp.concatenate(
        [source_ref[...].astype(F32), jnp.zeros((near_count, LANES - leaf_count), F32)], axis=1
    )
    sources = jnp.concatenate([sources, jnp.zeros((tile_rows - near_count, LANES), F32)], axis=0)
    shared_ref[block_rows:, :] = sources.astype(BF16)
    step = group * width
    root = jnp.zeros((columns, rank), F32)
    for index in range(leaf_count // group):
        spots = slice(index * step, (index + 1) * step)
        start = (leaf_count // group + index) * LANES
        high, low = halves(bases_ref[:, spots])
        basis = split_dot(
            dot_nn, chain_ref[:, start : start + LANES],
            spread_bases(high, group), spread_bases(low, group),
        )
        high, low = halves(basis)
        halves_ref[:rank, spots] = high
        halves_ref[rank:, spots] = low
        dens = dens_ref[:, spots]
        root += dot_nt(dens, high) + dot_nt(dens, low)
    root = jnp.concatenate([root, jnp.zeros((columns, LANES - rank), F32)], axis=1)
    high = root.astype(BF16).astype(F32)
    rest = root - high
    middle = rest.astype(BF16).astype(F32)
    last = (rest - middle).astype(BF16).astype(F32)
    packed = high + pltpu.roll(middle, rank, 1) + pltpu.roll(last, 2 * rank, 1)
    root_ref[...] = packed.astype(BF16)
    copies[3].wait()
    for copy in copies[5:]:
        copy.wait()


def select_kernel(
    faces, far_groups, send_ref, dens_ref, root_ref, *refs,
):
    other_refs, out_refs = refs[: far_groups - 1], refs[far_groups - 1 :]
    device = lax.axis_index("leaf")
    columns = dens_ref.shape[0]
    cap, device_count = send_ref.shape[1:]
    own = lax.broadcasted_iota(jnp.int32, (cap, device_count), 1) == device
    for (directions, stride), out_ref in zip(faces, out_refs):
        table = send_ref[directions[0]]
        if len(directions) > 1:
            table = jnp.where(device // stride % 2 == 0, table, send_ref[directions[1]])
        picks = jnp.max(jnp.where(own, table.astype(F32), 0.0), axis=1, keepdims=True)
        for place in range(cap):
            leaf = picks[place, 0].astype(jnp.int32)
            for part, panel_ref in enumerate((dens_ref, *other_refs)):
                row = (place * far_groups + part) * columns
                out_ref[row : row + columns, :] = panel_ref[
                    :, pl.ds(pl.multiple_of(leaf * LANES, LANES), LANES)
                ]
        out_ref[cap * far_groups * columns :, :] = root_ref[...]


def near_kernel(
    faces, far_groups, share, *refs,
):
    dens_ref, refs = refs[0], refs[1:]
    other_refs, refs = refs[: far_groups - 1], refs[far_groups - 1 :]
    got_refs, refs = refs[: len(faces)], refs[len(faces) :]
    block_ref, refs = refs[0], refs[1:]
    mate_refs, refs = refs[: share - 1], refs[share - 1 :]
    refs = refs[1:]
    out_refs, refs = refs[:far_groups], refs[far_groups:]
    power_refs, refs = refs[: far_groups - 1], refs[far_groups - 1 :]
    (buffer_ref,) = refs
    columns, points = dens_ref.shape
    width = block_ref.shape[1]
    leaf_count = points // width
    block_rows = block_ref.shape[0] // width * width
    near_count = block_rows // width // leaf_count
    cap = (buffer_ref.shape[0] - leaf_count) // len(FACE_SIGNS)
    for (directions, _), got_ref in zip(faces, got_refs):
        for direction in directions:
            for place in range(cap):
                row = place * far_groups * columns
                buffer_ref[leaf_count + direction * cap + place] = got_ref[
                    row : row + far_groups * columns, :
                ]
    for part, panel_ref in enumerate((dens_ref, *other_refs)):
        rows = slice(part * columns, (part + 1) * columns)
        for leaf in range(leaf_count):
            buffer_ref[leaf, rows, :] = panel_ref[:, leaf * width : (leaf + 1) * width]
    tables = [ref[block_rows:, :].astype(F32) for ref in (block_ref, *mate_refs)]
    tables = jnp.concatenate([table[:near_count] for table in tables], axis=0)
    words = packed_words(tables.astype(jnp.int32))
    own_ref, sent_refs = out_refs[0], out_refs[1:]
    for leaf in range(leaf_count):
        panels = [buffer_ref[slot] for slot in unpacked(words, near_count * share, leaf)]
        blocks = [
            blocks_ref[(leaf * near_count + block) * width : (leaf * near_count + block + 1) * width, :]
            for blocks_ref in (block_ref, *mate_refs)
            for block in range(near_count)
        ]
        total = dot_nt(jnp.concatenate(panels, axis=1), jnp.concatenate(blocks, axis=1))
        lanes = slice(leaf * width, (leaf + 1) * width)
        own_ref[:, lanes] = total[:columns]
        for part, (sent_ref, power_ref) in enumerate(zip(sent_refs, power_refs), 1):
            term = total[part * columns : (part + 1) * columns]
            peak = jnp.max(jnp.abs(term), axis=0, keepdims=True)
            power = jnp.floor(jnp.log2(jnp.maximum(peak, 2.0**-100))) + 1.0
            steps = jnp.floor(term * (STEPS * jnp.exp2(-power)) + 0.5)
            sent_ref[:, lanes] = steps.astype(jnp.int32).astype(jnp.int16)
            power_ref[leaf : leaf + 1, :] = power
    for sent_ref, power_ref in zip(sent_refs, power_refs):
        power = power_ref[...].astype(jnp.int32).astype(jnp.int16)
        for first in range(0, leaf_count, columns):
            spot = points + first // columns * width
            sent_ref[:, spot : spot + width] = power[first : first + columns]


def coupled(leaves, table_ref, coupling_ref, turned_ref):
    far_count, rank = coupling_ref.shape[1:3]
    columns = turned_ref.shape[1] // 2
    group = LANES // rank
    words = packed_words(table_ref[...])
    parts = []
    for leaf in leaves:
        maps = jnp.concatenate([coupling_ref[leaf, j] for j in range(far_count)], axis=1)
        maps = jnp.concatenate(halves(maps), axis=0)
        picked = jnp.concatenate(
            [
                turned_ref[pl.ds(pl.multiple_of(source * rank, rank), rank), :]
                for source in unpacked(words, far_count, leaf)
            ],
            axis=0,
        )
        out = dot_nn(maps, picked)
        parts.append(out[:rank] + out[rank:])
        if len(parts) == group:
            turned = jnp.concatenate(parts, axis=0).T
            yield turned[:columns] + turned[columns:]
            parts = []


def couple_kernel(
    table_ref, coupling_ref, dens_ref, bases_ref, turned_ref, out_ref,
):
    columns, points = dens_ref.shape
    leaf_count, _, rank = coupling_ref.shape[:3]
    width = points // leaf_count
    upper = lax.broadcasted_iota(jnp.int32, (rank, 2 * columns), 1) < columns
    for leaf in range(leaf_count):
        spots = slice(leaf * width, (leaf + 1) * width)
        rows = jnp.concatenate(halves(bases_ref[:, spots]), axis=0)
        dens = dens_ref[:, spots]
        twice = dot_nt(rows, jnp.concatenate([dens, dens], axis=0))
        high, low = halves(twice[:rank] + twice[rank:])
        turned_ref[leaf * rank : (leaf + 1) * rank, :] = jnp.where(
            upper, high.astype(F32), low.astype(F32)
        ).astype(BF16)
    leaves = range(out_ref.shape[1] // rank)
    for index, field in enumerate(coupled(leaves, table_ref, coupling_ref, turned_ref)):
        out_ref[:, index * LANES : (index + 1) * LANES] = field


def project_kernel(
    table_ref, coupling_ref, turned_ref, first_ref, bases_ref, near_ref, out_ref,
):
    rank, points = bases_ref.shape
    leaf_count = coupling_ref.shape[0]
    group = LANES // rank
    step = group * points // leaf_count

    def project(index, field):
        spots = slice(index * step, (index + 1) * step)
        high, low = halves(bases_ref[:, spots])
        out_ref[:, spots] = near_ref[:, spots] + split_dot(
            dot_nn, field, spread_bases(high, group), spread_bases(low, group)
        )

    done = first_ref.shape[1] // LANES
    for index in range(done):
        project(index, first_ref[:, index * LANES : (index + 1) * LANES])
    leaves = range(done * group, leaf_count)
    for index, field in enumerate(coupled(leaves, table_ref, coupling_ref, turned_ref)):
        project(done + index, field)


def paths_kernel(turns, exchanged, upper_ref, cross_ref, high_ref, low_ref, map_ref):
    device = lax.axis_index("leaf")
    rank = upper_ref.shape[1]
    device_count = upper_ref.shape[0] // 2
    downs = {device_count: None}
    level = device_count
    while level > 4:
        node = level + device // (device_count // level)
        below = downs[level]
        matrix = upper_ref[node]
        downs[level // 2] = matrix if below is None else split_dot(dot_nn, below, *halves(matrix))
        level //= 2
    for level in sorted(downs):
        place = device // (device_count // level)
        for index in range(level):
            if level == 4:
                map_ref[level + index] = jnp.zeros((rank, rank), F32)
            else:
                above = map_ref[(level + index) // 2]
                map_ref[level + index] = split_dot(
                    dot_nt, above, *halves(upper_ref[level + index])
                )
        third = jnp.where(place % 2 == 0, place + 3, place - 3)
        for slot, other in enumerate((place - 2, place + 2, third)):
            inside = (other >= 0) & (other < level)
            matrix = cross_ref[level + place, slot]
            if downs[level] is not None:
                matrix = split_dot(dot_nn, downs[level], *halves(matrix))
            node = level + jnp.clip(other, 0, level - 1)
            map_ref[node] = map_ref[node] + jnp.where(inside, matrix, 0.0)
    zero = jnp.zeros((rank, LANES - 3 * rank), F32)
    for place, turn in enumerate(turns):
        matrix = map_ref[device_count + (device ^ turn if exchanged else turn)]
        matrix = jnp.concatenate([matrix] * 3 + [zero], axis=1)
        high, low = halves(matrix)
        high_ref[:, place * LANES : (place + 1) * LANES] = high
        low_ref[:, place * LANES : (place + 1) * LANES] = low


def far_kernel(
    tiles, path_high_ref, path_low_ref, halves_ref, term_ref, *refs,
):
    root_refs, out_ref = refs[:-1], refs[-1]
    columns, points = out_ref.shape
    pieces = []
    for rows, root_ref in zip(tiles, root_refs):
        pieces += [root_ref[row : row + columns, :] for row in rows]
    roots = jnp.concatenate(pieces, axis=1)
    field = dot_nt(roots, path_high_ref[...]) + dot_nt(roots, path_low_ref[...])
    rows = jnp.concatenate(halves(field), axis=0)
    rows = jnp.concatenate([rows, rows], axis=1)
    step = 4 * LANES
    for first in range(0, points, step):
        spots = slice(first, first + step)
        out = dot_nn(rows, halves_ref[:, spots])
        out_ref[:, spots] = term_ref[:, spots] + (out[:columns] + out[columns:])


def add_kernel(leaf_count, term_ref, *refs):
    sent_refs, (out_hbm, sum_ref, sems) = refs[:-3], refs[-3:]
    columns, points = sum_ref.shape
    width = points // leaf_count
    factors = []
    for sent_ref in sent_refs:
        powers = [
            sent_ref[:, points + first // columns * width :][:, :width]
            for first in range(0, leaf_count, columns)
        ]
        power = jnp.concatenate([p.astype(jnp.int32).astype(F32) for p in powers], axis=0)
        factors.append(jnp.exp2(power) * (1.0 / STEPS))
    chunk_count = sems.shape[0]
    step = points // chunk_count
    copies = []
    for index in range(chunk_count):
        spots = slice(index * step, (index + 1) * step)
        total = term_ref[:, spots]
        for sent_ref, factor in zip(sent_refs, factors):
            steps = sent_ref[:, spots].astype(jnp.int32).astype(F32)
            leaves = range(index * leaf_count // chunk_count, (index + 1) * leaf_count // chunk_count)
            scale = jnp.concatenate([factor[leaf : leaf + 1] for leaf in leaves], axis=1)
            total = total + steps * scale
        sum_ref[:, spots] = total
        copies += fetch(
            [(sum_ref.at[:, pl.ds(index * step, step)], out_hbm.at[:, pl.ds(index * step, step)])],
            sems.at[pl.ds(index, 1)],
        )
    for copy in copies:
        copy.wait()


def hbm(value):
    return pltpu.with_memory_space_constraint(value, pltpu.HBM)


def hint(micros):
    return pl.CostEstimate(flops=0, bytes_accessed=int(micros * 3.69e6), transcendentals=0)


def local(
    densities,
    bases,
    near_blocks,
    near_src,
    send_leaf,
    far_src,
    leaf_coupling,
    local_transfer,
    upper_transfer,
    up_coupling,
):
    leaf_devices = lax.axis_size("leaf")
    far_groups = lax.axis_size("far")
    share = lax.axis_size("mate")
    side = cube_side(leaf_devices)
    offsets = face_offsets(leaf_devices)
    columns, points = densities.shape
    leaf_count, near_count, width, _ = near_blocks.shape
    rank = bases.shape[0]
    cap = send_leaf.shape[2]
    node_count = local_transfer.shape[1]
    params = pltpu.CompilerParams(vmem_limit_bytes=16 * 2**20)
    dma = pltpu.SemaphoreType.DMA

    def rotated(value, axis, shift):
        count = lax.axis_size(axis)
        return lax.ppermute(value, axis, [(i, (i - shift) % count) for i in range(count)])

    def crossed(value, turn):
        return lax.ppermute(value, "leaf", [(i, i ^ turn) for i in range(leaf_devices)])

    sources = near_src.T
    others = [rotated(densities, "far", part) for part in range(1, far_groups)]
    send = send_leaf.transpose(1, 2, 0)
    moved = [
        densities, send, sources, far_src.T, upper_transfer, up_coupling, leaf_coupling,
        near_blocks.reshape(-1, width),
    ]
    (
        basis, dens, send, sources, far_table, upper, cross, coupling, blocks, subtree, root,
    ) = pl.pallas_call(
        up_kernel,
        out_shape=[jax.ShapeDtypeStruct(value.shape, value.dtype) for value in (bases, *moved[:-1])]
        + [jax.ShapeDtypeStruct((moved[-1].shape[0] + 16, width), BF16)]
        + [
            jax.ShapeDtypeStruct((2 * rank, points), BF16),
            jax.ShapeDtypeStruct((columns, LANES), BF16),
        ],
        in_specs=[HBM] * (2 + len(moved)),
        out_specs=[VMEM] * (3 + len(moved)),
        scratch_shapes=[
            pltpu.VMEM((rank, rank, node_count), F32),
            pltpu.VMEM((node_count * rank, LANES), F32),
            pltpu.VMEM((rank, node_count * rank), F32),
            dma((2 + len(moved),)),
        ],
        compiler_params=params,
        cost_estimate=hint(3.5),
        name="up",
    )(hbm(local_transfer[0].transpose(1, 2, 0)), hbm(bases), *map(hbm, moved))

    later_blocks, others, root = lax.optimization_barrier((blocks, others, root))
    mate_blocks = [rotated(later_blocks, "mate", part) for part in range(1, share)]

    if side == 2:
        faces = [((2 * axis, 2 * axis + 1), 2**axis) for axis in (2, 1, 0)]
    else:
        faces = [((direction,), offset) for direction, offset in enumerate(offsets)]
    chunk = (cap * far_groups + 1) * columns
    outgoing = pl.pallas_call(
        functools.partial(select_kernel, faces, far_groups),
        out_shape=[jax.ShapeDtypeStruct((chunk, LANES), BF16)] * len(faces),
        in_specs=[VMEM] * (2 + far_groups),
        out_specs=[VMEM] * len(faces),
        compiler_params=params,
        cost_estimate=hint(1),
        name="select",
    )(send, dens, root, *others)
    outgoing, dens = lax.optimization_barrier((outgoing, dens))
    first_leaves = leaf_count // 2
    turned, leaf_local = pl.pallas_call(
        couple_kernel,
        out_shape=[
            jax.ShapeDtypeStruct((leaf_count * rank, 2 * columns), BF16),
            jax.ShapeDtypeStruct((columns, first_leaves * rank), F32),
        ],
        in_specs=[VMEM] * 4,
        out_specs=[VMEM] * 2,
        compiler_params=params,
        cost_estimate=hint(2),
        name="couple",
    )(far_table, coupling, dens, basis)
    tail = cap * far_groups * columns
    if side == 2:
        arrived = [crossed(value, stride) for (_, stride), value in zip(faces, outgoing)]
        far_one, near_two, _ = (value[tail : tail + columns] for value in arrived)
        later, leaf_local = lax.optimization_barrier((arrived[0][-4 * columns :], leaf_local))
        across = crossed(later, 2)
        held = jnp.concatenate([near_two, far_one, across[-columns:]], axis=0)
        beside = crossed(held, 1)
        turns = [0] + [stride for _, stride in faces] + [6, 3, 5, 7]
        roots = [([0], root)] + [([tail], value) for value in arrived]
        roots += [([3 * columns], across), ([0, columns, 2 * columns], beside)]
    else:
        arrived = [shifted(value, "leaf", stride) for (_, stride), value in zip(faces, outgoing)]
        turns = list(range(leaf_devices))
        everyone = lax.all_gather(root, "leaf", axis=0, tiled=True)
        roots = [([turn * columns for turn in turns], everyone)]
    slots = leaf_count + len(offsets) * cap
    tables = -(-leaf_count // columns) * width
    partials = pl.pallas_call(
        functools.partial(near_kernel, faces, far_groups, share),
        out_shape=[jax.ShapeDtypeStruct((columns, points), F32)]
        + [jax.ShapeDtypeStruct((columns, points + tables), jnp.int16)] * (far_groups - 1),
        in_specs=[VMEM] * (share + far_groups + len(faces) + 1),
        out_specs=[VMEM] * far_groups,
        scratch_shapes=[pltpu.VMEM((leaf_count, width), F32)] * (far_groups - 1)
        + [
            pltpu.VMEM((slots, far_groups * columns, width), BF16),
        ],
        compiler_params=params,
        cost_estimate=hint(3),
        name="near",
    )(
        dens, *others, *arrived, blocks, *mate_blocks, leaf_local,
    )
    upper, cross, near_own = lax.optimization_barrier((upper, cross, partials[0]))
    paths = pl.pallas_call(
        functools.partial(paths_kernel, turns, side == 2),
        out_shape=[jax.ShapeDtypeStruct((rank, leaf_devices * LANES), BF16)] * 2,
        in_specs=[VMEM] * 2,
        out_specs=[VMEM] * 2,
        scratch_shapes=[pltpu.VMEM((2 * leaf_devices, rank, rank), F32)],
        compiler_params=params,
        cost_estimate=hint(0.7),
        name="paths",
    )(upper, cross)
    received = [rotated(partials[part], "far", -part) for part in range(1, far_groups)]
    partial = pl.pallas_call(
        project_kernel,
        out_shape=jax.ShapeDtypeStruct((columns, points), F32),
        in_specs=[VMEM] * 6,
        out_specs=VMEM,
        compiler_params=params,
        cost_estimate=hint(1.5),
        name="project",
    )(far_table, coupling, turned, leaf_local, basis, near_own)
    total = pl.pallas_call(
        functools.partial(far_kernel, [rows for rows, _ in roots]),
        out_shape=jax.ShapeDtypeStruct((columns, points), F32),
        in_specs=[VMEM] * (4 + len(roots)),
        out_specs=VMEM,
        compiler_params=params,
        cost_estimate=hint(0.6),
        name="far",
    )(*paths, subtree, partial, *[value for _, value in roots])
    return pl.pallas_call(
        functools.partial(add_kernel, leaf_count),
        out_shape=jax.ShapeDtypeStruct((columns, points), F32),
        in_specs=[VMEM] * (1 + len(received)),
        out_specs=HBM,
        scratch_shapes=[pltpu.VMEM((columns, points), F32), dma((4,))],
        compiler_params=params,
        cost_estimate=hint(0.5),
        name="add",
    )(total, *received)


def solution(mesh):
    leaf_devices, rhs_devices = mesh.shape["leaf"], mesh.shape["rhs"]
    share = 2 if rhs_devices % 2 == 0 else 1
    split = Mesh(
        mesh.devices.reshape(leaf_devices, rhs_devices // share, share), ("leaf", "far", "mate")
    )
    rhs = ("far", "mate")
    in_specs = (
        P(rhs, "leaf"),
        P(None, "leaf"),
        P("leaf", rhs, None, None),
        P("leaf", rhs),
        P(),
        P("leaf", None),
        P("leaf", None, None, None),
        P("leaf", None, None, None),
        P(),
        P(),
    )
    return jax.shard_map(
        local, mesh=split, in_specs=in_specs, out_specs=P(rhs, "leaf"), check_vma=False
    )
```

```python
import functools

import jax
import jax.numpy as jnp
from jax import lax
from jax.experimental import pallas as pl
from jax.experimental.pallas import tpu as pltpu
from jax.sharding import Mesh
from jax.sharding import PartitionSpec as P

FACE_SIGNS = ((1, 0), (-1, 0), (1, 1), (-1, 1), (1, 2), (-1, 2))
F32 = jnp.float32
BF16 = jnp.bfloat16
LANES = 128
STEPS = 32000.0
VMEM = pl.BlockSpec(memory_space=pltpu.VMEM)
HBM = pl.BlockSpec(memory_space=pltpu.HBM)


def cube_side(device_count):
    return max((edge_len for edge_len in range(1, 65) if edge_len**3 <= device_count))


def face_offsets(device_count):
    side_len = cube_side(device_count)
    return [face_sign * side_len**axis_pos for face_sign, axis_pos in FACE_SIGNS]


def shifted(value, axis, steps):
    count = lax.axis_size(axis)
    first, last = (max(0, -steps), min(count, count - steps))
    return lax.ppermute(value, axis, [(source, source + steps) for source in range(first, last)])


def halves(value):
    high = value.astype(BF16)
    return high, (value - high.astype(F32)).astype(BF16)


def dot_nn(left, right):
    return lax.dot_general(left, right, (((1,), (0,)), ((), ())), preferred_element_type=F32)


def dot_nt(left, right):
    return lax.dot_general(left, right, (((1,), (1,)), ((), ())), preferred_element_type=F32)


def split_dot(dot, rows, right_high, right_low):
    count = rows.shape[0]
    high, low = halves(rows)
    both = jnp.concatenate([high, low], axis=0)
    out = dot(both, right_high) + dot(both, right_low)
    return out[:count] + out[count:]


def spread_bases(block, group):
    rank, lanes = block.shape
    width = lanes // group
    zero = jnp.zeros((rank, width), block.dtype)
    rows = []
    for slot in range(group):
        pieces = [zero] * group
        pieces[slot] = block[:, slot * width : (slot + 1) * width]
        rows.append(jnp.concatenate(pieces, axis=1))
    return jnp.concatenate(rows, axis=0)


def packed_words(table):
    words = []
    for first in range(0, table.shape[0], 4):
        word = table[first : first + 1]
        for row in range(first + 1, min(first + 4, table.shape[0])):
            word = word + (table[row : row + 1] << (8 * (row - first)))
        words.append(word)
    return words


def unpacked(words, count, place):
    values = [word[0, place] for word in words]
    return [(values[row // 4] >> (8 * (row % 4))) & 255 for row in range(count)]


def fetch(pairs, sems):
    copies = []
    for index, (source, target) in enumerate(pairs):
        copy = pltpu.make_async_copy(source, target, sems.at[index])
        copy.start()
        copies.append(copy)
    return copies


def up_kernel(
    maps_hbm, bases_hbm, *refs,
):
    count = (len(refs) - 7) // 2
    hbm_refs, bases_ref, vmem_refs = refs[:count], refs[count], refs[count + 1 : 2 * count + 1]
    halves_ref, root_ref, maps_ref, spread_ref, chain_ref, sems = refs[2 * count + 1 :]
    dens_ref = vmem_refs[0]
    copies = fetch(
        [(maps_hbm, maps_ref), (bases_hbm, bases_ref), *zip(hbm_refs, vmem_refs)], sems
    )
    columns, points = dens_ref.shape
    rank, _, node_count = maps_ref.shape
    group = LANES // rank
    leaf_count = node_count // 2
    width = points // leaf_count
    copies[0].wait()
    node = lax.broadcasted_iota(jnp.int32, (node_count, LANES), 0)
    block = lax.broadcasted_iota(jnp.int32, (node_count, LANES), 1) // rank
    parent = node // 2 % group
    for first in range(0, rank, group):
        slab = maps_ref[first : first + group].reshape(group * rank, node_count).T
        turned = [slab] + [pltpu.roll(slab, turn * rank, 1) for turn in range(1, group)]
        for row in range(group):
            placed = jnp.zeros_like(slab)
            for place in range(group):
                here = (parent == place) & (block == place)
                placed = jnp.where(here, turned[(place - row) % group], placed)
            spread_ref[pl.ds(first + row, node_count, stride=rank), :] = placed
    tile = 2 * group * rank

    def children(parents, index):
        high, low = halves(spread_ref[index * tile : (index + 1) * tile, :])
        return split_dot(dot_nt, parents, high, low)

    row = lax.broadcasted_iota(jnp.int32, (rank, LANES), 0)
    lane = lax.broadcasted_iota(jnp.int32, (rank, LANES), 1)
    level = 1
    parents = jnp.where(lane == row + rank, 1.0, 0.0)
    while level < group:
        below = children(parents, 0)
        level *= 2
        parents = below[:, (level // group) * LANES : (level // group + 1) * LANES]
    chain_ref[:, LANES : 2 * LANES] = parents
    while level < leaf_count:
        for index in range(level // group, 2 * level // group):
            lanes = slice(index * LANES, (index + 1) * LANES)
            chain_ref[:, index * tile : (index + 1) * tile] = children(chain_ref[:, lanes], index)
        level *= 2
    copies[1].wait()
    copies[2].wait()
    step = group * width
    root = jnp.zeros((columns, rank), F32)
    for index in range(leaf_count // group):
        spots = slice(index * step, (index + 1) * step)
        start = (leaf_count // group + index) * LANES
        high, low = halves(bases_ref[:, spots])
        basis = split_dot(
            dot_nn, chain_ref[:, start : start + LANES],
            spread_bases(high, group), spread_bases(low, group),
        )
        high, low = halves(basis)
        halves_ref[:rank, spots] = high
        halves_ref[rank:, spots] = low
        dens = dens_ref[:, spots]
        root += dot_nt(dens, high) + dot_nt(dens, low)
    root = jnp.concatenate([root, jnp.zeros((columns, LANES - rank), F32)], axis=1)
    high = root.astype(BF16).astype(F32)
    rest = root - high
    middle = rest.astype(BF16).astype(F32)
    last = (rest - middle).astype(BF16).astype(F32)
    packed = high + pltpu.roll(middle, rank, 1) + pltpu.roll(last, 2 * rank, 1)
    root_ref[...] = packed.astype(BF16)
    for copy in copies[3:]:
        copy.wait()


def select_kernel(
    faces, far_groups, send_ref, dens_ref, root_ref, *refs,
):
    other_refs, out_refs = refs[: far_groups - 1], refs[far_groups - 1 :]
    device = lax.axis_index("leaf")
    columns = dens_ref.shape[0]
    cap, device_count = send_ref.shape[1:]
    own = lax.broadcasted_iota(jnp.int32, (cap, device_count), 1) == device
    for (directions, stride), out_ref in zip(faces, out_refs):
        table = send_ref[directions[0]]
        if len(directions) > 1:
            table = jnp.where(device // stride % 2 == 0, table, send_ref[directions[1]])
        picks = jnp.max(jnp.where(own, table.astype(F32), 0.0), axis=1, keepdims=True)
        for place in range(cap):
            leaf = picks[place, 0].astype(jnp.int32)
            for part, panel_ref in enumerate((dens_ref, *other_refs)):
                row = (place * far_groups + part) * columns
                out_ref[row : row + columns, :] = panel_ref[
                    :, pl.ds(pl.multiple_of(leaf * LANES, LANES), LANES)
                ]
        out_ref[cap * far_groups * columns :, :] = root_ref[...]


def near_kernel(
    faces, far_groups, share, *refs,
):
    source_refs, refs = refs[:share], refs[share:]
    dens_ref, refs = refs[0], refs[1:]
    other_refs, refs = refs[: far_groups - 1], refs[far_groups - 1 :]
    got_refs, refs = refs[: len(faces)], refs[len(faces) :]
    block_ref, refs = refs[0], refs[1:]
    mate_refs, refs = refs[: share - 1], refs[share - 1 :]
    refs = refs[1:]
    out_refs, refs = refs[:far_groups], refs[far_groups:]
    power_refs, refs = refs[: far_groups - 1], refs[far_groups - 1 :]
    (buffer_ref,) = refs
    columns, points = dens_ref.shape
    leaf_count, near_count, width, _ = block_ref.shape
    cap = (buffer_ref.shape[0] - leaf_count) // len(FACE_SIGNS)
    for (directions, _), got_ref in zip(faces, got_refs):
        for direction in directions:
            for place in range(cap):
                row = place * far_groups * columns
                buffer_ref[leaf_count + direction * cap + place] = got_ref[
                    row : row + far_groups * columns, :
                ]
    for part, panel_ref in enumerate((dens_ref, *other_refs)):
        rows = slice(part * columns, (part + 1) * columns)
        for leaf in range(leaf_count):
            buffer_ref[leaf, rows, :] = panel_ref[:, leaf * width : (leaf + 1) * width]
    words = packed_words(jnp.concatenate([source_ref[...] for source_ref in source_refs], axis=0))
    own_ref, sent_refs = out_refs[0], out_refs[1:]
    for leaf in range(leaf_count):
        panels = [buffer_ref[slot] for slot in unpacked(words, near_count * share, leaf)]
        blocks = [
            blocks_ref[leaf, block]
            for blocks_ref in (block_ref, *mate_refs)
            for block in range(near_count)
        ]
        total = dot_nt(jnp.concatenate(panels, axis=1), jnp.concatenate(blocks, axis=1))
        lanes = slice(leaf * width, (leaf + 1) * width)
        own_ref[:, lanes] = total[:columns]
        for part, (sent_ref, power_ref) in enumerate(zip(sent_refs, power_refs), 1):
            term = total[part * columns : (part + 1) * columns]
            peak = jnp.max(jnp.abs(term), axis=0, keepdims=True)
            power = jnp.floor(jnp.log2(jnp.maximum(peak, 2.0**-100))) + 1.0
            steps = jnp.floor(term * (STEPS * jnp.exp2(-power)) + 0.5)
            sent_ref[:, lanes] = steps.astype(jnp.int32).astype(jnp.int16)
            power_ref[leaf : leaf + 1, :] = power
    for sent_ref, power_ref in zip(sent_refs, power_refs):
        power = power_ref[...].astype(jnp.int32).astype(jnp.int16)
        for first in range(0, leaf_count, columns):
            spot = points + first // columns * width
            sent_ref[:, spot : spot + width] = power[first : first + columns]


def coupled(leaves, table_ref, coupling_ref, turned_ref):
    far_count, rank = coupling_ref.shape[1:3]
    columns = turned_ref.shape[1] // 2
    group = LANES // rank
    words = packed_words(table_ref[...])
    parts = []
    for leaf in leaves:
        maps = jnp.concatenate([coupling_ref[leaf, j] for j in range(far_count)], axis=1)
        maps = jnp.concatenate(halves(maps), axis=0)
        picked = jnp.concatenate(
            [
                turned_ref[pl.ds(pl.multiple_of(source * rank, rank), rank), :]
                for source in unpacked(words, far_count, leaf)
            ],
            axis=0,
        )
        out = dot_nn(maps, picked)
        parts.append(out[:rank] + out[rank:])
        if len(parts) == group:
            turned = jnp.concatenate(parts, axis=0).T
            yield turned[:columns] + turned[columns:]
            parts = []


def couple_kernel(
    table_ref, coupling_ref, dens_ref, bases_ref, turned_ref, out_ref,
):
    columns, points = dens_ref.shape
    leaf_count, _, rank = coupling_ref.shape[:3]
    width = points // leaf_count
    upper = lax.broadcasted_iota(jnp.int32, (rank, 2 * columns), 1) < columns
    for leaf in range(leaf_count):
        spots = slice(leaf * width, (leaf + 1) * width)
        rows = jnp.concatenate(halves(bases_ref[:, spots]), axis=0)
        dens = dens_ref[:, spots]
        twice = dot_nt(rows, jnp.concatenate([dens, dens], axis=0))
        high, low = halves(twice[:rank] + twice[rank:])
        turned_ref[leaf * rank : (leaf + 1) * rank, :] = jnp.where(
            upper, high.astype(F32), low.astype(F32)
        ).astype(BF16)
    leaves = range(out_ref.shape[1] // rank)
    for index, field in enumerate(coupled(leaves, table_ref, coupling_ref, turned_ref)):
        out_ref[:, index * LANES : (index + 1) * LANES] = field


def project_kernel(
    table_ref, coupling_ref, turned_ref, first_ref, bases_ref, near_ref, out_ref,
):
    rank, points = bases_ref.shape
    leaf_count = coupling_ref.shape[0]
    group = LANES // rank
    step = group * points // leaf_count

    def project(index, field):
        spots = slice(index * step, (index + 1) * step)
        high, low = halves(bases_ref[:, spots])
        out_ref[:, spots] = near_ref[:, spots] + split_dot(
            dot_nn, field, spread_bases(high, group), spread_bases(low, group)
        )

    done = first_ref.shape[1] // LANES
    for index in range(done):
        project(index, first_ref[:, index * LANES : (index + 1) * LANES])
    leaves = range(done * group, leaf_count)
    for index, field in enumerate(coupled(leaves, table_ref, coupling_ref, turned_ref)):
        project(done + index, field)


def paths_kernel(turns, exchanged, upper_ref, cross_ref, high_ref, low_ref, map_ref):
    device = lax.axis_index("leaf")
    rank = upper_ref.shape[1]
    device_count = upper_ref.shape[0] // 2
    downs = {device_count: None}
    level = device_count
    while level > 4:
        node = level + device // (device_count // level)
        below = downs[level]
        matrix = upper_ref[node]
        downs[level // 2] = matrix if below is None else split_dot(dot_nn, below, *halves(matrix))
        level //= 2
    for level in sorted(downs):
        place = device // (device_count // level)
        for index in range(level):
            if level == 4:
                map_ref[level + index] = jnp.zeros((rank, rank), F32)
            else:
                above = map_ref[(level + index) // 2]
                map_ref[level + index] = split_dot(
                    dot_nt, above, *halves(upper_ref[level + index])
                )
        third = jnp.where(place % 2 == 0, place + 3, place - 3)
        for slot, other in enumerate((place - 2, place + 2, third)):
            inside = (other >= 0) & (other < level)
            matrix = cross_ref[level + place, slot]
            if downs[level] is not None:
                matrix = split_dot(dot_nn, downs[level], *halves(matrix))
            node = level + jnp.clip(other, 0, level - 1)
            map_ref[node] = map_ref[node] + jnp.where(inside, matrix, 0.0)
    zero = jnp.zeros((rank, LANES - 3 * rank), F32)
    for place, turn in enumerate(turns):
        matrix = map_ref[device_count + (device ^ turn if exchanged else turn)]
        matrix = jnp.concatenate([matrix] * 3 + [zero], axis=1)
        high, low = halves(matrix)
        high_ref[:, place * LANES : (place + 1) * LANES] = high
        low_ref[:, place * LANES : (place + 1) * LANES] = low


def far_kernel(
    tiles, path_high_ref, path_low_ref, halves_ref, term_ref, *refs,
):
    root_refs, out_ref = refs[:-1], refs[-1]
    columns, points = out_ref.shape
    pieces = []
    for rows, root_ref in zip(tiles, root_refs):
        pieces += [root_ref[row : row + columns, :] for row in rows]
    roots = jnp.concatenate(pieces, axis=1)
    field = dot_nt(roots, path_high_ref[...]) + dot_nt(roots, path_low_ref[...])
    rows = jnp.concatenate(halves(field), axis=0)
    rows = jnp.concatenate([rows, rows], axis=1)
    step = 4 * LANES
    for first in range(0, points, step):
        spots = slice(first, first + step)
        out = dot_nn(rows, halves_ref[:, spots])
        out_ref[:, spots] = term_ref[:, spots] + (out[:columns] + out[columns:])


def add_kernel(leaf_count, term_ref, *refs):
    sent_refs, (out_hbm, sum_ref, sems) = refs[:-3], refs[-3:]
    columns, points = sum_ref.shape
    width = points // leaf_count
    factors = []
    for sent_ref in sent_refs:
        powers = [
            sent_ref[:, points + first // columns * width :][:, :width]
            for first in range(0, leaf_count, columns)
        ]
        power = jnp.concatenate([p.astype(jnp.int32).astype(F32) for p in powers], axis=0)
        factors.append(jnp.exp2(power) * (1.0 / STEPS))
    chunk_count = sems.shape[0]
    step = points // chunk_count
    copies = []
    for index in range(chunk_count):
        spots = slice(index * step, (index + 1) * step)
        total = term_ref[:, spots]
        for sent_ref, factor in zip(sent_refs, factors):
            steps = sent_ref[:, spots].astype(jnp.int32).astype(F32)
            leaves = range(index * leaf_count // chunk_count, (index + 1) * leaf_count // chunk_count)
            scale = jnp.concatenate([factor[leaf : leaf + 1] for leaf in leaves], axis=1)
            total = total + steps * scale
        sum_ref[:, spots] = total
        copies += fetch(
            [(sum_ref.at[:, pl.ds(index * step, step)], out_hbm.at[:, pl.ds(index * step, step)])],
            sems.at[pl.ds(index, 1)],
        )
    for copy in copies:
        copy.wait()


def hbm(value):
    return pltpu.with_memory_space_constraint(value, pltpu.HBM)


def hint(micros):
    return pl.CostEstimate(flops=0, bytes_accessed=int(micros * 3.69e6), transcendentals=0)


def local(
    densities,
    bases,
    near_blocks,
    near_src,
    send_leaf,
    far_src,
    leaf_coupling,
    local_transfer,
    upper_transfer,
    up_coupling,
):
    leaf_devices = lax.axis_size("leaf")
    far_groups = lax.axis_size("far")
    share = lax.axis_size("mate")
    side = cube_side(leaf_devices)
    offsets = face_offsets(leaf_devices)
    columns, points = densities.shape
    leaf_count, near_count, width, _ = near_blocks.shape
    rank = bases.shape[0]
    cap = send_leaf.shape[2]
    node_count = local_transfer.shape[1]
    params = pltpu.CompilerParams(vmem_limit_bytes=16 * 2**20)
    dma = pltpu.SemaphoreType.DMA

    def rotated(value, axis, shift):
        count = lax.axis_size(axis)
        return lax.ppermute(value, axis, [(i, (i - shift) % count) for i in range(count)])

    def crossed(value, turn):
        return lax.ppermute(value, "leaf", [(i, i ^ turn) for i in range(leaf_devices)])

    sources = near_src.T
    others = [rotated(densities, "far", part) for part in range(1, far_groups)]
    all_sources = [sources] + [rotated(sources, "mate", part) for part in range(1, share)]
    send = send_leaf.transpose(1, 2, 0)
    moved = [
        densities, send, sources, far_src.T, upper_transfer, up_coupling, leaf_coupling, near_blocks,
    ]
    (
        basis, dens, send, sources, far_table, upper, cross, coupling, blocks, subtree, root,
    ) = pl.pallas_call(
        up_kernel,
        out_shape=[jax.ShapeDtypeStruct(value.shape, value.dtype) for value in (bases, *moved)]
        + [
            jax.ShapeDtypeStruct((2 * rank, points), BF16),
            jax.ShapeDtypeStruct((columns, LANES), BF16),
        ],
        in_specs=[HBM] * (2 + len(moved)),
        out_specs=[VMEM] * (3 + len(moved)),
        scratch_shapes=[
            pltpu.VMEM((rank, rank, node_count), F32),
            pltpu.VMEM((node_count * rank, LANES), F32),
            pltpu.VMEM((rank, node_count * rank), F32),
            dma((2 + len(moved),)),
        ],
        compiler_params=params,
        cost_estimate=hint(3.5),
        name="up",
    )(hbm(local_transfer[0].transpose(1, 2, 0)), hbm(bases), *map(hbm, moved))
    all_sources[0] = sources

    later_blocks, others, all_sources, root = lax.optimization_barrier(
        (blocks, others, all_sources, root)
    )
    mate_blocks = [rotated(later_blocks, "mate", part) for part in range(1, share)]

    if side == 2:
        faces = [((2 * axis, 2 * axis + 1), 2**axis) for axis in (2, 1, 0)]
    else:
        faces = [((direction,), offset) for direction, offset in enumerate(offsets)]
    chunk = (cap * far_groups + 1) * columns
    outgoing = pl.pallas_call(
        functools.partial(select_kernel, faces, far_groups),
        out_shape=[jax.ShapeDtypeStruct((chunk, LANES), BF16)] * len(faces),
        in_specs=[VMEM] * (2 + far_groups),
        out_specs=[VMEM] * len(faces),
        compiler_params=params,
        cost_estimate=hint(1),
        name="select",
    )(send, dens, root, *others)
    outgoing, dens = lax.optimization_barrier((outgoing, dens))
    first_leaves = leaf_count // 2
    turned, leaf_local = pl.pallas_call(
        couple_kernel,
        out_shape=[
            jax.ShapeDtypeStruct((leaf_count * rank, 2 * columns), BF16),
            jax.ShapeDtypeStruct((columns, first_leaves * rank), F32),
        ],
        in_specs=[VMEM] * 4,
        out_specs=[VMEM] * 2,
        compiler_params=params,
        cost_estimate=hint(2),
        name="couple",
    )(far_table, coupling, dens, basis)
    tail = cap * far_groups * columns
    if side == 2:
        arrived = [crossed(value, stride) for (_, stride), value in zip(faces, outgoing)]
        far_one, near_two, _ = (value[tail : tail + columns] for value in arrived)
        later, leaf_local = lax.optimization_barrier((arrived[0][-4 * columns :], leaf_local))
        across = crossed(later, 2)
        held = jnp.concatenate([near_two, far_one, across[-columns:]], axis=0)
        beside = crossed(held, 1)
        turns = [0] + [stride for _, stride in faces] + [6, 3, 5, 7]
        roots = [([0], root)] + [([tail], value) for value in arrived]
        roots += [([3 * columns], across), ([0, columns, 2 * columns], beside)]
    else:
        arrived = [shifted(value, "leaf", stride) for (_, stride), value in zip(faces, outgoing)]
        turns = list(range(leaf_devices))
        everyone = lax.all_gather(root, "leaf", axis=0, tiled=True)
        roots = [([turn * columns for turn in turns], everyone)]
    slots = leaf_count + len(offsets) * cap
    tables = -(-leaf_count // columns) * width
    partials = pl.pallas_call(
        functools.partial(near_kernel, faces, far_groups, share),
        out_shape=[jax.ShapeDtypeStruct((columns, points), F32)]
        + [jax.ShapeDtypeStruct((columns, points + tables), jnp.int16)] * (far_groups - 1),
        in_specs=[VMEM] * (2 * share + far_groups + len(faces) + 1),
        out_specs=[VMEM] * far_groups,
        scratch_shapes=[pltpu.VMEM((leaf_count, width), F32)] * (far_groups - 1)
        + [
            pltpu.VMEM((slots, far_groups * columns, width), BF16),
        ],
        compiler_params=params,
        cost_estimate=hint(3),
        name="near",
    )(
        *all_sources, dens, *others, *arrived, blocks, *mate_blocks, leaf_local,
    )
    upper, cross, near_own = lax.optimization_barrier((upper, cross, partials[0]))
    paths = pl.pallas_call(
        functools.partial(paths_kernel, turns, side == 2),
        out_shape=[jax.ShapeDtypeStruct((rank, leaf_devices * LANES), BF16)] * 2,
        in_specs=[VMEM] * 2,
        out_specs=[VMEM] * 2,
        scratch_shapes=[pltpu.VMEM((2 * leaf_devices, rank, rank), F32)],
        compiler_params=params,
        cost_estimate=hint(0.7),
        name="paths",
    )(upper, cross)
    received = [rotated(partials[part], "far", -part) for part in range(1, far_groups)]
    partial = pl.pallas_call(
        project_kernel,
        out_shape=jax.ShapeDtypeStruct((columns, points), F32),
        in_specs=[VMEM] * 6,
        out_specs=VMEM,
        compiler_params=params,
        cost_estimate=hint(1.5),
        name="project",
    )(far_table, coupling, turned, leaf_local, basis, near_own)
    total = pl.pallas_call(
        functools.partial(far_kernel, [rows for rows, _ in roots]),
        out_shape=jax.ShapeDtypeStruct((columns, points), F32),
        in_specs=[VMEM] * (4 + len(roots)),
        out_specs=VMEM,
        compiler_params=params,
        cost_estimate=hint(0.6),
        name="far",
    )(*paths, subtree, partial, *[value for _, value in roots])
    return pl.pallas_call(
        functools.partial(add_kernel, leaf_count),
        out_shape=jax.ShapeDtypeStruct((columns, points), F32),
        in_specs=[VMEM] * (1 + len(received)),
        out_specs=HBM,
        scratch_shapes=[pltpu.VMEM((columns, points), F32), dma((2,))],
        compiler_params=params,
        cost_estimate=hint(0.5),
        name="add",
    )(total, *received)


def solution(mesh):
    leaf_devices, rhs_devices = mesh.shape["leaf"], mesh.shape["rhs"]
    share = 2 if rhs_devices % 2 == 0 else 1
    split = Mesh(
        mesh.devices.reshape(leaf_devices, rhs_devices // share, share), ("leaf", "far", "mate")
    )
    rhs = ("far", "mate")
    in_specs = (
        P(rhs, "leaf"),
        P(None, "leaf"),
        P("leaf", rhs, None, None),
        P("leaf", rhs),
        P(),
        P("leaf", None),
        P("leaf", None, None, None),
        P("leaf", None, None, None),
        P(),
        P(),
    )
    return jax.shard_map(
        local, mesh=split, in_specs=in_specs, out_specs=P(rhs, "leaf"), check_vma=False
    )
```
